32 devices in a mesh: seq: 4 (over y, core), chan: 8 (over z, x).
Axes of the slice: x: 2, y: 2, z: 4, core: 2. Of those that a mesh axis runs over, the one named last changes fastest.
Arguments:
- queries: bfloat16 [8, 512, 4096], P('chan', 'seq'), may hold values from -256 to 256
- keys: bfloat16 [8, 512, 1024], P('chan', 'seq'), may hold values from -6 to 6
- values: bfloat16 [8, 512, 1024], P('chan', 'seq'), may hold values from -6 to 6
- doc_lengths: int32 [8, 16], P('chan'), may hold values from 1 to 256, 512 in all within a row
- rank_in: bfloat16 [4096, 256], replicated, may hold values from -0.09375 to 0.09375
- bc_weight: bfloat16 [4096, 32], replicated, may hold values from -0.09375 to 0.09375
- rank_out: bfloat16 [256, 4096], replicated, may hold values from -0.375 to 0.375
- dt_bias: float32 [4096], replicated, may hold values from -8 to -6
- a_log: float32 [4096, 16], replicated, may hold values from -10 to 4
- skip_gain: float32 [4096], replicated, may hold values from 0.5 to 1.5
Outputs:
- attn_out: bfloat16 [8, 512, 4096], P('chan', 'seq')
- ssm_out: bfloat16 [8, 512, 4096], P('chan', None, 'seq')
The draws below stay inside these ranges and needn't reach their ends.
Inputs may be any that keep to these rules, and one draw needn't show every extreme that they name: `doc_lengths`: each row's entries are the lengths of its 16 documents in order and sum to 512; some document of every row is 256 long.
All inputs are finite; a program needn't handle non-finite values.
Results may differ from the reference program's by a relative error of at most 0.0091.
Values may be sent and summed in bfloat16 or wider, within the bound.
No kernel may reach another device: no remote copies, remote signals or barrier semaphores. Data moves between devices by JAX's collectives and lax.ppermute only.
A program may use at most 128 MiB of HBM per device.

```python
import math
import jax
import jax.numpy as jnp
import numpy as np
from jax import lax

QUERY_HEADS = 32
KEY_VALUE_HEADS = 8
HEAD_SIZE = 128
NS = 16
RANK = 256
CH = 4096
TOK_DEV = 128
REACH = 2
NDOCS = 16
ROW_POSITIONS = 512
STREAM_ROWS = 8
STREAM = 4096
DOCMAX = 256
N_SEQ = 4


def paired_heads(key):
    base_key = jax.random.fold_in(key, 11)
    key_sample, query_draw = jax.random.split(base_key, 2)
    rows_of_keys = jax.random.truncated_normal(key_sample, -6.0, 6.0, (STREAM_ROWS, ROW_POSITIONS, KEY_VALUE_HEADS * HEAD_SIZE), jnp.float32)
    rows_of_queries = jax.random.truncated_normal(query_draw, -6.0, 6.0, (STREAM_ROWS, ROW_POSITIONS, QUERY_HEADS * HEAD_SIZE), jnp.float32)
    return (rows_of_queries, rows_of_keys)


def draw_queries(key, part):
    return paired_heads(key)[0].astype(jnp.bfloat16)


def draw_keys(key, part):
    return paired_heads(key)[1].astype(jnp.bfloat16)


def draw_a_log(key, part):
    flip_draw, slow_draw, fast_draw = jax.random.split(jax.random.fold_in(key, 23), 3)
    slow_share = 0.5
    slow_mask = jax.random.bernoulli(flip_draw, slow_share, (CH, NS))
    chain_log = math.log(0.0015 * STREAM)
    slow_values = jax.random.uniform(slow_draw, (CH, NS), jnp.float32, math.log(0.1), 0.0) - chain_log
    fast_values = jax.random.uniform(fast_draw, (CH, NS), jnp.float32, -chain_log, -math.log(0.0015 * 30.0))
    return jnp.where(slow_mask, slow_values, fast_values)


def steps_of(own_key, extent, shards, smallest, largest):
    def one(axis_at, parts):
        draws = jax.random.uniform(jax.random.fold_in(jax.random.fold_in(own_key, 6), axis_at), (parts,), jnp.float32, smallest / len(shards), largest / len(shards))
        return jnp.repeat(jnp.exp(draws), extent[axis_at] // parts).reshape((-1,) + (1,) * (len(extent) - axis_at - 1))

    loudness = one(*shards[0])
    for cut in shards[1:]:
        loudness = loudness * one(*cut)
    return loudness


def split_up(count, total, limit, skew):
    loads = [(1 << 20) // math.isqrt(standing ** skew) + 1 for standing in range(2, count + 1)]
    spare, holding = total - limit - (count - 1), [1] * (count - 1)
    while spare > 0:
        free = [i for i in range(count - 1) if holding[i] < limit]
        mass, remaining = sum([loads[i] for i in free]), spare
        for i in free:
            addition = min(limit - holding[i], max(1, remaining * loads[i] // mass), spare)
            holding[i] = holding[i] + addition
            spare = spare - addition
    return np.array([limit] + holding)


def ragged_sizes(rng, count, total, bound, lean):
    if count == 2:
        one = jax.random.randint(rng, (), max(1, total - bound), min(bound, total - 1) + 1)
        return jnp.stack([one, total - one])
    tallies = jnp.asarray(split_up(count, total, bound, lean), jnp.int32)
    couples = (count - 1) // 2
    giver, receiver = tallies[1:1 + 2 * couples:2], tallies[2:2 + 2 * couples:2]
    slack = jnp.minimum(giver - 1, bound - receiver)
    shifted = jax.random.randint(jax.random.fold_in(rng, 1), (couples,), 0, 1 << 20) % (slack + 1)
    tallies = tallies.at[1:1 + 2 * couples:2].set(giver - shifted).at[2:2 + 2 * couples:2].set(receiver + shifted)
    return tallies[jax.random.permutation(jax.random.fold_in(rng, 2), count)]


def centred(own_key, dims, scale, reach, shards=(), kind=jnp.bfloat16):
    array = jax.random.normal(own_key, dims, jnp.float32) * scale
    if len(shards) > 0:
        array = steps_of(own_key, dims, shards, -0.22, 0.18) * array
    return jnp.clip(array, min=-reach, max=reach).astype(kind)


def setup_inputs(seed: int = 0) -> dict:
    seeds = jax.random.split(jax.random.key(seed), 11)
    queries = draw_queries(jax.random.fold_in(seeds[10], 71), 0)
    keys = draw_keys(jax.random.fold_in(seeds[10], 71), 0)
    values = centred(seeds[2], (STREAM_ROWS, ROW_POSITIONS, KEY_VALUE_HEADS * HEAD_SIZE), 1.0, 6.0, ((0, 8), (1, 4)))
    doc_lengths = jax.vmap(lambda own: ragged_sizes(own, NDOCS, ROW_POSITIONS, DOCMAX, 2))(jax.random.split(seeds[3], STREAM_ROWS)).reshape((STREAM_ROWS, NDOCS)).astype(jnp.int32)
    rank_in = centred(seeds[4], (CH, RANK), CH ** -0.5, 0.09375)
    bc_weight = centred(seeds[5], (CH, 2 * NS), CH ** -0.5, 0.09375)
    rank_out = centred(seeds[6], (RANK, CH), RANK ** -0.5, 0.375)
    dt_bias = jnp.clip(jax.random.uniform(seeds[7], (CH,), jnp.float32, -8.0, -6.0), -8.0, -6.0)
    a_log = draw_a_log(jax.random.fold_in(seeds[10], 71), 0)
    skip_gain = jnp.clip(jax.random.uniform(seeds[9], (CH,), jnp.float32, 0.5, 1.5), 0.5, 1.5)
    return {"queries": queries, "keys": keys, "values": values, "doc_lengths": doc_lengths, "rank_in": rank_in, "bc_weight": bc_weight, "rank_out": rank_out, "dt_bias": dt_bias, "a_log": a_log, "skip_gain": skip_gain}


masked_fill = -1e+30

def doc_numbers(positions, doc_bounds):
    return lax.optimization_barrier(jnp.sum((doc_bounds[None, :] <= positions[:, None]).astype(jnp.int32), axis=1))

def attend_core(query_tile, key_tile, value_tile, query_pos, key_pos, doc_bounds):
    query_row_count = query_tile.shape[0]
    key_row_count = key_tile.shape[0]
    positions_per_row = QUERY_HEADS // KEY_VALUE_HEADS
    heads_for_queries = query_tile.astype(jnp.float32).reshape(query_row_count, KEY_VALUE_HEADS, positions_per_row, HEAD_SIZE)
    heads_for_keys = key_tile.astype(jnp.float32).reshape(key_row_count, KEY_VALUE_HEADS, HEAD_SIZE)
    heads_for_values = value_tile.astype(jnp.float32).reshape(key_row_count, KEY_VALUE_HEADS, HEAD_SIZE)
    scores = jnp.einsum('tgjd,kgd->gjtk', heads_for_queries, heads_for_keys) * (1.0 / math.sqrt(HEAD_SIZE))
    allowed = (key_pos[None, :] <= query_pos[:, None]) & (key_pos[None, :] >= 0)
    allowed = allowed & (doc_numbers(key_pos, doc_bounds)[None, :] == doc_numbers(query_pos, doc_bounds)[:, None])
    scores = jnp.where(allowed[None, None], scores, masked_fill)
    peak = lax.optimization_barrier(jnp.max(scores, axis=3, keepdims=True))
    raw_weights = jnp.exp(scores - peak)
    weights = (raw_weights / lax.optimization_barrier(jnp.sum(raw_weights, axis=3, keepdims=True))).astype(jnp.bfloat16)
    mixed = jnp.einsum('gjtk,kgd->tgjd', weights.astype(jnp.float32), heads_for_values)
    return mixed.reshape(query_row_count, QUERY_HEADS * HEAD_SIZE).astype(jnp.bfloat16)

def reference(queries, keys, values, doc_lengths, rank_in, bc_weight, rank_out, dt_bias, a_log, skip_gain):
    padding_rows = REACH * TOK_DEV
    window_rows = padding_rows + TOK_DEV

    def attend_row(row_data):
        query_row, single_key_row, single_value_row, row_lengths = row_data
        doc_bounds = jnp.cumsum(row_lengths).astype(jnp.int32)
        padded_keys = jnp.concatenate([jnp.zeros((padding_rows, KEY_VALUE_HEADS * HEAD_SIZE), single_key_row.dtype), single_key_row], axis=0)
        padded_values = jnp.concatenate([jnp.zeros((padding_rows, KEY_VALUE_HEADS * HEAD_SIZE), single_value_row.dtype), single_value_row], axis=0)

        def attend_block(block_index):
            first_row = (block_index * TOK_DEV).astype(jnp.int32)
            query_tile = lax.dynamic_slice_in_dim(query_row, first_row, TOK_DEV, 0)
            key_tile = lax.dynamic_slice_in_dim(padded_keys, first_row, window_rows, 0)
            value_tile = lax.dynamic_slice_in_dim(padded_values, first_row, window_rows, 0)
            query_pos = first_row + jnp.arange(TOK_DEV, dtype=jnp.int32)
            key_pos = first_row - padding_rows + jnp.arange(window_rows, dtype=jnp.int32)
            return attend_core(query_tile, key_tile, value_tile, query_pos, key_pos, doc_bounds)
        block_outs = lax.map(attend_block, jnp.arange(N_SEQ, dtype=jnp.int32))
        return block_outs.reshape(ROW_POSITIONS, QUERY_HEADS * HEAD_SIZE)
    attn_out = lax.map(attend_row, (queries, keys, values, doc_lengths))
    stream = attn_out.reshape(STREAM, CH)
    dt_low = jnp.dot(stream, rank_in, preferred_element_type=jnp.float32).astype(jnp.bfloat16)
    state_maps = jnp.dot(stream, bc_weight, preferred_element_type=jnp.float32)
    decay_rates = -jnp.exp(a_log)

    def outer_step(carry_state, block_data):
        low_block, maps_block, input_block = block_data
        step_sizes = jax.nn.softplus(jnp.dot(low_block, rank_out, preferred_element_type=jnp.float32) + dt_bias)
        input_float = input_block.astype(jnp.float32)

        def inner_step(inner_state, item_data):
            step_row, input_row, maps_row = item_data
            next_state = jnp.exp(step_row[:, None] * decay_rates) * inner_state
            next_state = next_state + (step_row * input_row)[:, None] * maps_row[None, :NS]
            return (next_state, lax.optimization_barrier(jnp.sum(next_state * maps_row[None, NS:], axis=1)))
        carry_state, outputs = lax.scan(inner_step, carry_state, (step_sizes, input_float, maps_block))
        return (carry_state, outputs + skip_gain[None, :] * input_float)
    block_count = STREAM // TOK_DEV
    start_state = jnp.zeros((CH, NS), jnp.float32)
    _, outputs = lax.scan(outer_step, start_state, (dt_low.reshape(block_count, TOK_DEV, RANK), state_maps.reshape(block_count, TOK_DEV, 2 * NS), stream.reshape(block_count, TOK_DEV, CH)))
    ssm_out = outputs.reshape(STREAM_ROWS, ROW_POSITIONS, CH).astype(jnp.bfloat16)
    return (attn_out, ssm_out)
```

```python
import functools
import math

import jax
import jax.numpy as jnp
from jax import lax
from jax.experimental import pallas as pl
from jax.experimental.pallas import tpu as pltpu
from jax.sharding import PartitionSpec as P

QUERY_HEADS = 32
KEY_VALUE_HEADS = 8
HEAD_SIZE = 128
GROUP = QUERY_HEADS // KEY_VALUE_HEADS
NS = 16
RANK = 256
REACH = 2
EXTRA = 384
LANES = 128
UNROLL = 8
LOG2E = 1.4426950408889634

masked_fill = -1e30


def from_behind(value, axis, steps):
    count = lax.axis_size(axis)
    return lax.ppermute(value, axis, [(source, source + steps) for source in range(count - steps)])


def attend_kernel(
    place_ref, doc_ref, q_ref, k0_ref, k1_ref, k2_ref, v0_ref, v1_ref, v2_ref, rank_ref, map_ref,
    attn_ref, pack_ref, mask_ref, low_ref, bc_ref, *, width,
):
    group = pl.program_id(0)
    rows = q_ref.shape[0]
    window = (REACH + 1) * rows
    place = place_ref[0]

    @pl.when(group == 0)
    def _():
        first = place * rows
        query_pos = first + lax.broadcasted_iota(jnp.int32, (rows, window), 0)
        key_pos = first - REACH * rows + lax.broadcasted_iota(jnp.int32, (rows, window), 1)
        start = jnp.zeros((rows, window), jnp.int32)
        bound = jnp.int32(0)
        for doc in range(doc_ref.shape[1]):
            bound = bound + doc_ref[0, doc]
            start = jnp.where(query_pos >= bound, bound, start)
        allowed = (key_pos >= start) & (key_pos <= query_pos)
        mask_ref[...] = jnp.where(allowed, 0.0, 1.0)
        low_ref[...] = jnp.zeros_like(low_ref)
        bc_ref[...] = jnp.zeros_like(bc_ref)

    keys = jnp.concatenate([k0_ref[...], k1_ref[...], k2_ref[...]], axis=0)
    values = jnp.concatenate([v0_ref[...], v1_ref[...], v2_ref[...]], axis=0)
    scale = LOG2E / math.sqrt(HEAD_SIZE)
    parts = []
    for item in range(GROUP):
        query = q_ref[:, item * HEAD_SIZE : (item + 1) * HEAD_SIZE]
        scores = lax.dot_general(
            query, keys, (((1,), (1,)), ((), ())), preferred_element_type=jnp.float32
        )
        scores = jnp.where(mask_ref[...] == 0.0, scores, masked_fill)
        peak = jnp.max(scores, axis=1, keepdims=True)
        raw = jnp.exp2((scores - peak) * scale)
        total = jnp.sum(raw, axis=1, keepdims=True)
        weights = (raw * (1.0 / total)).astype(jnp.bfloat16)
        mixed = jnp.dot(weights, values, preferred_element_type=jnp.float32).astype(jnp.bfloat16)
        parts.append(mixed)
        attn_ref[:, item * HEAD_SIZE : (item + 1) * HEAD_SIZE] = mixed
        column = (group * GROUP + item) * HEAD_SIZE
        owner = column // width
        offset = pl.multiple_of(column - owner * width, HEAD_SIZE)
        pack_ref[owner, :, pl.ds(offset, HEAD_SIZE)] = mixed
    block = jnp.concatenate(parts, axis=1)
    low_ref[...] += jnp.dot(block, rank_ref[...], preferred_element_type=jnp.float32)
    bc_ref[...] += jnp.dot(block, map_ref[...], preferred_element_type=jnp.float32)

    @pl.when(group == pl.num_programs(0) - 1)
    def _():
        low = low_ref[...].astype(jnp.bfloat16)
        coarse = bc_ref[...].astype(jnp.bfloat16)
        fine = (bc_ref[...] - coarse.astype(jnp.float32)).astype(jnp.bfloat16)
        rest = jnp.zeros((rows, LANES - 4 * NS), jnp.bfloat16)
        maps = jnp.concatenate([coarse, fine, rest], axis=1)
        for owner in range(pack_ref.shape[0]):
            pack_ref[owner, :, width : width + RANK] = low
            pack_ref[owner, :, width + RANK : width + EXTRA] = maps


def attend(place, doc_lengths, queries, keys, values, rank_in, bc_weight, owners):
    rows, columns = queries.shape
    width = columns // owners
    wide = GROUP * HEAD_SIZE

    def columns_at(size):
        return pl.BlockSpec((rows, size), lambda g, s: (0, g))

    return pl.pallas_call(
        functools.partial(attend_kernel, width=width),
        grid_spec=pltpu.PrefetchScalarGridSpec(
            num_scalar_prefetch=1,
            grid=(KEY_VALUE_HEADS,),
            in_specs=[pl.BlockSpec(memory_space=pltpu.SMEM), columns_at(wide)]
            + [columns_at(HEAD_SIZE)] * 6
            + [
                pl.BlockSpec((wide, RANK), lambda g, s: (g, 0)),
                pl.BlockSpec((wide, 2 * NS), lambda g, s: (g, 0)),
            ],
            out_specs=[
                columns_at(wide),
                pl.BlockSpec((owners, rows, width + EXTRA), lambda g, s: (0, 0, 0)),
            ],
            scratch_shapes=[
                pltpu.VMEM((rows, (REACH + 1) * rows), jnp.float32),
                pltpu.VMEM((rows, RANK), jnp.float32),
                pltpu.VMEM((rows, 2 * NS), jnp.float32),
            ],
        ),
        out_shape=[
            jax.ShapeDtypeStruct((rows, columns), jnp.bfloat16),
            jax.ShapeDtypeStruct((owners, rows, width + EXTRA), jnp.bfloat16),
        ],
        compiler_params=pltpu.CompilerParams(vmem_limit_bytes=32 << 20),
        name="attend",
    )(place, doc_lengths, queries, *keys, *values, rank_in, bc_weight)


def spread_maps(maps, spread_ref, first, count):
    rows = maps.shape[0]
    for item in range(count):
        row = lax.broadcasted_iota(jnp.int32, (LANES, LANES), 0)
        pick = (row == first + item) | (row == first + item + 2 * NS)
        chosen = jnp.where(pick, 1.0, 0.0).astype(jnp.bfloat16)
        spread_ref[item * rows : (item + 1) * rows, :] = jnp.dot(
            maps, chosen, preferred_element_type=jnp.float32
        )


def final_kernel(
    place_ref, pack_ref, cols_ref, bias_ref, rates_ref, steps_ref, drive_ref, carry_ref,
    state_ref, sum_ref, spread_ref,
):
    block = pl.program_id(0)
    rows = pack_ref.shape[1]
    width = cols_ref.shape[1]
    tile = width // LANES

    @pl.when(block == 0)
    def _():
        state_ref[...] = jnp.zeros_like(state_ref)
        sum_ref[...] = jnp.zeros_like(sum_ref)

    low = pack_ref[0, :, width : width + RANK]
    logits = jnp.dot(low, cols_ref[...], preferred_element_type=jnp.float32) + bias_ref[...]
    steps = jnp.maximum(logits, 0.0) + jnp.log1p(jnp.exp(-jnp.abs(logits)))
    drive = steps * pack_ref[0, :, :width].astype(jnp.float32)
    for item in range(tile):
        lanes = slice(item * LANES, (item + 1) * LANES)
        steps_ref[pl.ds(item, rows, stride=tile), :] = steps[:, lanes]
        drive_ref[pl.ds(item, rows, stride=tile), :] = drive[:, lanes]
    spread_maps(pack_ref[0, :, width + RANK :], spread_ref, 0, NS)

    def some(index, held):
        total, states = held[0], list(held[1:])
        base = index * UNROLL
        for near in range(UNROLL):
            at = pl.multiple_of((base + near) * tile, tile)
            step = steps_ref[pl.ds(at, tile), :]
            push = drive_ref[pl.ds(at, tile), :]
            total = total + step
            for n in range(NS):
                rate = rates_ref[n * tile : (n + 1) * tile, :]
                into = spread_ref[pl.ds(n * rows + base + near, 1), :]
                states[n] = jnp.exp2(step * rate) * states[n] + push * into
        return (total, *states)

    held = (sum_ref[...],) + tuple(
        state_ref[n * tile : (n + 1) * tile, :] for n in range(NS)
    )
    held = lax.fori_loop(0, rows // UNROLL, some, held)
    sum_ref[...] = held[0]
    for n in range(NS):
        state_ref[n * tile : (n + 1) * tile, :] = held[1 + n]

    @pl.when(block == pl.num_programs(0) - 1)
    def _():
        for target in range(carry_ref.shape[0]):
            carry_ref[target, : NS * tile, :] = state_ref[...]
            carry_ref[target, NS * tile :, :] = sum_ref[...]


def final_states(place, packed, rank_out, dt_bias, rates, targets):
    blocks, rows, packed_width = packed.shape
    width = packed_width - EXTRA
    tile = width // LANES
    folded = jax.ShapeDtypeStruct((blocks * rows * tile, LANES), jnp.float32)
    return pl.pallas_call(
        final_kernel,
        grid_spec=pltpu.PrefetchScalarGridSpec(
            num_scalar_prefetch=1,
            grid=(blocks,),
            in_specs=[
                pl.BlockSpec((1, rows, packed_width), lambda b, s: (b, 0, 0)),
                pl.BlockSpec((RANK, width), lambda b, s: (0, s[0])),
                pl.BlockSpec((1, width), lambda b, s: (0, s[0])),
                pl.BlockSpec((NS * tile, LANES), lambda b, s: (0, 0)),
            ],
            out_specs=[
                pl.BlockSpec((rows * tile, LANES), lambda b, s: (b, 0)),
                pl.BlockSpec((rows * tile, LANES), lambda b, s: (b, 0)),
                pl.BlockSpec((targets, (NS + 1) * tile, LANES), lambda b, s: (0, 0, 0)),
            ],
            scratch_shapes=[
                pltpu.VMEM((NS * tile, LANES), jnp.float32),
                pltpu.VMEM((tile, LANES), jnp.float32),
                pltpu.VMEM((NS * rows, LANES), jnp.float32),
            ],
        ),
        out_shape=[
            folded,
            folded,
            jax.ShapeDtypeStruct((targets, (NS + 1) * tile, LANES), jnp.float32),
        ],
        compiler_params=pltpu.CompilerParams(vmem_limit_bytes=32 << 20),
        name="final_states",
    )(place, packed, rank_out, dt_bias, rates)


def scan_kernel(
    place_ref, pack_ref, gain_ref, rates_ref, steps_ref, drive_ref, carry_ref, out_ref,
    state_ref, spread_ref, folded_ref,
):
    block = pl.program_id(0)
    rows = pack_ref.shape[1]
    width = out_ref.shape[1]
    tile = width // LANES

    @pl.when(block == 0)
    def _():
        state_ref[...] = jnp.zeros_like(state_ref)

        def compose(row, nothing):
            total = carry_ref[row, NS * tile :, :]
            for n in range(NS):
                part = slice(n * tile, (n + 1) * tile)
                decay = jnp.exp2(rates_ref[part, :] * total)
                state_ref[part, :] = decay * state_ref[part, :] + carry_ref[row, part, :]
            return nothing

        lax.fori_loop(0, place_ref[0], compose, 0)

    spread_maps(pack_ref[0, :, width + RANK :], spread_ref, 0, 2 * NS)

    def some(index, states):
        states = list(states)
        base = index * UNROLL
        for near in range(UNROLL):
            at = pl.multiple_of((base + near) * tile, tile)
            step = steps_ref[pl.ds(at, tile), :]
            push = drive_ref[pl.ds(at, tile), :]
            sums = [None, None]
            for n in range(NS):
                rate = rates_ref[n * tile : (n + 1) * tile, :]
                into = spread_ref[pl.ds(n * rows + base + near, 1), :]
                out_of = spread_ref[pl.ds((NS + n) * rows + base + near, 1), :]
                states[n] = jnp.exp2(step * rate) * states[n] + push * into
                term = states[n] * out_of
                sums[n % 2] = term if sums[n % 2] is None else sums[n % 2] + term
            folded_ref[pl.ds(at, tile), :] = sums[0] + sums[1]
        return tuple(states)

    held = tuple(state_ref[n * tile : (n + 1) * tile, :] for n in range(NS))
    held = lax.fori_loop(0, rows // UNROLL, some, held)
    for n in range(NS):
        state_ref[n * tile : (n + 1) * tile, :] = held[n]
    for item in range(tile):
        lanes = slice(item * LANES, (item + 1) * LANES)
        direct = gain_ref[:, lanes] * pack_ref[0, :, lanes].astype(jnp.float32)
        mixed = folded_ref[pl.ds(item, rows, stride=tile), :]
        out_ref[:, lanes] = (mixed + direct).astype(jnp.bfloat16)


def scan_rows(places, packed, skip_gain, rates, steps, drive, carries):
    blocks, rows, packed_width = packed.shape
    width = packed_width - EXTRA
    tile = width // LANES
    folded = pl.BlockSpec((rows * tile, LANES), lambda b, s: (b, 0))
    return pl.pallas_call(
        scan_kernel,
        grid_spec=pltpu.PrefetchScalarGridSpec(
            num_scalar_prefetch=1,
            grid=(blocks,),
            in_specs=[
                pl.BlockSpec((1, rows, packed_width), lambda b, s: (b, 0, 0)),
                pl.BlockSpec((1, width), lambda b, s: (0, s[1])),
                pl.BlockSpec((NS * tile, LANES), lambda b, s: (0, 0)),
                folded,
                folded,
                pl.BlockSpec(carries.shape, lambda b, s: (0, 0, 0)),
            ],
            out_specs=pl.BlockSpec((rows, width), lambda b, s: (b, 0)),
            scratch_shapes=[
                pltpu.VMEM((NS * tile, LANES), jnp.float32),
                pltpu.VMEM((2 * NS * rows, LANES), jnp.float32),
                pltpu.VMEM((rows * tile, LANES), jnp.float32),
            ],
        ),
        out_shape=jax.ShapeDtypeStruct((blocks * rows, width), jnp.bfloat16),
        compiler_params=pltpu.CompilerParams(vmem_limit_bytes=32 << 20),
        name="scan_rows",
    )(places, packed, skip_gain, rates, steps, drive, carries)


def local(
    queries, keys, values, doc_lengths, rank_in, bc_weight, rank_out, dt_bias, a_log, skip_gain
):
    owners = lax.axis_size("seq")
    targets = lax.axis_size("chan")
    seq_place = lax.axis_index("seq").astype(jnp.int32)
    chan_place = lax.axis_index("chan").astype(jnp.int32)
    width = queries.shape[2] // owners
    key_parts, value_parts = [keys[0]], [values[0]]
    for shift_by in range(1, REACH + 1):
        key_parts.insert(0, from_behind(keys[0], "seq", shift_by))
        value_parts.insert(0, from_behind(values[0], "seq", shift_by))
    attn_rows, packed = attend(
        seq_place[None], doc_lengths, queries[0], key_parts, value_parts, rank_in, bc_weight, owners
    )
    packed = lax.all_to_all(packed, "seq", split_axis=0, concat_axis=0, tiled=True)
    logs = lax.dynamic_slice_in_dim(a_log, seq_place * width, width, 0)
    rates = (-LOG2E * jnp.exp(logs)).T.reshape(NS * width // LANES, LANES)
    steps, drive, carry = final_states(
        seq_place[None], packed, rank_out, dt_bias[None], rates, targets
    )
    carries = lax.all_to_all(carry, "chan", split_axis=0, concat_axis=0, tiled=True)
    places = jnp.stack([chan_place, seq_place])
    ssm_rows = scan_rows(places, packed, skip_gain[None], rates, steps, drive, carries)
    return (attn_rows[None], ssm_rows[None])


def solution(mesh):
    return jax.shard_map(
        local,
        mesh=mesh,
        in_specs=(
            P("chan", "seq", None),
            P("chan", "seq", None),
            P("chan", "seq", None),
            P("chan", None),
            P(),
            P(),
            P(),
            P(),
            P(),
            P(),
        ),
        out_specs=(P("chan", "seq", None), P("chan", None, "seq")),
        check_vma=False,
    )
```

```python
import functools
import math

import jax
import jax.numpy as jnp
from jax import lax
from jax.experimental import pallas as pl
from jax.experimental.pallas import tpu as pltpu
from jax.sharding import PartitionSpec as P

QUERY_HEADS = 32
KEY_VALUE_HEADS = 8
HEAD_SIZE = 128
GROUP = QUERY_HEADS // KEY_VALUE_HEADS
NS = 16
RANK = 256
REACH = 2
PAIR = 2
EXTRA = 384
LANES = 128
UNROLL = 8
LOG2E = 1.4426950408889634

masked_fill = -1e30


def from_behind(value, axis, steps):
    count = lax.axis_size(axis)
    return lax.ppermute(value, axis, [(source, source + steps) for source in range(count - steps)])


def attend_kernel(
    place_ref, doc_ref, q_ref, k0_ref, k1_ref, k2_ref, v0_ref, v1_ref, v2_ref, rank_ref, map_ref,
    attn_ref, pack_ref, mask_ref, low_ref, bc_ref, *, width,
):
    group = pl.program_id(0)
    rows = q_ref.shape[0]
    window = (REACH + 1) * rows
    place = place_ref[0]

    @pl.when(group == 0)
    def _():
        first = place * rows
        query_pos = first + lax.broadcasted_iota(jnp.int32, (rows, window), 0)
        key_pos = first - REACH * rows + lax.broadcasted_iota(jnp.int32, (rows, window), 1)
        start = jnp.zeros((rows, window), jnp.int32)
        bound = jnp.int32(0)
        for doc in range(doc_ref.shape[1]):
            bound = bound + doc_ref[0, doc]
            start = jnp.where(query_pos >= bound, bound, start)
        allowed = (key_pos >= start) & (key_pos <= query_pos)
        mask_ref[...] = jnp.where(allowed, 0.0, masked_fill)
        low_ref[...] = jnp.zeros_like(low_ref)
        bc_ref[...] = jnp.zeros_like(bc_ref)

    scale = LOG2E / math.sqrt(HEAD_SIZE)
    ones = jnp.ones((window, HEAD_SIZE), jnp.bfloat16)
    scores = []
    for head in range(PAIR):
        lanes = slice(head * HEAD_SIZE, (head + 1) * HEAD_SIZE)
        keys = jnp.concatenate([k0_ref[:, lanes], k1_ref[:, lanes], k2_ref[:, lanes]], axis=0)
        first = head * GROUP
        stacked = jnp.concatenate(
            [q_ref[:, (first + i) * HEAD_SIZE : (first + i + 1) * HEAD_SIZE] for i in range(GROUP)],
            axis=0,
        )
        scores.append(
            lax.dot_general(
                stacked, keys, (((1,), (1,)), ((), ())), preferred_element_type=jnp.float32
            )
        )
    parts = []
    for head in range(PAIR):
        lanes = slice(head * HEAD_SIZE, (head + 1) * HEAD_SIZE)
        values = jnp.concatenate([v0_ref[:, lanes], v1_ref[:, lanes], v2_ref[:, lanes]], axis=0)
        fill = mask_ref[...]
        kept = jnp.concatenate(
            [scores[head][i * rows : (i + 1) * rows, :] + fill for i in range(GROUP)], axis=0
        )
        peak = jnp.max(kept, axis=1, keepdims=True)
        raw = jnp.exp2((kept - peak) * scale).astype(jnp.bfloat16)
        both = jnp.dot(
            raw, jnp.concatenate([values, ones], axis=1), preferred_element_type=jnp.float32
        )
        mixed = (both[:, :HEAD_SIZE] / both[:, HEAD_SIZE:]).astype(jnp.bfloat16)
        parts.extend(mixed[i * rows : (i + 1) * rows, :] for i in range(GROUP))
    for item, mixed in enumerate(parts):
        attn_ref[:, item * HEAD_SIZE : (item + 1) * HEAD_SIZE] = mixed
        column = (group * PAIR * GROUP + item) * HEAD_SIZE
        owner = column // width
        offset = pl.multiple_of(column - owner * width, HEAD_SIZE)
        pack_ref[owner, :, pl.ds(offset, HEAD_SIZE)] = mixed
    block = jnp.concatenate(parts, axis=1)
    low_ref[...] += jnp.dot(block, rank_ref[...], preferred_element_type=jnp.float32)
    bc_ref[...] += jnp.dot(block, map_ref[...], preferred_element_type=jnp.float32)

    @pl.when(group == pl.num_programs(0) - 1)
    def _():
        low = low_ref[...].astype(jnp.bfloat16)
        coarse = bc_ref[...].astype(jnp.bfloat16)
        fine = (bc_ref[...] - coarse.astype(jnp.float32)).astype(jnp.bfloat16)
        rest = jnp.zeros((rows, LANES - 4 * NS), jnp.bfloat16)
        maps = jnp.concatenate([coarse, fine, rest], axis=1)
        for owner in range(pack_ref.shape[0]):
            pack_ref[owner, :, width : width + RANK] = low
            pack_ref[owner, :, width + RANK : width + EXTRA] = maps


def attend(place, doc_lengths, queries, keys, values, rank_in, bc_weight, owners):
    rows, columns = queries.shape
    width = columns // owners
    wide = PAIR * GROUP * HEAD_SIZE

    def columns_at(size):
        return pl.BlockSpec((rows, size), lambda g, s: (0, g))

    return pl.pallas_call(
        functools.partial(attend_kernel, width=width),
        grid_spec=pltpu.PrefetchScalarGridSpec(
            num_scalar_prefetch=1,
            grid=(KEY_VALUE_HEADS // PAIR,),
            in_specs=[pl.BlockSpec(memory_space=pltpu.SMEM), columns_at(wide)]
            + [columns_at(PAIR * HEAD_SIZE)] * 6
            + [
                pl.BlockSpec((wide, RANK), lambda g, s: (g, 0)),
                pl.BlockSpec((wide, 2 * NS), lambda g, s: (g, 0)),
            ],
            out_specs=[
                columns_at(wide),
                pl.BlockSpec((owners, rows, width + EXTRA), lambda g, s: (0, 0, 0)),
            ],
            scratch_shapes=[
                pltpu.VMEM((rows, (REACH + 1) * rows), jnp.float32),
                pltpu.VMEM((rows, RANK), jnp.float32),
                pltpu.VMEM((rows, 2 * NS), jnp.float32),
            ],
        ),
        out_shape=[
            jax.ShapeDtypeStruct((rows, columns), jnp.bfloat16),
            jax.ShapeDtypeStruct((owners, rows, width + EXTRA), jnp.bfloat16),
        ],
        compiler_params=pltpu.CompilerParams(vmem_limit_bytes=60 << 20),
        name="attend",
    )(place, doc_lengths, queries, *keys, *values, rank_in, bc_weight)


def spread_maps(maps, spread_ref, first, count):
    rows = maps.shape[0]
    for item in range(count):
        row = lax.broadcasted_iota(jnp.int32, (LANES, LANES), 0)
        pick = (row == first + item) | (row == first + item + 2 * NS)
        chosen = jnp.where(pick, 1.0, 0.0).astype(jnp.bfloat16)
        spread_ref[item * rows : (item + 1) * rows, :] = jnp.dot(
            maps, chosen, preferred_element_type=jnp.float32
        )


def final_kernel(
    place_ref, pack_ref, cols_ref, bias_ref, rates_ref, steps_ref, drive_ref, carry_ref,
    state_ref, sum_ref, spread_ref,
):
    block = pl.program_id(0)
    rows = pack_ref.shape[1]
    width = cols_ref.shape[1]
    tile = width // LANES

    @pl.when(block == 0)
    def _():
        state_ref[...] = jnp.zeros_like(state_ref)
        sum_ref[...] = jnp.zeros_like(sum_ref)

    low = pack_ref[0, :, width : width + RANK]
    logits = jnp.dot(low, cols_ref[...], preferred_element_type=jnp.float32) + bias_ref[...]
    steps = jnp.maximum(logits, 0.0) + jnp.log1p(jnp.exp(-jnp.abs(logits)))
    drive = steps * pack_ref[0, :, :width].astype(jnp.float32)
    for item in range(tile):
        lanes = slice(item * LANES, (item + 1) * LANES)
        steps_ref[pl.ds(item, rows, stride=tile), :] = steps[:, lanes]
        drive_ref[pl.ds(item, rows, stride=tile), :] = drive[:, lanes]
    spread_maps(pack_ref[0, :, width + RANK :], spread_ref, 0, NS)

    def some(index, held):
        total, states = held[0], list(held[1:])
        base = index * UNROLL
        for near in range(UNROLL):
            at = pl.multiple_of((base + near) * tile, tile)
            step = steps_ref[pl.ds(at, tile), :]
            push = drive_ref[pl.ds(at, tile), :]
            total = total + step
            for n in range(NS):
                rate = rates_ref[n * tile : (n + 1) * tile, :]
                into = spread_ref[pl.ds(n * rows + base + near, 1), :]
                states[n] = jnp.exp2(step * rate) * states[n] + push * into
        return (total, *states)

    held = (sum_ref[...],) + tuple(
        state_ref[n * tile : (n + 1) * tile, :] for n in range(NS)
    )
    held = lax.fori_loop(0, rows // UNROLL, some, held)
    sum_ref[...] = held[0]
    for n in range(NS):
        state_ref[n * tile : (n + 1) * tile, :] = held[1 + n]

    @pl.when(block == pl.num_programs(0) - 1)
    def _():
        coarse = sum_ref[...].astype(jnp.bfloat16)
        fine = (sum_ref[...] - coarse.astype(jnp.float32)).astype(jnp.bfloat16)
        whole = jnp.concatenate([state_ref[...].astype(jnp.bfloat16), coarse, fine], axis=0)
        for target in range(carry_ref.shape[0]):
            carry_ref[target] = whole


def final_states(place, packed, rank_out, dt_bias, rates, targets):
    blocks, rows, packed_width = packed.shape
    width = packed_width - EXTRA
    tile = width // LANES
    folded = jax.ShapeDtypeStruct((blocks * rows * tile, LANES), jnp.float32)
    return pl.pallas_call(
        final_kernel,
        grid_spec=pltpu.PrefetchScalarGridSpec(
            num_scalar_prefetch=1,
            grid=(blocks,),
            in_specs=[
                pl.BlockSpec((1, rows, packed_width), lambda b, s: (b, 0, 0)),
                pl.BlockSpec((RANK, width), lambda b, s: (0, s[0])),
                pl.BlockSpec((1, width), lambda b, s: (0, s[0])),
                pl.BlockSpec((NS * tile, LANES), lambda b, s: (0, 0)),
            ],
            out_specs=[
                pl.BlockSpec((rows * tile, LANES), lambda b, s: (b, 0)),
                pl.BlockSpec((rows * tile, LANES), lambda b, s: (b, 0)),
                pl.BlockSpec((targets, (NS + 2) * tile, LANES), lambda b, s: (0, 0, 0)),
            ],
            scratch_shapes=[
                pltpu.VMEM((NS * tile, LANES), jnp.float32),
                pltpu.VMEM((tile, LANES), jnp.float32),
                pltpu.VMEM((NS * rows, LANES), jnp.float32),
            ],
        ),
        out_shape=[
            folded,
            folded,
            jax.ShapeDtypeStruct((targets, (NS + 2) * tile, LANES), jnp.bfloat16),
        ],
        compiler_params=pltpu.CompilerParams(vmem_limit_bytes=60 << 20),
        name="final_states",
    )(place, packed, rank_out, dt_bias, rates)


def scan_kernel(
    place_ref, pack_ref, gain_ref, rates_ref, steps_ref, drive_ref, carry_ref, out_ref,
    state_ref, spread_ref, folded_ref,
):
    block = pl.program_id(0)
    rows = pack_ref.shape[1]
    width = out_ref.shape[1]
    tile = width // LANES

    @pl.when(block == 0)
    def _():
        state_ref[...] = jnp.zeros_like(state_ref)

        def compose(row, nothing):
            whole = carry_ref[row].astype(jnp.float32)
            total = whole[NS * tile : (NS + 1) * tile, :] + whole[(NS + 1) * tile :, :]
            for n in range(NS):
                part = slice(n * tile, (n + 1) * tile)
                decay = jnp.exp2(rates_ref[part, :] * total)
                state_ref[part, :] = decay * state_ref[part, :] + whole[part, :]
            return nothing

        lax.fori_loop(0, place_ref[0], compose, 0)

    spread_maps(pack_ref[0, :, width + RANK :], spread_ref, 0, 2 * NS)

    def some(index, states):
        states = list(states)
        base = index * UNROLL
        for near in range(UNROLL):
            at = pl.multiple_of((base + near) * tile, tile)
            step = steps_ref[pl.ds(at, tile), :]
            push = drive_ref[pl.ds(at, tile), :]
            sums = [None, None]
            for n in range(NS):
                rate = rates_ref[n * tile : (n + 1) * tile, :]
                into = spread_ref[pl.ds(n * rows + base + near, 1), :]
                out_of = spread_ref[pl.ds((NS + n) * rows + base + near, 1), :]
                states[n] = jnp.exp2(step * rate) * states[n] + push * into
                term = states[n] * out_of
                sums[n % 2] = term if sums[n % 2] is None else sums[n % 2] + term
            folded_ref[pl.ds(at, tile), :] = sums[0] + sums[1]
        return tuple(states)

    held = tuple(state_ref[n * tile : (n + 1) * tile, :] for n in range(NS))
    held = lax.fori_loop(0, rows // UNROLL, some, held)
    for n in range(NS):
        state_ref[n * tile : (n + 1) * tile, :] = held[n]
    for item in range(tile):
        lanes = slice(item * LANES, (item + 1) * LANES)
        direct = gain_ref[:, lanes] * pack_ref[0, :, lanes].astype(jnp.float32)
        mixed = folded_ref[pl.ds(item, rows, stride=tile), :]
        out_ref[:, lanes] = (mixed + direct).astype(jnp.bfloat16)


def scan_rows(places, packed, skip_gain, rates, steps, drive, carries):
    blocks, rows, packed_width = packed.shape
    width = packed_width - EXTRA
    tile = width // LANES
    folded = pl.BlockSpec((rows * tile, LANES), lambda b, s: (b, 0))
    return pl.pallas_call(
        scan_kernel,
        grid_spec=pltpu.PrefetchScalarGridSpec(
            num_scalar_prefetch=1,
            grid=(blocks,),
            in_specs=[
                pl.BlockSpec((1, rows, packed_width), lambda b, s: (b, 0, 0)),
                pl.BlockSpec((1, width), lambda b, s: (0, s[1])),
                pl.BlockSpec((NS * tile, LANES), lambda b, s: (0, 0)),
                folded,
                folded,
                pl.BlockSpec(carries.shape, lambda b, s: (0, 0, 0)),
            ],
            out_specs=pl.BlockSpec((rows, width), lambda b, s: (b, 0)),
            scratch_shapes=[
                pltpu.VMEM((NS * tile, LANES), jnp.float32),
                pltpu.VMEM((2 * NS * rows, LANES), jnp.float32),
                pltpu.VMEM((rows * tile, LANES), jnp.float32),
            ],
        ),
        out_shape=jax.ShapeDtypeStruct((blocks * rows, width), jnp.bfloat16),
        compiler_params=pltpu.CompilerParams(vmem_limit_bytes=60 << 20),
        name="scan_rows",
    )(places, packed, skip_gain, rates, steps, drive, carries)


def local(
    queries, keys, values, doc_lengths, rank_in, bc_weight, rank_out, dt_bias, a_log, skip_gain
):
    owners = lax.axis_size("seq")
    targets = lax.axis_size("chan")
    seq_place = lax.axis_index("seq").astype(jnp.int32)
    chan_place = lax.axis_index("chan").astype(jnp.int32)
    width = queries.shape[2] // owners
    key_parts, value_parts = [keys[0]], [values[0]]
    for shift_by in range(1, REACH + 1):
        key_parts.insert(0, from_behind(keys[0], "seq", shift_by))
        value_parts.insert(0, from_behind(values[0], "seq", shift_by))
    attn_rows, packed = attend(
        seq_place[None], doc_lengths, queries[0], key_parts, value_parts, rank_in, bc_weight, owners
    )
    packed = lax.all_to_all(packed, "seq", split_axis=0, concat_axis=0, tiled=True)
    logs = lax.dynamic_slice_in_dim(a_log, seq_place * width, width, 0)
    rates = (-LOG2E * jnp.exp(logs)).T.reshape(NS * width // LANES, LANES)
    steps, drive, carry = final_states(
        seq_place[None], packed, rank_out, dt_bias[None], rates, targets
    )
    carries = lax.all_to_all(carry, "chan", split_axis=0, concat_axis=0, tiled=True)
    places = jnp.stack([chan_place, seq_place])
    ssm_rows = scan_rows(places, packed, skip_gain[None], rates, steps, drive, carries)
    return (attn_rows[None], ssm_rows[None])


def solution(mesh):
    return jax.shard_map(
        local,
        mesh=mesh,
        in_specs=(
            P("chan", "seq", None),
            P("chan", "seq", None),
            P("chan", "seq", None),
            P("chan", None),
            P(),
            P(),
            P(),
            P(),
            P(),
            P(),
        ),
        out_specs=(P("chan", "seq", None), P("chan", None, "seq")),
        check_vma=False,
    )
```

```python
import functools
import math

import jax
import jax.numpy as jnp
from jax import lax
from jax.experimental import pallas as pl
from jax.experimental.pallas import tpu as pltpu
from jax.sharding import PartitionSpec as P

QUERY_HEADS = 32
KEY_VALUE_HEADS = 8
HEAD_SIZE = 128
GROUP = QUERY_HEADS // KEY_VALUE_HEADS
NS = 16
RANK = 256
REACH = 2
PAIR = 2
EXTRA = 384
LANES = 128
LOG2E = 1.4426950408889634

masked_fill = -1e30


def from_behind(value, axis, steps):
    count = lax.axis_size(axis)
    return lax.ppermute(value, axis, [(source, source + steps) for source in range(count - steps)])


def attend_kernel(
    place_ref, doc_ref, q_ref, k0_ref, k1_ref, k2_ref, v0_ref, v1_ref, v2_ref, rank_ref, map_ref,
    attn_ref, pack_ref, mask_ref, low_ref, bc_ref, *, width,
):
    group = pl.program_id(0)
    rows = q_ref.shape[0]
    window = (REACH + 1) * rows
    place = place_ref[0]

    @pl.when(group == 0)
    def _():
        first = place * rows
        query_pos = first + lax.broadcasted_iota(jnp.int32, (rows, window), 0)
        key_pos = first - REACH * rows + lax.broadcasted_iota(jnp.int32, (rows, window), 1)
        start = jnp.zeros((rows, window), jnp.int32)
        bound = jnp.int32(0)
        for doc in range(doc_ref.shape[1]):
            bound = bound + doc_ref[0, doc]
            start = jnp.where(query_pos >= bound, bound, start)
        allowed = (key_pos >= start) & (key_pos <= query_pos)
        mask_ref[...] = jnp.where(allowed, 0.0, masked_fill)
        low_ref[...] = jnp.zeros_like(low_ref)
        bc_ref[...] = jnp.zeros_like(bc_ref)

    scale = LOG2E / math.sqrt(HEAD_SIZE)
    ones = jnp.ones((window, HEAD_SIZE), jnp.bfloat16)
    scores = []
    for head in range(PAIR):
        lanes = slice(head * HEAD_SIZE, (head + 1) * HEAD_SIZE)
        keys = jnp.concatenate([k0_ref[:, lanes], k1_ref[:, lanes], k2_ref[:, lanes]], axis=0)
        first = head * GROUP
        stacked = jnp.concatenate(
            [q_ref[:, (first + i) * HEAD_SIZE : (first + i + 1) * HEAD_SIZE] for i in range(GROUP)],
            axis=0,
        )
        scores.append(
            lax.dot_general(
                stacked, keys, (((1,), (1,)), ((), ())), preferred_element_type=jnp.float32
            )
        )
    parts = []
    for head in range(PAIR):
        lanes = slice(head * HEAD_SIZE, (head + 1) * HEAD_SIZE)
        values = jnp.concatenate([v0_ref[:, lanes], v1_ref[:, lanes], v2_ref[:, lanes]], axis=0)
        fill = mask_ref[...]
        kept = jnp.concatenate(
            [scores[head][i * rows : (i + 1) * rows, :] + fill for i in range(GROUP)], axis=0
        )
        peak = jnp.max(kept, axis=1, keepdims=True)
        raw = jnp.exp2((kept - peak) * scale).astype(jnp.bfloat16)
        both = jnp.dot(
            raw, jnp.concatenate([values, ones], axis=1), preferred_element_type=jnp.float32
        )
        mixed = (both[:, :HEAD_SIZE] / both[:, HEAD_SIZE:]).astype(jnp.bfloat16)
        parts.extend(mixed[i * rows : (i + 1) * rows, :] for i in range(GROUP))
    for item, mixed in enumerate(parts):
        attn_ref[:, item * HEAD_SIZE : (item + 1) * HEAD_SIZE] = mixed
        column = (group * PAIR * GROUP + item) * HEAD_SIZE
        owner = column // width
        offset = pl.multiple_of(column - owner * width, HEAD_SIZE)
        pack_ref[owner, :, pl.ds(offset, HEAD_SIZE)] = mixed
    block = jnp.concatenate(parts, axis=1)
    low_ref[...] += jnp.dot(block, rank_ref[...], preferred_element_type=jnp.float32)
    bc_ref[...] += jnp.dot(block, map_ref[...], preferred_element_type=jnp.float32)

    @pl.when(group == pl.num_programs(0) - 1)
    def _():
        low = low_ref[...].astype(jnp.bfloat16)
        coarse = bc_ref[...].astype(jnp.bfloat16)
        fine = (bc_ref[...] - coarse.astype(jnp.float32)).astype(jnp.bfloat16)
        rest = jnp.zeros((rows, LANES - 4 * NS), jnp.bfloat16)
        maps = jnp.concatenate([coarse, fine, rest], axis=1)
        for owner in range(pack_ref.shape[0]):
            pack_ref[owner, :, width : width + RANK] = low
            pack_ref[owner, :, width + RANK : width + EXTRA] = maps


def attend(place, doc_lengths, queries, keys, values, rank_in, bc_weight, owners):
    rows, columns = queries.shape
    width = columns // owners
    wide = PAIR * GROUP * HEAD_SIZE

    def columns_at(size):
        return pl.BlockSpec((rows, size), lambda g, s: (0, g))

    return pl.pallas_call(
        functools.partial(attend_kernel, width=width),
        grid_spec=pltpu.PrefetchScalarGridSpec(
            num_scalar_prefetch=1,
            grid=(KEY_VALUE_HEADS // PAIR,),
            in_specs=[pl.BlockSpec(memory_space=pltpu.SMEM), columns_at(wide)]
            + [columns_at(PAIR * HEAD_SIZE)] * 6
            + [
                pl.BlockSpec((wide, RANK), lambda g, s: (g, 0)),
                pl.BlockSpec((wide, 2 * NS), lambda g, s: (g, 0)),
            ],
            out_specs=[
                columns_at(wide),
                pl.BlockSpec((owners, rows, width + EXTRA), lambda g, s: (0, 0, 0)),
            ],
            scratch_shapes=[
                pltpu.VMEM((rows, (REACH + 1) * rows), jnp.float32),
                pltpu.VMEM((rows, RANK), jnp.float32),
                pltpu.VMEM((rows, 2 * NS), jnp.float32),
            ],
        ),
        out_shape=[
            jax.ShapeDtypeStruct((rows, columns), jnp.bfloat16),
            jax.ShapeDtypeStruct((owners, rows, width + EXTRA), jnp.bfloat16),
        ],
        compiler_params=pltpu.CompilerParams(vmem_limit_bytes=60 << 20),
        name="attend",
    )(place, doc_lengths, queries, *keys, *values, rank_in, bc_weight)


def both_parts(maps):
    turned = maps.astype(jnp.float32).T
    return turned[: 2 * NS, :] + turned[2 * NS : 4 * NS, :]


def split(value):
    coarse = value.astype(jnp.bfloat16)
    return coarse, (value - coarse.astype(jnp.float32)).astype(jnp.bfloat16)


def step_kernel(
    pack_ref, cols_ref, bias_ref, rates_ref, steps_ref, sums_ref, carry_ref,
    wide_ref, state_ref, total_ref, turn_ref,
):
    blocks, rows, _ = pack_ref.shape
    width = cols_ref.shape[1]
    tile = width // LANES
    for n in range(NS):
        wide_ref[n * NS : (n + 1) * NS, :] = jnp.broadcast_to(
            rates_ref[n : n + 1, :], (NS, width)
        ).astype(jnp.bfloat16)
    state_ref[...] = jnp.zeros_like(state_ref)
    total_ref[...] = jnp.zeros_like(total_ref)
    at = lax.broadcasted_iota(jnp.int32, (rows, 2 * rows), 0)
    of = lax.broadcasted_iota(jnp.int32, (rows, 2 * rows), 1)
    upto = jnp.where(lax.rem(of, rows) <= at, 1.0, 0.0).astype(jnp.bfloat16)
    state_row = lax.broadcasted_iota(jnp.int32, (NS, rows), 0)

    def one(block, nothing):
        low = pack_ref[block, :, width : width + RANK]
        logits = jnp.dot(low, cols_ref[...], preferred_element_type=jnp.float32) + bias_ref[...]
        steps = jnp.maximum(logits, 0.0) + jnp.log1p(jnp.exp(-jnp.abs(logits)))
        here = pl.ds(pl.multiple_of(block * rows, rows), rows)
        steps_ref[here, :] = steps
        within = jnp.dot(
            upto, jnp.concatenate(split(steps), axis=0), preferred_element_type=jnp.float32
        )
        sums_ref[here, :] = (within + total_ref[...]).astype(jnp.bfloat16)
        whole = within[rows - 1 :, :]
        left = (whole - within).astype(jnp.bfloat16).reshape(rows // NS, NS, width)
        push = steps * pack_ref[block, :, :width].astype(jnp.float32)
        push = push.astype(jnp.bfloat16).reshape(rows // NS, NS, width)
        map_in = both_parts(pack_ref[block, :, width + RANK :])[:NS, :]
        added = jnp.zeros((NS, width), jnp.float32)
        for n in range(0, NS, 2):
            pushed, chosen = [], []
            for m in (n, n + 1):
                decay = jnp.exp2(left * wide_ref[m * NS : (m + 1) * NS, :][None])
                pushed.append((decay * push).reshape(rows, width))
                chosen.append(jnp.where(state_row == m, map_in, 0.0).astype(jnp.bfloat16))
            added = added + jnp.dot(
                jnp.concatenate(chosen, axis=1),
                jnp.concatenate(pushed, axis=0),
                preferred_element_type=jnp.float32,
            )
        state_ref[...] = jnp.exp2(rates_ref[...] * whole) * state_ref[...] + added
        total_ref[...] = total_ref[...] + whole
        return nothing

    lax.fori_loop(0, blocks, one, 0)
    turn_ref[...] = jnp.zeros_like(turn_ref)
    for item in range(tile):
        turn_ref[item : item + 1, :] = total_ref[:, item * LANES : (item + 1) * LANES]
    coarse = turn_ref[...].astype(jnp.bfloat16)
    fine = (turn_ref[...] - coarse.astype(jnp.float32)).astype(jnp.bfloat16)
    sums = jnp.concatenate([coarse, fine], axis=0)
    state = state_ref[...].astype(jnp.bfloat16)
    for target in range(carry_ref.shape[0]):
        for item in range(tile):
            carry_ref[target, item * NS : (item + 1) * NS, :] = state[
                :, item * LANES : (item + 1) * LANES
            ]
        carry_ref[target, tile * NS :, :] = sums


def in_vmem(count):
    return [pl.BlockSpec(memory_space=pltpu.VMEM)] * count


def step_sizes(packed, cols, bias, rates, targets):
    blocks, rows, packed_width = packed.shape
    width = cols.shape[1]
    tile = width // LANES
    return pl.pallas_call(
        step_kernel,
        in_specs=in_vmem(4),
        out_specs=in_vmem(3),
        out_shape=[
            jax.ShapeDtypeStruct((blocks * rows, width), jnp.float32),
            jax.ShapeDtypeStruct((blocks * rows, width), jnp.bfloat16),
            jax.ShapeDtypeStruct((targets, (tile + 1) * NS, LANES), jnp.bfloat16),
        ],
        scratch_shapes=[
            pltpu.VMEM((NS * NS, width), jnp.bfloat16),
            pltpu.VMEM((NS, width), jnp.float32),
            pltpu.VMEM((1, width), jnp.float32),
            pltpu.VMEM((8, LANES), jnp.float32),
        ],
        compiler_params=pltpu.CompilerParams(vmem_limit_bytes=32 << 20),
        name="step_sizes",
    )(packed, cols, bias, rates)


def scan_kernel(
    pack_ref, steps_ref, rates_ref, gain_ref, out_ref, state_ref, push_ref, map_ref, cross_ref,
    *hist_refs,
):
    blocks, rows, _ = pack_ref.shape
    width = rates_ref.shape[1]
    state_ref[...] = jnp.zeros_like(state_ref)
    source = lax.broadcasted_iota(jnp.int32, (LANES, NS * NS), 0)
    column = lax.rem(lax.broadcasted_iota(jnp.int32, (LANES, NS * NS), 1), NS)
    pick = (source == NS + column) | (source == 3 * NS + column)
    pick = jnp.where(pick, 1.0, 0.0).astype(jnp.bfloat16)
    token = lax.rem(lax.broadcasted_iota(jnp.int32, (rows, NS * NS), 0), NS)
    slot = lax.broadcasted_iota(jnp.int32, (rows, NS * NS), 1) // NS
    spans = rows // NS

    def one(block, nothing):
        maps = pack_ref[block, :, width + RANK :]
        map_ref[...] = both_parts(maps)[:NS, :]
        spread = jnp.dot(maps, pick, preferred_element_type=jnp.float32)
        cross_ref[...] = jnp.where(token == slot, spread, 0.0).astype(jnp.bfloat16)
        start = pl.multiple_of(block * rows, rows)
        push_ref[...] = steps_ref[pl.ds(start, rows), :] * pack_ref[block, :, :width].astype(
            jnp.float32
        )

        def finish(first, hist_ref):
            mixed = jnp.dot(
                cross_ref[pl.ds(first, NS), :], hist_ref[...], preferred_element_type=jnp.float32
            )
            direct = gain_ref[...] * pack_ref[block, pl.ds(first, NS), :width].astype(jnp.float32)
            out_ref[pl.ds(start + first, NS), :] = mixed + direct

        def advance(first, hist_ref, state):
            into = pltpu.roll(map_ref[...], lax.rem(rows - first, rows), 1)
            for near in range(NS):
                step = steps_ref[pl.ds(start + first + near, 1), :]
                push = push_ref[pl.ds(first + near, 1), :]
                state = jnp.exp2(rates_ref[...] * step) * state + into[:, near : near + 1] * push
                hist_ref[near * NS : (near + 1) * NS, :] = state.astype(jnp.bfloat16)
            return state

        def pair(index, state):
            first = pl.multiple_of(index * 2 * NS, 2 * NS)
            state = advance(first, hist_refs[0], state)
            finish(first, hist_refs[0])
            second = pl.multiple_of(first + NS, NS)
            state = advance(second, hist_refs[1], state)
            finish(second, hist_refs[1])
            return state

        state_ref[...] = lax.fori_loop(0, spans // 2, pair, state_ref[...])
        return nothing

    lax.fori_loop(0, blocks, one, 0)


def scan_rows(packed, steps, rates, gain):
    blocks, rows, _ = packed.shape
    width = rates.shape[1]
    return pl.pallas_call(
        scan_kernel,
        in_specs=in_vmem(4),
        out_specs=in_vmem(1)[0],
        out_shape=jax.ShapeDtypeStruct((blocks * rows, width), jnp.float32),
        scratch_shapes=[
            pltpu.VMEM((NS, width), jnp.float32),
            pltpu.VMEM((rows, width), jnp.float32),
            pltpu.VMEM((NS, rows), jnp.float32),
            pltpu.VMEM((rows, NS * NS), jnp.bfloat16),
            pltpu.VMEM((NS * NS, width), jnp.bfloat16),
            pltpu.VMEM((NS * NS, width), jnp.bfloat16),
        ],
        compiler_params=pltpu.CompilerParams(vmem_limit_bytes=32 << 20),
        cost_estimate=pl.CostEstimate(
            flops=blocks * rows * width * NS * 256, bytes_accessed=1 << 23, transcendentals=0
        ),
        name="scan_rows",
    )(packed, steps, rates, gain)


def carried_kernel(
    place_ref, pack_ref, part_ref, sums_ref, rates_ref, carry_ref, out_ref,
    state_ref, wide_ref, begin_ref, spread_ref,
):
    blocks, rows, _ = pack_ref.shape
    width = rates_ref.shape[1]
    tile = width // LANES
    state_ref[...] = jnp.zeros_like(state_ref)

    def compose(row, nothing):
        sums = carry_ref[row, tile * NS :, :].astype(jnp.float32)
        sums = sums[: NS // 2, :] + sums[NS // 2 :, :]
        for item in range(tile):
            lanes = slice(item * LANES, (item + 1) * LANES)
            decay = jnp.exp2(rates_ref[:, lanes] * sums[item : item + 1, :])
            added = carry_ref[row, item * NS : (item + 1) * NS, :].astype(jnp.float32)
            state_ref[:, lanes] = decay * state_ref[:, lanes] + added
        return nothing

    lax.fori_loop(0, place_ref[0], compose, 0)
    for n in range(NS):
        here = slice(n * NS, (n + 1) * NS)
        wide_ref[here, :] = jnp.broadcast_to(rates_ref[n : n + 1, :], (NS, width)).astype(
            jnp.bfloat16
        )
        begin_ref[here, :] = jnp.broadcast_to(state_ref[n : n + 1, :], (NS, width)).astype(
            jnp.bfloat16
        )
    source = lax.broadcasted_iota(jnp.int32, (LANES, NS * LANES), 0)
    column = lax.broadcasted_iota(jnp.int32, (LANES, NS * LANES), 1) // LANES
    pick = (source == NS + column) | (source == 3 * NS + column)
    pick = jnp.where(pick, 1.0, 0.0).astype(jnp.bfloat16)

    def one(block, nothing):
        maps = pack_ref[block, :, width + RANK :]
        spread_ref[...] = jnp.dot(maps, pick, preferred_element_type=jnp.float32).astype(
            jnp.bfloat16
        )

        def some(index, nothing):
            near = pl.multiple_of(index * NS, NS)
            here = pl.ds(pl.multiple_of(block * rows + near, NS), NS)
            sums = sums_ref[here, :]
            total = part_ref[here, :]
            for first in range(0, NS, 4):
                terms = []
                for n in range(first, first + 4):
                    part = slice(n * NS, (n + 1) * NS)
                    out_of = spread_ref[pl.ds(near, NS), n * LANES : (n + 1) * LANES]
                    decay = jnp.exp2(sums * wide_ref[part, :])
                    terms.append(
                        decay * begin_ref[part, :] * jnp.concatenate([out_of] * tile, axis=1)
                    )
                four = (terms[0] + terms[1]) + (terms[2] + terms[3])
                total = total + four.astype(jnp.float32)
            out_ref[here, :] = total.astype(jnp.bfloat16)
            return nothing

        return lax.fori_loop(0, rows // NS, some, nothing)

    lax.fori_loop(0, blocks, one, 0)


def add_carried(place, packed, part, sums, rates, carries):
    blocks, rows, _ = packed.shape
    width = rates.shape[1]
    return pl.pallas_call(
        carried_kernel,
        in_specs=[pl.BlockSpec(memory_space=pltpu.SMEM)] + in_vmem(5),
        out_specs=in_vmem(1)[0],
        out_shape=jax.ShapeDtypeStruct((blocks * rows, width), jnp.bfloat16),
        scratch_shapes=[
            pltpu.VMEM((NS, width), jnp.float32),
            pltpu.VMEM((NS * NS, width), jnp.bfloat16),
            pltpu.VMEM((NS * NS, width), jnp.bfloat16),
            pltpu.VMEM((rows, NS * LANES), jnp.bfloat16),
        ],
        compiler_params=pltpu.CompilerParams(vmem_limit_bytes=32 << 20),
        name="add_carried",
    )(place, packed, part, sums, rates, carries)


def local(
    queries, keys, values, doc_lengths, rank_in, bc_weight, rank_out, dt_bias, a_log, skip_gain
):
    owners = lax.axis_size("seq")
    targets = lax.axis_size("chan")
    seq_place = lax.axis_index("seq").astype(jnp.int32)
    chan_place = lax.axis_index("chan").astype(jnp.int32)
    width = queries.shape[2] // owners
    key_parts, value_parts = [keys[0]], [values[0]]
    for shift_by in range(1, REACH + 1):
        key_parts.insert(0, from_behind(keys[0], "seq", shift_by))
        value_parts.insert(0, from_behind(values[0], "seq", shift_by))
    attn_rows, packed = attend(
        seq_place[None], doc_lengths, queries[0], key_parts, value_parts, rank_in, bc_weight, owners
    )
    packed = lax.all_to_all(packed, "seq", split_axis=0, concat_axis=0, tiled=True)
    first = seq_place * width
    logs = lax.dynamic_slice_in_dim(a_log, first, width, 0)
    rates = (-LOG2E * jnp.exp(logs)).T
    cols = lax.dynamic_slice_in_dim(rank_out, first, width, 1)
    bias = lax.dynamic_slice_in_dim(dt_bias, first, width, 0)[None]
    gain = lax.dynamic_slice_in_dim(skip_gain, first, width, 0)[None]
    steps, sums, carry = step_sizes(packed, cols, bias, rates, targets)
    carries = lax.all_to_all(carry, "chan", split_axis=0, concat_axis=0, tiled=True)
    part = scan_rows(packed, steps, rates, gain)
    ssm_rows = add_carried(chan_place[None], packed, part, sums, rates, carries)
    return (attn_rows[None], ssm_rows[None])


def solution(mesh):
    return jax.shard_map(
        local,
        mesh=mesh,
        in_specs=(
            P("chan", "seq", None),
            P("chan", "seq", None),
            P("chan", "seq", None),
            P("chan", None),
            P(),
            P(),
            P(),
            P(),
            P(),
            P(),
        ),
        out_specs=(P("chan", "seq", None), P("chan", None, "seq")),
        check_vma=False,
    )
```

```python
import functools
import math

import jax
import jax.numpy as jnp
from jax import lax
from jax.experimental import pallas as pl
from jax.experimental.pallas import tpu as pltpu
from jax.sharding import PartitionSpec as P

QUERY_HEADS = 32
KEY_VALUE_HEADS = 8
HEAD_SIZE = 128
GROUP = QUERY_HEADS // KEY_VALUE_HEADS
NS = 16
RANK = 256
CORES = 2
LANES = 128
SUBLANES = 8
MAPS = 4 * NS
LOG2E = 1.4426950408889634

masked_fill = -1e30
params = pltpu.CompilerParams(vmem_limit_bytes=60 << 20)


def split(value):
    coarse = value.astype(jnp.bfloat16)
    return coarse, (value - coarse.astype(jnp.float32)).astype(jnp.bfloat16)


def select_kernel(place_ref, key_ref, value_ref, out_ref):
    out_ref[0] = key_ref[...]
    out_ref[1] = value_ref[...]


def select_heads(place, keys, values, chips, wide, swap):
    rows, columns = keys.shape
    halves = columns // (chips * wide)

    def of_core(c, s):
        core = 1 - s[1] if swap else s[1]
        return (0, c * halves + (core if halves == CORES else 0))

    return pl.pallas_call(
        select_kernel,
        grid_spec=pltpu.PrefetchScalarGridSpec(
            num_scalar_prefetch=1,
            grid=(chips,),
            in_specs=[pl.BlockSpec((rows, wide), of_core)] * 2,
            out_specs=pl.BlockSpec((2, rows, wide), lambda c, s: (0, 0, c)),
        ),
        out_shape=jax.ShapeDtypeStruct((2, rows, chips * wide), keys.dtype),
        compiler_params=params,
        name="select_heads",
    )(place, keys, values)


def copy_kernel(place_ref, in_ref, out_ref):
    out_ref[...] = in_ref[...]


def other_queries(place, queries, chips):
    rows, columns = queries.shape
    width = columns // (chips * CORES)
    return pl.pallas_call(
        copy_kernel,
        grid_spec=pltpu.PrefetchScalarGridSpec(
            num_scalar_prefetch=1,
            grid=(chips,),
            in_specs=[pl.BlockSpec((rows, width), lambda c, s: (0, c * CORES + 1 - s[1]))],
            out_specs=pl.BlockSpec((rows, width), lambda c, s: (0, c)),
        ),
        out_shape=jax.ShapeDtypeStruct((rows, chips * width), queries.dtype),
        compiler_params=params,
        name="other_queries",
    )(place, queries)


def attend_kernel(
    place_ref, doc_ref, mine_ref, theirs_ref, own_ref, swap_ref, near_ref, far_ref,
    rank_ref, map_ref, part_in_ref, kept_ref, given_ref,
    kept_out_ref, given_out_ref, send_ref, part_ref, mask_ref,
):
    del kept_ref, given_ref
    step = pl.program_id(0)
    rows = mine_ref.shape[0]
    window = 3 * rows
    width = mine_ref.shape[1]
    heads = own_ref.shape[2] // HEAD_SIZE
    group = width // HEAD_SIZE // heads
    chip, core = place_ref[0], place_ref[1]
    first_core = core == 0

    @pl.when(step == 0)
    def _():
        part_ref[...] = part_in_ref[...]
        own = chip * CORES + core
        swapped = chip * CORES + 1 - core
        near, far = own - CORES, swapped - CORES
        lane = lax.broadcasted_iota(jnp.int32, (rows, window), 1)
        row = lax.broadcasted_iota(jnp.int32, (rows, window), 0)
        block = lane // rows
        for item, (place, blocks) in enumerate(
            (
                (own, (near, jnp.where(first_core, far, swapped), own)),
                (swapped, (far, jnp.where(first_core, own, near), swapped)),
            )
        ):
            query_pos = place * rows + row
            begin = jnp.where(block == 0, blocks[0], jnp.where(block == 1, blocks[1], blocks[2]))
            key_pos = begin * rows + lane - block * rows
            start = jnp.zeros((rows, window), jnp.int32)
            bound = jnp.int32(0)
            for doc in range(doc_ref.shape[1]):
                bound = bound + doc_ref[0, doc]
                start = jnp.where(query_pos >= bound, bound, start)
            allowed = (key_pos >= start) & (key_pos <= query_pos)
            mask_ref[item] = jnp.where(allowed, 0.0, masked_fill)

    scale = LOG2E / math.sqrt(HEAD_SIZE)
    ones = jnp.ones((window, HEAD_SIZE), jnp.bfloat16)

    def windows(kind, head):
        lanes = slice(head * HEAD_SIZE, (head + 1) * HEAD_SIZE)
        own, swapped = own_ref[kind, :, lanes], swap_ref[kind, :, lanes]
        near, far = near_ref[kind, :, lanes], far_ref[kind, :, lanes]
        return (
            jnp.concatenate([near, jnp.where(first_core, far, swapped), own], axis=0),
            jnp.concatenate([far, jnp.where(first_core, own, near), swapped], axis=0),
        )

    units, scores = [], []
    for head in range(heads):
        keys = windows(0, head)
        for item, query_ref in enumerate((mine_ref, theirs_ref)):
            first = head * group
            stacked = jnp.concatenate(
                [
                    query_ref[:, (first + i) * HEAD_SIZE : (first + i + 1) * HEAD_SIZE]
                    for i in range(group)
                ],
                axis=0,
            )
            units.append((head, item))
            scores.append(
                lax.dot_general(
                    stacked, keys[item], (((1,), (1,)), ((), ())),
                    preferred_element_type=jnp.float32,
                )
            )
    parts = ([], [])
    for (head, item), score in zip(units, scores):
        values = windows(1, head)[item]
        fill = mask_ref[item]
        kept = jnp.concatenate(
            [score[i * rows : (i + 1) * rows, :] + fill for i in range(group)], axis=0
        )
        peak = jnp.max(kept, axis=1, keepdims=True)
        raw = jnp.exp2((kept - peak) * scale).astype(jnp.bfloat16)
        both = jnp.dot(
            raw, jnp.concatenate([values, ones], axis=1), preferred_element_type=jnp.float32
        )
        mixed = (both[:, :HEAD_SIZE] / both[:, HEAD_SIZE:]).astype(jnp.bfloat16)
        parts[item].extend(mixed[i * rows : (i + 1) * rows, :] for i in range(group))
    outputs = [jnp.concatenate(part, axis=1) for part in parts]
    kept_out_ref[0] = outputs[0]
    given_out_ref[0] = outputs[1]
    for place, output in zip((core, 1 - core), outputs):
        here = pl.ds(pl.multiple_of(place * rows, rows), rows)
        send_ref[0, here, :] = output
        part_ref[here, :RANK] += jnp.dot(
            output, rank_ref[...], preferred_element_type=jnp.float32
        )
        part_ref[here, RANK : RANK + 2 * NS] += jnp.dot(
            output, map_ref[...], preferred_element_type=jnp.float32
        )


def attend(place, doc_lengths, queries, blocks, rank_in, bc_weight, part, kept, given, first, count):
    mine, theirs = queries
    chips, rows, width = kept.shape
    wide = blocks[0].shape[2] // chips

    def owner(j, s):
        return lax.rem(s[0] + first + j, chips)

    def owned(j, s):
        return owner(j, s) * CORES + s[1]

    whole = pl.BlockSpec((CORES * rows, RANK + LANES), lambda j, s: (0, 0))
    result = pl.BlockSpec((1, rows, width), lambda j, s: (owner(j, s), 0, 0))
    return pl.pallas_call(
        attend_kernel,
        grid_spec=pltpu.PrefetchScalarGridSpec(
            num_scalar_prefetch=1,
            grid=(count,),
            in_specs=[
                pl.BlockSpec(memory_space=pltpu.SMEM),
                pl.BlockSpec((rows, width), lambda j, s: (0, owned(j, s))),
                pl.BlockSpec((rows, width), lambda j, s: (0, owner(j, s))),
            ]
            + [pl.BlockSpec((2, rows, wide), lambda j, s: (0, 0, owner(j, s)))] * 4
            + [
                pl.BlockSpec((width, RANK), lambda j, s: (owned(j, s), 0)),
                pl.BlockSpec((width, 2 * NS), lambda j, s: (owned(j, s), 0)),
                whole,
                pl.BlockSpec(memory_space=pl.ANY),
                pl.BlockSpec(memory_space=pl.ANY),
            ],
            out_specs=[
                result,
                result,
                pl.BlockSpec((1, CORES * rows, width), lambda j, s: (j, 0, 0)),
                whole,
            ],
            scratch_shapes=[pltpu.VMEM((2, rows, 3 * rows), jnp.float32)],
        ),
        out_shape=[
            jax.ShapeDtypeStruct(kept.shape, jnp.bfloat16),
            jax.ShapeDtypeStruct(given.shape, jnp.bfloat16),
            jax.ShapeDtypeStruct((count, CORES * rows, width), jnp.bfloat16),
            jax.ShapeDtypeStruct(part.shape, jnp.float32),
        ],
        input_output_aliases={11: 0, 12: 1},
        compiler_params=params,
        name="attend",
    )(place, doc_lengths, mine, theirs, *blocks, rank_in, bc_weight, part, kept, given)


def low_kernel(mine_ref, theirs_ref, out_ref):
    rows = mine_ref.shape[0]
    total = mine_ref[...] + theirs_ref[...]
    out_ref[:rows, :] = total[:, :RANK].astype(jnp.bfloat16)
    turned = jnp.concatenate(
        [total[i * LANES : (i + 1) * LANES, RANK:].T for i in range(rows // LANES)], axis=1
    )
    out_ref[rows:, :] = jnp.concatenate(split(turned[: 2 * NS, :]), axis=0)


def low_and_maps(mine, theirs):
    rows = mine.shape[0]
    return pl.pallas_call(
        low_kernel,
        out_shape=jax.ShapeDtypeStruct((rows + MAPS, RANK), jnp.bfloat16),
        compiler_params=params,
        name="low_and_maps",
    )(mine, theirs)


def step_kernel(
    place_ref, own_ref, come_ref, low_own_ref, low_come_ref, cols_ref, bias_ref, rates_ref,
    steps_ref, stream_ref, maps_ref, carry_ref, state_ref, total_ref, turn_ref,
):
    chip_block = pl.program_id(0)
    rows, width = own_ref.shape[1:]
    tile = width // LANES
    here = chip_block == place_ref[0]

    @pl.when(chip_block == 0)
    def _():
        state_ref[...] = jnp.zeros_like(state_ref)
        total_ref[...] = jnp.zeros_like(total_ref)

    stream = jnp.where(here, own_ref[0], come_ref[0])
    stream_ref[...] = stream
    lows = jnp.where(here, low_own_ref[...], low_come_ref[0])
    logits = (
        jnp.dot(lows[:rows, :], cols_ref[...], preferred_element_type=jnp.float32) + bias_ref[...]
    )
    steps_ref[...] = jnp.maximum(logits, 0.0) + jnp.log1p(jnp.exp(-jnp.abs(logits)))
    maps = lows[rows:, :].astype(jnp.float32)
    maps = maps[: 2 * NS, :] + maps[2 * NS :, :]
    maps_ref[0] = maps
    at = lax.broadcasted_iota(jnp.int32, (LANES, 2 * LANES), 0)
    of = lax.broadcasted_iota(jnp.int32, (LANES, 2 * LANES), 1)
    upto = jnp.where(lax.rem(of, LANES) <= at, 1.0, 0.0).astype(jnp.bfloat16)
    state_row = lax.broadcasted_iota(jnp.int32, (NS, LANES), 0)
    for block in range(rows // LANES):
        span = slice(block * LANES, (block + 1) * LANES)
        steps = steps_ref[span, :]
        within = jnp.dot(
            upto, jnp.concatenate(split(steps), axis=0), preferred_element_type=jnp.float32
        )
        whole = within[LANES - 1 :, :]
        left = whole - within
        push = (steps * stream_ref[span, :].astype(jnp.float32)).astype(jnp.bfloat16)
        map_in = maps[:NS, span]
        added = jnp.zeros((NS, width), jnp.float32)
        for n in range(0, NS, 2):
            pushed, chosen = [], []
            for m in (n, n + 1):
                decay = jnp.exp2(left * rates_ref[m : m + 1, :]).astype(jnp.bfloat16)
                pushed.append(decay * push)
                chosen.append(jnp.where(state_row == m, map_in, 0.0).astype(jnp.bfloat16))
            added = added + jnp.dot(
                jnp.concatenate(chosen, axis=1),
                jnp.concatenate(pushed, axis=0),
                preferred_element_type=jnp.float32,
            )
        state_ref[...] = jnp.exp2(rates_ref[...] * whole) * state_ref[...] + added
        total_ref[...] = total_ref[...] + whole

    @pl.when(chip_block == pl.num_programs(0) - 1)
    def _():
        turn_ref[...] = jnp.zeros_like(turn_ref)
        for item in range(tile):
            turn_ref[item : item + 1, :] = total_ref[:, item * LANES : (item + 1) * LANES]
        sums = jnp.concatenate(split(turn_ref[...]), axis=0)
        state = state_ref[...].astype(jnp.bfloat16)
        for target in range(carry_ref.shape[0]):
            for item in range(tile):
                carry_ref[target, item * NS : (item + 1) * NS, :] = state[
                    :, item * LANES : (item + 1) * LANES
                ]
            carry_ref[target, tile * NS :, :] = sums


def step_sizes(place, own, come, low_own, low_come, cols, bias, rates, targets):
    _, rows, width = own.shape
    chips = come.shape[0] + 1
    tile = width // LANES

    def slot(b, s):
        return jnp.maximum(lax.rem(s[0] - b + chips, chips) - 1, 0)

    def fixed(*shape):
        return pl.BlockSpec(shape, lambda b, s: (0,) * len(shape))

    return pl.pallas_call(
        step_kernel,
        grid_spec=pltpu.PrefetchScalarGridSpec(
            num_scalar_prefetch=1,
            grid=(chips,),
            in_specs=[
                fixed(*own.shape),
                pl.BlockSpec((1, rows, width), lambda b, s: (slot(b, s), 0, 0)),
                fixed(*low_own.shape),
                pl.BlockSpec((1, *low_own.shape), lambda b, s: (slot(b, s), 0, 0)),
                fixed(*cols.shape),
                fixed(*bias.shape),
                fixed(*rates.shape),
            ],
            out_specs=[
                pl.BlockSpec((rows, width), lambda b, s: (b, 0)),
                pl.BlockSpec((rows, width), lambda b, s: (b, 0)),
                pl.BlockSpec((1, 2 * NS, rows), lambda b, s: (b, 0, 0)),
                fixed(targets, (tile + 1) * NS, LANES),
            ],
            scratch_shapes=[
                pltpu.VMEM((NS, width), jnp.float32),
                pltpu.VMEM((1, width), jnp.float32),
                pltpu.VMEM((SUBLANES, LANES), jnp.float32),
            ],
        ),
        out_shape=[
            jax.ShapeDtypeStruct((chips * rows, width), jnp.float32),
            jax.ShapeDtypeStruct((chips * rows, width), jnp.bfloat16),
            jax.ShapeDtypeStruct((chips, 2 * NS, rows), jnp.float32),
            jax.ShapeDtypeStruct((targets, (tile + 1) * NS, LANES), jnp.bfloat16),
        ],
        compiler_params=params,
        name="step_sizes",
    )(place, own, come, low_own, low_come, cols, bias, rates)


def scan_kernel(
    place_ref, steps_ref, stream_ref, maps_ref, rates_ref, gain_ref, carry_ref, out_ref,
    state_ref, push_ref, cross_ref, *hist_refs,
):
    chip_block = pl.program_id(0)
    rows, width = steps_ref.shape
    tile = width // LANES

    @pl.when(chip_block == 0)
    def _():
        state_ref[...] = jnp.zeros_like(state_ref)

        def compose(row, nothing):
            sums = carry_ref[row, tile * NS :, :].astype(jnp.float32)
            sums = sums[:SUBLANES, :] + sums[SUBLANES:, :]
            for item in range(tile):
                lanes = slice(item * LANES, (item + 1) * LANES)
                decay = jnp.exp2(rates_ref[:, lanes] * sums[item : item + 1, :])
                added = carry_ref[row, item * NS : (item + 1) * NS, :].astype(jnp.float32)
                state_ref[:, lanes] = decay * state_ref[:, lanes] + added
            return nothing

        lax.fori_loop(0, place_ref[0], compose, 0)

    source = lax.broadcasted_iota(jnp.int32, (LANES, NS * NS), 0)
    column = lax.rem(lax.broadcasted_iota(jnp.int32, (LANES, NS * NS), 1), NS)
    pick = jnp.where(source == NS + column, 1.0, 0.0).astype(jnp.bfloat16)
    token = lax.rem(lax.broadcasted_iota(jnp.int32, (LANES, NS * NS), 0), NS)
    slot = lax.broadcasted_iota(jnp.int32, (LANES, NS * NS), 1) // NS
    for block in range(rows // LANES):
        span = slice(block * LANES, (block + 1) * LANES)
        columns = jnp.concatenate(
            [maps_ref[0, :, span], jnp.zeros((LANES - 2 * NS, LANES), jnp.float32)], axis=0
        ).T.astype(jnp.bfloat16)
        spread = jnp.dot(columns, pick, preferred_element_type=jnp.float32)
        cross_ref[span, :] = jnp.where(token == slot, spread, 0.0).astype(jnp.bfloat16)
    push_ref[...] = steps_ref[...] * stream_ref[...].astype(jnp.float32)
    rates = (rates_ref[:SUBLANES, :], rates_ref[SUBLANES:, :])

    def finish(first, hist_ref):
        here = pl.ds(first, NS)
        mixed = jnp.dot(cross_ref[here, :], hist_ref[...], preferred_element_type=jnp.float32)
        direct = gain_ref[...] * stream_ref[here, :].astype(jnp.float32)
        out_ref[here, :] = (mixed + direct).astype(jnp.bfloat16)

    def advance(first, hist_ref, states):
        into = pltpu.roll(maps_ref[0, :NS, :], lax.rem(rows - first, rows), 1)
        for near in range(NS):
            step = steps_ref[pl.ds(first + near, 1), :]
            push = push_ref[pl.ds(first + near, 1), :]
            states = [
                jnp.exp2(rate * step) * state + column * push
                for rate, state, column in zip(
                    rates,
                    states,
                    (into[:SUBLANES, near : near + 1], into[SUBLANES:, near : near + 1]),
                )
            ]
            hist_ref[near * NS : (near + 1) * NS, :] = jnp.concatenate(states, axis=0).astype(
                jnp.bfloat16
            )
        return states

    def pair(index, states):
        first = pl.multiple_of(index * 2 * NS, 2 * NS)
        states = advance(first, hist_refs[0], states)
        finish(first, hist_refs[0])
        second = pl.multiple_of(first + NS, NS)
        states = advance(second, hist_refs[1], states)
        finish(second, hist_refs[1])
        return tuple(states)

    states = (state_ref[:SUBLANES, :], state_ref[SUBLANES:, :])
    states = lax.fori_loop(0, rows // (2 * NS), pair, states)
    state_ref[:SUBLANES, :] = states[0]
    state_ref[SUBLANES:, :] = states[1]


def scan_rows(place, steps, stream, maps, rates, gain, carries):
    chips, _, rows = maps.shape
    width = rates.shape[1]

    def fixed(*shape):
        return pl.BlockSpec(shape, lambda b, s: (0,) * len(shape))

    block = pl.BlockSpec((rows, width), lambda b, s: (b, 0))
    return pl.pallas_call(
        scan_kernel,
        grid_spec=pltpu.PrefetchScalarGridSpec(
            num_scalar_prefetch=1,
            grid=(chips,),
            in_specs=[
                block,
                block,
                pl.BlockSpec((1, 2 * NS, rows), lambda b, s: (b, 0, 0)),
                fixed(*rates.shape),
                fixed(*gain.shape),
                fixed(*carries.shape),
            ],
            out_specs=block,
            scratch_shapes=[
                pltpu.VMEM((NS, width), jnp.float32),
                pltpu.VMEM((rows, width), jnp.float32),
                pltpu.VMEM((rows, NS * NS), jnp.bfloat16),
                pltpu.VMEM((NS * NS, width), jnp.bfloat16),
                pltpu.VMEM((NS * NS, width), jnp.bfloat16),
            ],
        ),
        out_shape=jax.ShapeDtypeStruct((chips * rows, width), jnp.bfloat16),
        compiler_params=params,
        name="scan_rows",
    )(place, steps, stream, maps, rates, gain, carries)


def local(
    queries, keys, values, doc_lengths, rank_in, bc_weight, rank_out, dt_bias, a_log, skip_gain
):
    devices = lax.axis_size("seq")
    chips = devices // CORES
    targets = lax.axis_size("chan")
    seq_place = lax.axis_index("seq").astype(jnp.int32)
    chan_place = lax.axis_index("chan").astype(jnp.int32)
    chip, core = seq_place // CORES, lax.rem(seq_place, CORES)
    place = jnp.stack([chip, core])
    rows, columns = queries.shape[1:]
    width = columns // devices
    wide = max(HEAD_SIZE, keys.shape[2] // devices)

    def other(device):
        return device + 1 - 2 * (device % CORES)

    swap = [(device, other(device)) for device in range(devices)]
    near = [(device, device + CORES) for device in range(devices - CORES)]
    far = [(device, other(device + CORES)) for device in range(devices - CORES)]

    def onward(chips_on):
        return [(device, (device + chips_on * CORES) % devices) for device in range(devices)]

    own = select_heads(place, keys[0], values[0], chips, wide, False)
    theirs = select_heads(place, keys[0], values[0], chips, wide, True)
    from_near = lax.ppermute(own, "seq", near)
    from_far = lax.ppermute(theirs, "seq", far)
    swapped = lax.ppermute(theirs, "seq", swap)
    their_queries = lax.ppermute(other_queries(place, queries[0], chips), "seq", swap)
    blocks = (own, swapped, from_near, from_far)
    both_queries = (queries[0], their_queries)

    empty = jnp.zeros((chips, rows, width), jnp.bfloat16)
    part = jnp.zeros((CORES * rows, RANK + LANES), jnp.float32)
    kept, given, sent, part = attend(
        place, doc_lengths, both_queries, blocks, rank_in, bc_weight, part, empty, empty, 1, chips - 1
    )
    come = [lax.ppermute(sent[step], "seq", onward(step + 1)) for step in range(chips - 1)]
    kept, given, stayed, part = attend(
        place, doc_lengths, both_queries, blocks, rank_in, bc_weight, part, kept, given, 0, 1
    )
    low_own = low_and_maps(part, lax.ppermute(part, "seq", swap))
    low_come = [lax.ppermute(low_own, "seq", onward(step + 1)) for step in range(chips - 1)]
    got = lax.ppermute(given, "seq", swap)
    pair = jnp.where(core == 0, jnp.stack([kept, got], 2), jnp.stack([got, kept], 2))
    attn_rows = pair.transpose(1, 0, 2, 3).reshape(rows, columns)

    first = seq_place * width
    logs = lax.dynamic_slice_in_dim(a_log, first, width, 0)
    rates = (-LOG2E * jnp.exp(logs)).T
    cols = lax.dynamic_slice_in_dim(rank_out, first, width, 1)
    bias = lax.dynamic_slice_in_dim(dt_bias, first, width, 0)[None]
    gain = lax.dynamic_slice_in_dim(skip_gain, first, width, 0)[None]
    steps, stream, maps, carry = step_sizes(
        place, stayed, jnp.stack(come), low_own, jnp.stack(low_come), cols, bias, rates, targets
    )
    carries = lax.all_to_all(carry, "chan", split_axis=0, concat_axis=0, tiled=True)
    ssm_rows = scan_rows(chan_place[None], steps, stream, maps, rates, gain, carries)
    return (attn_rows[None], ssm_rows[None])


def solution(mesh):
    return jax.shard_map(
        local,
        mesh=mesh,
        in_specs=(
            P("chan", "seq", None),
            P("chan", "seq", None),
            P("chan", "seq", None),
            P("chan", None),
            P(),
            P(),
            P(),
            P(),
            P(),
            P(),
        ),
        out_specs=(P("chan", "seq", None), P("chan", None, "seq")),
        check_vma=False,
    )
```

```python
import math

import jax
import jax.numpy as jnp
from jax import lax
from jax.experimental import pallas as pl
from jax.experimental.pallas import tpu as pltpu
from jax.sharding import PartitionSpec as P

QUERY_HEADS = 32
KEY_VALUE_HEADS = 8
HEAD_SIZE = 128
GROUP = QUERY_HEADS // KEY_VALUE_HEADS
NS = 16
RANK = 256
CORES = 2
LANES = 128
SUBLANES = 8
MAPS = 4 * NS
LOG2E = 1.4426950408889634

masked_fill = -1e30
params = pltpu.CompilerParams(vmem_limit_bytes=60 << 20)


def split(value):
    coarse = value.astype(jnp.bfloat16)
    return coarse, (value - coarse.astype(jnp.float32)).astype(jnp.bfloat16)


def run_copies(pairs, sems):
    copies = [
        pltpu.make_async_copy(source, target, sems.at[i]) for i, (source, target) in enumerate(pairs)
    ]
    for copy in copies:
        copy.start()
    for copy in copies:
        copy.wait()


def columns_of(ref, index, size):
    return ref.at[:, pl.ds(pl.multiple_of(index * size, LANES), size)]


def heads_kernel(key_ref, value_ref, own_ref, their_ref, sems):
    core = lax.rem(lax.axis_index("seq"), CORES)
    wide = own_ref.shape[3]
    halves = key_ref.shape[1] // wide // own_ref.shape[0]
    pairs = []
    for target, which in ((own_ref, core), (their_ref, 1 - core)):
        for chip in range(own_ref.shape[0]):
            index = chip * halves + (which if halves == CORES else 0)
            for kind, source in enumerate((key_ref, value_ref)):
                pairs.append((columns_of(source, index, wide), target.at[chip, kind]))
    run_copies(pairs, sems)


def select_heads(keys, values, chips, wide):
    shape = jax.ShapeDtypeStruct((chips, 2, keys.shape[0], wide), keys.dtype)
    return pl.pallas_call(
        heads_kernel,
        in_specs=[pl.BlockSpec(memory_space=pl.ANY)] * 2,
        out_specs=[pl.BlockSpec(memory_space=pl.ANY)] * 2,
        out_shape=[shape, shape],
        scratch_shapes=[pltpu.SemaphoreType.DMA((4 * chips,))],
        compiler_params=params,
        name="select_heads",
    )(keys, values)


def queries_kernel(after_ref, query_ref, out_ref, sems):
    del after_ref
    core = lax.rem(lax.axis_index("seq"), CORES)
    chips, _, width = out_ref.shape
    run_copies(
        [
            (columns_of(query_ref, chip * CORES + 1 - core, width), out_ref.at[chip])
            for chip in range(chips)
        ],
        sems,
    )


def other_queries(after, queries, chips):
    rows, columns = queries.shape
    width = columns // (chips * CORES)
    return pl.pallas_call(
        queries_kernel,
        in_specs=[pl.BlockSpec(memory_space=pl.ANY)] * 2,
        out_specs=pl.BlockSpec(memory_space=pl.ANY),
        out_shape=jax.ShapeDtypeStruct((chips, rows, width), queries.dtype),
        scratch_shapes=[pltpu.SemaphoreType.DMA((chips,))],
        compiler_params=params,
        name="other_queries",
    )(after, queries)


def join_kernel(kept_ref, got_ref, out_ref, sems):
    core = lax.rem(lax.axis_index("seq"), CORES)
    chips, _, width = kept_ref.shape
    pairs = []
    for chip in range(chips):
        for ref, which in ((kept_ref, core), (got_ref, 1 - core)):
            pairs.append((ref.at[chip], columns_of(out_ref, chip * CORES + which, width)))
    run_copies(pairs, sems)


def join_heads(kept, got):
    chips, rows, width = kept.shape
    return pl.pallas_call(
        join_kernel,
        in_specs=[pl.BlockSpec(memory_space=pl.ANY)] * 2,
        out_specs=pl.BlockSpec(memory_space=pl.ANY),
        out_shape=jax.ShapeDtypeStruct((rows, chips * CORES * width), kept.dtype),
        scratch_shapes=[pltpu.SemaphoreType.DMA((CORES * chips,))],
        compiler_params=params,
        name="join_heads",
    )(kept, got)


def attend_kernel(
    place_ref, doc_ref, mine_ref, theirs_ref, own_ref, swap_ref, near_ref, far_ref,
    rank_ref, map_ref, *rest,
):
    earlier_ref = rest[0] if len(rest) > 5 else None
    kept_ref, given_ref, send_ref, part_ref, mask_ref = rest[-5:]
    step = pl.program_id(0)
    rows = mine_ref.shape[0]
    width = mine_ref.shape[1]
    heads = own_ref.shape[3] // HEAD_SIZE
    group = width // HEAD_SIZE // heads
    chip, core = place_ref[0], place_ref[1]
    first_core = core == 0

    def above(shape):
        row = lax.rem(lax.broadcasted_iota(jnp.int32, shape, 0), rows)
        return lax.broadcasted_iota(jnp.int32, shape, 1) > row

    @pl.when(step == 0)
    def _():
        part_ref[...] = jnp.zeros_like(part_ref) if earlier_ref is None else earlier_ref[...]
        own = chip * CORES + core
        swapped = chip * CORES + 1 - core
        near, far = own - CORES, swapped - CORES
        lane = lax.broadcasted_iota(jnp.int32, (rows, rows), 1)
        row = lax.broadcasted_iota(jnp.int32, (rows, rows), 0)
        for item, (place, before, middle) in enumerate(
            (
                (own, near, jnp.where(first_core, far, swapped)),
                (swapped, far, jnp.where(first_core, own, near)),
            )
        ):
            query_pos = place * rows + row
            start = jnp.zeros((rows, rows), jnp.int32)
            bound = jnp.int32(0)
            for doc in range(doc_ref.shape[1]):
                bound = bound + doc_ref[0, doc]
                start = jnp.where(query_pos >= bound, bound, start)
            ends = jnp.where(lane > row, before, place) * rows + lane
            mask_ref[item, :, :rows] = jnp.where(
                (ends >= start) & (ends <= query_pos), 0.0, masked_fill
            )
            mask_ref[item, :, rows:] = jnp.where(
                middle * rows + lane >= start, 0.0, masked_fill
            )

    scale = LOG2E / math.sqrt(HEAD_SIZE)
    ones = jnp.ones((3 * rows, HEAD_SIZE), jnp.bfloat16)

    def windows(kind, head):
        lanes = slice(head * HEAD_SIZE, (head + 1) * HEAD_SIZE)
        own, swapped = own_ref[0, kind, :, lanes], swap_ref[0, kind, :, lanes]
        near, far = near_ref[0, kind, :, lanes], far_ref[0, kind, :, lanes]
        return (
            jnp.concatenate([near, own, jnp.where(first_core, far, swapped)], axis=0),
            jnp.concatenate([far, swapped, jnp.where(first_core, own, near)], axis=0),
        )

    queries = (mine_ref[...], theirs_ref[0])
    units, scores = [], []
    for head in range(heads):
        keys = windows(0, head)
        for item, query in enumerate(queries):
            first = head * group
            stacked = jnp.concatenate(
                [
                    query[:, (first + i) * HEAD_SIZE : (first + i + 1) * HEAD_SIZE]
                    for i in range(group)
                ],
                axis=0,
            )
            units.append((head, item))
            scores.append(
                lax.dot_general(
                    stacked, keys[item], (((1,), (1,)), ((), ())),
                    preferred_element_type=jnp.float32,
                )
            )
    parts = ([], [])
    before = above((group * rows, rows))
    for (head, item), score in zip(units, scores):
        values = windows(1, head)[item]
        fill = mask_ref[item]
        ends = jnp.where(before, score[:, :rows], score[:, rows : 2 * rows])
        kept = jnp.concatenate([ends, score[:, 2 * rows :]], axis=1)
        kept = jnp.concatenate(
            [kept[i * rows : (i + 1) * rows, :] + fill for i in range(group)], axis=0
        )
        peak = jnp.max(kept, axis=1, keepdims=True)
        raw = jnp.exp2((kept - peak) * scale)
        ends = raw[:, :rows]
        spread = jnp.concatenate(
            [jnp.where(before, ends, 0.0), jnp.where(before, 0.0, ends), raw[:, rows:]], axis=1
        ).astype(jnp.bfloat16)
        both = jnp.dot(
            spread, jnp.concatenate([values, ones], axis=1), preferred_element_type=jnp.float32
        )
        mixed = (both[:, :HEAD_SIZE] / both[:, HEAD_SIZE:]).astype(jnp.bfloat16)
        parts[item].extend(mixed[i * rows : (i + 1) * rows, :] for i in range(group))
    outputs = [jnp.concatenate(part, axis=1) for part in parts]
    kept_ref[0] = outputs[0]
    given_ref[0] = outputs[1]
    for place, output in zip((core, 1 - core), outputs):
        here = pl.ds(pl.multiple_of(place * rows, rows), rows)
        send_ref[0, here, :] = output
        part_ref[here, :RANK] += jnp.dot(
            output, rank_ref[...], preferred_element_type=jnp.float32
        )
        part_ref[here, RANK : RANK + 2 * NS] += jnp.dot(
            output, map_ref[...], preferred_element_type=jnp.float32
        )


def attend(place, doc_lengths, queries, blocks, rank_in, bc_weight, earlier, first, count):
    mine, theirs = queries
    chips, rows, width = theirs.shape
    wide = blocks[0].shape[3]

    def owner(j, s):
        return lax.rem(s[0] + first + j, chips)

    def owned(j, s):
        return owner(j, s) * CORES + s[1]

    whole = pl.BlockSpec((CORES * rows, RANK + LANES), lambda j, s: (0, 0))
    result = pl.BlockSpec((1, rows, width), lambda j, s: (owner(j, s), 0, 0))
    more_specs, more, aliases = [], [], {}
    if earlier is not None:
        more_specs = [whole] + [pl.BlockSpec(memory_space=pl.ANY)] * 2
        more = [earlier[3], earlier[0], earlier[1]]
        aliases = {11: 0, 12: 1}
        kernel = later_kernel
    else:
        kernel = attend_kernel
    folded = jax.ShapeDtypeStruct((chips, rows, width), jnp.bfloat16)
    return pl.pallas_call(
        kernel,
        grid_spec=pltpu.PrefetchScalarGridSpec(
            num_scalar_prefetch=1,
            grid=(count,),
            in_specs=[
                pl.BlockSpec(memory_space=pltpu.SMEM),
                pl.BlockSpec((rows, width), lambda j, s: (0, owned(j, s))),
                pl.BlockSpec((1, rows, width), lambda j, s: (owner(j, s), 0, 0)),
            ]
            + [pl.BlockSpec((1, 2, rows, wide), lambda j, s: (owner(j, s), 0, 0, 0))] * 4
            + [
                pl.BlockSpec((width, RANK), lambda j, s: (owned(j, s), 0)),
                pl.BlockSpec((width, 2 * NS), lambda j, s: (owned(j, s), 0)),
            ]
            + more_specs,
            out_specs=[
                result,
                result,
                pl.BlockSpec((1, CORES * rows, width), lambda j, s: (j, 0, 0)),
                whole,
            ],
            scratch_shapes=[pltpu.VMEM((2, rows, 2 * rows), jnp.float32)],
        ),
        out_shape=[
            folded,
            folded,
            jax.ShapeDtypeStruct((count, CORES * rows, width), jnp.bfloat16),
            jax.ShapeDtypeStruct((CORES * rows, RANK + LANES), jnp.float32),
        ],
        input_output_aliases=aliases,
        compiler_params=params,
        cost_estimate=pl.CostEstimate(flops=5 * 10**9, bytes_accessed=1 << 22, transcendentals=0),
        name="attend",
    )(place, doc_lengths, mine, theirs, *blocks, rank_in, bc_weight, *more)


def later_kernel(*refs):
    attend_kernel(*refs[:11], *refs[13:])


def low_kernel(mine_ref, theirs_ref, out_ref):
    rows = mine_ref.shape[0]
    total = mine_ref[...] + theirs_ref[...]
    out_ref[:rows, :] = total[:, :RANK].astype(jnp.bfloat16)
    turned = jnp.concatenate(
        [total[i * LANES : (i + 1) * LANES, RANK:].T for i in range(rows // LANES)], axis=1
    )
    out_ref[rows:, :] = jnp.concatenate(split(turned[: 2 * NS, :]), axis=0)


def low_and_maps(mine, theirs):
    rows = mine.shape[0]
    return pl.pallas_call(
        low_kernel,
        out_shape=jax.ShapeDtypeStruct((rows + MAPS, RANK), jnp.bfloat16),
        compiler_params=params,
        name="low_and_maps",
    )(mine, theirs)


def softplus(value):
    small = jnp.exp(-jnp.abs(value))
    series = small * (1.0 - small * (0.5 - small * (1.0 / 3.0)))
    return jnp.maximum(value, 0.0) + jnp.where(small < 0.015625, series, jnp.log(1.0 + small))


def step_kernel(
    place_ref, own_ref, come_ref, low_own_ref, low_come_ref, cols_ref, bias_ref, rates_ref,
    steps_ref, stream_ref, maps_ref, carry_ref, state_ref, total_ref, turn_ref, wide_ref,
):
    chip_block = pl.program_id(0)
    rows, width = own_ref.shape[1:]
    tile = width // LANES
    here = chip_block == place_ref[0]

    @pl.when(chip_block == 0)
    def _():
        state_ref[...] = jnp.zeros_like(state_ref)
        total_ref[...] = jnp.zeros_like(total_ref)
        for n in range(NS):
            wide_ref[n * NS : (n + 1) * NS, :] = jnp.broadcast_to(
                rates_ref[n : n + 1, :], (NS, width)
            ).astype(jnp.bfloat16)

    stream = jnp.where(here, own_ref[0], come_ref[0])
    stream_ref[...] = stream
    lows = jnp.where(here, low_own_ref[...], low_come_ref[0])
    maps = lows[rows:, :].astype(jnp.float32)
    maps = maps[: 2 * NS, :] + maps[2 * NS :, :]
    maps_ref[0] = maps
    at = lax.broadcasted_iota(jnp.int32, (LANES, LANES), 0)
    of = lax.broadcasted_iota(jnp.int32, (LANES, LANES), 1)
    upto = jnp.where(of <= at, 1.0, 0.0).astype(jnp.bfloat16)
    state_row = lax.broadcasted_iota(jnp.int32, (NS, LANES), 0)
    chunk = CORES * LANES
    for block in range(rows // LANES):
        span = slice(block * LANES, (block + 1) * LANES)
        logits = jnp.dot(lows[span, :], cols_ref[...], preferred_element_type=jnp.float32)
        steps = softplus(logits + bias_ref[...]).astype(jnp.bfloat16)
        steps_ref[span, :] = steps
        push = steps * stream[span, :]
        within = jnp.dot(upto, steps, preferred_element_type=jnp.float32)
        whole = within[LANES - 1 :, :]
        left = (whole - within).astype(jnp.bfloat16)
        map_in = maps[:NS, span]
        chosen = [
            jnp.concatenate(
                [jnp.where(state_row == m, map_in, 0.0).astype(jnp.bfloat16) for m in (n, n + 1)],
                axis=1,
            )
            for n in range(0, NS, 2)
        ]
        for item in range(width // chunk):
            lanes = slice(item * chunk, (item + 1) * chunk)
            left_here = left[:, lanes].reshape(LANES // NS, NS, chunk)
            push_here = push[:, lanes].reshape(LANES // NS, NS, chunk)
            added = jnp.exp2(rates_ref[:, lanes] * whole[:, lanes]) * state_ref[:, lanes]
            for n in range(0, NS, 2):
                pushed = []
                for m in (n, n + 1):
                    decay = jnp.exp2(left_here * wide_ref[m * NS : (m + 1) * NS, lanes][None])
                    pushed.append((decay * push_here).reshape(LANES, chunk))
                added = added + jnp.dot(
                    chosen[n // 2],
                    jnp.concatenate(pushed, axis=0),
                    preferred_element_type=jnp.float32,
                )
            state_ref[:, lanes] = added
        total_ref[...] = total_ref[...] + whole

    @pl.when(chip_block == pl.num_programs(0) - 1)
    def _():
        turn_ref[...] = jnp.zeros_like(turn_ref)
        for item in range(tile):
            turn_ref[item : item + 1, :] = total_ref[:, item * LANES : (item + 1) * LANES]
        sums = jnp.concatenate(split(turn_ref[...]), axis=0)
        state = state_ref[...].astype(jnp.bfloat16)
        for target in range(carry_ref.shape[0]):
            for item in range(tile):
                carry_ref[target, item * NS : (item + 1) * NS, :] = state[
                    :, item * LANES : (item + 1) * LANES
                ]
            carry_ref[target, tile * NS :, :] = sums


def step_sizes(place, own, come, low_own, low_come, cols, bias, rates, targets):
    _, rows, width = own.shape
    chips = come.shape[0] + 1
    tile = width // LANES

    def slot(b, s):
        return jnp.maximum(lax.rem(s[0] - b + chips, chips) - 1, 0)

    def fixed(*shape):
        return pl.BlockSpec(shape, lambda b, s: (0,) * len(shape))

    return pl.pallas_call(
        step_kernel,
        grid_spec=pltpu.PrefetchScalarGridSpec(
            num_scalar_prefetch=1,
            grid=(chips,),
            in_specs=[
                fixed(*own.shape),
                pl.BlockSpec((1, rows, width), lambda b, s: (slot(b, s), 0, 0)),
                fixed(*low_own.shape),
                pl.BlockSpec((1, *low_own.shape), lambda b, s: (slot(b, s), 0, 0)),
                fixed(*cols.shape),
                fixed(*bias.shape),
                fixed(*rates.shape),
            ],
            out_specs=[
                pl.BlockSpec((rows, width), lambda b, s: (b, 0)),
                pl.BlockSpec((rows, width), lambda b, s: (b, 0)),
                pl.BlockSpec((1, 2 * NS, rows), lambda b, s: (b, 0, 0)),
                fixed(targets, (tile + 1) * NS, LANES),
            ],
            scratch_shapes=[
                pltpu.VMEM((NS, width), jnp.float32),
                pltpu.VMEM((1, width), jnp.float32),
                pltpu.VMEM((SUBLANES, LANES), jnp.float32),
                pltpu.VMEM((NS * NS, width), jnp.bfloat16),
            ],
        ),
        out_shape=[
            jax.ShapeDtypeStruct((chips * rows, width), jnp.bfloat16),
            jax.ShapeDtypeStruct((chips * rows, width), jnp.bfloat16),
            jax.ShapeDtypeStruct((chips, 2 * NS, rows), jnp.float32),
            jax.ShapeDtypeStruct((targets, (tile + 1) * NS, LANES), jnp.bfloat16),
        ],
        compiler_params=params,
        name="step_sizes",
    )(place, own, come, low_own, low_come, cols, bias, rates)


def scan_kernel(
    place_ref, steps_ref, stream_ref, maps_ref, rates_ref, gain_ref, carry_ref, out_ref,
    state_ref, cross_ref, *hist_refs,
):
    chip_block = pl.program_id(0)
    rows, width = steps_ref.shape
    tile = width // LANES

    @pl.when(chip_block == 0)
    def _():
        state_ref[...] = jnp.zeros_like(state_ref)

        def compose(row, nothing):
            sums = carry_ref[row, tile * NS :, :].astype(jnp.float32)
            sums = sums[:SUBLANES, :] + sums[SUBLANES:, :]
            for item in range(tile):
                lanes = slice(item * LANES, (item + 1) * LANES)
                decay = jnp.exp2(rates_ref[:, lanes] * sums[item : item + 1, :])
                added = carry_ref[row, item * NS : (item + 1) * NS, :].astype(jnp.float32)
                state_ref[:, lanes] = decay * state_ref[:, lanes] + added
            return nothing

        lax.fori_loop(0, place_ref[0], compose, 0)

    source = lax.broadcasted_iota(jnp.int32, (LANES, NS * NS), 0)
    column = lax.rem(lax.broadcasted_iota(jnp.int32, (LANES, NS * NS), 1), NS)
    pick = jnp.where(source == NS + column, 1.0, 0.0).astype(jnp.bfloat16)
    token = lax.rem(lax.broadcasted_iota(jnp.int32, (LANES, NS * NS), 0), NS)
    slot = lax.broadcasted_iota(jnp.int32, (LANES, NS * NS), 1) // NS
    for block in range(rows // LANES):
        span = slice(block * LANES, (block + 1) * LANES)
        columns = jnp.concatenate(
            [maps_ref[0, :, span], jnp.zeros((LANES - 2 * NS, LANES), jnp.float32)], axis=0
        ).T.astype(jnp.bfloat16)
        spread = jnp.dot(columns, pick, preferred_element_type=jnp.float32)
        cross_ref[span, :] = jnp.where(token == slot, spread, 0.0).astype(jnp.bfloat16)
    half = width // 2

    def finish(first, hist_ref):
        here = pl.ds(first, NS)
        mixed = jnp.dot(cross_ref[here, :], hist_ref[...], preferred_element_type=jnp.float32)
        direct = gain_ref[...] * stream_ref[here, :].astype(jnp.float32)
        out_ref[here, :] = (mixed + direct).astype(jnp.bfloat16)

    def advance(first, hist_ref):
        here = pl.ds(first, NS)
        into = pltpu.roll(maps_ref[0, :NS, :], lax.rem(rows - first, rows), 1)
        for lanes in (slice(0, half), slice(half, width)):
            state = state_ref[:, lanes]
            rates = rates_ref[:, lanes]
            steps = steps_ref[here, lanes].astype(jnp.float32)
            push = steps * stream_ref[here, lanes].astype(jnp.float32)
            for near in range(NS):
                this = slice(near, near + 1)
                state = jnp.exp2(rates * steps[this, :]) * state + into[:, this] * push[this, :]
                hist_ref[near * NS : (near + 1) * NS, lanes] = state.astype(jnp.bfloat16)
            state_ref[:, lanes] = state

    def pair(index, nothing):
        first = pl.multiple_of(index * 2 * NS, 2 * NS)
        advance(first, hist_refs[0])
        finish(first, hist_refs[0])
        second = pl.multiple_of(first + NS, NS)
        advance(second, hist_refs[1])
        finish(second, hist_refs[1])
        return nothing

    lax.fori_loop(0, rows // (2 * NS), pair, 0)


def scan_rows(place, steps, stream, maps, rates, gain, carries):
    chips, _, rows = maps.shape
    width = rates.shape[1]

    def fixed(*shape):
        return pl.BlockSpec(shape, lambda b, s: (0,) * len(shape))

    block = pl.BlockSpec((rows, width), lambda b, s: (b, 0))
    return pl.pallas_call(
        scan_kernel,
        grid_spec=pltpu.PrefetchScalarGridSpec(
            num_scalar_prefetch=1,
            grid=(chips,),
            in_specs=[
                block,
                block,
                pl.BlockSpec((1, 2 * NS, rows), lambda b, s: (b, 0, 0)),
                fixed(*rates.shape),
                fixed(*gain.shape),
                fixed(*carries.shape),
            ],
            out_specs=block,
            scratch_shapes=[
                pltpu.VMEM((NS, width), jnp.float32),
                pltpu.VMEM((rows, NS * NS), jnp.bfloat16),
                pltpu.VMEM((NS * NS, width), jnp.bfloat16),
                pltpu.VMEM((NS * NS, width), jnp.bfloat16),
            ],
        ),
        out_shape=jax.ShapeDtypeStruct((chips * rows, width), jnp.bfloat16),
        compiler_params=params,
        name="scan_rows",
    )(place, steps, stream, maps, rates, gain, carries)


def local(
    queries, keys, values, doc_lengths, rank_in, bc_weight, rank_out, dt_bias, a_log, skip_gain
):
    devices = lax.axis_size("seq")
    chips = devices // CORES
    targets = lax.axis_size("chan")
    seq_place = lax.axis_index("seq").astype(jnp.int32)
    chan_place = lax.axis_index("chan").astype(jnp.int32)
    chip, core = seq_place // CORES, lax.rem(seq_place, CORES)
    place = jnp.stack([chip, core])
    width = queries.shape[2] // devices
    wide = max(HEAD_SIZE, keys.shape[2] // devices)

    def other(device):
        return device + 1 - 2 * (device % CORES)

    swap = [(device, other(device)) for device in range(devices)]
    near = [(device, device + CORES) for device in range(devices - CORES)]
    far = [(device, other(device + CORES)) for device in range(devices - CORES)]

    def onward(chips_on):
        return [(device, (device + chips_on * CORES) % devices) for device in range(devices)]

    own, theirs = select_heads(keys[0], values[0], chips, wide)
    from_near = lax.ppermute(own, "seq", near)
    from_far = lax.ppermute(theirs, "seq", far)
    swapped = lax.ppermute(theirs, "seq", swap)
    their_queries = lax.ppermute(other_queries(own, queries[0], chips), "seq", swap)
    blocks = (own, swapped, from_near, from_far)
    both_queries = (queries[0], their_queries)

    earlier = attend(
        place, doc_lengths, both_queries, blocks, rank_in, bc_weight, None, 1, chips - 1
    )
    sent = earlier[2]
    come = [lax.ppermute(sent[step], "seq", onward(step + 1)) for step in range(chips - 1)]
    kept, given, stayed, part = attend(
        place, doc_lengths, both_queries, blocks, rank_in, bc_weight, earlier, 0, 1
    )
    low_own = low_and_maps(part, lax.ppermute(part, "seq", swap))
    low_come = [lax.ppermute(low_own, "seq", onward(step + 1)) for step in range(chips - 1)]
    attn_rows = join_heads(kept, lax.ppermute(given, "seq", swap))

    first = seq_place * width
    logs = lax.dynamic_slice_in_dim(a_log, first, width, 0)
    rates = (-LOG2E * jnp.exp(logs)).T
    cols = lax.dynamic_slice_in_dim(rank_out, first, width, 1)
    bias = lax.dynamic_slice_in_dim(dt_bias, first, width, 0)[None]
    gain = lax.dynamic_slice_in_dim(skip_gain, first, width, 0)[None]
    steps, stream, maps, carry = step_sizes(
        place, stayed, jnp.stack(come), low_own, jnp.stack(low_come), cols, bias, rates, targets
    )
    carries = lax.all_to_all(carry, "chan", split_axis=0, concat_axis=0, tiled=True)
    ssm_rows = scan_rows(chan_place[None], steps, stream, maps, rates, gain, carries)
    return (attn_rows[None], ssm_rows[None])


def solution(mesh):
    return jax.shard_map(
        local,
        mesh=mesh,
        in_specs=(
            P("chan", "seq", None),
            P("chan", "seq", None),
            P("chan", "seq", None),
            P("chan", None),
            P(),
            P(),
            P(),
            P(),
            P(),
            P(),
        ),
        out_specs=(P("chan", "seq", None), P("chan", None, "seq")),
        check_vma=False,
    )
```

```python
import math

import jax
import jax.numpy as jnp
from jax import lax
from jax.experimental import pallas as pl
from jax.experimental.pallas import tpu as pltpu
from jax.sharding import PartitionSpec as P

QUERY_HEADS = 32
KEY_VALUE_HEADS = 8
HEAD_SIZE = 128
GROUP = QUERY_HEADS // KEY_VALUE_HEADS
NS = 16
RANK = 256
CORES = 2
LANES = 128
SUBLANES = 8
MAPS = 4 * NS
LOG2E = 1.4426950408889634

masked_fill = -1e30
params = pltpu.CompilerParams(vmem_limit_bytes=60 << 20)


def split(value):
    coarse = value.astype(jnp.bfloat16)
    return coarse, (value - coarse.astype(jnp.float32)).astype(jnp.bfloat16)


def run_copies(pairs, sems):
    copies = [
        pltpu.make_async_copy(source, target, sems.at[i]) for i, (source, target) in enumerate(pairs)
    ]
    for copy in copies:
        copy.start()
    for copy in copies:
        copy.wait()


def columns_of(ref, index, size):
    return ref.at[:, pl.ds(pl.multiple_of(index * size, LANES), size)]


def heads_kernel(key_ref, value_ref, own_ref, their_ref, sems):
    core = lax.rem(lax.axis_index("seq"), CORES)
    wide = own_ref.shape[3]
    halves = key_ref.shape[1] // wide // own_ref.shape[0]
    pairs = []
    for target, which in ((own_ref, core), (their_ref, 1 - core)):
        for chip in range(own_ref.shape[0]):
            index = chip * halves + (which if halves == CORES else 0)
            for kind, source in enumerate((key_ref, value_ref)):
                pairs.append((columns_of(source, index, wide), target.at[chip, kind]))
    run_copies(pairs, sems)


def select_heads(keys, values, chips, wide):
    shape = jax.ShapeDtypeStruct((chips, 2, keys.shape[0], wide), keys.dtype)
    return pl.pallas_call(
        heads_kernel,
        in_specs=[pl.BlockSpec(memory_space=pl.ANY)] * 2,
        out_shape=[shape, shape],
        scratch_shapes=[pltpu.SemaphoreType.DMA((4 * chips,))],
        compiler_params=params,
        name="select_heads",
    )(keys, values)


def queries_kernel(after_ref, query_ref, out_ref, sems):
    del after_ref
    core = lax.rem(lax.axis_index("seq"), CORES)
    chips, _, width = out_ref.shape
    run_copies(
        [
            (columns_of(query_ref, chip * CORES + 1 - core, width), out_ref.at[chip])
            for chip in range(chips)
        ],
        sems,
    )


def other_queries(after, queries, chips):
    rows, columns = queries.shape
    width = columns // (chips * CORES)
    return pl.pallas_call(
        queries_kernel,
        in_specs=[pl.BlockSpec(memory_space=pl.ANY)] * 2,
        out_shape=jax.ShapeDtypeStruct((chips, rows, width), queries.dtype),
        scratch_shapes=[pltpu.SemaphoreType.DMA((chips,))],
        compiler_params=params,
        name="other_queries",
    )(after, queries)


def join_kernel(sent_ref, stayed_ref, got_sent_ref, got_stayed_ref, out_ref, sems):
    place = lax.axis_index("seq")
    core, chip = lax.rem(place, CORES), place // CORES
    rows = out_ref.shape[0]
    others, _, width = sent_ref.shape
    here = pl.ds(pl.multiple_of(core * rows, rows), rows)
    pairs = []
    for first, rest, which in (
        (stayed_ref, sent_ref, core), (got_stayed_ref, got_sent_ref, 1 - core)
    ):
        for step in range(others + 1):
            source = first.at[0, here, :] if step == 0 else rest.at[step - 1, here, :]
            owner = lax.rem(chip + step, others + 1)
            pairs.append((source, columns_of(out_ref, owner * CORES + which, width)))
    run_copies(pairs, sems)


def join_heads(sent, stayed, got_sent, got_stayed):
    others, rows, width = sent.shape
    return pl.pallas_call(
        join_kernel,
        in_specs=[pl.BlockSpec(memory_space=pl.ANY)] * 4,
        out_shape=jax.ShapeDtypeStruct(
            (rows // CORES, (others + 1) * CORES * width), sent.dtype
        ),
        scratch_shapes=[pltpu.SemaphoreType.DMA((CORES * (others + 1),))],
        compiler_params=params,
        name="join_heads",
    )(sent, stayed, got_sent, got_stayed)


def attend_kernel(
    place_ref, doc_ref, mine_ref, theirs_ref, own_ref, swap_ref, near_ref, far_ref,
    rank_ref, map_ref, *rest,
):
    earlier_ref = rest[0] if len(rest) > 3 else None
    send_ref, part_ref, mask_ref = rest[-3:]
    step = pl.program_id(0)
    rows = mine_ref.shape[0]
    group = mine_ref.shape[1] // HEAD_SIZE
    chip, core = place_ref[0], place_ref[1]
    first_core = core == 0

    def above(shape):
        row = lax.rem(lax.broadcasted_iota(jnp.int32, shape, 0), rows)
        return lax.broadcasted_iota(jnp.int32, shape, 1) > row

    @pl.when(step == 0)
    def _():
        part_ref[...] = jnp.zeros_like(part_ref) if earlier_ref is None else earlier_ref[...]
        own = chip * CORES + core
        swapped = chip * CORES + 1 - core
        near, far = own - CORES, swapped - CORES
        lane = lax.broadcasted_iota(jnp.int32, (rows, rows), 1)
        row = lax.broadcasted_iota(jnp.int32, (rows, rows), 0)
        for item, (place, before, middle) in enumerate(
            (
                (own, near, jnp.where(first_core, far, swapped)),
                (swapped, far, jnp.where(first_core, own, near)),
            )
        ):
            query_pos = place * rows + row
            start = jnp.zeros((rows, rows), jnp.int32)
            bound = jnp.int32(0)
            for doc in range(doc_ref.shape[1]):
                bound = bound + doc_ref[0, doc]
                start = jnp.where(query_pos >= bound, bound, start)
            ends = jnp.where(lane > row, before, place) * rows + lane
            mask_ref[item, :, :rows] = jnp.where(
                (ends >= start) & (ends <= query_pos), 0.0, masked_fill
            )
            mask_ref[item, :, rows:] = jnp.where(
                middle * rows + lane >= start, 0.0, masked_fill
            )

    scale = LOG2E / math.sqrt(HEAD_SIZE)
    ones = jnp.ones((3 * rows, HEAD_SIZE), jnp.bfloat16)

    def windows(kind):
        own, swapped = own_ref[0, kind], swap_ref[0, kind]
        near, far = near_ref[0, kind], far_ref[0, kind]
        return (
            jnp.concatenate([near, own, jnp.where(first_core, far, swapped)], axis=0),
            jnp.concatenate([far, swapped, jnp.where(first_core, own, near)], axis=0),
        )

    scores = []
    for keys, query in zip(windows(0), (mine_ref[...], theirs_ref[0])):
        stacked = jnp.concatenate(
            [query[:, i * HEAD_SIZE : (i + 1) * HEAD_SIZE] for i in range(group)], axis=0
        )
        scores.append(
            lax.dot_general(
                stacked, keys, (((1,), (1,)), ((), ())), preferred_element_type=jnp.float32
            )
        )
    outputs = []
    before = above((group * rows, rows))
    for item, (values, score) in enumerate(zip(windows(1), scores)):
        fill = mask_ref[item]
        ends = jnp.where(before, score[:, :rows], score[:, rows : 2 * rows])
        kept = jnp.concatenate([ends, score[:, 2 * rows :]], axis=1)
        kept = jnp.concatenate(
            [kept[i * rows : (i + 1) * rows, :] + fill for i in range(group)], axis=0
        )
        peak = jnp.max(kept, axis=1, keepdims=True)
        raw = jnp.exp2((kept - peak) * scale).astype(jnp.bfloat16)
        ends = raw[:, :rows]
        none = jnp.zeros_like(ends)
        spread = jnp.concatenate(
            [jnp.where(before, ends, none), jnp.where(before, none, ends), raw[:, rows:]], axis=1
        )
        both = jnp.dot(
            spread, jnp.concatenate([values, ones], axis=1), preferred_element_type=jnp.float32
        )
        mixed = both[:, :HEAD_SIZE] * pl.reciprocal(both[:, HEAD_SIZE:])
        mixed = mixed.astype(jnp.bfloat16)
        outputs.append(
            jnp.concatenate([mixed[i * rows : (i + 1) * rows, :] for i in range(group)], axis=1)
        )
    for place, output in zip((core, 1 - core), outputs):
        here = pl.ds(pl.multiple_of(place * rows, rows), rows)
        send_ref[0, here, :] = output
        part_ref[here, :RANK] += jnp.dot(
            output, rank_ref[...], preferred_element_type=jnp.float32
        )
        part_ref[here, RANK : RANK + 2 * NS] += jnp.dot(
            output, map_ref[...], preferred_element_type=jnp.float32
        )


def attend(place, doc_lengths, queries, blocks, rank_in, bc_weight, earlier, first, count):
    mine, theirs = queries
    chips, rows, width = theirs.shape
    heads = blocks[0].shape[3] // HEAD_SIZE
    wide = width // heads

    def owner(j, s):
        return lax.rem(s[0] + first + j // heads, chips)

    def column(j, s):
        return (owner(j, s) * CORES + s[1]) * heads + lax.rem(j, heads)

    whole = pl.BlockSpec((CORES * rows, RANK + LANES), lambda j, s: (0, 0))
    block = pl.BlockSpec(
        (1, 2, rows, HEAD_SIZE), lambda j, s: (owner(j, s), 0, 0, lax.rem(j, heads))
    )
    more = [] if earlier is None else [earlier]
    return pl.pallas_call(
        attend_kernel,
        grid_spec=pltpu.PrefetchScalarGridSpec(
            num_scalar_prefetch=1,
            grid=(count * heads,),
            in_specs=[
                pl.BlockSpec(memory_space=pltpu.SMEM),
                pl.BlockSpec((rows, wide), lambda j, s: (0, column(j, s))),
                pl.BlockSpec((1, rows, wide), lambda j, s: (owner(j, s), 0, lax.rem(j, heads))),
            ]
            + [block] * 4
            + [
                pl.BlockSpec((wide, RANK), lambda j, s: (column(j, s), 0)),
                pl.BlockSpec((wide, 2 * NS), lambda j, s: (column(j, s), 0)),
            ]
            + [whole] * len(more),
            out_specs=[
                pl.BlockSpec(
                    (1, CORES * rows, wide), lambda j, s: (j // heads, 0, lax.rem(j, heads))
                ),
                whole,
            ],
            scratch_shapes=[pltpu.VMEM((2, rows, 2 * rows), jnp.float32)],
        ),
        out_shape=[
            jax.ShapeDtypeStruct((count, CORES * rows, width), jnp.bfloat16),
            jax.ShapeDtypeStruct((CORES * rows, RANK + LANES), jnp.float32),
        ],
        compiler_params=params,
        cost_estimate=pl.CostEstimate(flops=5 * 10**9, bytes_accessed=1 << 22, transcendentals=0),
        name="attend",
    )(place, doc_lengths, mine, theirs, *blocks, rank_in, bc_weight, *more)


def low_kernel(mine_ref, theirs_ref, out_ref):
    rows = mine_ref.shape[0]
    total = mine_ref[...] + theirs_ref[...]
    out_ref[:rows, :] = total[:, :RANK].astype(jnp.bfloat16)
    turned = jnp.concatenate(
        [total[i * LANES : (i + 1) * LANES, RANK:].T for i in range(rows // LANES)], axis=1
    )
    out_ref[rows:, :] = jnp.concatenate(split(turned[: 2 * NS, :]), axis=0)


def low_and_maps(mine, theirs):
    rows = mine.shape[0]
    return pl.pallas_call(
        low_kernel,
        out_shape=jax.ShapeDtypeStruct((rows + MAPS, RANK), jnp.bfloat16),
        compiler_params=params,
        cost_estimate=pl.CostEstimate(flops=1, bytes_accessed=1, transcendentals=0),
        name="low_and_maps",
    )(mine, theirs)


def softplus(value):
    small = jnp.exp(-jnp.abs(value))
    tail = jnp.where(small < 0.00390625, small * (1.0 - 0.5 * small), jnp.log(1.0 + small))
    return jnp.maximum(value, 0.0) + tail


def step_kernel(
    place_ref, own_ref, come_ref, low_own_ref, low_come_ref, map_own_ref, map_come_ref,
    cols_ref, bias_ref, rates_ref,
    steps_ref, stream_ref, maps_ref, carry_ref, state_ref, total_ref, turn_ref, wide_ref,
):
    step = pl.program_id(0)
    rows, width = own_ref.shape[1:]
    tile = width // LANES
    here = step // CORES == place_ref[0]

    @pl.when(step == 0)
    def _():
        state_ref[...] = jnp.zeros_like(state_ref)
        total_ref[...] = jnp.zeros_like(total_ref)
        for n in range(NS):
            wide_ref[n * SUBLANES : (n + 1) * SUBLANES, :] = jnp.broadcast_to(
                rates_ref[n : n + 1, :], (SUBLANES, width)
            )

    stream = jnp.where(here, own_ref[0], come_ref[0])
    stream_ref[...] = stream
    lows = jnp.where(here, low_own_ref[...], low_come_ref[0])
    maps = jnp.where(here, map_own_ref[...], map_come_ref[0]).astype(jnp.float32)
    maps = maps[: 2 * NS, :] + maps[2 * NS :, :]
    maps_ref[0] = maps
    logits = jnp.dot(lows, cols_ref[...], preferred_element_type=jnp.float32)
    steps = softplus(logits + bias_ref[...]).astype(jnp.bfloat16)
    steps_ref[...] = steps
    push = steps * stream
    at = lax.broadcasted_iota(jnp.int32, (rows, rows), 0)
    of = lax.broadcasted_iota(jnp.int32, (rows, rows), 1)
    upto = jnp.where(of <= at, 1.0, 0.0).astype(jnp.bfloat16)
    within = jnp.dot(upto, steps, preferred_element_type=jnp.float32)
    whole = within[rows - 1 :, :]
    left = whole - within
    some, chunk, several = rows // 2, CORES * LANES, 4
    state_row = lax.broadcasted_iota(jnp.int32, (NS, some), 0)
    for first in range(0, rows, some):
        span = slice(first, first + some)
        chosen = [
            jnp.concatenate(
                [
                    jnp.where(state_row == m, maps[:NS, span], 0.0).astype(jnp.bfloat16)
                    for m in range(n, n + several)
                ],
                axis=1,
            )
            for n in range(0, NS, several)
        ]
        for item in range(width // chunk):
            lanes = slice(item * chunk, (item + 1) * chunk)
            left_here = left[span, lanes].reshape(some // SUBLANES, SUBLANES, chunk)
            push_here = push[span, lanes]
            added = state_ref[:, lanes]
            if first == 0:
                added = jnp.exp2(rates_ref[:, lanes] * whole[:, lanes]) * added
            for n in range(0, NS, several):
                pushed = []
                for m in range(n, n + several):
                    rate = wide_ref[m * SUBLANES : (m + 1) * SUBLANES, lanes]
                    decay = jnp.exp2(left_here * rate[None]).reshape(some, chunk)
                    pushed.append(decay.astype(jnp.bfloat16) * push_here)
                added = added + jnp.dot(
                    chosen[n // several],
                    jnp.concatenate(pushed, axis=0),
                    preferred_element_type=jnp.float32,
                )
            state_ref[:, lanes] = added
    total_ref[...] = total_ref[...] + whole

    @pl.when(step == pl.num_programs(0) - 1)
    def _():
        turn_ref[...] = jnp.zeros_like(turn_ref)
        for item in range(tile):
            turn_ref[item : item + 1, :] = total_ref[:, item * LANES : (item + 1) * LANES]
        sums = jnp.concatenate(split(turn_ref[...]), axis=0)
        state = state_ref[...].astype(jnp.bfloat16)
        for target in range(carry_ref.shape[0]):
            for item in range(tile):
                carry_ref[target, item * NS : (item + 1) * NS, :] = state[
                    :, item * LANES : (item + 1) * LANES
                ]
            carry_ref[target, tile * NS :, :] = sums


def step_sizes(place, own, come, low_own, low_come, cols, bias, rates, targets):
    chips = come.shape[0] + 1
    rows, width = own.shape[1] // CORES, own.shape[2]
    tile = width // LANES
    map_row = CORES * rows // MAPS

    def slot(b, s):
        return jnp.maximum(lax.rem(s[0] - b // CORES + chips, chips) - 1, 0)

    def core(b):
        return lax.rem(b, CORES)

    def fixed(*shape):
        return pl.BlockSpec(shape, lambda b, s: (0,) * len(shape))

    return pl.pallas_call(
        step_kernel,
        grid_spec=pltpu.PrefetchScalarGridSpec(
            num_scalar_prefetch=1,
            grid=(chips * CORES,),
            in_specs=[
                pl.BlockSpec((1, rows, width), lambda b, s: (0, core(b), 0)),
                pl.BlockSpec((1, rows, width), lambda b, s: (slot(b, s), core(b), 0)),
                pl.BlockSpec((rows, RANK), lambda b, s: (core(b), 0)),
                pl.BlockSpec((1, rows, RANK), lambda b, s: (slot(b, s), core(b), 0)),
                pl.BlockSpec((MAPS, rows), lambda b, s: (map_row, core(b))),
                pl.BlockSpec((1, MAPS, rows), lambda b, s: (slot(b, s), map_row, core(b))),
                fixed(*cols.shape),
                fixed(*bias.shape),
                fixed(*rates.shape),
            ],
            out_specs=[
                pl.BlockSpec((rows, width), lambda b, s: (b, 0)),
                pl.BlockSpec((rows, width), lambda b, s: (b, 0)),
                pl.BlockSpec((1, 2 * NS, rows), lambda b, s: (b, 0, 0)),
                fixed(targets, (tile + 1) * NS, LANES),
            ],
            scratch_shapes=[
                pltpu.VMEM((NS, width), jnp.float32),
                pltpu.VMEM((1, width), jnp.float32),
                pltpu.VMEM((SUBLANES, LANES), jnp.float32),
                pltpu.VMEM((NS * SUBLANES, width), jnp.float32),
            ],
        ),
        out_shape=[
            jax.ShapeDtypeStruct((chips * CORES * rows, width), jnp.bfloat16),
            jax.ShapeDtypeStruct((chips * CORES * rows, width), jnp.bfloat16),
            jax.ShapeDtypeStruct((chips * CORES, 2 * NS, rows), jnp.float32),
            jax.ShapeDtypeStruct((targets, (tile + 1) * NS, LANES), jnp.bfloat16),
        ],
        compiler_params=params,
        name="step_sizes",
    )(place, own, come, low_own, low_come, low_own, low_come, cols, bias, rates)


def scan_kernel(
    place_ref, steps_ref, stream_ref, maps_ref, rates_ref, gain_ref, carry_ref, out_ref,
    state_ref, into_ref, out_of_ref, *work_refs,
):
    step = pl.program_id(0)
    rows, width = steps_ref.shape
    tile = width // LANES
    hist_refs, drive_refs = work_refs[:2], work_refs[2:]

    @pl.when(step == 0)
    def _():
        state_ref[...] = jnp.zeros_like(state_ref)

        def compose(row, nothing):
            sums = carry_ref[row, tile * NS :, :].astype(jnp.float32)
            sums = sums[:SUBLANES, :] + sums[SUBLANES:, :]
            for item in range(tile):
                lanes = slice(item * LANES, (item + 1) * LANES)
                decay = jnp.exp2(rates_ref[:, lanes] * sums[item : item + 1, :])
                added = carry_ref[row, item * NS : (item + 1) * NS, :].astype(jnp.float32)
                state_ref[:, lanes] = decay * state_ref[:, lanes] + added
            return nothing

        lax.fori_loop(0, place_ref[0], compose, 0)

    source = lax.broadcasted_iota(jnp.int32, (LANES, NS * NS), 0)
    column = lax.rem(lax.broadcasted_iota(jnp.int32, (LANES, NS * NS), 1), NS)
    token = lax.rem(lax.broadcasted_iota(jnp.int32, (rows, NS * NS), 0), NS)
    slot = lax.broadcasted_iota(jnp.int32, (rows, NS * NS), 1) // NS
    turned = jnp.concatenate(
        [maps_ref[0], jnp.zeros((LANES - 2 * NS, rows), jnp.float32)], axis=0
    ).T.astype(jnp.bfloat16)
    for ref, base in ((into_ref, 0), (out_of_ref, NS)):
        pick = jnp.where(source == base + column, 1.0, 0.0).astype(jnp.bfloat16)
        spread = jnp.dot(turned, pick, preferred_element_type=jnp.float32)
        ref[...] = jnp.where(token == slot, spread, 0.0).astype(jnp.bfloat16)
    half = width // 2

    def fill(first, drive_ref):
        here = pl.ds(first, NS)
        push = steps_ref[here, :] * stream_ref[here, :]
        drive_ref[...] = lax.dot_general(
            into_ref[here, :], push, (((0,), (0,)), ((), ())), preferred_element_type=jnp.float32
        )

    def finish(first, hist_ref):
        here = pl.ds(first, NS)
        mixed = jnp.dot(out_of_ref[here, :], hist_ref[...], preferred_element_type=jnp.float32)
        direct = gain_ref[...] * stream_ref[here, :].astype(jnp.float32)
        out_ref[here, :] = (mixed + direct).astype(jnp.bfloat16)

    def advance(first, hist_ref, drive_ref):
        here = pl.ds(first, NS)
        for lanes in (slice(0, half), slice(half, width)):
            state = state_ref[:, lanes]
            rates = rates_ref[:, lanes]
            steps = steps_ref[here, lanes].astype(jnp.float32)
            for near in range(NS):
                part = slice(near * NS, (near + 1) * NS)
                decay = jnp.exp2(rates * steps[near : near + 1, :])
                state = decay * state + drive_ref[part, lanes]
                hist_ref[part, lanes] = state.astype(jnp.bfloat16)
            state_ref[:, lanes] = state

    def pair(index, nothing):
        first = pl.multiple_of(index * 2 * NS, 2 * NS)
        second = pl.multiple_of(first + NS, NS)
        after = pl.multiple_of(jnp.minimum(second + NS, rows - NS), NS)
        fill(second, drive_refs[1])
        advance(first, hist_refs[0], drive_refs[0])
        finish(first, hist_refs[0])
        fill(after, drive_refs[0])
        advance(second, hist_refs[1], drive_refs[1])
        finish(second, hist_refs[1])
        return nothing

    fill(0, drive_refs[0])
    lax.fori_loop(0, rows // (2 * NS), pair, 0)


def scan_rows(place, steps, stream, maps, rates, gain, carries):
    blocks, _, rows = maps.shape
    width = rates.shape[1]

    def fixed(*shape):
        return pl.BlockSpec(shape, lambda b, s: (0,) * len(shape))

    block = pl.BlockSpec((rows, width), lambda b, s: (b, 0))
    return pl.pallas_call(
        scan_kernel,
        grid_spec=pltpu.PrefetchScalarGridSpec(
            num_scalar_prefetch=1,
            grid=(blocks,),
            in_specs=[
                block,
                block,
                pl.BlockSpec((1, 2 * NS, rows), lambda b, s: (b, 0, 0)),
                fixed(*rates.shape),
                fixed(*gain.shape),
                fixed(*carries.shape),
            ],
            out_specs=block,
            scratch_shapes=[
                pltpu.VMEM((NS, width), jnp.float32),
                pltpu.VMEM((rows, NS * NS), jnp.bfloat16),
                pltpu.VMEM((rows, NS * NS), jnp.bfloat16),
                pltpu.VMEM((NS * NS, width), jnp.bfloat16),
                pltpu.VMEM((NS * NS, width), jnp.bfloat16),
                pltpu.VMEM((NS * NS, width), jnp.float32),
                pltpu.VMEM((NS * NS, width), jnp.float32),
            ],
        ),
        out_shape=jax.ShapeDtypeStruct((blocks * rows, width), jnp.bfloat16),
        compiler_params=params,
        name="scan_rows",
    )(place, steps, stream, maps, rates, gain, carries)


def local(
    queries, keys, values, doc_lengths, rank_in, bc_weight, rank_out, dt_bias, a_log, skip_gain
):
    devices = lax.axis_size("seq")
    chips = devices // CORES
    targets = lax.axis_size("chan")
    seq_place = lax.axis_index("seq").astype(jnp.int32)
    chan_place = lax.axis_index("chan").astype(jnp.int32)
    chip, core = seq_place // CORES, lax.rem(seq_place, CORES)
    place = jnp.stack([chip, core])
    width = queries.shape[2] // devices
    wide = max(HEAD_SIZE, keys.shape[2] // devices)

    def other(device):
        return device + 1 - 2 * (device % CORES)

    swap = [(device, other(device)) for device in range(devices)]
    near = [(device, device + CORES) for device in range(devices - CORES)]
    far = [(device, other(device + CORES)) for device in range(devices - CORES)]

    def onward(chips_on):
        return [(device, (device + chips_on * CORES) % devices) for device in range(devices)]

    own, theirs = select_heads(keys[0], values[0], chips, wide)
    from_near = lax.ppermute(own, "seq", near)
    from_far = lax.ppermute(theirs, "seq", far)
    swapped = lax.ppermute(theirs, "seq", swap)
    their_queries = lax.ppermute(other_queries(own, queries[0], chips), "seq", swap)
    blocks = (own, swapped, from_near, from_far)
    both_queries = (queries[0], their_queries)

    sent, part = attend(
        place, doc_lengths, both_queries, blocks, rank_in, bc_weight, None, 1, chips - 1
    )
    come = [lax.ppermute(sent[step], "seq", onward(step + 1)) for step in range(chips - 1)]
    stayed, part = attend(
        place, doc_lengths, both_queries, blocks, rank_in, bc_weight, part, 0, 1
    )
    low_own = low_and_maps(part, lax.ppermute(part, "seq", swap))
    low_come = [lax.ppermute(low_own, "seq", onward(step + 1)) for step in range(chips - 1)]
    got_sent = lax.ppermute(sent, "seq", swap)
    got_stayed = lax.ppermute(stayed, "seq", swap)
    attn_rows = join_heads(sent, stayed, got_sent, got_stayed)

    first = seq_place * width
    logs = lax.dynamic_slice_in_dim(a_log, first, width, 0)
    rates = (-LOG2E * jnp.exp(logs)).T
    cols = lax.dynamic_slice_in_dim(rank_out, first, width, 1)
    bias = lax.dynamic_slice_in_dim(dt_bias, first, width, 0)[None]
    gain = lax.dynamic_slice_in_dim(skip_gain, first, width, 0)[None]
    steps, stream, maps, carry = step_sizes(
        place, stayed, jnp.stack(come), low_own, jnp.stack(low_come), cols, bias, rates, targets
    )
    carries = lax.all_to_all(carry, "chan", split_axis=0, concat_axis=0, tiled=True)
    ssm_rows = scan_rows(chan_place[None], steps, stream, maps, rates, gain, carries)
    return (attn_rows[None], ssm_rows[None])


def solution(mesh):
    return jax.shard_map(
        local,
        mesh=mesh,
        in_specs=(
            P("chan", "seq", None),
            P("chan", "seq", None),
            P("chan", "seq", None),
            P("chan", None),
            P(),
            P(),
            P(),
            P(),
            P(),
            P(),
        ),
        out_specs=(P("chan", "seq", None), P("chan", None, "seq")),
        check_vma=False,
    )
```

```python
import functools
import math

import jax
import jax.numpy as jnp
from jax import lax
from jax.experimental import pallas as pl
from jax.experimental.pallas import tpu as pltpu
from jax.sharding import PartitionSpec as P

QUERY_HEADS = 32
KEY_VALUE_HEADS = 8
HEAD_SIZE = 128
GROUP = QUERY_HEADS // KEY_VALUE_HEADS
NS = 16
RANK = 256
CORES = 2
LANES = 128
SUBLANES = 8
MAPS = 4 * NS
UNROLL = 8
LOG2E = 1.4426950408889634

masked_fill = -1e30
params = pltpu.CompilerParams(vmem_limit_bytes=60 << 20)


def split(value):
    coarse = value.astype(jnp.bfloat16)
    return coarse, (value - coarse.astype(jnp.float32)).astype(jnp.bfloat16)


def run_copies(pairs, sems):
    copies = [
        pltpu.make_async_copy(source, target, sems.at[i]) for i, (source, target) in enumerate(pairs)
    ]
    for copy in copies:
        copy.start()
    for copy in copies:
        copy.wait()


def columns_of(ref, index, size):
    return ref.at[:, pl.ds(pl.multiple_of(index * size, LANES), size)]


def heads_kernel(key_ref, value_ref, own_ref, their_ref, sems):
    core = lax.rem(lax.axis_index("seq"), CORES)
    wide = own_ref.shape[3]
    halves = key_ref.shape[1] // wide // own_ref.shape[0]
    pairs = []
    for target, which in ((own_ref, core), (their_ref, 1 - core)):
        for chip in range(own_ref.shape[0]):
            index = chip * halves + (which if halves == CORES else 0)
            for kind, source in enumerate((key_ref, value_ref)):
                pairs.append((columns_of(source, index, wide), target.at[chip, kind]))
    run_copies(pairs, sems)


def select_heads(keys, values, chips, wide):
    shape = jax.ShapeDtypeStruct((chips, 2, keys.shape[0], wide), keys.dtype)
    return pl.pallas_call(
        heads_kernel,
        in_specs=[pl.BlockSpec(memory_space=pl.ANY)] * 2,
        out_shape=[shape, shape],
        scratch_shapes=[pltpu.SemaphoreType.DMA((4 * chips,))],
        compiler_params=params,
        name="select_heads",
    )(keys, values)


def join_kernel(sent_ref, stayed_ref, got_sent_ref, got_stayed_ref, out_ref, sems):
    place = lax.axis_index("seq")
    core, chip = lax.rem(place, CORES), place // CORES
    rows = out_ref.shape[0]
    others, _, width = sent_ref.shape
    here = pl.ds(pl.multiple_of(core * rows, rows), rows)
    pairs = []
    for first, rest, which in (
        (stayed_ref, sent_ref, core), (got_stayed_ref, got_sent_ref, 1 - core)
    ):
        for step in range(others + 1):
            source = first.at[0, here, :] if step == 0 else rest.at[step - 1, here, :]
            owner = lax.rem(chip + step, others + 1)
            pairs.append((source, columns_of(out_ref, owner * CORES + which, width)))
    run_copies(pairs, sems)


def join_heads(sent, stayed, got_sent, got_stayed):
    others, rows, width = sent.shape
    return pl.pallas_call(
        join_kernel,
        in_specs=[pl.BlockSpec(memory_space=pl.ANY)] * 4,
        out_shape=jax.ShapeDtypeStruct(
            (rows // CORES, (others + 1) * CORES * width), sent.dtype
        ),
        scratch_shapes=[pltpu.SemaphoreType.DMA((CORES * (others + 1),))],
        compiler_params=params,
        name="join_heads",
    )(sent, stayed, got_sent, got_stayed)


def attend_kernel(
    place_ref, doc_ref, mine_ref, theirs_ref, own_ref, swap_ref, near_ref, far_ref,
    rank_ref, map_ref, send_ref, stay_ref, low_ref, maps_ref, mask_ref, *, chips,
):
    step = pl.program_id(0)
    rows = mine_ref.shape[0]
    group = mine_ref.shape[1] // HEAD_SIZE
    chip, core = place_ref[0], place_ref[1]
    first_core = core == 0

    def above(shape):
        row = lax.rem(lax.broadcasted_iota(jnp.int32, shape, 0), rows)
        return lax.broadcasted_iota(jnp.int32, shape, 1) > row

    @pl.when(step == 0)
    def _():
        low_ref[...] = jnp.zeros_like(low_ref)
        maps_ref[...] = jnp.zeros_like(maps_ref)
        own = chip * CORES + core
        swapped = chip * CORES + 1 - core
        near, far = own - CORES, swapped - CORES
        lane = lax.broadcasted_iota(jnp.int32, (rows, rows), 1)
        row = lax.broadcasted_iota(jnp.int32, (rows, rows), 0)
        for item, (place, before, middle) in enumerate(
            (
                (own, near, jnp.where(first_core, far, swapped)),
                (swapped, far, jnp.where(first_core, own, near)),
            )
        ):
            query_pos = place * rows + row
            start = jnp.zeros((rows, rows), jnp.int32)
            bound = jnp.int32(0)
            for doc in range(doc_ref.shape[1]):
                bound = bound + doc_ref[0, doc]
                start = jnp.where(query_pos >= bound, bound, start)
            ends = jnp.where(lane > row, before, place) * rows + lane
            mask_ref[item, :, :rows] = jnp.where(
                (ends >= start) & (ends <= query_pos), 0.0, masked_fill
            )
            mask_ref[item, :, rows:] = jnp.where(
                middle * rows + lane >= start, 0.0, masked_fill
            )

    scale = LOG2E / math.sqrt(HEAD_SIZE)
    ones = jnp.ones((3 * rows, HEAD_SIZE), jnp.bfloat16)

    def windows(kind):
        own, swapped = own_ref[0, kind], swap_ref[0, kind]
        near, far = near_ref[0, kind], far_ref[0, kind]
        return (
            jnp.concatenate([near, own, jnp.where(first_core, far, swapped)], axis=0),
            jnp.concatenate([far, swapped, jnp.where(first_core, own, near)], axis=0),
        )

    scores = []
    for keys, query in zip(windows(0), (mine_ref[...], theirs_ref[...])):
        stacked = jnp.concatenate(
            [query[:, i * HEAD_SIZE : (i + 1) * HEAD_SIZE] for i in range(group)], axis=0
        )
        scores.append(
            lax.dot_general(
                stacked, keys, (((1,), (1,)), ((), ())), preferred_element_type=jnp.float32
            )
        )
    outputs = []
    before = above((group * rows, rows))
    for item, (values, score) in enumerate(zip(windows(1), scores)):
        fill = mask_ref[item]
        ends = jnp.where(before, score[:, :rows], score[:, rows : 2 * rows])
        kept = jnp.concatenate([ends, score[:, 2 * rows :]], axis=1)
        kept = jnp.concatenate(
            [kept[i * rows : (i + 1) * rows, :] + fill for i in range(group)], axis=0
        )
        peak = jnp.max(kept, axis=1, keepdims=True)
        raw = jnp.exp2((kept - peak) * scale).astype(jnp.bfloat16)
        ends = raw[:, :rows]
        none = jnp.zeros_like(ends)
        spread = jnp.concatenate(
            [jnp.where(before, ends, none), jnp.where(before, none, ends), raw[:, rows:]], axis=1
        )
        both = jnp.dot(
            spread, jnp.concatenate([values, ones], axis=1), preferred_element_type=jnp.float32
        )
        mixed = both[:, :HEAD_SIZE] * pl.reciprocal(both[:, HEAD_SIZE:])
        mixed = mixed.astype(jnp.bfloat16)
        outputs.append(
            jnp.concatenate([mixed[i * rows : (i + 1) * rows, :] for i in range(group)], axis=1)
        )
    stream = jnp.concatenate(
        [
            jnp.where(first_core, outputs[0], outputs[1]),
            jnp.where(first_core, outputs[1], outputs[0]),
        ],
        axis=0,
    )
    last = step >= pl.num_programs(0) - pl.num_programs(0) // chips

    @pl.when(last)
    def _():
        stay_ref[0] = stream

    @pl.when(jnp.logical_not(last))
    def _():
        send_ref[0] = stream

    low_ref[...] += jnp.dot(stream, rank_ref[...], preferred_element_type=jnp.float32)
    maps_ref[...] += lax.dot_general(
        map_ref[...], stream, (((1,), (1,)), ((), ())), preferred_element_type=jnp.float32
    )


def attend(place, doc_lengths, queries, blocks, rank_in, map_rows):
    mine, theirs = queries
    chips, _, rows, columns = blocks[0].shape
    heads = columns // HEAD_SIZE
    width = mine.shape[1] // (chips * CORES)
    wide = width // heads

    def owner(j, s):
        return lax.rem(s[0] + 1 + j // heads, chips)

    def column(j, s):
        return (owner(j, s) * CORES + s[1]) * heads + lax.rem(j, heads)

    def sent(j, s):
        at = jnp.minimum(j, (chips - 1) * heads - 1)
        return (at // heads, 0, lax.rem(at, heads))

    query = pl.BlockSpec((rows, wide), lambda j, s: (0, column(j, s)))
    block = pl.BlockSpec(
        (1, 2, rows, HEAD_SIZE), lambda j, s: (owner(j, s), 0, 0, lax.rem(j, heads))
    )
    return pl.pallas_call(
        functools.partial(attend_kernel, chips=chips),
        grid_spec=pltpu.PrefetchScalarGridSpec(
            num_scalar_prefetch=1,
            grid=(chips * heads,),
            in_specs=[pl.BlockSpec(memory_space=pltpu.SMEM), query, query]
            + [block] * 4
            + [
                pl.BlockSpec((wide, RANK), lambda j, s: (column(j, s), 0)),
                pl.BlockSpec((2 * NS, wide), lambda j, s: (0, column(j, s))),
            ],
            out_specs=[
                pl.BlockSpec((1, CORES * rows, wide), sent),
                pl.BlockSpec(
                    (1, CORES * rows, wide),
                    lambda j, s: (0, 0, jnp.maximum(j - (chips - 1) * heads, 0)),
                ),
                pl.BlockSpec((CORES * rows, RANK), lambda j, s: (0, 0)),
                pl.BlockSpec((2 * NS, CORES * rows), lambda j, s: (0, 0)),
            ],
            scratch_shapes=[pltpu.VMEM((2, rows, 2 * rows), jnp.float32)],
        ),
        out_shape=[
            jax.ShapeDtypeStruct((chips - 1, CORES * rows, width), jnp.bfloat16),
            jax.ShapeDtypeStruct((1, CORES * rows, width), jnp.bfloat16),
            jax.ShapeDtypeStruct((CORES * rows, RANK), jnp.float32),
            jax.ShapeDtypeStruct((2 * NS, CORES * rows), jnp.float32),
        ],
        compiler_params=params,
        cost_estimate=pl.CostEstimate(flops=5 * 10**9, bytes_accessed=1 << 22, transcendentals=0),
        name="attend",
    )(place, doc_lengths, mine, theirs, *blocks, rank_in, map_rows)


def low_kernel(low_ref, maps_ref, their_low_ref, their_maps_ref, out_ref):
    rows = low_ref.shape[0]
    out_ref[:rows, :] = (low_ref[...] + their_low_ref[...]).astype(jnp.bfloat16)
    out_ref[rows:, :] = jnp.concatenate(split(maps_ref[...] + their_maps_ref[...]), axis=0)


def low_and_maps(low, maps, their_low, their_maps):
    rows = low.shape[0]
    return pl.pallas_call(
        low_kernel,
        out_shape=jax.ShapeDtypeStruct((rows + MAPS, RANK), jnp.bfloat16),
        compiler_params=params,
        cost_estimate=pl.CostEstimate(flops=1, bytes_accessed=1, transcendentals=0),
        name="low_and_maps",
    )(low, maps, their_low, their_maps)


def softplus(value):
    small = jnp.exp(-jnp.abs(value))
    tail = jnp.where(small < 0.00390625, small * (1.0 - 0.5 * small), jnp.log(1.0 + small))
    return jnp.maximum(value, 0.0) + tail


def spread_maps(maps, spread_ref, first, count):
    rows = maps.shape[0]
    for n in range(count):
        spread_ref[n * rows : (n + 1) * rows, :] = jnp.broadcast_to(
            maps[:, first + n : first + n + 1], (rows, LANES)
        )


def step_kernel(
    place_ref, own_ref, come_ref, low_own_ref, low_come_ref, map_own_ref, map_come_ref,
    cols_ref, bias_ref, rates_ref,
    steps_ref, push_ref, stream_ref, maps_ref, carry_ref, state_ref, total_ref, spread_ref,
):
    block = pl.program_id(0)
    rows, width = own_ref.shape[1:]
    tile = width // LANES
    here = block // CORES == place_ref[0]

    @pl.when(block == 0)
    def _():
        state_ref[...] = jnp.zeros_like(state_ref)
        total_ref[...] = jnp.zeros_like(total_ref)

    stream = jnp.where(here, own_ref[0], come_ref[0])
    stream_ref[...] = stream
    lows = jnp.where(here, low_own_ref[...], low_come_ref[0])
    maps = jnp.where(here, map_own_ref[...], map_come_ref[0]).astype(jnp.float32)
    maps = maps[: 2 * NS, :] + maps[2 * NS :, :]
    maps = jnp.concatenate([maps, jnp.zeros((LANES - 2 * NS, rows), jnp.float32)], axis=0).T
    maps_ref[...] = maps
    spread_maps(maps, spread_ref, 0, NS)
    logits = jnp.dot(lows, cols_ref[...], preferred_element_type=jnp.float32)
    steps = softplus(logits + bias_ref[...])
    push = steps * stream.astype(jnp.float32)
    for item in range(tile):
        lanes = slice(item * LANES, (item + 1) * LANES)
        steps_ref[pl.ds(item, rows, stride=tile), :] = steps[:, lanes]
        push_ref[pl.ds(item, rows, stride=tile), :] = push[:, lanes]

    rates = [rates_ref[n * tile : (n + 1) * tile, :] for n in range(NS)]

    def some(index, held):
        total, states = held[0], list(held[1:])
        base = pl.multiple_of(index * UNROLL, UNROLL)
        for near in range(UNROLL):
            at = pl.multiple_of((base + near) * tile, tile)
            step = steps_ref[pl.ds(at, tile), :]
            push = push_ref[pl.ds(at, tile), :]
            total = total + step
            for n in range(NS):
                into = spread_ref[pl.ds(n * rows + base + near, 1), :]
                states[n] = jnp.exp2(step * rates[n]) * states[n] + push * into
        return (total, *states)

    held = (total_ref[...],) + tuple(state_ref[n * tile : (n + 1) * tile, :] for n in range(NS))
    held = lax.fori_loop(0, rows // UNROLL, some, held)
    total_ref[...] = held[0]
    for n in range(NS):
        state_ref[n * tile : (n + 1) * tile, :] = held[1 + n]

    @pl.when(block == pl.num_programs(0) - 1)
    def _():
        whole = jnp.concatenate([state_ref[...].astype(jnp.bfloat16), *split(total_ref[...])], axis=0)
        for target in range(carry_ref.shape[0]):
            carry_ref[target] = whole


def step_sizes(place, own, come, low_own, low_come, cols, bias, rates, targets):
    chips = come.shape[0] + 1
    rows, width = own.shape[1] // CORES, own.shape[2]
    tile = width // LANES
    map_row = CORES * rows // MAPS
    blocks = chips * CORES

    def slot(b, s):
        return jnp.maximum(lax.rem(s[0] - b // CORES + chips, chips) - 1, 0)

    def core(b):
        return lax.rem(b, CORES)

    def fixed(*shape):
        return pl.BlockSpec(shape, lambda b, s: (0,) * len(shape))

    folded = jax.ShapeDtypeStruct((blocks * rows * tile, LANES), jnp.float32)
    folded_block = pl.BlockSpec((rows * tile, LANES), lambda b, s: (b, 0))
    return pl.pallas_call(
        step_kernel,
        grid_spec=pltpu.PrefetchScalarGridSpec(
            num_scalar_prefetch=1,
            grid=(blocks,),
            in_specs=[
                pl.BlockSpec((1, rows, width), lambda b, s: (0, core(b), 0)),
                pl.BlockSpec((1, rows, width), lambda b, s: (slot(b, s), core(b), 0)),
                pl.BlockSpec((rows, RANK), lambda b, s: (core(b), 0)),
                pl.BlockSpec((1, rows, RANK), lambda b, s: (slot(b, s), core(b), 0)),
                pl.BlockSpec((MAPS, rows), lambda b, s: (map_row, core(b))),
                pl.BlockSpec((1, MAPS, rows), lambda b, s: (slot(b, s), map_row, core(b))),
                fixed(*cols.shape),
                fixed(*bias.shape),
                fixed(*rates.shape),
            ],
            out_specs=[
                folded_block,
                folded_block,
                pl.BlockSpec((rows, width), lambda b, s: (b, 0)),
                pl.BlockSpec((rows, LANES), lambda b, s: (b, 0)),
                fixed(targets, (NS + 2) * tile, LANES),
            ],
            scratch_shapes=[
                pltpu.VMEM((NS * tile, LANES), jnp.float32),
                pltpu.VMEM((tile, LANES), jnp.float32),
                pltpu.VMEM((NS * rows, LANES), jnp.float32),
            ],
        ),
        out_shape=[
            folded,
            folded,
            jax.ShapeDtypeStruct((blocks * rows, width), jnp.bfloat16),
            jax.ShapeDtypeStruct((blocks * rows, LANES), jnp.float32),
            jax.ShapeDtypeStruct((targets, (NS + 2) * tile, LANES), jnp.bfloat16),
        ],
        compiler_params=params,
        name="step_sizes",
    )(place, own, come, low_own, low_come, low_own, low_come, cols, bias, rates)


def scan_kernel(
    place_ref, steps_ref, push_ref, stream_ref, maps_ref, rates_ref, gain_ref, carry_ref, out_ref,
    state_ref, spread_ref, folded_ref,
):
    block = pl.program_id(0)
    rows, width = stream_ref.shape
    tile = width // LANES

    @pl.when(block == 0)
    def _():
        state_ref[...] = jnp.zeros_like(state_ref)

        def compose(row, nothing):
            whole = carry_ref[row].astype(jnp.float32)
            total = whole[NS * tile : (NS + 1) * tile, :] + whole[(NS + 1) * tile :, :]
            for n in range(NS):
                part = slice(n * tile, (n + 1) * tile)
                decay = jnp.exp2(rates_ref[part, :] * total)
                state_ref[part, :] = decay * state_ref[part, :] + whole[part, :]
            return nothing

        lax.fori_loop(0, place_ref[0], compose, 0)

    spread_maps(maps_ref[...], spread_ref, 0, 2 * NS)
    rates = [rates_ref[n * tile : (n + 1) * tile, :] for n in range(NS)]

    def some(index, states):
        states = list(states)
        base = pl.multiple_of(index * UNROLL, UNROLL)
        for near in range(UNROLL):
            at = pl.multiple_of((base + near) * tile, tile)
            step = steps_ref[pl.ds(at, tile), :]
            push = push_ref[pl.ds(at, tile), :]
            sums = [None, None]
            for n in range(NS):
                into = spread_ref[pl.ds(n * rows + base + near, 1), :]
                out_of = spread_ref[pl.ds((NS + n) * rows + base + near, 1), :]
                states[n] = jnp.exp2(step * rates[n]) * states[n] + push * into
                term = states[n] * out_of
                sums[n % 2] = term if sums[n % 2] is None else sums[n % 2] + term
            folded_ref[pl.ds(at, tile), :] = sums[0] + sums[1]
        return tuple(states)

    held = tuple(state_ref[n * tile : (n + 1) * tile, :] for n in range(NS))
    held = lax.fori_loop(0, rows // UNROLL, some, held)
    for n in range(NS):
        state_ref[n * tile : (n + 1) * tile, :] = held[n]
    for item in range(tile):
        lanes = slice(item * LANES, (item + 1) * LANES)
        direct = gain_ref[:, lanes] * stream_ref[:, lanes].astype(jnp.float32)
        mixed = folded_ref[pl.ds(item, rows, stride=tile), :]
        out_ref[:, lanes] = (mixed + direct).astype(jnp.bfloat16)


def scan_rows(place, steps, push, stream, maps, rates, gain, carries, rows):
    length, width = stream.shape
    tile = width // LANES

    def fixed(*shape):
        return pl.BlockSpec(shape, lambda b, s: (0,) * len(shape))

    block = pl.BlockSpec((rows, width), lambda b, s: (b, 0))
    folded = pl.BlockSpec((rows * tile, LANES), lambda b, s: (b, 0))
    return pl.pallas_call(
        scan_kernel,
        grid_spec=pltpu.PrefetchScalarGridSpec(
            num_scalar_prefetch=1,
            grid=(length // rows,),
            in_specs=[
                folded,
                folded,
                block,
                pl.BlockSpec((rows, LANES), lambda b, s: (b, 0)),
                fixed(*rates.shape),
                fixed(*gain.shape),
                fixed(*carries.shape),
            ],
            out_specs=block,
            scratch_shapes=[
                pltpu.VMEM((NS * tile, LANES), jnp.float32),
                pltpu.VMEM((2 * NS * rows, LANES), jnp.float32),
                pltpu.VMEM((rows * tile, LANES), jnp.float32),
            ],
        ),
        out_shape=jax.ShapeDtypeStruct((length, width), jnp.bfloat16),
        compiler_params=params,
        name="scan_rows",
    )(place, steps, push, stream, maps, rates, gain, carries)


def local(
    queries, keys, values, doc_lengths, rank_in, bc_weight, rank_out, dt_bias, a_log, skip_gain
):
    devices = lax.axis_size("seq")
    chips = devices // CORES
    targets = lax.axis_size("chan")
    seq_place = lax.axis_index("seq").astype(jnp.int32)
    chan_place = lax.axis_index("chan").astype(jnp.int32)
    chip, core = seq_place // CORES, lax.rem(seq_place, CORES)
    place = jnp.stack([chip, core])
    width = queries.shape[2] // devices
    wide = max(HEAD_SIZE, keys.shape[2] // devices)

    def other(device):
        return device + 1 - 2 * (device % CORES)

    swap = [(device, other(device)) for device in range(devices)]
    near = [(device, device + CORES) for device in range(devices - CORES)]
    far = [(device, other(device + CORES)) for device in range(devices - CORES)]

    def onward(chips_on):
        return [(device, (device + chips_on * CORES) % devices) for device in range(devices)]

    own, theirs = select_heads(keys[0], values[0], chips, wide)
    from_near = lax.ppermute(own, "seq", near)
    from_far = lax.ppermute(theirs, "seq", far)
    swapped = lax.ppermute(theirs, "seq", swap)
    their_queries = lax.ppermute(queries[0], "seq", swap)
    blocks = (own, swapped, from_near, from_far)

    sent, stayed, low, maps = attend(
        place, doc_lengths, (queries[0], their_queries), blocks, rank_in, bc_weight.T
    )
    come = [lax.ppermute(sent[step], "seq", onward(step + 1)) for step in range(chips - 1)]
    low_own = low_and_maps(low, maps, *lax.ppermute((low, maps), "seq", swap))
    low_come = [lax.ppermute(low_own, "seq", onward(step + 1)) for step in range(chips - 1)]
    got_sent = lax.ppermute(sent, "seq", swap)
    got_stayed = lax.ppermute(stayed, "seq", swap)
    attn_rows = join_heads(sent, stayed, got_sent, got_stayed)

    first = seq_place * width
    logs = lax.dynamic_slice_in_dim(a_log, first, width, 0)
    rates = (-LOG2E * jnp.exp(logs)).T.reshape(NS * width // LANES, LANES)
    cols = lax.dynamic_slice_in_dim(rank_out, first, width, 1)
    bias = lax.dynamic_slice_in_dim(dt_bias, first, width, 0)[None]
    gain = lax.dynamic_slice_in_dim(skip_gain, first, width, 0)[None]
    steps, push, stream, maps, carry = step_sizes(
        place, stayed, jnp.stack(come), low_own, jnp.stack(low_come), cols, bias, rates, targets
    )
    carries = lax.all_to_all(carry, "chan", split_axis=0, concat_axis=0, tiled=True)
    ssm_rows = scan_rows(
        chan_place[None], steps, push, stream, maps, rates, gain, carries, queries.shape[1]
    )
    return (attn_rows[None], ssm_rows[None])


def solution(mesh):
    return jax.shard_map(
        local,
        mesh=mesh,
        in_specs=(
            P("chan", "seq", None),
            P("chan", "seq", None),
            P("chan", "seq", None),
            P("chan", None),
            P(),
            P(),
            P(),
            P(),
            P(),
            P(),
        ),
        out_specs=(P("chan", "seq", None), P("chan", None, "seq")),
        check_vma=False,
    )
```

```python
import functools
import math

import jax
import jax.numpy as jnp
from jax import lax
from jax.experimental import pallas as pl
from jax.experimental.pallas import tpu as pltpu
from jax.sharding import PartitionSpec as P

QUERY_HEADS = 32
KEY_VALUE_HEADS = 8
HEAD_SIZE = 128
GROUP = QUERY_HEADS // KEY_VALUE_HEADS
NS = 16
RANK = 256
CORES = 2
LANES = 128
SUBLANES = 8
MAPS = 4 * NS
UNROLL = 8

masked_fill = -1e30
params = pltpu.CompilerParams(vmem_limit_bytes=60 << 20)


def split(value):
    coarse = value.astype(jnp.bfloat16)
    return coarse, (value - coarse.astype(jnp.float32)).astype(jnp.bfloat16)


def run_copies(pairs, sems):
    copies = [
        pltpu.make_async_copy(source, target, sems.at[i]) for i, (source, target) in enumerate(pairs)
    ]
    for copy in copies:
        copy.start()
    for copy in copies:
        copy.wait()


def columns_of(ref, index, size):
    return ref.at[:, pl.ds(pl.multiple_of(index * size, LANES), size)]


def heads_kernel(key_ref, value_ref, own_ref, their_ref, sems):
    core = lax.rem(lax.axis_index("seq"), CORES)
    wide = own_ref.shape[3]
    halves = key_ref.shape[1] // wide // own_ref.shape[0]
    pairs = []
    for target, which in ((own_ref, core), (their_ref, 1 - core)):
        for chip in range(own_ref.shape[0]):
            index = chip * halves + (which if halves == CORES else 0)
            for kind, source in enumerate((key_ref, value_ref)):
                pairs.append((columns_of(source, index, wide), target.at[chip, kind]))
    run_copies(pairs, sems)


def select_heads(keys, values, chips, wide):
    shape = jax.ShapeDtypeStruct((chips, 2, keys.shape[0], wide), keys.dtype)
    return pl.pallas_call(
        heads_kernel,
        in_specs=[pl.BlockSpec(memory_space=pl.ANY)] * 2,
        out_shape=[shape, shape],
        scratch_shapes=[pltpu.SemaphoreType.DMA((4 * chips,))],
        compiler_params=params,
        name="select_heads",
    )(keys, values)


def join_kernel(sent_ref, stayed_ref, got_sent_ref, got_stayed_ref, out_ref, sems):
    place = lax.axis_index("seq")
    core, chip = lax.rem(place, CORES), place // CORES
    rows = out_ref.shape[0]
    others, _, width = sent_ref.shape
    here = pl.ds(pl.multiple_of(core * rows, rows), rows)
    pairs = []
    for first, rest, which in (
        (stayed_ref, sent_ref, core), (got_stayed_ref, got_sent_ref, 1 - core)
    ):
        for step in range(others + 1):
            source = first.at[0, here, :] if step == 0 else rest.at[step - 1, here, :]
            owner = lax.rem(chip + step, others + 1)
            pairs.append((source, columns_of(out_ref, owner * CORES + which, width)))
    run_copies(pairs, sems)


def join_heads(sent, stayed, got_sent, got_stayed):
    others, rows, width = sent.shape
    return pl.pallas_call(
        join_kernel,
        in_specs=[pl.BlockSpec(memory_space=pl.ANY)] * 4,
        out_shape=jax.ShapeDtypeStruct(
            (rows // CORES, (others + 1) * CORES * width), sent.dtype
        ),
        scratch_shapes=[pltpu.SemaphoreType.DMA((CORES * (others + 1),))],
        compiler_params=params,
        name="join_heads",
    )(sent, stayed, got_sent, got_stayed)


def attend_kernel(
    place_ref, doc_ref, mine_ref, theirs_ref, own_ref, swap_ref, near_ref, far_ref,
    rank_ref, map_ref, send_ref, stay_ref, low_ref, maps_ref, mask_ref, *, chips,
):
    step = pl.program_id(0)
    rows = mine_ref.shape[0]
    group = mine_ref.shape[1] // HEAD_SIZE
    chip, core = place_ref[0], place_ref[1]
    first_core = core == 0

    def above(shape):
        row = lax.rem(lax.broadcasted_iota(jnp.int32, shape, 0), rows)
        return lax.broadcasted_iota(jnp.int32, shape, 1) > row

    @pl.when(step == 0)
    def _():
        low_ref[...] = jnp.zeros_like(low_ref)
        maps_ref[...] = jnp.zeros_like(maps_ref)
        own = chip * CORES + core
        swapped = chip * CORES + 1 - core
        near, far = own - CORES, swapped - CORES
        lane = lax.broadcasted_iota(jnp.int32, (rows, rows), 1)
        row = lax.broadcasted_iota(jnp.int32, (rows, rows), 0)
        for item, (place, before, middle) in enumerate(
            (
                (own, near, jnp.where(first_core, far, swapped)),
                (swapped, far, jnp.where(first_core, own, near)),
            )
        ):
            query_pos = place * rows + row
            start = jnp.zeros((rows, rows), jnp.int32)
            bound = jnp.int32(0)
            for doc in range(doc_ref.shape[1]):
                bound = bound + doc_ref[0, doc]
                start = jnp.where(query_pos >= bound, bound, start)
            ends = jnp.where(lane > row, before, place) * rows + lane
            mask_ref[item, :, :rows] = jnp.where(
                (ends >= start) & (ends <= query_pos), 0.0, masked_fill
            )
            mask_ref[item, :, rows:] = jnp.where(
                middle * rows + lane >= start, 0.0, masked_fill
            )

    scale = 1.0 / math.sqrt(HEAD_SIZE)
    ones = jnp.ones((3 * rows, HEAD_SIZE), jnp.bfloat16)

    def windows(kind):
        own, swapped = own_ref[0, kind], swap_ref[0, kind]
        near, far = near_ref[0, kind], far_ref[0, kind]
        return (
            jnp.concatenate([near, own, jnp.where(first_core, far, swapped)], axis=0),
            jnp.concatenate([far, swapped, jnp.where(first_core, own, near)], axis=0),
        )

    scores = []
    for keys, query in zip(windows(0), (mine_ref[...], theirs_ref[...])):
        stacked = jnp.concatenate(
            [query[:, i * HEAD_SIZE : (i + 1) * HEAD_SIZE] for i in range(group)], axis=0
        )
        scores.append(
            lax.dot_general(
                stacked, keys, (((1,), (1,)), ((), ())), preferred_element_type=jnp.float32
            )
        )
    outputs = []
    before = above((group * rows, rows))
    for item, (values, score) in enumerate(zip(windows(1), scores)):
        fill = mask_ref[item]
        ends = jnp.where(before, score[:, :rows], score[:, rows : 2 * rows])
        kept = jnp.concatenate([ends, score[:, 2 * rows :]], axis=1)
        kept = jnp.concatenate(
            [kept[i * rows : (i + 1) * rows, :] + fill for i in range(group)], axis=0
        )
        peak = jnp.max(kept, axis=1, keepdims=True)
        raw = jnp.exp((kept - peak) * scale).astype(jnp.bfloat16)
        ends = raw[:, :rows]
        none = jnp.zeros_like(ends)
        spread = jnp.concatenate(
            [jnp.where(before, ends, none), jnp.where(before, none, ends), raw[:, rows:]], axis=1
        )
        both = jnp.dot(
            spread, jnp.concatenate([values, ones], axis=1), preferred_element_type=jnp.float32
        )
        mixed = both[:, :HEAD_SIZE] * pl.reciprocal(both[:, HEAD_SIZE:])
        mixed = mixed.astype(jnp.bfloat16)
        outputs.append(
            jnp.concatenate([mixed[i * rows : (i + 1) * rows, :] for i in range(group)], axis=1)
        )
    stream = jnp.concatenate(
        [
            jnp.where(first_core, outputs[0], outputs[1]),
            jnp.where(first_core, outputs[1], outputs[0]),
        ],
        axis=0,
    )
    last = step >= pl.num_programs(0) - pl.num_programs(0) // chips

    @pl.when(last)
    def _():
        stay_ref[0] = stream

    @pl.when(jnp.logical_not(last))
    def _():
        send_ref[0] = stream

    low_ref[...] += jnp.dot(stream, rank_ref[...], preferred_element_type=jnp.float32)
    maps_ref[...] += lax.dot_general(
        map_ref[...], stream, (((1,), (1,)), ((), ())), preferred_element_type=jnp.float32
    )


def attend(place, doc_lengths, queries, blocks, rank_in, map_rows):
    mine, theirs = queries
    chips, _, rows, columns = blocks[0].shape
    heads = columns // HEAD_SIZE
    width = mine.shape[1] // (chips * CORES)
    wide = width // heads

    def owner(j, s):
        return lax.rem(s[0] + 1 + j // heads, chips)

    def column(j, s):
        return (owner(j, s) * CORES + s[1]) * heads + lax.rem(j, heads)

    def sent(j, s):
        at = jnp.minimum(j, (chips - 1) * heads - 1)
        return (at // heads, 0, lax.rem(at, heads))

    query = pl.BlockSpec((rows, wide), lambda j, s: (0, column(j, s)))
    block = pl.BlockSpec(
        (1, 2, rows, HEAD_SIZE), lambda j, s: (owner(j, s), 0, 0, lax.rem(j, heads))
    )
    return pl.pallas_call(
        functools.partial(attend_kernel, chips=chips),
        grid_spec=pltpu.PrefetchScalarGridSpec(
            num_scalar_prefetch=1,
            grid=(chips * heads,),
            in_specs=[pl.BlockSpec(memory_space=pltpu.SMEM), query, query]
            + [block] * 4
            + [
                pl.BlockSpec((wide, RANK), lambda j, s: (column(j, s), 0)),
                pl.BlockSpec((2 * NS, wide), lambda j, s: (0, column(j, s))),
            ],
            out_specs=[
                pl.BlockSpec((1, CORES * rows, wide), sent),
                pl.BlockSpec(
                    (1, CORES * rows, wide),
                    lambda j, s: (0, 0, jnp.maximum(j - (chips - 1) * heads, 0)),
                ),
                pl.BlockSpec((CORES * rows, RANK), lambda j, s: (0, 0)),
                pl.BlockSpec((2 * NS, CORES * rows), lambda j, s: (0, 0)),
            ],
            scratch_shapes=[pltpu.VMEM((2, rows, 2 * rows), jnp.float32)],
        ),
        out_shape=[
            jax.ShapeDtypeStruct((chips - 1, CORES * rows, width), jnp.bfloat16),
            jax.ShapeDtypeStruct((1, CORES * rows, width), jnp.bfloat16),
            jax.ShapeDtypeStruct((CORES * rows, RANK), jnp.float32),
            jax.ShapeDtypeStruct((2 * NS, CORES * rows), jnp.float32),
        ],
        compiler_params=params,
        cost_estimate=pl.CostEstimate(flops=5 * 10**9, bytes_accessed=1 << 22, transcendentals=0),
        name="attend",
    )(place, doc_lengths, mine, theirs, *blocks, rank_in, map_rows)


def low_kernel(low_ref, maps_ref, their_low_ref, their_maps_ref, out_ref):
    rows = low_ref.shape[0]
    out_ref[:rows, :] = (low_ref[...] + their_low_ref[...]).astype(jnp.bfloat16)
    out_ref[rows:, :] = jnp.concatenate(split(maps_ref[...] + their_maps_ref[...]), axis=0)


def low_and_maps(low, maps, their_low, their_maps):
    rows = low.shape[0]
    return pl.pallas_call(
        low_kernel,
        out_shape=jax.ShapeDtypeStruct((rows + MAPS, RANK), jnp.bfloat16),
        compiler_params=params,
        cost_estimate=pl.CostEstimate(flops=1, bytes_accessed=1, transcendentals=0),
        name="low_and_maps",
    )(low, maps, their_low, their_maps)


def softplus(value):
    small = jnp.exp(-jnp.abs(value))
    tail = jnp.where(small < 0.00390625, small * (1.0 - 0.5 * small), jnp.log(1.0 + small))
    return jnp.maximum(value, 0.0) + tail


def spread_maps(maps, spread_ref, first, count):
    rows = maps.shape[0]
    for n in range(count):
        spread_ref[n * rows : (n + 1) * rows, :] = jnp.broadcast_to(
            maps[:, first + n : first + n + 1], (rows, LANES)
        )


def step_kernel(
    place_ref, own_ref, come_ref, low_own_ref, low_come_ref, map_own_ref, map_come_ref,
    cols_ref, bias_ref, rates_ref,
    steps_ref, push_ref, stream_ref, maps_ref, carry_ref, state_ref, total_ref, spread_ref,
):
    block = pl.program_id(0)
    rows, width = own_ref.shape[1:]
    tile = width // LANES
    here = block // CORES == place_ref[0]

    @pl.when(block == 0)
    def _():
        state_ref[...] = jnp.zeros_like(state_ref)
        total_ref[...] = jnp.zeros_like(total_ref)

    stream = jnp.where(here, own_ref[0], come_ref[0])
    stream_ref[...] = stream
    lows = jnp.where(here, low_own_ref[...], low_come_ref[0])
    maps = jnp.where(here, map_own_ref[...], map_come_ref[0]).astype(jnp.float32)
    maps = maps[: 2 * NS, :] + maps[2 * NS :, :]
    maps = jnp.concatenate([maps, jnp.zeros((LANES - 2 * NS, rows), jnp.float32)], axis=0).T
    maps_ref[...] = maps
    spread_maps(maps, spread_ref, 0, NS)
    logits = jnp.dot(lows, cols_ref[...], preferred_element_type=jnp.float32)
    steps = softplus(logits + bias_ref[...])
    push = steps * stream.astype(jnp.float32)
    for item in range(tile):
        lanes = slice(item * LANES, (item + 1) * LANES)
        steps_ref[pl.ds(item, rows, stride=tile), :] = steps[:, lanes]
        push_ref[pl.ds(item, rows, stride=tile), :] = push[:, lanes]

    rates = [rates_ref[n * tile : (n + 1) * tile, :] for n in range(NS)]

    def some(index, held):
        total, states = held[0], list(held[1:])
        base = pl.multiple_of(index * UNROLL, UNROLL)
        for near in range(UNROLL):
            at = pl.multiple_of((base + near) * tile, tile)
            step = steps_ref[pl.ds(at, tile), :]
            push = push_ref[pl.ds(at, tile), :]
            total = total + step
            for n in range(NS):
                into = spread_ref[pl.ds(n * rows + base + near, 1), :]
                states[n] = jnp.exp(step * rates[n]) * states[n] + push * into
        return (total, *states)

    held = (total_ref[...],) + tuple(state_ref[n * tile : (n + 1) * tile, :] for n in range(NS))
    held = lax.fori_loop(0, rows // UNROLL, some, held)
    total_ref[...] = held[0]
    for n in range(NS):
        state_ref[n * tile : (n + 1) * tile, :] = held[1 + n]

    @pl.when(block == pl.num_programs(0) - 1)
    def _():
        whole = jnp.concatenate([state_ref[...].astype(jnp.bfloat16), *split(total_ref[...])], axis=0)
        for target in range(carry_ref.shape[0]):
            carry_ref[target] = whole


def step_sizes(place, own, come, low_own, low_come, cols, bias, rates, targets):
    chips = come.shape[0] + 1
    rows, width = own.shape[1] // CORES, own.shape[2]
    tile = width // LANES
    map_row = CORES * rows // MAPS
    blocks = chips * CORES

    def slot(b, s):
        return jnp.maximum(lax.rem(s[0] - b // CORES + chips, chips) - 1, 0)

    def core(b):
        return lax.rem(b, CORES)

    def fixed(*shape):
        return pl.BlockSpec(shape, lambda b, s: (0,) * len(shape))

    folded = jax.ShapeDtypeStruct((blocks * rows * tile, LANES), jnp.float32)
    folded_block = pl.BlockSpec((rows * tile, LANES), lambda b, s: (b, 0))
    return pl.pallas_call(
        step_kernel,
        grid_spec=pltpu.PrefetchScalarGridSpec(
            num_scalar_prefetch=1,
            grid=(blocks,),
            in_specs=[
                pl.BlockSpec((1, rows, width), lambda b, s: (0, core(b), 0)),
                pl.BlockSpec((1, rows, width), lambda b, s: (slot(b, s), core(b), 0)),
                pl.BlockSpec((rows, RANK), lambda b, s: (core(b), 0)),
                pl.BlockSpec((1, rows, RANK), lambda b, s: (slot(b, s), core(b), 0)),
                pl.BlockSpec((MAPS, rows), lambda b, s: (map_row, core(b))),
                pl.BlockSpec((1, MAPS, rows), lambda b, s: (slot(b, s), map_row, core(b))),
                fixed(*cols.shape),
                fixed(*bias.shape),
                fixed(*rates.shape),
            ],
            out_specs=[
                folded_block,
                folded_block,
                pl.BlockSpec((rows, width), lambda b, s: (b, 0)),
                pl.BlockSpec((rows, LANES), lambda b, s: (b, 0)),
                fixed(targets, (NS + 2) * tile, LANES),
            ],
            scratch_shapes=[
                pltpu.VMEM((NS * tile, LANES), jnp.float32),
                pltpu.VMEM((tile, LANES), jnp.float32),
                pltpu.VMEM((NS * rows, LANES), jnp.float32),
            ],
        ),
        out_shape=[
            folded,
            folded,
            jax.ShapeDtypeStruct((blocks * rows, width), jnp.bfloat16),
            jax.ShapeDtypeStruct((blocks * rows, LANES), jnp.float32),
            jax.ShapeDtypeStruct((targets, (NS + 2) * tile, LANES), jnp.bfloat16),
        ],
        compiler_params=params,
        name="step_sizes",
    )(place, own, come, low_own, low_come, low_own, low_come, cols, bias, rates)


def scan_kernel(
    place_ref, steps_ref, push_ref, stream_ref, maps_ref, rates_ref, gain_ref, carry_ref, out_ref,
    state_ref, spread_ref, folded_ref,
):
    block = pl.program_id(0)
    rows, width = stream_ref.shape
    tile = width // LANES

    @pl.when(block == 0)
    def _():
        state_ref[...] = jnp.zeros_like(state_ref)

        def compose(row, nothing):
            whole = carry_ref[row].astype(jnp.float32)
            total = whole[NS * tile : (NS + 1) * tile, :] + whole[(NS + 1) * tile :, :]
            for n in range(NS):
                part = slice(n * tile, (n + 1) * tile)
                decay = jnp.exp(rates_ref[part, :] * total)
                state_ref[part, :] = decay * state_ref[part, :] + whole[part, :]
            return nothing

        lax.fori_loop(0, place_ref[0], compose, 0)

    spread_maps(maps_ref[...], spread_ref, 0, 2 * NS)
    rates = [rates_ref[n * tile : (n + 1) * tile, :] for n in range(NS)]

    def some(index, states):
        states = list(states)
        base = pl.multiple_of(index * UNROLL, UNROLL)
        for near in range(UNROLL):
            at = pl.multiple_of((base + near) * tile, tile)
            step = steps_ref[pl.ds(at, tile), :]
            push = push_ref[pl.ds(at, tile), :]
            sums = [None, None]
            for n in range(NS):
                into = spread_ref[pl.ds(n * rows + base + near, 1), :]
                out_of = spread_ref[pl.ds((NS + n) * rows + base + near, 1), :]
                states[n] = jnp.exp(step * rates[n]) * states[n] + push * into
                term = states[n] * out_of
                sums[n % 2] = term if sums[n % 2] is None else sums[n % 2] + term
            folded_ref[pl.ds(at, tile), :] = sums[0] + sums[1]
        return tuple(states)

    held = tuple(state_ref[n * tile : (n + 1) * tile, :] for n in range(NS))
    held = lax.fori_loop(0, rows // UNROLL, some, held)
    for n in range(NS):
        state_ref[n * tile : (n + 1) * tile, :] = held[n]
    for item in range(tile):
        lanes = slice(item * LANES, (item + 1) * LANES)
        direct = gain_ref[:, lanes] * stream_ref[:, lanes].astype(jnp.float32)
        mixed = folded_ref[pl.ds(item, rows, stride=tile), :]
        out_ref[:, lanes] = (mixed + direct).astype(jnp.bfloat16)


def scan_rows(place, steps, push, stream, maps, rates, gain, carries, rows):
    length, width = stream.shape
    tile = width // LANES

    def fixed(*shape):
        return pl.BlockSpec(shape, lambda b, s: (0,) * len(shape))

    block = pl.BlockSpec((rows, width), lambda b, s: (b, 0))
    folded = pl.BlockSpec((rows * tile, LANES), lambda b, s: (b, 0))
    return pl.pallas_call(
        scan_kernel,
        grid_spec=pltpu.PrefetchScalarGridSpec(
            num_scalar_prefetch=1,
            grid=(length // rows,),
            in_specs=[
                folded,
                folded,
                block,
                pl.BlockSpec((rows, LANES), lambda b, s: (b, 0)),
                fixed(*rates.shape),
                fixed(*gain.shape),
                fixed(*carries.shape),
            ],
            out_specs=block,
            scratch_shapes=[
                pltpu.VMEM((NS * tile, LANES), jnp.float32),
                pltpu.VMEM((2 * NS * rows, LANES), jnp.float32),
                pltpu.VMEM((rows * tile, LANES), jnp.float32),
            ],
        ),
        out_shape=jax.ShapeDtypeStruct((length, width), jnp.bfloat16),
        compiler_params=params,
        name="scan_rows",
    )(place, steps, push, stream, maps, rates, gain, carries)


def local(
    queries, keys, values, doc_lengths, rank_in, bc_weight, rank_out, dt_bias, a_log, skip_gain
):
    devices = lax.axis_size("seq")
    chips = devices // CORES
    targets = lax.axis_size("chan")
    seq_place = lax.axis_index("seq").astype(jnp.int32)
    chan_place = lax.axis_index("chan").astype(jnp.int32)
    chip, core = seq_place // CORES, lax.rem(seq_place, CORES)
    place = jnp.stack([chip, core])
    width = queries.shape[2] // devices
    wide = max(HEAD_SIZE, keys.shape[2] // devices)

    def other(device):
        return device + 1 - 2 * (device % CORES)

    swap = [(device, other(device)) for device in range(devices)]
    near = [(device, device + CORES) for device in range(devices - CORES)]
    far = [(device, other(device + CORES)) for device in range(devices - CORES)]

    def onward(chips_on):
        return [(device, (device + chips_on * CORES) % devices) for device in range(devices)]

    own, theirs = select_heads(keys[0], values[0], chips, wide)
    from_near = lax.ppermute(own, "seq", near)
    from_far = lax.ppermute(theirs, "seq", far)
    swapped = lax.ppermute(theirs, "seq", swap)
    their_queries = lax.ppermute(queries[0], "seq", swap)
    blocks = (own, swapped, from_near, from_far)

    sent, stayed, low, maps = attend(
        place, doc_lengths, (queries[0], their_queries), blocks, rank_in, bc_weight.T
    )
    come = [lax.ppermute(sent[step], "seq", onward(step + 1)) for step in range(chips - 1)]
    low_own = low_and_maps(low, maps, *lax.ppermute((low, maps), "seq", swap))
    low_come = [lax.ppermute(low_own, "seq", onward(step + 1)) for step in range(chips - 1)]
    got_sent = lax.ppermute(sent, "seq", swap)
    got_stayed = lax.ppermute(stayed, "seq", swap)
    attn_rows = join_heads(sent, stayed, got_sent, got_stayed)

    first = seq_place * width
    logs = lax.dynamic_slice_in_dim(a_log, first, width, 0)
    rates = (-jnp.exp(logs)).T.reshape(NS * width // LANES, LANES)
    cols = lax.dynamic_slice_in_dim(rank_out, first, width, 1)
    bias = lax.dynamic_slice_in_dim(dt_bias, first, width, 0)[None]
    gain = lax.dynamic_slice_in_dim(skip_gain, first, width, 0)[None]
    steps, push, stream, maps, carry = step_sizes(
        place, stayed, jnp.stack(come), low_own, jnp.stack(low_come), cols, bias, rates, targets
    )
    carries = lax.all_to_all(carry, "chan", split_axis=0, concat_axis=0, tiled=True)
    ssm_rows = scan_rows(
        chan_place[None], steps, push, stream, maps, rates, gain, carries, queries.shape[1]
    )
    return (attn_rows[None], ssm_rows[None])


def solution(mesh):
    return jax.shard_map(
        local,
        mesh=mesh,
        in_specs=(
            P("chan", "seq", None),
            P("chan", "seq", None),
            P("chan", "seq", None),
            P("chan", None),
            P(),
            P(),
            P(),
            P(),
            P(),
            P(),
        ),
        out_specs=(P("chan", "seq", None), P("chan", None, "seq")),
        check_vma=False,
    )
```

```python
import functools
import math

import jax
import jax.numpy as jnp
from jax import lax
from jax.experimental import pallas as pl
from jax.experimental.pallas import tpu as pltpu
from jax.sharding import PartitionSpec as P

QUERY_HEADS = 32
KEY_VALUE_HEADS = 8
HEAD_SIZE = 128
GROUP = QUERY_HEADS // KEY_VALUE_HEADS
NS = 16
RANK = 256
CORES = 2
LANES = 128
SUBLANES = 8
MAPS = 4 * NS
UNROLL = 8
LOG2E = 1.4426950408889634

masked_fill = -1e30
params = pltpu.CompilerParams(vmem_limit_bytes=60 << 20)


def split(value):
    coarse = value.astype(jnp.bfloat16)
    return coarse, (value - coarse.astype(jnp.float32)).astype(jnp.bfloat16)


def run_copies(pairs, sems):
    copies = [
        pltpu.make_async_copy(source, target, sems.at[i]) for i, (source, target) in enumerate(pairs)
    ]
    for copy in copies:
        copy.start()
    for copy in copies:
        copy.wait()


def columns_of(ref, index, size):
    return ref.at[:, pl.ds(pl.multiple_of(index * size, LANES), size)]


def heads_kernel(key_ref, value_ref, own_ref, their_ref, sems):
    core = lax.rem(lax.axis_index("seq"), CORES)
    wide = own_ref.shape[3]
    halves = key_ref.shape[1] // wide // own_ref.shape[0]
    pairs = []
    for target, which in ((own_ref, core), (their_ref, 1 - core)):
        for chip in range(own_ref.shape[0]):
            index = chip * halves + (which if halves == CORES else 0)
            for kind, source in enumerate((key_ref, value_ref)):
                pairs.append((columns_of(source, index, wide), target.at[chip, kind]))
    run_copies(pairs, sems)


def select_heads(keys, values, chips, wide):
    shape = jax.ShapeDtypeStruct((chips, 2, keys.shape[0], wide), keys.dtype)
    return pl.pallas_call(
        heads_kernel,
        in_specs=[pl.BlockSpec(memory_space=pl.ANY)] * 2,
        out_shape=[shape, shape],
        scratch_shapes=[pltpu.SemaphoreType.DMA((4 * chips,))],
        compiler_params=params,
        name="select_heads",
    )(keys, values)


def join_kernel(sent_ref, stayed_ref, got_sent_ref, got_stayed_ref, out_ref, sems):
    place = lax.axis_index("seq")
    core, chip = lax.rem(place, CORES), place // CORES
    rows = out_ref.shape[0]
    others, _, width = sent_ref.shape
    here = pl.ds(pl.multiple_of(core * rows, rows), rows)
    pairs = []
    for first, rest, which in (
        (stayed_ref, sent_ref, core), (got_stayed_ref, got_sent_ref, 1 - core)
    ):
        for step in range(others + 1):
            source = first.at[0, here, :] if step == 0 else rest.at[step - 1, here, :]
            owner = lax.rem(chip + step, others + 1)
            pairs.append((source, columns_of(out_ref, owner * CORES + which, width)))
    run_copies(pairs, sems)


def join_heads(sent, stayed, got_sent, got_stayed):
    others, rows, width = sent.shape
    return pl.pallas_call(
        join_kernel,
        in_specs=[pl.BlockSpec(memory_space=pl.ANY)] * 4,
        out_shape=jax.ShapeDtypeStruct(
            (rows // CORES, (others + 1) * CORES * width), sent.dtype
        ),
        scratch_shapes=[pltpu.SemaphoreType.DMA((CORES * (others + 1),))],
        compiler_params=params,
        name="join_heads",
    )(sent, stayed, got_sent, got_stayed)


def attend_kernel(
    place_ref, doc_ref, mine_ref, theirs_ref, own_ref, swap_ref, near_ref, far_ref,
    rank_ref, map_ref, send_ref, stay_ref, low_ref, maps_ref, mask_ref, *, chips,
):
    step = pl.program_id(0)
    rows = mine_ref.shape[0]
    group = mine_ref.shape[1] // HEAD_SIZE
    chip, core = place_ref[0], place_ref[1]
    first_core = core == 0

    def above(shape):
        row = lax.rem(lax.broadcasted_iota(jnp.int32, shape, 0), rows)
        return lax.broadcasted_iota(jnp.int32, shape, 1) > row

    @pl.when(step == 0)
    def _():
        low_ref[...] = jnp.zeros_like(low_ref)
        maps_ref[...] = jnp.zeros_like(maps_ref)
        own = chip * CORES + core
        swapped = chip * CORES + 1 - core
        near, far = own - CORES, swapped - CORES
        lane = lax.broadcasted_iota(jnp.int32, (rows, rows), 1)
        row = lax.broadcasted_iota(jnp.int32, (rows, rows), 0)
        for item, (place, before, middle) in enumerate(
            (
                (own, near, jnp.where(first_core, far, swapped)),
                (swapped, far, jnp.where(first_core, own, near)),
            )
        ):
            query_pos = place * rows + row
            start = jnp.zeros((rows, rows), jnp.int32)
            bound = jnp.int32(0)
            for doc in range(doc_ref.shape[1]):
                bound = bound + doc_ref[0, doc]
                start = jnp.where(query_pos >= bound, bound, start)
            ends = jnp.where(lane > row, before, place) * rows + lane
            mask_ref[item, :, :rows] = jnp.where(
                (ends >= start) & (ends <= query_pos), 0.0, masked_fill
            )
            mask_ref[item, :, rows:] = jnp.where(
                middle * rows + lane >= start, 0.0, masked_fill
            )

    scale = LOG2E / math.sqrt(HEAD_SIZE)
    ones = jnp.ones((3 * rows, HEAD_SIZE), jnp.bfloat16)

    def windows(kind):
        own, swapped = own_ref[0, kind], swap_ref[0, kind]
        near, far = near_ref[0, kind], far_ref[0, kind]
        return (
            jnp.concatenate([near, own, jnp.where(first_core, far, swapped)], axis=0),
            jnp.concatenate([far, swapped, jnp.where(first_core, own, near)], axis=0),
        )

    scores = []
    for keys, query in zip(windows(0), (mine_ref[...], theirs_ref[...])):
        stacked = jnp.concatenate(
            [query[:, i * HEAD_SIZE : (i + 1) * HEAD_SIZE] for i in range(group)], axis=0
        )
        scores.append(
            lax.dot_general(
                stacked, keys, (((1,), (1,)), ((), ())), preferred_element_type=jnp.float32
            )
        )
    outputs = []
    before = above((group * rows, rows))
    for item, (values, score) in enumerate(zip(windows(1), scores)):
        fill = mask_ref[item]
        ends = jnp.where(before, score[:, :rows], score[:, rows : 2 * rows])
        kept = jnp.concatenate([ends, score[:, 2 * rows :]], axis=1)
        kept = jnp.concatenate(
            [kept[i * rows : (i + 1) * rows, :] + fill for i in range(group)], axis=0
        )
        peak = jnp.max(kept, axis=1, keepdims=True)
        raw = jnp.exp2((kept - peak) * scale).astype(jnp.bfloat16)
        ends = raw[:, :rows]
        none = jnp.zeros_like(ends)
        spread = jnp.concatenate(
            [jnp.where(before, ends, none), jnp.where(before, none, ends), raw[:, rows:]], axis=1
        )
        both = jnp.dot(
            spread, jnp.concatenate([values, ones], axis=1), preferred_element_type=jnp.float32
        )
        mixed = both[:, :HEAD_SIZE] * pl.reciprocal(both[:, HEAD_SIZE:])
        mixed = mixed.astype(jnp.bfloat16)
        outputs.append(
            jnp.concatenate([mixed[i * rows : (i + 1) * rows, :] for i in range(group)], axis=1)
        )
    stream = jnp.concatenate(
        [
            jnp.where(first_core, outputs[0], outputs[1]),
            jnp.where(first_core, outputs[1], outputs[0]),
        ],
        axis=0,
    )
    last = step >= pl.num_programs(0) - pl.num_programs(0) // chips

    @pl.when(last)
    def _():
        stay_ref[0] = stream

    @pl.when(jnp.logical_not(last))
    def _():
        send_ref[0] = stream

    low_ref[...] += jnp.dot(stream, rank_ref[...], preferred_element_type=jnp.float32)
    maps_ref[...] += lax.dot_general(
        map_ref[...], stream, (((1,), (1,)), ((), ())), preferred_element_type=jnp.float32
    )


def attend(place, doc_lengths, queries, blocks, rank_in, map_rows):
    mine, theirs = queries
    chips, _, rows, columns = blocks[0].shape
    heads = columns // HEAD_SIZE
    width = mine.shape[1] // (chips * CORES)
    wide = width // heads

    def owner(j, s):
        return lax.rem(s[0] + 1 + j // heads, chips)

    def column(j, s):
        return (owner(j, s) * CORES + s[1]) * heads + lax.rem(j, heads)

    def sent(j, s):
        at = jnp.minimum(j, (chips - 1) * heads - 1)
        return (at // heads, 0, lax.rem(at, heads))

    query = pl.BlockSpec((rows, wide), lambda j, s: (0, column(j, s)))
    block = pl.BlockSpec(
        (1, 2, rows, HEAD_SIZE), lambda j, s: (owner(j, s), 0, 0, lax.rem(j, heads))
    )
    return pl.pallas_call(
        functools.partial(attend_kernel, chips=chips),
        grid_spec=pltpu.PrefetchScalarGridSpec(
            num_scalar_prefetch=1,
            grid=(chips * heads,),
            in_specs=[pl.BlockSpec(memory_space=pltpu.SMEM), query, query]
            + [block] * 4
            + [
                pl.BlockSpec((wide, RANK), lambda j, s: (column(j, s), 0)),
                pl.BlockSpec((2 * NS, wide), lambda j, s: (0, column(j, s))),
            ],
            out_specs=[
                pl.BlockSpec((1, CORES * rows, wide), sent),
                pl.BlockSpec(
                    (1, CORES * rows, wide),
                    lambda j, s: (0, 0, jnp.maximum(j - (chips - 1) * heads, 0)),
                ),
                pl.BlockSpec((CORES * rows, RANK), lambda j, s: (0, 0)),
                pl.BlockSpec((2 * NS, CORES * rows), lambda j, s: (0, 0)),
            ],
            scratch_shapes=[pltpu.VMEM((2, rows, 2 * rows), jnp.float32)],
        ),
        out_shape=[
            jax.ShapeDtypeStruct((chips - 1, CORES * rows, width), jnp.bfloat16),
            jax.ShapeDtypeStruct((1, CORES * rows, width), jnp.bfloat16),
            jax.ShapeDtypeStruct((CORES * rows, RANK), jnp.float32),
            jax.ShapeDtypeStruct((2 * NS, CORES * rows), jnp.float32),
        ],
        compiler_params=params,
        cost_estimate=pl.CostEstimate(flops=5 * 10**9, bytes_accessed=1 << 22, transcendentals=0),
        name="attend",
    )(place, doc_lengths, mine, theirs, *blocks, rank_in, map_rows)


def low_kernel(low_ref, maps_ref, their_low_ref, their_maps_ref, out_ref):
    rows = low_ref.shape[0]
    out_ref[:rows, :] = (low_ref[...] + their_low_ref[...]).astype(jnp.bfloat16)
    out_ref[rows:, :] = jnp.concatenate(split(maps_ref[...] + their_maps_ref[...]), axis=0)


def low_and_maps(low, maps, their_low, their_maps):
    rows = low.shape[0]
    return pl.pallas_call(
        low_kernel,
        out_shape=jax.ShapeDtypeStruct((rows + MAPS, RANK), jnp.bfloat16),
        compiler_params=params,
        cost_estimate=pl.CostEstimate(flops=1, bytes_accessed=1, transcendentals=0),
        name="low_and_maps",
    )(low, maps, their_low, their_maps)


def softplus(value):
    small = jnp.exp(-jnp.abs(value))
    tail = jnp.where(small < 0.00390625, small * (1.0 - 0.5 * small), jnp.log(1.0 + small))
    return jnp.maximum(value, 0.0) + tail


def spread_maps(maps, spread_ref, first, count):
    rows = maps.shape[0]
    for n in range(count):
        spread_ref[n * rows : (n + 1) * rows, :] = jnp.broadcast_to(
            maps[:, first + n : first + n + 1], (rows, LANES)
        )


def step_kernel(
    place_ref, own_ref, come_ref, low_own_ref, low_come_ref, map_own_ref, map_come_ref,
    cols_ref, bias_ref, rates_ref,
    steps_ref, push_ref, stream_ref, maps_ref, carry_ref, state_ref, total_ref, spread_ref,
):
    block = pl.program_id(0)
    rows, width = own_ref.shape[1:]
    tile = width // LANES
    here = block // CORES == place_ref[0]

    @pl.when(block == 0)
    def _():
        state_ref[...] = jnp.zeros_like(state_ref)
        total_ref[...] = jnp.zeros_like(total_ref)

    stream = jnp.where(here, own_ref[0], come_ref[0])
    stream_ref[...] = stream
    lows = jnp.where(here, low_own_ref[...], low_come_ref[0])
    maps = jnp.where(here, map_own_ref[...], map_come_ref[0]).astype(jnp.float32)
    maps = maps[: 2 * NS, :] + maps[2 * NS :, :]
    maps = jnp.concatenate([maps, jnp.zeros((LANES - 2 * NS, rows), jnp.float32)], axis=0).T
    maps_ref[...] = maps
    spread_maps(maps, spread_ref, 0, NS)
    logits = jnp.dot(lows, cols_ref[...], preferred_element_type=jnp.float32)
    steps = softplus(logits + bias_ref[...])
    push = steps * stream.astype(jnp.float32)
    for item in range(tile):
        lanes = slice(item * LANES, (item + 1) * LANES)
        steps_ref[pl.ds(item, rows, stride=tile), :] = steps[:, lanes]
        push_ref[pl.ds(item, rows, stride=tile), :] = push[:, lanes]

    rates = [rates_ref[n * tile : (n + 1) * tile, :] for n in range(NS)]

    def some(index, held):
        total, states = held[0], list(held[1:])
        base = pl.multiple_of(index * UNROLL, UNROLL)
        for near in range(UNROLL):
            at = pl.multiple_of((base + near) * tile, tile)
            step = steps_ref[pl.ds(at, tile), :]
            push = push_ref[pl.ds(at, tile), :]
            total = total + step
            for n in range(NS):
                into = spread_ref[pl.ds(n * rows + base + near, tile, stride=0), :]
                states[n] = jnp.exp2(step * rates[n]) * states[n] + push * into
        return (total, *states)

    held = (total_ref[...],) + tuple(state_ref[n * tile : (n + 1) * tile, :] for n in range(NS))
    held = lax.fori_loop(0, rows // UNROLL, some, held)
    total_ref[...] = held[0]
    for n in range(NS):
        state_ref[n * tile : (n + 1) * tile, :] = held[1 + n]

    @pl.when(block == pl.num_programs(0) - 1)
    def _():
        whole = jnp.concatenate([state_ref[...].astype(jnp.bfloat16), *split(total_ref[...])], axis=0)
        for target in range(carry_ref.shape[0]):
            carry_ref[target] = whole


def step_sizes(place, own, come, low_own, low_come, cols, bias, rates, targets):
    chips = come.shape[0] + 1
    rows, width = own.shape[1] // CORES, own.shape[2]
    tile = width // LANES
    map_row = CORES * rows // MAPS
    blocks = chips * CORES

    def slot(b, s):
        return jnp.maximum(lax.rem(s[0] - b // CORES + chips, chips) - 1, 0)

    def core(b):
        return lax.rem(b, CORES)

    def fixed(*shape):
        return pl.BlockSpec(shape, lambda b, s: (0,) * len(shape))

    folded = jax.ShapeDtypeStruct((blocks * rows * tile, LANES), jnp.float32)
    folded_block = pl.BlockSpec((rows * tile, LANES), lambda b, s: (b, 0))
    return pl.pallas_call(
        step_kernel,
        grid_spec=pltpu.PrefetchScalarGridSpec(
            num_scalar_prefetch=1,
            grid=(blocks,),
            in_specs=[
                pl.BlockSpec((1, rows, width), lambda b, s: (0, core(b), 0)),
                pl.BlockSpec((1, rows, width), lambda b, s: (slot(b, s), core(b), 0)),
                pl.BlockSpec((rows, RANK), lambda b, s: (core(b), 0)),
                pl.BlockSpec((1, rows, RANK), lambda b, s: (slot(b, s), core(b), 0)),
                pl.BlockSpec((MAPS, rows), lambda b, s: (map_row, core(b))),
                pl.BlockSpec((1, MAPS, rows), lambda b, s: (slot(b, s), map_row, core(b))),
                fixed(*cols.shape),
                fixed(*bias.shape),
                fixed(*rates.shape),
            ],
            out_specs=[
                folded_block,
                folded_block,
                pl.BlockSpec((rows, width), lambda b, s: (b, 0)),
                pl.BlockSpec((rows, LANES), lambda b, s: (b, 0)),
                fixed(targets, (NS + 2) * tile, LANES),
            ],
            scratch_shapes=[
                pltpu.VMEM((NS * tile, LANES), jnp.float32),
                pltpu.VMEM((tile, LANES), jnp.float32),
                pltpu.VMEM((NS * rows, LANES), jnp.float32),
            ],
        ),
        out_shape=[
            folded,
            folded,
            jax.ShapeDtypeStruct((blocks * rows, width), jnp.bfloat16),
            jax.ShapeDtypeStruct((blocks * rows, LANES), jnp.float32),
            jax.ShapeDtypeStruct((targets, (NS + 2) * tile, LANES), jnp.bfloat16),
        ],
        compiler_params=params,
        name="step_sizes",
    )(place, own, come, low_own, low_come, low_own, low_come, cols, bias, rates)


def scan_kernel(
    place_ref, steps_ref, push_ref, stream_ref, maps_ref, rates_ref, gain_ref, carry_ref, out_ref,
    state_ref, spread_ref, folded_ref,
):
    block = pl.program_id(0)
    rows, width = stream_ref.shape
    tile = width // LANES

    @pl.when(block == 0)
    def _():
        state_ref[...] = jnp.zeros_like(state_ref)

        def compose(row, nothing):
            whole = carry_ref[row].astype(jnp.float32)
            total = whole[NS * tile : (NS + 1) * tile, :] + whole[(NS + 1) * tile :, :]
            for n in range(NS):
                part = slice(n * tile, (n + 1) * tile)
                decay = jnp.exp2(rates_ref[part, :] * total)
                state_ref[part, :] = decay * state_ref[part, :] + whole[part, :]
            return nothing

        lax.fori_loop(0, place_ref[0], compose, 0)

    spread_maps(maps_ref[...], spread_ref, 0, 2 * NS)
    rates = [rates_ref[n * tile : (n + 1) * tile, :] for n in range(NS)]

    def some(index, states):
        states = list(states)
        base = pl.multiple_of(index * UNROLL, UNROLL)
        for near in range(UNROLL):
            at = pl.multiple_of((base + near) * tile, tile)
            step = steps_ref[pl.ds(at, tile), :]
            push = push_ref[pl.ds(at, tile), :]
            sums = [None, None]
            for n in range(NS):
                into = spread_ref[pl.ds(n * rows + base + near, tile, stride=0), :]
                out_of = spread_ref[pl.ds((NS + n) * rows + base + near, tile, stride=0), :]
                states[n] = jnp.exp2(step * rates[n]) * states[n] + push * into
                term = states[n] * out_of
                sums[n % 2] = term if sums[n % 2] is None else sums[n % 2] + term
            folded_ref[pl.ds(at, tile), :] = sums[0] + sums[1]
        return tuple(states)

    held = tuple(state_ref[n * tile : (n + 1) * tile, :] for n in range(NS))
    held = lax.fori_loop(0, rows // UNROLL, some, held)
    for n in range(NS):
        state_ref[n * tile : (n + 1) * tile, :] = held[n]
    for item in range(tile):
        lanes = slice(item * LANES, (item + 1) * LANES)
        direct = gain_ref[:, lanes] * stream_ref[:, lanes].astype(jnp.float32)
        mixed = folded_ref[pl.ds(item, rows, stride=tile), :]
        out_ref[:, lanes] = (mixed + direct).astype(jnp.bfloat16)


def scan_rows(place, steps, push, stream, maps, rates, gain, carries, rows):
    length, width = stream.shape
    tile = width // LANES

    def fixed(*shape):
        return pl.BlockSpec(shape, lambda b, s: (0,) * len(shape))

    block = pl.BlockSpec((rows, width), lambda b, s: (b, 0))
    folded = pl.BlockSpec((rows * tile, LANES), lambda b, s: (b, 0))
    return pl.pallas_call(
        scan_kernel,
        grid_spec=pltpu.PrefetchScalarGridSpec(
            num_scalar_prefetch=1,
            grid=(length // rows,),
            in_specs=[
                folded,
                folded,
                block,
                pl.BlockSpec((rows, LANES), lambda b, s: (b, 0)),
                fixed(*rates.shape),
                fixed(*gain.shape),
                fixed(*carries.shape),
            ],
            out_specs=block,
            scratch_shapes=[
                pltpu.VMEM((NS * tile, LANES), jnp.float32),
                pltpu.VMEM((2 * NS * rows, LANES), jnp.float32),
                pltpu.VMEM((rows * tile, LANES), jnp.float32),
            ],
        ),
        out_shape=jax.ShapeDtypeStruct((length, width), jnp.bfloat16),
        compiler_params=params,
        name="scan_rows",
    )(place, steps, push, stream, maps, rates, gain, carries)


def local(
    queries, keys, values, doc_lengths, rank_in, bc_weight, rank_out, dt_bias, a_log, skip_gain
):
    devices = lax.axis_size("seq")
    chips = devices // CORES
    targets = lax.axis_size("chan")
    seq_place = lax.axis_index("seq").astype(jnp.int32)
    chan_place = lax.axis_index("chan").astype(jnp.int32)
    chip, core = seq_place // CORES, lax.rem(seq_place, CORES)
    place = jnp.stack([chip, core])
    width = queries.shape[2] // devices
    wide = max(HEAD_SIZE, keys.shape[2] // devices)

    def other(device):
        return device + 1 - 2 * (device % CORES)

    swap = [(device, other(device)) for device in range(devices)]
    near = [(device, device + CORES) for device in range(devices - CORES)]
    far = [(device, other(device + CORES)) for device in range(devices - CORES)]

    def onward(chips_on):
        return [(device, (device + chips_on * CORES) % devices) for device in range(devices)]

    own, theirs = select_heads(keys[0], values[0], chips, wide)
    from_near = lax.ppermute(own, "seq", near)
    from_far = lax.ppermute(theirs, "seq", far)
    swapped = lax.ppermute(theirs, "seq", swap)
    their_queries = lax.ppermute(queries[0], "seq", swap)
    blocks = (own, swapped, from_near, from_far)

    sent, stayed, low, maps = attend(
        place, doc_lengths, (queries[0], their_queries), blocks, rank_in, bc_weight.T
    )
    come = [lax.ppermute(sent[step], "seq", onward(step + 1)) for step in range(chips - 1)]
    low_own = low_and_maps(low, maps, *lax.ppermute((low, maps), "seq", swap))
    low_come = [lax.ppermute(low_own, "seq", onward(step + 1)) for step in range(chips - 1)]
    got_sent = lax.ppermute(sent, "seq", swap)
    got_stayed = lax.ppermute(stayed, "seq", swap)
    attn_rows = join_heads(sent, stayed, got_sent, got_stayed)

    first = seq_place * width
    logs = lax.dynamic_slice_in_dim(a_log, first, width, 0)
    rates = (-LOG2E * jnp.exp(logs)).T.reshape(NS * width // LANES, LANES)
    cols = lax.dynamic_slice_in_dim(rank_out, first, width, 1)
    bias = lax.dynamic_slice_in_dim(dt_bias, first, width, 0)[None]
    gain = lax.dynamic_slice_in_dim(skip_gain, first, width, 0)[None]
    steps, push, stream, maps, carry = step_sizes(
        place, stayed, jnp.stack(come), low_own, jnp.stack(low_come), cols, bias, rates, targets
    )
    carries = lax.all_to_all(carry, "chan", split_axis=0, concat_axis=0, tiled=True)
    ssm_rows = scan_rows(
        chan_place[None], steps, push, stream, maps, rates, gain, carries, queries.shape[1]
    )
    return (attn_rows[None], ssm_rows[None])


def solution(mesh):
    return jax.shard_map(
        local,
        mesh=mesh,
        in_specs=(
            P("chan", "seq", None),
            P("chan", "seq", None),
            P("chan", "seq", None),
            P("chan", None),
            P(),
            P(),
            P(),
            P(),
            P(),
            P(),
        ),
        out_specs=(P("chan", "seq", None), P("chan", None, "seq")),
        check_vma=False,
    )
```

```python
import functools
import math

import jax
import jax.numpy as jnp
from jax import lax
from jax.experimental import pallas as pl
from jax.experimental.pallas import tpu as pltpu
from jax.sharding import PartitionSpec as P

QUERY_HEADS = 32
KEY_VALUE_HEADS = 8
HEAD_SIZE = 128
GROUP = QUERY_HEADS // KEY_VALUE_HEADS
NS = 16
RANK = 256
CORES = 2
ROWS = 2
LANES = 128
SUBLANES = 8
MAPS = 4 * NS
LOG2E = 1.4426950408889634

masked_fill = -1e30
params = pltpu.CompilerParams(vmem_limit_bytes=60 << 20)


def split(value):
    coarse = value.astype(jnp.bfloat16)
    return coarse, (value - coarse.astype(jnp.float32)).astype(jnp.bfloat16)


def run_copies(pairs, sems):
    copies = [
        pltpu.make_async_copy(source, target, sems.at[i]) for i, (source, target) in enumerate(pairs)
    ]
    for copy in copies:
        copy.start()
    for copy in copies:
        copy.wait()


def columns_of(ref, index, size):
    return ref.at[:, pl.ds(pl.multiple_of(index * size, LANES), size)]


def heads_kernel(key_ref, value_ref, own_ref, their_ref, sems):
    core = lax.rem(lax.axis_index("seq"), CORES)
    wide = own_ref.shape[3]
    halves = key_ref.shape[1] // wide // own_ref.shape[0]
    pairs = []
    for target, which in ((own_ref, core), (their_ref, 1 - core)):
        for chip in range(own_ref.shape[0]):
            index = chip * halves + (which if halves == CORES else 0)
            for kind, source in enumerate((key_ref, value_ref)):
                pairs.append((columns_of(source, index, wide), target.at[chip, kind]))
    run_copies(pairs, sems)


def select_heads(keys, values, chips, wide):
    shape = jax.ShapeDtypeStruct((chips, 2, keys.shape[0], wide), keys.dtype)
    return pl.pallas_call(
        heads_kernel,
        in_specs=[pl.BlockSpec(memory_space=pl.ANY)] * 2,
        out_shape=[shape, shape],
        scratch_shapes=[pltpu.SemaphoreType.DMA((4 * chips,))],
        compiler_params=params,
        name="select_heads",
    )(keys, values)


def join_kernel(sent_ref, stayed_ref, got_sent_ref, got_stayed_ref, out_ref, sems):
    place = lax.axis_index("seq")
    core, chip = lax.rem(place, CORES), place // CORES
    rows = out_ref.shape[0]
    others, _, width = sent_ref.shape
    here = pl.ds(pl.multiple_of(core * rows, rows), rows)
    pairs = []
    for first, rest, which in (
        (stayed_ref, sent_ref, core), (got_stayed_ref, got_sent_ref, 1 - core)
    ):
        for step in range(others + 1):
            source = first.at[0, here, :] if step == 0 else rest.at[step - 1, here, :]
            owner = lax.rem(chip + step, others + 1)
            pairs.append((source, columns_of(out_ref, owner * CORES + which, width)))
    run_copies(pairs, sems)


def join_heads(sent, stayed, got_sent, got_stayed):
    others, rows, width = sent.shape
    return pl.pallas_call(
        join_kernel,
        in_specs=[pl.BlockSpec(memory_space=pl.ANY)] * 4,
        out_shape=jax.ShapeDtypeStruct(
            (rows // CORES, (others + 1) * CORES * width), sent.dtype
        ),
        scratch_shapes=[pltpu.SemaphoreType.DMA((CORES * (others + 1),))],
        compiler_params=params,
        name="join_heads",
    )(sent, stayed, got_sent, got_stayed)


def attend_kernel(
    place_ref, doc_ref, mine_ref, theirs_ref, own_ref, swap_ref, near_ref, far_ref,
    rank_ref, map_ref, *rest, chips,
):
    send_ref, stay_ref, low_ref, maps_ref, mask_ref = rest[-5:]
    step = pl.program_id(0)
    rows = mine_ref.shape[0]
    group = mine_ref.shape[1] // HEAD_SIZE
    chip, core = place_ref[0], place_ref[1]
    first_core = core == 0

    def above(shape):
        row = lax.rem(lax.broadcasted_iota(jnp.int32, shape, 0), rows)
        return lax.broadcasted_iota(jnp.int32, shape, 1) > row

    @pl.when(step == 0)
    def _():
        low_ref[...] = jnp.zeros_like(low_ref)
        maps_ref[...] = jnp.zeros_like(maps_ref)
        own = chip * CORES + core
        swapped = chip * CORES + 1 - core
        near, far = own - CORES, swapped - CORES
        lane = lax.broadcasted_iota(jnp.int32, (rows, rows), 1)
        row = lax.broadcasted_iota(jnp.int32, (rows, rows), 0)
        for item, (place, before, middle) in enumerate(
            (
                (own, near, jnp.where(first_core, far, swapped)),
                (swapped, far, jnp.where(first_core, own, near)),
            )
        ):
            query_pos = place * rows + row
            start = jnp.zeros((rows, rows), jnp.int32)
            bound = jnp.int32(0)
            for doc in range(doc_ref.shape[1]):
                bound = bound + doc_ref[0, doc]
                start = jnp.where(query_pos >= bound, bound, start)
            ends = jnp.where(lane > row, before, place) * rows + lane
            mask_ref[item, :, :rows] = jnp.where(
                (ends >= start) & (ends <= query_pos), 0.0, masked_fill
            )
            mask_ref[item, :, rows:] = jnp.where(
                middle * rows + lane >= start, 0.0, masked_fill
            )

    scale = LOG2E / math.sqrt(HEAD_SIZE)
    ones = jnp.ones((3 * rows, HEAD_SIZE), jnp.bfloat16)

    def windows(kind):
        own, swapped = own_ref[0, kind], swap_ref[0, kind]
        near, far = near_ref[0, kind], far_ref[0, kind]
        return (
            jnp.concatenate([near, own, jnp.where(first_core, far, swapped)], axis=0),
            jnp.concatenate([far, swapped, jnp.where(first_core, own, near)], axis=0),
        )

    scores = []
    for keys, query in zip(windows(0), (mine_ref[...], theirs_ref[...])):
        stacked = jnp.concatenate(
            [query[:, i * HEAD_SIZE : (i + 1) * HEAD_SIZE] for i in range(group)], axis=0
        )
        scores.append(
            lax.dot_general(
                stacked, keys, (((1,), (1,)), ((), ())), preferred_element_type=jnp.float32
            )
        )
    outputs = []
    before = above((group * rows, rows))
    for item, (values, score) in enumerate(zip(windows(1), scores)):
        fill = mask_ref[item]
        ends = jnp.where(before, score[:, :rows], score[:, rows : 2 * rows])
        kept = jnp.concatenate([ends, score[:, 2 * rows :]], axis=1)
        kept = jnp.concatenate(
            [kept[i * rows : (i + 1) * rows, :] + fill for i in range(group)], axis=0
        )
        peak = jnp.max(kept, axis=1, keepdims=True)
        raw = jnp.exp2((kept - peak) * scale).astype(jnp.bfloat16)
        ends = raw[:, :rows]
        none = jnp.zeros_like(ends)
        spread = jnp.concatenate(
            [jnp.where(before, ends, none), jnp.where(before, none, ends), raw[:, rows:]], axis=1
        )
        both = jnp.dot(
            spread, jnp.concatenate([values, ones], axis=1), preferred_element_type=jnp.float32
        )
        mixed = both[:, :HEAD_SIZE] * pl.reciprocal(both[:, HEAD_SIZE:])
        mixed = mixed.astype(jnp.bfloat16)
        outputs.append(
            jnp.concatenate([mixed[i * rows : (i + 1) * rows, :] for i in range(group)], axis=1)
        )
    stream = jnp.concatenate(
        [
            jnp.where(first_core, outputs[0], outputs[1]),
            jnp.where(first_core, outputs[1], outputs[0]),
        ],
        axis=0,
    )
    last = step >= pl.num_programs(0) - pl.num_programs(0) // chips

    @pl.when(last)
    def _():
        stay_ref[0] = stream

    @pl.when(jnp.logical_not(last))
    def _():
        send_ref[0] = stream

    low_ref[...] += jnp.dot(stream, rank_ref[...], preferred_element_type=jnp.float32)
    maps_ref[...] += lax.dot_general(
        map_ref[...], stream, (((1,), (1,)), ((), ())), preferred_element_type=jnp.float32
    )


def attend(place, doc_lengths, queries, blocks, rank_in, map_rows, after):
    mine, theirs = queries
    chips, _, rows, columns = blocks[0].shape
    heads = columns // HEAD_SIZE
    width = mine.shape[1] // (chips * CORES)
    wide = width // heads

    def owner(j, s):
        return lax.rem(s[0] + 1 + j // heads, chips)

    def column(j, s):
        return (owner(j, s) * CORES + s[1]) * heads + lax.rem(j, heads)

    def sent(j, s):
        at = jnp.minimum(j, (chips - 1) * heads - 1)
        return (at // heads, 0, lax.rem(at, heads))

    query = pl.BlockSpec((rows, wide), lambda j, s: (0, column(j, s)))
    block = pl.BlockSpec(
        (1, 2, rows, HEAD_SIZE), lambda j, s: (owner(j, s), 0, 0, lax.rem(j, heads))
    )
    return pl.pallas_call(
        functools.partial(attend_kernel, chips=chips),
        grid_spec=pltpu.PrefetchScalarGridSpec(
            num_scalar_prefetch=1,
            grid=(chips * heads,),
            in_specs=[pl.BlockSpec(memory_space=pltpu.SMEM), query, query]
            + [block] * 4
            + [
                pl.BlockSpec((wide, RANK), lambda j, s: (column(j, s), 0)),
                pl.BlockSpec((2 * NS, wide), lambda j, s: (0, column(j, s))),
            ]
            + [pl.BlockSpec(memory_space=pl.ANY)] * len(after),
            out_specs=[
                pl.BlockSpec((1, CORES * rows, wide), sent),
                pl.BlockSpec(
                    (1, CORES * rows, wide),
                    lambda j, s: (0, 0, jnp.maximum(j - (chips - 1) * heads, 0)),
                ),
                pl.BlockSpec((CORES * rows, RANK), lambda j, s: (0, 0)),
                pl.BlockSpec((2 * NS, CORES * rows), lambda j, s: (0, 0)),
            ],
            scratch_shapes=[pltpu.VMEM((2, rows, 2 * rows), jnp.float32)],
        ),
        out_shape=[
            jax.ShapeDtypeStruct((chips - 1, CORES * rows, width), jnp.bfloat16),
            jax.ShapeDtypeStruct((1, CORES * rows, width), jnp.bfloat16),
            jax.ShapeDtypeStruct((CORES * rows, RANK), jnp.float32),
            jax.ShapeDtypeStruct((2 * NS, CORES * rows), jnp.float32),
        ],
        compiler_params=params,
        cost_estimate=pl.CostEstimate(flops=5 * 10**9, bytes_accessed=1 << 22, transcendentals=0),
        name="attend",
    )(place, doc_lengths, mine, theirs, *blocks, rank_in, map_rows, *after)


def low_kernel(low_ref, maps_ref, their_low_ref, their_maps_ref, out_ref):
    rows = low_ref.shape[0]
    out_ref[:rows, :] = (low_ref[...] + their_low_ref[...]).astype(jnp.bfloat16)
    out_ref[rows:, :] = jnp.concatenate(split(maps_ref[...] + their_maps_ref[...]), axis=0)


def low_and_maps(low, maps, their_low, their_maps):
    rows = low.shape[0]
    return pl.pallas_call(
        low_kernel,
        out_shape=jax.ShapeDtypeStruct((rows + MAPS, RANK), jnp.bfloat16),
        compiler_params=params,
        cost_estimate=pl.CostEstimate(flops=1, bytes_accessed=1, transcendentals=0),
        name="low_and_maps",
    )(low, maps, their_low, their_maps)


def softplus(value):
    small = jnp.exp(-jnp.abs(value))
    tail = jnp.where(small < 0.00390625, small * (1.0 - 0.5 * small), jnp.log(1.0 + small))
    return jnp.maximum(value, 0.0) + tail


def add_states(rates_ref, state_ref, total_ref, states, totals):
    state_ref[...] = jnp.exp2(rates_ref[...] * totals) * state_ref[...] + states
    total_ref[...] = total_ref[...] + totals


def step_kernel(
    place_ref, stream_ref, low_ref, map_ref, cols_ref, bias_ref, rates_ref, *rest, blocks_of
):
    own_state_ref, own_total_ref = rest[:2] if blocks_of else (None, None)
    steps_ref, maps_ref, state_ref, total_ref = rest[-5:-1]
    wide_ref = rest[-1]
    block = pl.program_id(0)
    rows, width = stream_ref.shape[1:]

    @pl.when(block == 0)
    def _():
        state_ref[...] = jnp.zeros_like(state_ref)
        total_ref[...] = jnp.zeros_like(total_ref)
        for n in range(NS):
            wide_ref[n * SUBLANES : (n + 1) * SUBLANES, :] = jnp.broadcast_to(
                rates_ref[n : n + 1, :], (SUBLANES, width)
            )

    if blocks_of:

        @pl.when(block == place_ref[0] * blocks_of)
        def _():
            add_states(rates_ref, state_ref, total_ref, own_state_ref[...], own_total_ref[...])

    maps = map_ref[0].astype(jnp.float32)
    maps = maps[: 2 * NS, :] + maps[2 * NS :, :]
    maps_ref[0] = maps
    logits = jnp.dot(low_ref[0], cols_ref[...], preferred_element_type=jnp.float32)
    steps = softplus(logits + bias_ref[...]).astype(jnp.bfloat16)
    steps_ref[...] = steps
    push = steps * stream_ref[0]
    at = lax.broadcasted_iota(jnp.int32, (rows, rows), 0)
    of = lax.broadcasted_iota(jnp.int32, (rows, rows), 1)
    upto = jnp.where(of <= at, 1.0, 0.0).astype(jnp.bfloat16)
    within = jnp.dot(upto, steps, preferred_element_type=jnp.float32)
    whole = within[rows - 1 :, :]
    left = whole - within
    some, chunk, several = rows // 2, CORES * LANES, 4
    state_row = lax.broadcasted_iota(jnp.int32, (NS, some), 0)
    for first in range(0, rows, some):
        span = slice(first, first + some)
        chosen = [
            jnp.concatenate(
                [
                    jnp.where(state_row == m, maps[:NS, span], 0.0).astype(jnp.bfloat16)
                    for m in range(n, n + several)
                ],
                axis=1,
            )
            for n in range(0, NS, several)
        ]
        for item in range(width // chunk):
            lanes = slice(item * chunk, (item + 1) * chunk)
            left_here = left[span, lanes].reshape(some // SUBLANES, SUBLANES, chunk)
            push_here = push[span, lanes]
            added = state_ref[:, lanes]
            if first == 0:
                added = jnp.exp2(rates_ref[:, lanes] * whole[:, lanes]) * added
            for n in range(0, NS, several):
                pushed = []
                for m in range(n, n + several):
                    rate = wide_ref[m * SUBLANES : (m + 1) * SUBLANES, lanes]
                    decay = jnp.exp2(left_here * rate[None]).reshape(some, chunk)
                    pushed.append(decay.astype(jnp.bfloat16) * push_here)
                added = added + jnp.dot(
                    chosen[n // several],
                    jnp.concatenate(pushed, axis=0),
                    preferred_element_type=jnp.float32,
                )
            state_ref[:, lanes] = added
    total_ref[...] = total_ref[...] + whole

    if blocks_of:
        count = pl.num_programs(0)

        @pl.when((block == count - 1) & (place_ref[0] * blocks_of == count))
        def _():
            add_states(rates_ref, state_ref, total_ref, own_state_ref[...], own_total_ref[...])


def step_sizes(place, stream, lows, cols, bias, rates, own):
    others = stream.shape[0]
    chips = others + 1
    rows, width = stream.shape[1] // CORES, stream.shape[2]
    map_row = CORES * rows // MAPS
    blocks = others * CORES

    def slot(b, s):
        if own is None:
            return 0
        chip = b // CORES
        return lax.rem(s[0] - jnp.where(chip < s[0], chip, chip + 1) + chips, chips) - 1

    def core(b):
        return lax.rem(b, CORES)

    def fixed(*shape):
        return pl.BlockSpec(shape, lambda b, s: (0,) * len(shape))

    more = [] if own is None else list(own)
    return pl.pallas_call(
        functools.partial(step_kernel, blocks_of=CORES if more else 0),
        grid_spec=pltpu.PrefetchScalarGridSpec(
            num_scalar_prefetch=1,
            grid=(blocks,),
            in_specs=[
                pl.BlockSpec((1, rows, width), lambda b, s: (slot(b, s), core(b), 0)),
                pl.BlockSpec((1, rows, RANK), lambda b, s: (slot(b, s), core(b), 0)),
                pl.BlockSpec((1, MAPS, rows), lambda b, s: (slot(b, s), map_row, core(b))),
                fixed(*cols.shape),
                fixed(*bias.shape),
                fixed(*rates.shape),
            ]
            + [fixed(*value.shape) for value in more],
            out_specs=[
                pl.BlockSpec((rows, width), lambda b, s: (b, 0)),
                pl.BlockSpec((1, 2 * NS, rows), lambda b, s: (b, 0, 0)),
                fixed(NS, width),
                fixed(1, width),
            ],
            scratch_shapes=[pltpu.VMEM((NS * SUBLANES, width), jnp.float32)],
        ),
        out_shape=[
            jax.ShapeDtypeStruct((blocks * rows, width), jnp.bfloat16),
            jax.ShapeDtypeStruct((blocks, 2 * NS, rows), jnp.float32),
            jax.ShapeDtypeStruct((NS, width), jnp.float32),
            jax.ShapeDtypeStruct((1, width), jnp.float32),
        ],
        compiler_params=params,
        cost_estimate=pl.CostEstimate(flops=3 * 10**9, bytes_accessed=1 << 21, transcendentals=0),
        name="step_sizes",
    )(place, stream, lows, lows, cols, bias, rates, *more)


def write_carry(out_ref, state, total, turn_ref):
    tile = state.shape[1] // LANES
    turn_ref[...] = jnp.zeros_like(turn_ref)
    for item in range(tile):
        lanes = slice(item * LANES, (item + 1) * LANES)
        turn_ref[item : item + 1, :] = total[:, lanes]
        out_ref[item * NS : (item + 1) * NS, :] = state[:, lanes].astype(jnp.bfloat16)
    out_ref[tile * NS :, :] = jnp.concatenate(split(turn_ref[...]), axis=0)


def carry_kernel(state_ref, total_ref, out_ref, turn_ref):
    write_carry(out_ref, state_ref[...], total_ref[...], turn_ref)


def make_carry(state, total):
    tile = state.shape[1] // LANES
    return pl.pallas_call(
        carry_kernel,
        out_shape=jax.ShapeDtypeStruct(((tile + 1) * NS, LANES), jnp.bfloat16),
        scratch_shapes=[pltpu.VMEM((SUBLANES, LANES), jnp.float32)],
        compiler_params=params,
        name="make_carry",
    )(state, total)


def follow(carry_ref, rates_ref, state_ref):
    tile = state_ref.shape[1] // LANES
    sums = carry_ref[tile * NS :, :].astype(jnp.float32)
    sums = sums[:SUBLANES, :] + sums[SUBLANES:, :]
    for item in range(tile):
        lanes = slice(item * LANES, (item + 1) * LANES)
        decay = jnp.exp2(rates_ref[:, lanes] * sums[item : item + 1, :])
        added = carry_ref[item * NS : (item + 1) * NS, :].astype(jnp.float32)
        state_ref[:, lanes] = decay * state_ref[:, lanes] + added
    return sums


def pair_kernel(state_ref, total_ref, theirs_ref, rates_ref, out_ref, all_ref, other_ref, turn_ref):
    second = lax.rem(lax.axis_index("chan"), ROWS) == 1
    tile = state_ref.shape[1] // LANES
    all_ref[...] = jnp.zeros_like(all_ref)
    sums = follow(theirs_ref, rates_ref, all_ref)
    for item in range(tile):
        lanes = slice(item * LANES, (item + 1) * LANES)
        other_ref[:, lanes] = sums[item : item + 1, :]
    theirs, their_total = all_ref[...], other_ref[...]
    mine, total = state_ref[...], total_ref[...]
    first_state = jnp.where(second, theirs, mine)
    last_state = jnp.where(second, mine, theirs)
    last_total = jnp.where(second, total, their_total)
    state = jnp.exp2(rates_ref[...] * last_total) * first_state + last_state
    write_carry(out_ref, state, total + their_total, turn_ref)


def pair_carry(state, total, theirs, rates):
    width = state.shape[1]
    return pl.pallas_call(
        pair_kernel,
        out_shape=jax.ShapeDtypeStruct(theirs.shape, jnp.bfloat16),
        scratch_shapes=[
            pltpu.VMEM((NS, width), jnp.float32),
            pltpu.VMEM((1, width), jnp.float32),
            pltpu.VMEM((SUBLANES, LANES), jnp.float32),
        ],
        compiler_params=params,
        name="pair_carry",
    )(state, total, theirs, rates)


def scan_kernel(
    place_ref, own_ref, come_ref, steps_own_ref, steps_come_ref, maps_own_ref, maps_come_ref,
    rates_ref, gain_ref, partner_ref, *rest, pairs,
):
    pair_refs, (out_ref, state_ref, out_of_ref, stream_ref, steps_ref, *hist_refs) = (
        rest[:pairs],
        rest[pairs:],
    )
    block = pl.program_id(0)
    rows, width = stream_ref.shape
    here = block // CORES == place_ref[0]

    @pl.when(block == 0)
    def _():
        state_ref[...] = jnp.zeros_like(state_ref)
        for pair_ref in pair_refs[::-1]:
            follow(pair_ref, rates_ref, state_ref)

        @pl.when(place_ref[1] == 1)
        def _():
            follow(partner_ref, rates_ref, state_ref)

    stream_ref[...] = jnp.where(here, own_ref[0], come_ref[0])
    steps_ref[...] = jnp.where(here, steps_own_ref[...], steps_come_ref[...])
    maps = jnp.where(here, maps_own_ref[0], maps_come_ref[0])
    source = lax.broadcasted_iota(jnp.int32, (LANES, NS * NS), 0)
    column = lax.rem(lax.broadcasted_iota(jnp.int32, (LANES, NS * NS), 1), NS)
    token = lax.rem(lax.broadcasted_iota(jnp.int32, (rows, NS * NS), 0), NS)
    slot = lax.broadcasted_iota(jnp.int32, (rows, NS * NS), 1) // NS
    turned = jnp.concatenate(
        [maps, jnp.zeros((LANES - 2 * NS, rows), jnp.float32)], axis=0
    ).T.astype(jnp.bfloat16)
    pick = jnp.where(source == NS + column, 1.0, 0.0).astype(jnp.bfloat16)
    spread = jnp.dot(turned, pick, preferred_element_type=jnp.float32)
    out_of_ref[...] = jnp.where(token == slot, spread, 0.0).astype(jnp.bfloat16)
    map_in = maps[:NS, :]
    half = width // 2

    def finish(first, hist_ref):
        here = pl.ds(first, NS)
        mixed = jnp.dot(out_of_ref[here, :], hist_ref[...], preferred_element_type=jnp.float32)
        direct = gain_ref[...] * stream_ref[here, :].astype(jnp.float32)
        out_ref[here, :] = (mixed + direct).astype(jnp.bfloat16)

    def advance(first, hist_ref):
        here = pl.ds(first, NS)
        into = pltpu.roll(map_in, lax.rem(rows - first, rows), 1)
        for lanes in (slice(0, half), slice(half, width)):
            state = state_ref[:, lanes]
            rates = rates_ref[:, lanes]
            steps = steps_ref[here, lanes].astype(jnp.float32)
            push = steps * stream_ref[here, lanes].astype(jnp.float32)
            for near in range(NS):
                this = slice(near, near + 1)
                state = jnp.exp2(rates * steps[this, :]) * state + into[:, this] * push[this, :]
                hist_ref[near * NS : (near + 1) * NS, lanes] = state.astype(jnp.bfloat16)
            state_ref[:, lanes] = state

    def pair(index, nothing):
        first = pl.multiple_of(index * 2 * NS, 2 * NS)
        advance(first, hist_refs[0])
        finish(first, hist_refs[0])
        second = pl.multiple_of(first + NS, NS)
        advance(second, hist_refs[1])
        finish(second, hist_refs[1])
        return nothing

    lax.fori_loop(0, rows // (2 * NS), pair, 0)


def scan_rows(places, own, come, steps_own, steps_come, maps_own, maps_come, rates, gain, partner, pairs):
    chips = come.shape[0] + 1
    rows, width = own.shape[1] // CORES, own.shape[2]

    def slot(b, s):
        return jnp.maximum(lax.rem(s[0] - b // CORES + chips, chips) - 1, 0)

    def core(b):
        return lax.rem(b, CORES)

    def order(b, s):
        chip = b // CORES
        return jnp.minimum(jnp.where(chip < s[0], b, jnp.maximum(b - CORES, 0)), (chips - 1) * CORES - 1)

    def fixed(*shape):
        return pl.BlockSpec(shape, lambda b, s: (0,) * len(shape))

    return pl.pallas_call(
        functools.partial(scan_kernel, pairs=len(pairs)),
        grid_spec=pltpu.PrefetchScalarGridSpec(
            num_scalar_prefetch=1,
            grid=(chips * CORES,),
            in_specs=[
                pl.BlockSpec((1, rows, width), lambda b, s: (0, core(b), 0)),
                pl.BlockSpec((1, rows, width), lambda b, s: (slot(b, s), core(b), 0)),
                pl.BlockSpec((rows, width), lambda b, s: (core(b), 0)),
                pl.BlockSpec((rows, width), lambda b, s: (order(b, s), 0)),
                pl.BlockSpec((1, 2 * NS, rows), lambda b, s: (core(b), 0, 0)),
                pl.BlockSpec((1, 2 * NS, rows), lambda b, s: (order(b, s), 0, 0)),
                fixed(*rates.shape),
                fixed(*gain.shape),
            ]
            + [fixed(*partner.shape)] * (1 + len(pairs)),
            out_specs=pl.BlockSpec((rows, width), lambda b, s: (b, 0)),
            scratch_shapes=[
                pltpu.VMEM((NS, width), jnp.float32),
                pltpu.VMEM((rows, NS * NS), jnp.bfloat16),
                pltpu.VMEM((rows, width), jnp.bfloat16),
                pltpu.VMEM((rows, width), jnp.bfloat16),
                pltpu.VMEM((NS * NS, width), jnp.bfloat16),
                pltpu.VMEM((NS * NS, width), jnp.bfloat16),
            ],
        ),
        out_shape=jax.ShapeDtypeStruct((chips * CORES * rows, width), jnp.bfloat16),
        compiler_params=params,
        name="scan_rows",
    )(places, own, come, steps_own, steps_come, maps_own, maps_come, rates, gain, partner, *pairs)


def local(
    queries, keys, values, doc_lengths, rank_in, bc_weight, rank_out, dt_bias, a_log, skip_gain
):
    devices = lax.axis_size("seq")
    chips = devices // CORES
    targets = lax.axis_size("chan")
    seq_place = lax.axis_index("seq").astype(jnp.int32)
    chan_place = lax.axis_index("chan").astype(jnp.int32)
    chip, core = seq_place // CORES, lax.rem(seq_place, CORES)
    place = jnp.stack([chip, core])
    width = queries.shape[2] // devices
    wide = max(HEAD_SIZE, keys.shape[2] // devices)

    def other(device):
        return device + 1 - 2 * (device % CORES)

    swap = [(device, other(device)) for device in range(devices)]
    near = [(device, device + CORES) for device in range(devices - CORES)]
    far = [(device, other(device + CORES)) for device in range(devices - CORES)]

    def onward(chips_on):
        return [(device, (device + chips_on * CORES) % devices) for device in range(devices)]

    own, theirs = select_heads(keys[0], values[0], chips, wide)
    from_near = lax.ppermute(own, "seq", near)
    from_far = lax.ppermute(theirs, "seq", far)
    swapped = lax.ppermute(theirs, "seq", swap)
    their_queries = lax.ppermute(queries[0], "seq", swap)
    blocks = (own, swapped, from_near, from_far)

    first = seq_place * width
    logs = lax.dynamic_slice_in_dim(a_log, first, width, 0)
    rates = (-LOG2E * jnp.exp(logs)).T
    cols = lax.dynamic_slice_in_dim(rank_out, first, width, 1)
    bias = lax.dynamic_slice_in_dim(dt_bias, first, width, 0)[None]
    gain = lax.dynamic_slice_in_dim(skip_gain, first, width, 0)[None]

    sent, stayed, low, maps = attend(
        place, doc_lengths, (queries[0], their_queries), blocks, rank_in, bc_weight.T,
        (rates, cols, bias, gain),
    )
    come = [lax.ppermute(sent[step], "seq", onward(step + 1)) for step in range(chips - 1)]
    low_own = low_and_maps(low, maps, *lax.ppermute((low, maps), "seq", swap))
    low_come = [lax.ppermute(low_own, "seq", onward(step + 1)) for step in range(chips - 1)]
    got_sent = lax.ppermute(sent, "seq", swap)
    got_stayed = lax.ppermute(stayed, "seq", swap)
    attn_rows = join_heads(sent, stayed, got_sent, got_stayed)

    steps_own, maps_own, state, total = step_sizes(
        place, stayed, low_own[None], cols, bias, rates, None
    )
    come, low_come = jnp.stack(come), jnp.stack(low_come)
    steps_come, maps_come, state, total = step_sizes(
        place, come, low_come, cols, bias, rates, (state, total)
    )
    partners = [(row, row + 1 - 2 * (row % ROWS)) for row in range(targets)]
    partner = lax.ppermute(make_carry(state, total), "chan", partners)
    pair = pair_carry(state, total, partner, rates)
    pairs = [
        lax.ppermute(pair, "chan", [(row, row + ahead) for row in range(targets - ahead)])
        for ahead in range(ROWS, targets, ROWS)
    ]
    places = jnp.stack([chip, lax.rem(chan_place, ROWS)])
    ssm_rows = scan_rows(
        places, stayed, come, steps_own, steps_come, maps_own, maps_come, rates, gain, partner, pairs
    )
    return (attn_rows[None], ssm_rows[None])


def solution(mesh):
    return jax.shard_map(
        local,
        mesh=mesh,
        in_specs=(
            P("chan", "seq", None),
            P("chan", "seq", None),
            P("chan", "seq", None),
            P("chan", None),
            P(),
            P(),
            P(),
            P(),
            P(),
            P(),
        ),
        out_specs=(P("chan", "seq", None), P("chan", None, "seq")),
        check_vma=False,
    )
```

```python
import functools
import math

import jax
import jax.numpy as jnp
from jax import lax
from jax.experimental import pallas as pl
from jax.experimental.pallas import tpu as pltpu
from jax.sharding import PartitionSpec as P

QUERY_HEADS = 32
KEY_VALUE_HEADS = 8
HEAD_SIZE = 128
GROUP = QUERY_HEADS // KEY_VALUE_HEADS
NS = 16
RANK = 256
CORES = 2
LANES = 128
SUBLANES = 8
MAPS = 4 * NS
LOG2E = 1.4426950408889634

masked_fill = -1e30
params = pltpu.CompilerParams(vmem_limit_bytes=60 << 20)


def split(value):
    coarse = value.astype(jnp.bfloat16)
    return coarse, (value - coarse.astype(jnp.float32)).astype(jnp.bfloat16)


def run_copies(pairs, sems):
    copies = [
        pltpu.make_async_copy(source, target, sems.at[i]) for i, (source, target) in enumerate(pairs)
    ]
    for copy in copies:
        copy.start()
    for copy in copies:
        copy.wait()


def columns_of(ref, index, size):
    return ref.at[:, pl.ds(pl.multiple_of(index * size, LANES), size)]


def heads_kernel(key_ref, value_ref, own_ref, their_ref, sems):
    core = lax.rem(lax.axis_index("seq"), CORES)
    wide = own_ref.shape[3]
    halves = key_ref.shape[1] // wide // own_ref.shape[0]
    pairs = []
    for target, which in ((own_ref, core), (their_ref, 1 - core)):
        for chip in range(own_ref.shape[0]):
            index = chip * halves + (which if halves == CORES else 0)
            for kind, source in enumerate((key_ref, value_ref)):
                pairs.append((columns_of(source, index, wide), target.at[chip, kind]))
    run_copies(pairs, sems)


def select_heads(keys, values, chips, wide):
    shape = jax.ShapeDtypeStruct((chips, 2, keys.shape[0], wide), keys.dtype)
    return pl.pallas_call(
        heads_kernel,
        in_specs=[pl.BlockSpec(memory_space=pl.ANY)] * 2,
        out_shape=[shape, shape],
        scratch_shapes=[pltpu.SemaphoreType.DMA((4 * chips,))],
        compiler_params=params,
        name="select_heads",
    )(keys, values)


def join_kernel(sent_ref, stayed_ref, got_sent_ref, got_stayed_ref, out_ref, sems):
    place = lax.axis_index("seq")
    core, chip = lax.rem(place, CORES), place // CORES
    rows = out_ref.shape[0]
    others, _, width = sent_ref.shape
    here = pl.ds(pl.multiple_of(core * rows, rows), rows)
    pairs = []
    for first, rest, which in (
        (stayed_ref, sent_ref, core), (got_stayed_ref, got_sent_ref, 1 - core)
    ):
        for step in range(others + 1):
            source = first.at[0, here, :] if step == 0 else rest.at[step - 1, here, :]
            owner = lax.rem(chip + step, others + 1)
            pairs.append((source, columns_of(out_ref, owner * CORES + which, width)))
    run_copies(pairs, sems)


def join_heads(sent, stayed, got_sent, got_stayed):
    others, rows, width = sent.shape
    return pl.pallas_call(
        join_kernel,
        in_specs=[pl.BlockSpec(memory_space=pl.ANY)] * 4,
        out_shape=jax.ShapeDtypeStruct(
            (rows // CORES, (others + 1) * CORES * width), sent.dtype
        ),
        scratch_shapes=[pltpu.SemaphoreType.DMA((CORES * (others + 1),))],
        compiler_params=params,
        name="join_heads",
    )(sent, stayed, got_sent, got_stayed)


def attend_kernel(
    place_ref, doc_ref, mine_ref, theirs_ref, own_ref, swap_ref, near_ref, far_ref,
    rank_ref, map_ref, *rest, chips,
):
    send_ref, stay_ref, low_ref, maps_ref, mask_ref = rest[-5:]
    step = pl.program_id(0)
    rows = mine_ref.shape[0]
    group = mine_ref.shape[1] // HEAD_SIZE
    chip, core = place_ref[0], place_ref[1]
    first_core = core == 0

    def above(shape):
        row = lax.rem(lax.broadcasted_iota(jnp.int32, shape, 0), rows)
        return lax.broadcasted_iota(jnp.int32, shape, 1) > row

    @pl.when(step == 0)
    def _():
        low_ref[...] = jnp.zeros_like(low_ref)
        maps_ref[...] = jnp.zeros_like(maps_ref)
        own = chip * CORES + core
        swapped = chip * CORES + 1 - core
        near, far = own - CORES, swapped - CORES
        lane = lax.broadcasted_iota(jnp.int32, (rows, rows), 1)
        row = lax.broadcasted_iota(jnp.int32, (rows, rows), 0)
        for item, (place, before, middle) in enumerate(
            (
                (own, near, jnp.where(first_core, far, swapped)),
                (swapped, far, jnp.where(first_core, own, near)),
            )
        ):
            query_pos = place * rows + row
            start = jnp.zeros((rows, rows), jnp.int32)
            bound = jnp.int32(0)
            for doc in range(doc_ref.shape[1]):
                bound = bound + doc_ref[0, doc]
                start = jnp.where(query_pos >= bound, bound, start)
            ends = jnp.where(lane > row, before, place) * rows + lane
            mask_ref[item, :, :rows] = jnp.where(
                (ends >= start) & (ends <= query_pos), 0.0, masked_fill
            )
            mask_ref[item, :, rows:] = jnp.where(
                middle * rows + lane >= start, 0.0, masked_fill
            )

    scale = LOG2E / math.sqrt(HEAD_SIZE)
    ones = jnp.ones((3 * rows, HEAD_SIZE), jnp.bfloat16)

    def windows(kind):
        own, swapped = own_ref[0, kind], swap_ref[0, kind]
        near, far = near_ref[0, kind], far_ref[0, kind]
        return (
            jnp.concatenate([near, own, jnp.where(first_core, far, swapped)], axis=0),
            jnp.concatenate([far, swapped, jnp.where(first_core, own, near)], axis=0),
        )

    scores = []
    for keys, query in zip(windows(0), (mine_ref[...], theirs_ref[...])):
        stacked = jnp.concatenate(
            [query[:, i * HEAD_SIZE : (i + 1) * HEAD_SIZE] for i in range(group)], axis=0
        )
        scores.append(
            lax.dot_general(
                stacked, keys, (((1,), (1,)), ((), ())), preferred_element_type=jnp.float32
            )
        )
    outputs = []
    before = above((group * rows, rows))
    for item, (values, score) in enumerate(zip(windows(1), scores)):
        fill = mask_ref[item]
        ends = jnp.where(before, score[:, :rows], score[:, rows : 2 * rows])
        kept = jnp.concatenate([ends, score[:, 2 * rows :]], axis=1)
        kept = jnp.concatenate(
            [kept[i * rows : (i + 1) * rows, :] + fill for i in range(group)], axis=0
        )
        peak = jnp.max(kept, axis=1, keepdims=True)
        raw = jnp.exp2((kept - peak) * scale).astype(jnp.bfloat16)
        ends = raw[:, :rows]
        none = jnp.zeros_like(ends)
        spread = jnp.concatenate(
            [jnp.where(before, ends, none), jnp.where(before, none, ends), raw[:, rows:]], axis=1
        )
        both = jnp.dot(
            spread, jnp.concatenate([values, ones], axis=1), preferred_element_type=jnp.float32
        )
        mixed = both[:, :HEAD_SIZE] * pl.reciprocal(both[:, HEAD_SIZE:])
        mixed = mixed.astype(jnp.bfloat16)
        outputs.append(
            jnp.concatenate([mixed[i * rows : (i + 1) * rows, :] for i in range(group)], axis=1)
        )
    stream = jnp.concatenate(
        [
            jnp.where(first_core, outputs[0], outputs[1]),
            jnp.where(first_core, outputs[1], outputs[0]),
        ],
        axis=0,
    )
    last = step >= pl.num_programs(0) - pl.num_programs(0) // chips

    @pl.when(last)
    def _():
        stay_ref[0] = stream

    @pl.when(jnp.logical_not(last))
    def _():
        send_ref[0] = stream

    low_ref[...] += jnp.dot(stream, rank_ref[...], preferred_element_type=jnp.float32)
    maps_ref[...] += lax.dot_general(
        map_ref[...], stream, (((1,), (1,)), ((), ())), preferred_element_type=jnp.float32
    )


def attend(place, doc_lengths, queries, blocks, rank_in, map_rows, after):
    mine, theirs = queries
    chips, _, rows, columns = blocks[0].shape
    heads = columns // HEAD_SIZE
    width = mine.shape[1] // (chips * CORES)
    wide = width // heads

    def owner(j, s):
        return lax.rem(s[0] + 1 + j // heads, chips)

    def column(j, s):
        return (owner(j, s) * CORES + s[1]) * heads + lax.rem(j, heads)

    def sent(j, s):
        at = jnp.minimum(j, (chips - 1) * heads - 1)
        return (at // heads, 0, lax.rem(at, heads))

    query = pl.BlockSpec((rows, wide), lambda j, s: (0, column(j, s)))
    block = pl.BlockSpec(
        (1, 2, rows, HEAD_SIZE), lambda j, s: (owner(j, s), 0, 0, lax.rem(j, heads))
    )
    return pl.pallas_call(
        functools.partial(attend_kernel, chips=chips),
        grid_spec=pltpu.PrefetchScalarGridSpec(
            num_scalar_prefetch=1,
            grid=(chips * heads,),
            in_specs=[pl.BlockSpec(memory_space=pltpu.SMEM), query, query]
            + [block] * 4
            + [
                pl.BlockSpec((wide, RANK), lambda j, s: (column(j, s), 0)),
                pl.BlockSpec((2 * NS, wide), lambda j, s: (0, column(j, s))),
            ]
            + [pl.BlockSpec(memory_space=pl.ANY)] * len(after),
            out_specs=[
                pl.BlockSpec((1, CORES * rows, wide), sent),
                pl.BlockSpec(
                    (1, CORES * rows, wide),
                    lambda j, s: (0, 0, jnp.maximum(j - (chips - 1) * heads, 0)),
                ),
                pl.BlockSpec((CORES * rows, RANK), lambda j, s: (0, 0)),
                pl.BlockSpec((2 * NS, CORES * rows), lambda j, s: (0, 0)),
            ],
            scratch_shapes=[pltpu.VMEM((2, rows, 2 * rows), jnp.float32)],
        ),
        out_shape=[
            jax.ShapeDtypeStruct((chips - 1, CORES * rows, width), jnp.bfloat16),
            jax.ShapeDtypeStruct((1, CORES * rows, width), jnp.bfloat16),
            jax.ShapeDtypeStruct((CORES * rows, RANK), jnp.float32),
            jax.ShapeDtypeStruct((2 * NS, CORES * rows), jnp.float32),
        ],
        compiler_params=params,
        cost_estimate=pl.CostEstimate(flops=5 * 10**9, bytes_accessed=1 << 22, transcendentals=0),
        name="attend",
    )(place, doc_lengths, mine, theirs, *blocks, rank_in, map_rows, *after)


def low_kernel(low_ref, maps_ref, their_low_ref, their_maps_ref, out_ref):
    rows = low_ref.shape[0]
    out_ref[:rows, :] = (low_ref[...] + their_low_ref[...]).astype(jnp.bfloat16)
    out_ref[rows:, :] = jnp.concatenate(split(maps_ref[...] + their_maps_ref[...]), axis=0)


def low_and_maps(low, maps, their_low, their_maps):
    rows = low.shape[0]
    return pl.pallas_call(
        low_kernel,
        out_shape=jax.ShapeDtypeStruct((rows + MAPS, RANK), jnp.bfloat16),
        compiler_params=params,
        cost_estimate=pl.CostEstimate(flops=1, bytes_accessed=1, transcendentals=0),
        name="low_and_maps",
    )(low, maps, their_low, their_maps)


def softplus(value):
    small = jnp.exp(-jnp.abs(value))
    tail = jnp.where(small < 0.00390625, small * (1.0 - 0.5 * small), jnp.log(1.0 + small))
    return jnp.maximum(value, 0.0) + tail


def add_states(rates_ref, state_ref, total_ref, states, totals):
    state_ref[...] = jnp.exp2(rates_ref[...] * totals) * state_ref[...] + states
    total_ref[...] = total_ref[...] + totals


def sums_within(steps):
    rows = steps.shape[0]
    at = lax.broadcasted_iota(jnp.int32, (rows, rows), 0)
    of = lax.broadcasted_iota(jnp.int32, (rows, rows), 1)
    upto = jnp.where(of <= at, 1.0, 0.0).astype(jnp.bfloat16)
    return jnp.dot(upto, steps, preferred_element_type=jnp.float32)


def step_kernel(
    place_ref, stream_ref, low_ref, map_ref, cols_ref, bias_ref, rates_ref, *rest
):
    own_state_ref, own_total_ref = rest[:2]
    steps_ref, sums_ref, maps_ref, carry_ref, state_ref, total_ref, wide_ref, turn_ref = rest[2:]
    block = pl.program_id(0)
    rows, width = stream_ref.shape[1:]

    @pl.when(block == 0)
    def _():
        state_ref[...] = jnp.zeros_like(state_ref)
        total_ref[...] = jnp.zeros_like(total_ref)
        for n in range(NS):
            wide_ref[n * SUBLANES : (n + 1) * SUBLANES, :] = jnp.broadcast_to(
                rates_ref[n : n + 1, :], (SUBLANES, width)
            )

    @pl.when(block == place_ref[0] * CORES)
    def _():
        add_states(rates_ref, state_ref, total_ref, own_state_ref[...], own_total_ref[...])

    maps = map_ref[0].astype(jnp.float32)
    maps = maps[: 2 * NS, :] + maps[2 * NS :, :]
    maps_ref[0] = maps
    logits = jnp.dot(low_ref[0], cols_ref[...], preferred_element_type=jnp.float32)
    steps = softplus(logits + bias_ref[...]).astype(jnp.bfloat16)
    steps_ref[...] = steps
    push = steps * stream_ref[0]
    within = sums_within(steps)
    sums_ref[...] = within.astype(jnp.bfloat16)
    whole = within[rows - 1 :, :]
    left = whole - within
    some, chunk, several = rows // 2, CORES * LANES, 4
    state_row = lax.broadcasted_iota(jnp.int32, (NS, some), 0)
    for first in range(0, rows, some):
        span = slice(first, first + some)
        chosen = [
            jnp.concatenate(
                [
                    jnp.where(state_row == m, maps[:NS, span], 0.0).astype(jnp.bfloat16)
                    for m in range(n, n + several)
                ],
                axis=1,
            )
            for n in range(0, NS, several)
        ]
        for item in range(width // chunk):
            lanes = slice(item * chunk, (item + 1) * chunk)
            left_here = left[span, lanes].reshape(some // SUBLANES, SUBLANES, chunk)
            push_here = push[span, lanes]
            added = state_ref[:, lanes]
            if first == 0:
                added = jnp.exp2(rates_ref[:, lanes] * whole[:, lanes]) * added
            for n in range(0, NS, several):
                pushed = []
                for m in range(n, n + several):
                    rate = wide_ref[m * SUBLANES : (m + 1) * SUBLANES, lanes]
                    decay = jnp.exp2(left_here * rate[None]).reshape(some, chunk)
                    pushed.append(decay.astype(jnp.bfloat16) * push_here)
                added = added + jnp.dot(
                    chosen[n // several],
                    jnp.concatenate(pushed, axis=0),
                    preferred_element_type=jnp.float32,
                )
            state_ref[:, lanes] = added
    total_ref[...] = total_ref[...] + whole

    count = pl.num_programs(0)

    @pl.when(block == count - 1)
    def _():
        @pl.when(place_ref[0] * CORES == count)
        def _():
            add_states(rates_ref, state_ref, total_ref, own_state_ref[...], own_total_ref[...])

        write_carry(carry_ref.at[0], state_ref[...], total_ref[...], turn_ref)
        for target in range(1, carry_ref.shape[0]):
            carry_ref[target] = carry_ref[0]


def step_sizes(place, stream, lows, cols, bias, rates, state, total, targets):
    others = stream.shape[0]
    chips = others + 1
    rows, width = stream.shape[1] // CORES, stream.shape[2]
    map_row = CORES * rows // MAPS
    blocks = others * CORES
    carry = (targets, (width // LANES + 1) * NS, LANES)

    def slot(b, s):
        chip = b // CORES
        return lax.rem(s[0] - jnp.where(chip < s[0], chip, chip + 1) + chips, chips) - 1

    def core(b):
        return lax.rem(b, CORES)

    def fixed(*shape):
        return pl.BlockSpec(shape, lambda b, s: (0,) * len(shape))

    return pl.pallas_call(
        step_kernel,
        grid_spec=pltpu.PrefetchScalarGridSpec(
            num_scalar_prefetch=1,
            grid=(blocks,),
            in_specs=[
                pl.BlockSpec((1, rows, width), lambda b, s: (slot(b, s), core(b), 0)),
                pl.BlockSpec((1, rows, RANK), lambda b, s: (slot(b, s), core(b), 0)),
                pl.BlockSpec((1, MAPS, rows), lambda b, s: (slot(b, s), map_row, core(b))),
                fixed(*cols.shape),
                fixed(*bias.shape),
                fixed(*rates.shape),
                fixed(*state.shape),
                fixed(*total.shape),
            ],
            out_specs=[
                pl.BlockSpec((rows, width), lambda b, s: (b, 0)),
                pl.BlockSpec((rows, width), lambda b, s: (b, 0)),
                pl.BlockSpec((1, 2 * NS, rows), lambda b, s: (b, 0, 0)),
                fixed(*carry),
            ],
            scratch_shapes=[
                pltpu.VMEM((NS, width), jnp.float32),
                pltpu.VMEM((1, width), jnp.float32),
                pltpu.VMEM((NS * SUBLANES, width), jnp.float32),
                pltpu.VMEM((SUBLANES, LANES), jnp.float32),
            ],
        ),
        out_shape=[
            jax.ShapeDtypeStruct((blocks * rows, width), jnp.bfloat16),
            jax.ShapeDtypeStruct((blocks * rows, width), jnp.bfloat16),
            jax.ShapeDtypeStruct((blocks, 2 * NS, rows), jnp.float32),
            jax.ShapeDtypeStruct(carry, jnp.bfloat16),
        ],
        compiler_params=params,
        name="step_sizes",
    )(place, stream, lows, lows, cols, bias, rates, state, total)


def write_carry(out_ref, state, total, turn_ref):
    tile = state.shape[1] // LANES
    turn_ref[...] = jnp.zeros_like(turn_ref)
    for item in range(tile):
        lanes = slice(item * LANES, (item + 1) * LANES)
        turn_ref[item : item + 1, :] = total[:, lanes]
        out_ref[item * NS : (item + 1) * NS, :] = state[:, lanes].astype(jnp.bfloat16)
    out_ref[tile * NS :, :] = jnp.concatenate(split(turn_ref[...]), axis=0)


def follow(carry_ref, rates_ref, state_ref):
    tile = state_ref.shape[1] // LANES
    sums = carry_ref[tile * NS :, :].astype(jnp.float32)
    sums = sums[:SUBLANES, :] + sums[SUBLANES:, :]
    for item in range(tile):
        lanes = slice(item * LANES, (item + 1) * LANES)
        decay = jnp.exp2(rates_ref[:, lanes] * sums[item : item + 1, :])
        added = carry_ref[item * NS : (item + 1) * NS, :].astype(jnp.float32)
        state_ref[:, lanes] = decay * state_ref[:, lanes] + added
    return sums


def scan_blocks(stream_ref, steps_ref, maps, rates_ref, gain_ref, out_ref, state_ref, work_refs):
    out_of_ref, *hist_refs = work_refs
    rows, width = steps_ref.shape
    source = lax.broadcasted_iota(jnp.int32, (LANES, NS * NS), 0)
    column = lax.rem(lax.broadcasted_iota(jnp.int32, (LANES, NS * NS), 1), NS)
    token = lax.rem(lax.broadcasted_iota(jnp.int32, (rows, NS * NS), 0), NS)
    slot = lax.broadcasted_iota(jnp.int32, (rows, NS * NS), 1) // NS
    turned = jnp.concatenate(
        [maps, jnp.zeros((LANES - 2 * NS, rows), jnp.float32)], axis=0
    ).T.astype(jnp.bfloat16)
    pick = jnp.where(source == NS + column, 1.0, 0.0).astype(jnp.bfloat16)
    spread = jnp.dot(turned, pick, preferred_element_type=jnp.float32)
    out_of_ref[...] = jnp.where(token == slot, spread, 0.0).astype(jnp.bfloat16)
    map_in = maps[:NS, :]
    half = width // 2

    def finish(first, hist_ref):
        here = pl.ds(first, NS)
        mixed = jnp.dot(out_of_ref[here, :], hist_ref[...], preferred_element_type=jnp.float32)
        direct = gain_ref[...] * stream_ref[0, here, :].astype(jnp.float32)
        out_ref[here, :] = (mixed + direct).astype(jnp.bfloat16)

    def advance(first, hist_ref):
        here = pl.ds(first, NS)
        into = pltpu.roll(map_in, lax.rem(rows - first, rows), 1)
        for lanes in (slice(0, half), slice(half, width)):
            state = state_ref[:, lanes]
            rates = rates_ref[:, lanes]
            steps = steps_ref[here, lanes].astype(jnp.float32)
            push = steps * stream_ref[0, here, lanes].astype(jnp.float32)
            for near in range(NS):
                this = slice(near, near + 1)
                state = jnp.exp2(rates * steps[this, :]) * state + into[:, this] * push[this, :]
                hist_ref[near * NS : (near + 1) * NS, lanes] = state.astype(jnp.bfloat16)
            state_ref[:, lanes] = state

    def pair(index, nothing):
        first = pl.multiple_of(index * 2 * NS, 2 * NS)
        advance(first, hist_refs[0])
        finish(first, hist_refs[0])
        second = pl.multiple_of(first + NS, NS)
        advance(second, hist_refs[1])
        finish(second, hist_refs[1])
        return nothing

    lax.fori_loop(0, rows // (2 * NS), pair, 0)


def work_shapes(rows, width):
    return [
        pltpu.VMEM((rows, NS * NS), jnp.bfloat16),
        pltpu.VMEM((NS * NS, width), jnp.bfloat16),
        pltpu.VMEM((NS * NS, width), jnp.bfloat16),
    ]


def own_kernel(
    stream_ref, low_ref, map_ref, cols_ref, bias_ref, rates_ref, gain_ref,
    out_ref, sums_ref, maps_ref, state_ref, total_ref, steps_ref, *work_refs
):
    rows = steps_ref.shape[0]

    @pl.when(pl.program_id(0) == 0)
    def _():
        state_ref[...] = jnp.zeros_like(state_ref)
        total_ref[...] = jnp.zeros_like(total_ref)

    maps = map_ref[...].astype(jnp.float32)
    maps = maps[: 2 * NS, :] + maps[2 * NS :, :]
    maps_ref[0] = maps
    logits = jnp.dot(low_ref[...], cols_ref[...], preferred_element_type=jnp.float32)
    steps = softplus(logits + bias_ref[...]).astype(jnp.bfloat16)
    steps_ref[...] = steps
    within = sums_within(steps)
    sums_ref[...] = within.astype(jnp.bfloat16)
    total_ref[...] = total_ref[...] + within[rows - 1 :, :]
    scan_blocks(stream_ref, steps_ref, maps, rates_ref, gain_ref, out_ref, state_ref, work_refs)


def scan_own(stream, lows, cols, bias, rates, gain):
    rows, width = stream.shape[1] // CORES, stream.shape[2]
    map_row = CORES * rows // MAPS

    def fixed(*shape):
        return pl.BlockSpec(shape, lambda b: (0,) * len(shape))

    block = pl.BlockSpec((rows, width), lambda b: (b, 0))
    return pl.pallas_call(
        own_kernel,
        grid=(CORES,),
        in_specs=[
            pl.BlockSpec((1, rows, width), lambda b: (0, b, 0)),
            pl.BlockSpec((rows, RANK), lambda b: (b, 0)),
            pl.BlockSpec((MAPS, rows), lambda b: (map_row, b)),
            fixed(*cols.shape),
            fixed(*bias.shape),
            fixed(*rates.shape),
            fixed(*gain.shape),
        ],
        out_specs=[
            block,
            block,
            pl.BlockSpec((1, 2 * NS, rows), lambda b: (b, 0, 0)),
            fixed(NS, width),
            fixed(1, width),
        ],
        out_shape=[
            jax.ShapeDtypeStruct((CORES * rows, width), jnp.bfloat16),
            jax.ShapeDtypeStruct((CORES * rows, width), jnp.bfloat16),
            jax.ShapeDtypeStruct((CORES, 2 * NS, rows), jnp.float32),
            jax.ShapeDtypeStruct((NS, width), jnp.float32),
            jax.ShapeDtypeStruct((1, width), jnp.float32),
        ],
        scratch_shapes=[pltpu.VMEM((rows, width), jnp.bfloat16)] + work_shapes(rows, width),
        compiler_params=params,
        cost_estimate=pl.CostEstimate(flops=4 * 10**9, bytes_accessed=1 << 21, transcendentals=0),
        name="scan_own",
    )(stream, lows, lows, cols, bias, rates, gain)


def others_kernel(
    place_ref, stream_ref, steps_ref, maps_ref, rates_ref, gain_ref, out_ref, last_ref, *work_refs
):
    @pl.when(lax.rem(pl.program_id(0), CORES) == 0)
    def _():
        last_ref[...] = jnp.zeros_like(last_ref)

    scan_blocks(
        stream_ref, steps_ref, maps_ref[0], rates_ref, gain_ref, out_ref, last_ref.at[0], work_refs
    )


def scan_others(place, stream, steps, maps, rates, gain):
    others = stream.shape[0]
    chips = others + 1
    rows, width = stream.shape[1] // CORES, stream.shape[2]

    def slot(b, s):
        chip = b // CORES
        return lax.rem(s[0] - jnp.where(chip < s[0], chip, chip + 1) + chips, chips) - 1

    def fixed(*shape):
        return pl.BlockSpec(shape, lambda b, s: (0,) * len(shape))

    block = pl.BlockSpec((rows, width), lambda b, s: (b, 0))
    return pl.pallas_call(
        others_kernel,
        grid_spec=pltpu.PrefetchScalarGridSpec(
            num_scalar_prefetch=1,
            grid=(others * CORES,),
            in_specs=[
                pl.BlockSpec((1, rows, width), lambda b, s: (slot(b, s), lax.rem(b, CORES), 0)),
                block,
                pl.BlockSpec((1, 2 * NS, rows), lambda b, s: (b, 0, 0)),
                fixed(*rates.shape),
                fixed(*gain.shape),
            ],
            out_specs=[block, pl.BlockSpec((1, NS, width), lambda b, s: (b // CORES, 0, 0))],
            scratch_shapes=work_shapes(rows, width),
        ),
        out_shape=[
            jax.ShapeDtypeStruct((others * CORES * rows, width), jnp.bfloat16),
            jax.ShapeDtypeStruct((others, NS, width), jnp.float32),
        ],
        compiler_params=params,
        cost_estimate=pl.CostEstimate(flops=4 * 10**9, bytes_accessed=1 << 21, transcendentals=0),
        name="scan_others",
    )(place, stream, steps, maps, rates, gain)


def carried_kernel(
    places_ref, part_own_ref, part_come_ref, sums_own_ref, sums_come_ref,
    maps_own_ref, maps_come_ref, last_own_ref, last_come_ref, rates_ref, carries_ref,
    out_ref, state_ref, wide_ref, begin_ref, spread_ref, sums_ref,
):
    block = pl.program_id(0)
    rows, width = out_ref.shape
    chip = block // CORES
    here = chip == places_ref[0]

    @pl.when(block == 0)
    def _():
        state_ref[...] = jnp.zeros_like(state_ref)

        def compose(row, nothing):
            follow(carries_ref.at[row], rates_ref, state_ref)
            return nothing

        lax.fori_loop(0, places_ref[1], compose, 0)
        for n in range(NS):
            wide_ref[n * SUBLANES : (n + 1) * SUBLANES, :] = jnp.broadcast_to(
                rates_ref[n : n + 1, :], (SUBLANES, width)
            )

    @pl.when((block > 0) & (lax.rem(block, CORES) == 0))
    def _():
        before = jnp.where(chip - 1 == places_ref[0], last_own_ref[...], last_come_ref[0])
        state_ref[...] = state_ref[...] + before

    state = state_ref[...]
    for n in range(NS):
        begin_ref[n * NS : (n + 1) * NS, :] = jnp.broadcast_to(
            state[n : n + 1, :], (NS, width)
        ).astype(jnp.bfloat16)
    maps = jnp.where(here, maps_own_ref[0], maps_come_ref[0])
    maps = jnp.concatenate([maps, jnp.zeros((LANES - 2 * NS, rows), jnp.float32)], axis=0).T
    for n in range(NS):
        spread_ref[:, n * LANES : (n + 1) * LANES] = jnp.broadcast_to(
            maps[:, NS + n : NS + n + 1], (rows, LANES)
        ).astype(jnp.bfloat16)
    sums = jnp.where(here, sums_own_ref[...], sums_come_ref[...]).astype(jnp.float32)
    sums_ref[...] = sums
    state_ref[...] = jnp.exp2(rates_ref[...] * sums[rows - 1 :, :]) * state
    chunk, several = CORES * LANES, 4

    def some(index, nothing):
        near = pl.ds(pl.multiple_of(index * NS, NS), NS)
        for item in range(width // chunk):
            lanes = slice(item * chunk, (item + 1) * chunk)
            part = jnp.where(here, part_own_ref[near, lanes], part_come_ref[near, lanes])
            total = part.astype(jnp.float32)
            sums = sums_ref[near, lanes].reshape(NS // SUBLANES, SUBLANES, chunk)
            for first in range(0, NS, several):
                terms = []
                for n in range(first, first + several):
                    rate = wide_ref[n * SUBLANES : (n + 1) * SUBLANES, lanes]
                    decay = jnp.exp2(sums * rate[None]).reshape(NS, chunk).astype(jnp.bfloat16)
                    out_of = spread_ref[near, n * LANES : (n + 1) * LANES]
                    out_of = jnp.concatenate([out_of] * (chunk // LANES), axis=1)
                    terms.append(decay * begin_ref[n * NS : (n + 1) * NS, lanes] * out_of)
                four = (terms[0] + terms[1]) + (terms[2] + terms[3])
                total = total + four.astype(jnp.float32)
            out_ref[near, lanes] = total.astype(jnp.bfloat16)
        return nothing

    lax.fori_loop(0, rows // NS, some, 0)


def add_carried(places, parts, sums, maps, lasts, rates, carries):
    blocks_come, _, rows = maps[1].shape
    chips = blocks_come // CORES + 1
    width = rates.shape[1]

    def core(b):
        return lax.rem(b, CORES)

    def order(b, s):
        chip = b // CORES
        return jnp.minimum(
            jnp.where(chip < s[0], b, jnp.maximum(b - CORES, 0)), blocks_come - 1
        )

    def before(b, s):
        chip = jnp.maximum(b // CORES - 1, 0)
        return jnp.minimum(jnp.where(chip < s[0], chip, jnp.maximum(chip - 1, 0)), chips - 2)

    def fixed(*shape):
        return pl.BlockSpec(shape, lambda b, s: (0,) * len(shape))

    own = pl.BlockSpec((rows, width), lambda b, s: (core(b), 0))
    come = pl.BlockSpec((rows, width), lambda b, s: (order(b, s), 0))
    return pl.pallas_call(
        carried_kernel,
        grid_spec=pltpu.PrefetchScalarGridSpec(
            num_scalar_prefetch=1,
            grid=(chips * CORES,),
            in_specs=[
                own,
                come,
                own,
                come,
                pl.BlockSpec((1, 2 * NS, rows), lambda b, s: (core(b), 0, 0)),
                pl.BlockSpec((1, 2 * NS, rows), lambda b, s: (order(b, s), 0, 0)),
                fixed(NS, width),
                pl.BlockSpec((1, NS, width), lambda b, s: (before(b, s), 0, 0)),
                fixed(*rates.shape),
                fixed(*carries.shape),
            ],
            out_specs=pl.BlockSpec((rows, width), lambda b, s: (b, 0)),
            scratch_shapes=[
                pltpu.VMEM((NS, width), jnp.float32),
                pltpu.VMEM((NS * SUBLANES, width), jnp.float32),
                pltpu.VMEM((NS * NS, width), jnp.bfloat16),
                pltpu.VMEM((rows, NS * LANES), jnp.bfloat16),
                pltpu.VMEM((rows, width), jnp.float32),
            ],
        ),
        out_shape=jax.ShapeDtypeStruct((chips * CORES * rows, width), jnp.bfloat16),
        compiler_params=params,
        name="add_carried",
    )(places, *parts, *sums, *maps, *lasts, rates, carries)


def local(
    queries, keys, values, doc_lengths, rank_in, bc_weight, rank_out, dt_bias, a_log, skip_gain
):
    devices = lax.axis_size("seq")
    chips = devices // CORES
    targets = lax.axis_size("chan")
    seq_place = lax.axis_index("seq").astype(jnp.int32)
    chan_place = lax.axis_index("chan").astype(jnp.int32)
    chip, core = seq_place // CORES, lax.rem(seq_place, CORES)
    place = jnp.stack([chip, core])
    width = queries.shape[2] // devices
    wide = max(HEAD_SIZE, keys.shape[2] // devices)

    def other(device):
        return device + 1 - 2 * (device % CORES)

    swap = [(device, other(device)) for device in range(devices)]
    near = [(device, device + CORES) for device in range(devices - CORES)]
    far = [(device, other(device + CORES)) for device in range(devices - CORES)]

    def onward(chips_on):
        return [(device, (device + chips_on * CORES) % devices) for device in range(devices)]

    own, theirs = select_heads(keys[0], values[0], chips, wide)
    from_near = lax.ppermute(own, "seq", near)
    from_far = lax.ppermute(theirs, "seq", far)
    swapped = lax.ppermute(theirs, "seq", swap)
    their_queries = lax.ppermute(queries[0], "seq", swap)
    blocks = (own, swapped, from_near, from_far)

    first = seq_place * width
    logs = lax.dynamic_slice_in_dim(a_log, first, width, 0)
    rates = (-LOG2E * jnp.exp(logs)).T
    cols = lax.dynamic_slice_in_dim(rank_out, first, width, 1)
    bias = lax.dynamic_slice_in_dim(dt_bias, first, width, 0)[None]
    gain = lax.dynamic_slice_in_dim(skip_gain, first, width, 0)[None]

    sent, stayed, low, maps = attend(
        place, doc_lengths, (queries[0], their_queries), blocks, rank_in, bc_weight.T,
        (rates, cols, bias, gain),
    )
    come = [lax.ppermute(sent[step], "seq", onward(step + 1)) for step in range(chips - 1)]
    low_own = low_and_maps(low, maps, *lax.ppermute((low, maps), "seq", swap))
    low_come = [lax.ppermute(low_own, "seq", onward(step + 1)) for step in range(chips - 1)]
    got_sent = lax.ppermute(sent, "seq", swap)
    got_stayed = lax.ppermute(stayed, "seq", swap)
    attn_rows = join_heads(sent, stayed, got_sent, got_stayed)

    part_own, sums_own, maps_own, state, total = scan_own(stayed, low_own, cols, bias, rates, gain)
    come, low_come = jnp.stack(come), jnp.stack(low_come)
    steps, sums_come, maps_come, carry = step_sizes(
        place, come, low_come, cols, bias, rates, state, total, targets
    )
    carries = lax.all_to_all(carry, "chan", split_axis=0, concat_axis=0, tiled=True)
    part_come, last_come = scan_others(place, come, steps, maps_come, rates, gain)
    ssm_rows = add_carried(
        jnp.stack([chip, chan_place]), (part_own, part_come), (sums_own, sums_come),
        (maps_own, maps_come), (state, last_come), rates, carries,
    )
    return (attn_rows[None], ssm_rows[None])


def solution(mesh):
    return jax.shard_map(
        local,
        mesh=mesh,
        in_specs=(
            P("chan", "seq", None),
            P("chan", "seq", None),
            P("chan", "seq", None),
            P("chan", None),
            P(),
            P(),
            P(),
            P(),
            P(),
            P(),
        ),
        out_specs=(P("chan", "seq", None), P("chan", None, "seq")),
        check_vma=False,
    )
```

```python
import functools
import math

import jax
import jax.numpy as jnp
from jax import lax
from jax.experimental import pallas as pl
from jax.experimental.pallas import tpu as pltpu
from jax.sharding import PartitionSpec as P

QUERY_HEADS = 32
KEY_VALUE_HEADS = 8
HEAD_SIZE = 128
GROUP = QUERY_HEADS // KEY_VALUE_HEADS
NS = 16
RANK = 256
CORES = 2
LANES = 128
SUBLANES = 8
MAPS = 4 * NS
LOG2E = 1.4426950408889634

masked_fill = -1e30
params = pltpu.CompilerParams(vmem_limit_bytes=60 << 20)


def split(value):
    coarse = value.astype(jnp.bfloat16)
    return coarse, (value - coarse.astype(jnp.float32)).astype(jnp.bfloat16)


def run_copies(pairs, sems):
    copies = [
        pltpu.make_async_copy(source, target, sems.at[i]) for i, (source, target) in enumerate(pairs)
    ]
    for copy in copies:
        copy.start()
    for copy in copies:
        copy.wait()


def columns_of(ref, index, size):
    return ref.at[:, pl.ds(pl.multiple_of(index * size, LANES), size)]


def heads_kernel(key_ref, value_ref, *refs):
    near_ref, near_last_ref, far_ref, far_last_ref, sems = refs
    place = lax.axis_index("seq")
    chip, core = place // CORES, lax.rem(place, CORES)
    others, _, _, wide = near_ref.shape
    halves = key_ref.shape[1] // wide // (others + 1)
    pairs = []
    for target, last, which in ((near_ref, near_last_ref, core), (far_ref, far_last_ref, 1 - core)):
        for step in range(others + 1):
            owner = lax.rem(chip + 2 + step, others + 1)
            index = owner * halves + (which if halves == CORES else 0)
            place_in = target.at[step] if step < others else last.at[0]
            for kind, source in enumerate((key_ref, value_ref)):
                pairs.append((columns_of(source, index, wide), place_in.at[kind]))
    run_copies(pairs, sems)


def select_heads(keys, values, chips, wide):
    part = jax.ShapeDtypeStruct((chips - 1, 2, keys.shape[0], wide), keys.dtype)
    last = jax.ShapeDtypeStruct((1, 2, keys.shape[0], wide), keys.dtype)
    return pl.pallas_call(
        heads_kernel,
        in_specs=[pl.BlockSpec(memory_space=pl.ANY)] * 2,
        out_shape=[part, last, part, last],
        scratch_shapes=[pltpu.SemaphoreType.DMA((4 * chips,))],
        compiler_params=params,
        name="select_heads",
    )(keys, values)


def join_kernel(sent_ref, stayed_ref, got_sent_ref, got_stayed_ref, out_ref, sems):
    place = lax.axis_index("seq")
    core, chip = lax.rem(place, CORES), place // CORES
    rows = out_ref.shape[0]
    others, _, width = sent_ref.shape
    here = pl.ds(pl.multiple_of(core * rows, rows), rows)
    pairs = []
    for first, rest, which in (
        (stayed_ref, sent_ref, core), (got_stayed_ref, got_sent_ref, 1 - core)
    ):
        for step in range(others + 1):
            source = first.at[0, here, :] if step == 0 else rest.at[step - 1, here, :]
            owner = lax.rem(chip + step, others + 1)
            pairs.append((source, columns_of(out_ref, owner * CORES + which, width)))
    run_copies(pairs, sems)


def join_heads(sent, stayed, got_sent, got_stayed):
    others, rows, width = sent.shape
    return pl.pallas_call(
        join_kernel,
        in_specs=[pl.BlockSpec(memory_space=pl.ANY)] * 4,
        out_shape=jax.ShapeDtypeStruct(
            (rows // CORES, (others + 1) * CORES * width), sent.dtype
        ),
        scratch_shapes=[pltpu.SemaphoreType.DMA((CORES * (others + 1),))],
        compiler_params=params,
        name="join_heads",
    )(sent, stayed, got_sent, got_stayed)


def attend_kernel(
    place_ref, doc_ref, mine_ref, theirs_ref, own_key_ref, own_value_ref, swap_key_ref,
    swap_value_ref, near_ref, far_ref, rank_ref, map_ref, *rest, after,
):
    earlier = rest[:2] if len(rest) > 4 + after else None
    out_ref, low_ref, maps_ref, mask_ref = rest[-4:]
    step = pl.program_id(0)
    rows = mine_ref.shape[0]
    group = mine_ref.shape[1] // HEAD_SIZE
    chip, core = place_ref[0], place_ref[1]
    first_core = core == 0

    def above(shape):
        row = lax.rem(lax.broadcasted_iota(jnp.int32, shape, 0), rows)
        return lax.broadcasted_iota(jnp.int32, shape, 1) > row

    @pl.when(step == 0)
    def _():
        low_ref[...] = earlier[0][...] if earlier else jnp.zeros_like(low_ref)
        maps_ref[...] = earlier[1][...] if earlier else jnp.zeros_like(maps_ref)
        own = chip * CORES + core
        swapped = chip * CORES + 1 - core
        near, far = own - CORES, swapped - CORES
        lane = lax.broadcasted_iota(jnp.int32, (rows, rows), 1)
        row = lax.broadcasted_iota(jnp.int32, (rows, rows), 0)
        for item, (place, before, middle) in enumerate(
            (
                (own, near, jnp.where(first_core, far, swapped)),
                (swapped, far, jnp.where(first_core, own, near)),
            )
        ):
            query_pos = place * rows + row
            start = jnp.zeros((rows, rows), jnp.int32)
            bound = jnp.int32(0)
            for doc in range(doc_ref.shape[1]):
                bound = bound + doc_ref[0, doc]
                start = jnp.where(query_pos >= bound, bound, start)
            ends = jnp.where(lane > row, before, place) * rows + lane
            mask_ref[item, :, :rows] = jnp.where(
                (ends >= start) & (ends <= query_pos), 0.0, masked_fill
            )
            mask_ref[item, :, rows:] = jnp.where(
                middle * rows + lane >= start, 0.0, masked_fill
            )

    scale = LOG2E / math.sqrt(HEAD_SIZE)
    ones = jnp.ones((3 * rows, HEAD_SIZE), jnp.bfloat16)

    def windows(kind):
        own = (own_key_ref, own_value_ref)[kind][...]
        swapped = (swap_key_ref, swap_value_ref)[kind][...]
        near, far = near_ref[0, kind], far_ref[0, kind]
        return (
            jnp.concatenate([near, own, jnp.where(first_core, far, swapped)], axis=0),
            jnp.concatenate([far, swapped, jnp.where(first_core, own, near)], axis=0),
        )

    scores = []
    for keys, query in zip(windows(0), (mine_ref[...], theirs_ref[...])):
        stacked = jnp.concatenate(
            [query[:, i * HEAD_SIZE : (i + 1) * HEAD_SIZE] for i in range(group)], axis=0
        )
        scores.append(
            lax.dot_general(
                stacked, keys, (((1,), (1,)), ((), ())), preferred_element_type=jnp.float32
            )
        )
    outputs = []
    before = above((group * rows, rows))
    for item, (values, score) in enumerate(zip(windows(1), scores)):
        fill = mask_ref[item]
        ends = jnp.where(before, score[:, :rows], score[:, rows : 2 * rows])
        kept = jnp.concatenate([ends, score[:, 2 * rows :]], axis=1)
        kept = jnp.concatenate(
            [kept[i * rows : (i + 1) * rows, :] + fill for i in range(group)], axis=0
        )
        peak = jnp.max(kept, axis=1, keepdims=True)
        raw = jnp.exp2((kept - peak) * scale).astype(jnp.bfloat16)
        ends = raw[:, :rows]
        none = jnp.zeros_like(ends)
        spread = jnp.concatenate(
            [jnp.where(before, ends, none), jnp.where(before, none, ends), raw[:, rows:]], axis=1
        )
        both = jnp.dot(
            spread, jnp.concatenate([values, ones], axis=1), preferred_element_type=jnp.float32
        )
        mixed = both[:, :HEAD_SIZE] * pl.reciprocal(both[:, HEAD_SIZE:])
        mixed = mixed.astype(jnp.bfloat16)
        outputs.append(
            jnp.concatenate([mixed[i * rows : (i + 1) * rows, :] for i in range(group)], axis=1)
        )
    stream = jnp.concatenate(
        [
            jnp.where(first_core, outputs[0], outputs[1]),
            jnp.where(first_core, outputs[1], outputs[0]),
        ],
        axis=0,
    )
    out_ref[0] = stream
    low_ref[...] += jnp.dot(stream, rank_ref[...], preferred_element_type=jnp.float32)
    maps_ref[...] += lax.dot_general(
        map_ref[...], stream, (((1,), (1,)), ((), ())), preferred_element_type=jnp.float32
    )


def attend(place, doc_lengths, queries, keys, values, blocks, rank_in, map_rows, first, earlier, after):
    mine, theirs = queries
    count, _, rows, columns = blocks[0].shape
    heads = columns // HEAD_SIZE
    chips = lax.axis_size("seq") // CORES
    width = mine.shape[1] // (chips * CORES)
    wide = width // heads
    halves = keys[0].shape[1] // columns // chips

    def owner(j, s):
        return lax.rem(s[0] + first + j // heads, chips)

    def column(j, s):
        return (owner(j, s) * CORES + s[1]) * heads + lax.rem(j, heads)

    def key_column(j, s):
        return column(j, s) if halves == CORES else owner(j, s) * heads + lax.rem(j, heads)

    query = pl.BlockSpec((rows, wide), lambda j, s: (0, column(j, s)))
    here = pl.BlockSpec((rows, HEAD_SIZE), lambda j, s: (0, key_column(j, s)))
    block = pl.BlockSpec(
        (1, 2, rows, HEAD_SIZE), lambda j, s: (j // heads, 0, 0, lax.rem(j, heads))
    )
    low = pl.BlockSpec((CORES * rows, RANK), lambda j, s: (0, 0))
    maps = pl.BlockSpec((2 * NS, CORES * rows), lambda j, s: (0, 0))
    return pl.pallas_call(
        functools.partial(attend_kernel, after=len(after)),
        grid_spec=pltpu.PrefetchScalarGridSpec(
            num_scalar_prefetch=1,
            grid=(count * heads,),
            in_specs=[pl.BlockSpec(memory_space=pltpu.SMEM), query, query]
            + [here] * 4
            + [block] * 2
            + [
                pl.BlockSpec((wide, RANK), lambda j, s: (column(j, s), 0)),
                pl.BlockSpec((2 * NS, wide), lambda j, s: (0, column(j, s))),
            ]
            + ([low, maps] if earlier else [])
            + [pl.BlockSpec(memory_space=pl.ANY)] * len(after),
            out_specs=[
                pl.BlockSpec(
                    (1, CORES * rows, wide), lambda j, s: (j // heads, 0, lax.rem(j, heads))
                ),
                low,
                maps,
            ],
            scratch_shapes=[pltpu.VMEM((2, rows, 2 * rows), jnp.float32)],
        ),
        out_shape=[
            jax.ShapeDtypeStruct((count, CORES * rows, width), jnp.bfloat16),
            jax.ShapeDtypeStruct((CORES * rows, RANK), jnp.float32),
            jax.ShapeDtypeStruct((2 * NS, CORES * rows), jnp.float32),
        ],
        compiler_params=params,
        cost_estimate=pl.CostEstimate(flops=3 * 10**9, bytes_accessed=1 << 21, transcendentals=0),
        name="attend",
    )(
        place, doc_lengths, mine, theirs, keys[0], values[0], keys[1], values[1], *blocks,
        rank_in, map_rows, *(earlier or ()), *after,
    )


def low_kernel(low_ref, maps_ref, their_low_ref, their_maps_ref, out_ref):
    rows = low_ref.shape[0]
    out_ref[:rows, :] = (low_ref[...] + their_low_ref[...]).astype(jnp.bfloat16)
    out_ref[rows:, :] = jnp.concatenate(split(maps_ref[...] + their_maps_ref[...]), axis=0)


def low_and_maps(low, maps, their_low, their_maps):
    rows = low.shape[0]
    return pl.pallas_call(
        low_kernel,
        out_shape=jax.ShapeDtypeStruct((rows + MAPS, RANK), jnp.bfloat16),
        compiler_params=params,
        cost_estimate=pl.CostEstimate(flops=1, bytes_accessed=1, transcendentals=0),
        name="low_and_maps",
    )(low, maps, their_low, their_maps)


def softplus(value):
    small = jnp.exp(-jnp.abs(value))
    tail = jnp.where(small < 0.00390625, small * (1.0 - 0.5 * small), jnp.log(1.0 + small))
    return jnp.maximum(value, 0.0) + tail


def add_states(rates_ref, state_ref, total_ref, states, totals):
    state_ref[...] = jnp.exp2(rates_ref[...] * totals) * state_ref[...] + states
    total_ref[...] = total_ref[...] + totals


def sums_within(steps):
    rows = steps.shape[0]
    at = lax.broadcasted_iota(jnp.int32, (rows, rows), 0)
    of = lax.broadcasted_iota(jnp.int32, (rows, rows), 1)
    upto = jnp.where(of <= at, 1.0, 0.0).astype(jnp.bfloat16)
    return jnp.dot(upto, steps, preferred_element_type=jnp.float32)


def step_kernel(
    place_ref, stream_ref, low_ref, map_ref, cols_ref, bias_ref, rates_ref, *rest
):
    own_state_ref, own_total_ref = rest[:2]
    steps_ref, sums_ref, maps_ref, carry_ref, state_ref, total_ref, wide_ref, turn_ref = rest[3:]
    block = pl.program_id(0)
    rows, width = stream_ref.shape[1:]

    @pl.when(block == 0)
    def _():
        state_ref[...] = jnp.zeros_like(state_ref)
        total_ref[...] = jnp.zeros_like(total_ref)
        for n in range(NS):
            wide_ref[n * SUBLANES : (n + 1) * SUBLANES, :] = jnp.broadcast_to(
                rates_ref[n : n + 1, :], (SUBLANES, width)
            )

    @pl.when(block == place_ref[0] * CORES)
    def _():
        add_states(rates_ref, state_ref, total_ref, own_state_ref[...], own_total_ref[...])

    maps = map_ref[0].astype(jnp.float32)
    maps = maps[: 2 * NS, :] + maps[2 * NS :, :]
    maps_ref[0] = maps
    logits = jnp.dot(low_ref[0], cols_ref[...], preferred_element_type=jnp.float32)
    steps = softplus(logits + bias_ref[...]).astype(jnp.bfloat16)
    steps_ref[...] = steps
    push = steps * stream_ref[0]
    within = sums_within(steps)
    sums_ref[...] = within.astype(jnp.bfloat16)
    whole = within[rows - 1 :, :]
    left = whole - within
    some, chunk, several = rows // 2, CORES * LANES, 4
    state_row = lax.broadcasted_iota(jnp.int32, (NS, some), 0)
    for first in range(0, rows, some):
        span = slice(first, first + some)
        chosen = [
            jnp.concatenate(
                [
                    jnp.where(state_row == m, maps[:NS, span], 0.0).astype(jnp.bfloat16)
                    for m in range(n, n + several)
                ],
                axis=1,
            )
            for n in range(0, NS, several)
        ]
        for item in range(width // chunk):
            lanes = slice(item * chunk, (item + 1) * chunk)
            left_here = left[span, lanes].reshape(some // SUBLANES, SUBLANES, chunk)
            push_here = push[span, lanes]
            added = state_ref[:, lanes]
            if first == 0:
                added = jnp.exp2(rates_ref[:, lanes] * whole[:, lanes]) * added
            for n in range(0, NS, several):
                pushed = []
                for m in range(n, n + several):
                    rate = wide_ref[m * SUBLANES : (m + 1) * SUBLANES, lanes]
                    decay = jnp.exp2(left_here * rate[None]).reshape(some, chunk)
                    pushed.append(decay.astype(jnp.bfloat16) * push_here)
                added = added + jnp.dot(
                    chosen[n // several],
                    jnp.concatenate(pushed, axis=0),
                    preferred_element_type=jnp.float32,
                )
            state_ref[:, lanes] = added
    total_ref[...] = total_ref[...] + whole

    count = pl.num_programs(0)

    @pl.when(block == count - 1)
    def _():
        @pl.when(place_ref[0] * CORES == count)
        def _():
            add_states(rates_ref, state_ref, total_ref, own_state_ref[...], own_total_ref[...])

        write_carry(carry_ref.at[0], state_ref[...], total_ref[...], turn_ref)
        for target in range(1, carry_ref.shape[0]):
            carry_ref[target] = carry_ref[0]


def step_sizes(place, stream, lows, cols, bias, rates, state, total, targets, after):
    others = stream.shape[0]
    chips = others + 1
    rows, width = stream.shape[1] // CORES, stream.shape[2]
    map_row = CORES * rows // MAPS
    blocks = others * CORES
    carry = (targets, (width // LANES + 1) * NS, LANES)

    def slot(b, s):
        chip = b // CORES
        return lax.rem(s[0] - jnp.where(chip < s[0], chip, chip + 1) + chips, chips) - 1

    def core(b):
        return lax.rem(b, CORES)

    def fixed(*shape):
        return pl.BlockSpec(shape, lambda b, s: (0,) * len(shape))

    return pl.pallas_call(
        step_kernel,
        grid_spec=pltpu.PrefetchScalarGridSpec(
            num_scalar_prefetch=1,
            grid=(blocks,),
            in_specs=[
                pl.BlockSpec((1, rows, width), lambda b, s: (slot(b, s), core(b), 0)),
                pl.BlockSpec((1, rows, RANK), lambda b, s: (slot(b, s), core(b), 0)),
                pl.BlockSpec((1, MAPS, rows), lambda b, s: (slot(b, s), map_row, core(b))),
                fixed(*cols.shape),
                fixed(*bias.shape),
                fixed(*rates.shape),
                fixed(*state.shape),
                fixed(*total.shape),
                pl.BlockSpec(memory_space=pl.ANY),
            ],
            out_specs=[
                pl.BlockSpec((rows, width), lambda b, s: (b, 0)),
                pl.BlockSpec((rows, width), lambda b, s: (b, 0)),
                pl.BlockSpec((1, 2 * NS, rows), lambda b, s: (b, 0, 0)),
                fixed(*carry),
            ],
            scratch_shapes=[
                pltpu.VMEM((NS, width), jnp.float32),
                pltpu.VMEM((1, width), jnp.float32),
                pltpu.VMEM((NS * SUBLANES, width), jnp.float32),
                pltpu.VMEM((SUBLANES, LANES), jnp.float32),
            ],
        ),
        out_shape=[
            jax.ShapeDtypeStruct((blocks * rows, width), jnp.bfloat16),
            jax.ShapeDtypeStruct((blocks * rows, width), jnp.bfloat16),
            jax.ShapeDtypeStruct((blocks, 2 * NS, rows), jnp.float32),
            jax.ShapeDtypeStruct(carry, jnp.bfloat16),
        ],
        compiler_params=params,
        name="step_sizes",
    )(place, stream, lows, lows, cols, bias, rates, state, total, after)


def write_carry(out_ref, state, total, turn_ref):
    tile = state.shape[1] // LANES
    turn_ref[...] = jnp.zeros_like(turn_ref)
    for item in range(tile):
        lanes = slice(item * LANES, (item + 1) * LANES)
        turn_ref[item : item + 1, :] = total[:, lanes]
        out_ref[item * NS : (item + 1) * NS, :] = state[:, lanes].astype(jnp.bfloat16)
    out_ref[tile * NS :, :] = jnp.concatenate(split(turn_ref[...]), axis=0)


def follow(carry_ref, rates_ref, state_ref):
    tile = state_ref.shape[1] // LANES
    sums = carry_ref[tile * NS :, :].astype(jnp.float32)
    sums = sums[:SUBLANES, :] + sums[SUBLANES:, :]
    for item in range(tile):
        lanes = slice(item * LANES, (item + 1) * LANES)
        decay = jnp.exp2(rates_ref[:, lanes] * sums[item : item + 1, :])
        added = carry_ref[item * NS : (item + 1) * NS, :].astype(jnp.float32)
        state_ref[:, lanes] = decay * state_ref[:, lanes] + added
    return sums


def scan_blocks(stream_ref, steps_ref, maps, rates_ref, gain_ref, out_ref, state_ref, work_refs):
    out_of_ref, *hist_refs = work_refs
    rows, width = steps_ref.shape
    source = lax.broadcasted_iota(jnp.int32, (LANES, NS * NS), 0)
    column = lax.rem(lax.broadcasted_iota(jnp.int32, (LANES, NS * NS), 1), NS)
    token = lax.rem(lax.broadcasted_iota(jnp.int32, (rows, NS * NS), 0), NS)
    slot = lax.broadcasted_iota(jnp.int32, (rows, NS * NS), 1) // NS
    turned = jnp.concatenate(
        [maps, jnp.zeros((LANES - 2 * NS, rows), jnp.float32)], axis=0
    ).T.astype(jnp.bfloat16)
    pick = jnp.where(source == NS + column, 1.0, 0.0).astype(jnp.bfloat16)
    spread = jnp.dot(turned, pick, preferred_element_type=jnp.float32)
    out_of_ref[...] = jnp.where(token == slot, spread, 0.0).astype(jnp.bfloat16)
    map_in = maps[:NS, :]
    half = width // 2

    def finish(first, hist_ref):
        here = pl.ds(first, NS)
        mixed = jnp.dot(out_of_ref[here, :], hist_ref[...], preferred_element_type=jnp.float32)
        direct = gain_ref[...] * stream_ref[0, here, :].astype(jnp.float32)
        out_ref[here, :] = (mixed + direct).astype(jnp.bfloat16)

    def advance(first, hist_ref):
        here = pl.ds(first, NS)
        into = pltpu.roll(map_in, lax.rem(rows - first, rows), 1)
        for lanes in (slice(0, half), slice(half, width)):
            state = state_ref[:, lanes]
            rates = rates_ref[:, lanes]
            steps = steps_ref[here, lanes].astype(jnp.float32)
            push = steps * stream_ref[0, here, lanes].astype(jnp.float32)
            for near in range(NS):
                this = slice(near, near + 1)
                state = jnp.exp2(rates * steps[this, :]) * state + into[:, this] * push[this, :]
                hist_ref[near * NS : (near + 1) * NS, lanes] = state.astype(jnp.bfloat16)
            state_ref[:, lanes] = state

    def pair(index, nothing):
        first = pl.multiple_of(index * 2 * NS, 2 * NS)
        advance(first, hist_refs[0])
        finish(first, hist_refs[0])
        second = pl.multiple_of(first + NS, NS)
        advance(second, hist_refs[1])
        finish(second, hist_refs[1])
        return nothing

    lax.fori_loop(0, rows // (2 * NS), pair, 0)


def work_shapes(rows, width):
    return [
        pltpu.VMEM((rows, NS * NS), jnp.bfloat16),
        pltpu.VMEM((NS * NS, width), jnp.bfloat16),
        pltpu.VMEM((NS * NS, width), jnp.bfloat16),
    ]


def own_kernel(
    stream_ref, low_ref, map_ref, cols_ref, bias_ref, rates_ref, gain_ref,
    out_ref, sums_ref, maps_ref, state_ref, total_ref, steps_ref, *work_refs
):
    rows = steps_ref.shape[0]

    @pl.when(pl.program_id(0) == 0)
    def _():
        state_ref[...] = jnp.zeros_like(state_ref)
        total_ref[...] = jnp.zeros_like(total_ref)

    maps = map_ref[...].astype(jnp.float32)
    maps = maps[: 2 * NS, :] + maps[2 * NS :, :]
    maps_ref[0] = maps
    logits = jnp.dot(low_ref[...], cols_ref[...], preferred_element_type=jnp.float32)
    steps = softplus(logits + bias_ref[...]).astype(jnp.bfloat16)
    steps_ref[...] = steps
    within = sums_within(steps)
    sums_ref[...] = within.astype(jnp.bfloat16)
    total_ref[...] = total_ref[...] + within[rows - 1 :, :]
    scan_blocks(stream_ref, steps_ref, maps, rates_ref, gain_ref, out_ref, state_ref, work_refs)


def scan_own(stream, lows, cols, bias, rates, gain):
    rows, width = stream.shape[1] // CORES, stream.shape[2]
    map_row = CORES * rows // MAPS

    def fixed(*shape):
        return pl.BlockSpec(shape, lambda b: (0,) * len(shape))

    block = pl.BlockSpec((rows, width), lambda b: (b, 0))
    return pl.pallas_call(
        own_kernel,
        grid=(CORES,),
        in_specs=[
            pl.BlockSpec((1, rows, width), lambda b: (0, b, 0)),
            pl.BlockSpec((rows, RANK), lambda b: (b, 0)),
            pl.BlockSpec((MAPS, rows), lambda b: (map_row, b)),
            fixed(*cols.shape),
            fixed(*bias.shape),
            fixed(*rates.shape),
            fixed(*gain.shape),
        ],
        out_specs=[
            block,
            block,
            pl.BlockSpec((1, 2 * NS, rows), lambda b: (b, 0, 0)),
            fixed(NS, width),
            fixed(1, width),
        ],
        out_shape=[
            jax.ShapeDtypeStruct((CORES * rows, width), jnp.bfloat16),
            jax.ShapeDtypeStruct((CORES * rows, width), jnp.bfloat16),
            jax.ShapeDtypeStruct((CORES, 2 * NS, rows), jnp.float32),
            jax.ShapeDtypeStruct((NS, width), jnp.float32),
            jax.ShapeDtypeStruct((1, width), jnp.float32),
        ],
        scratch_shapes=[pltpu.VMEM((rows, width), jnp.bfloat16)] + work_shapes(rows, width),
        compiler_params=params,
        cost_estimate=pl.CostEstimate(flops=4 * 10**9, bytes_accessed=1 << 21, transcendentals=0),
        name="scan_own",
    )(stream, lows, lows, cols, bias, rates, gain)


def others_kernel(
    place_ref, stream_ref, steps_ref, maps_ref, rates_ref, gain_ref, out_ref, last_ref, *work_refs
):
    @pl.when(lax.rem(pl.program_id(0), CORES) == 0)
    def _():
        last_ref[...] = jnp.zeros_like(last_ref)

    scan_blocks(
        stream_ref, steps_ref, maps_ref[0], rates_ref, gain_ref, out_ref, last_ref.at[0], work_refs
    )


def scan_others(place, stream, steps, maps, rates, gain):
    others = stream.shape[0]
    chips = others + 1
    rows, width = stream.shape[1] // CORES, stream.shape[2]

    def slot(b, s):
        chip = b // CORES
        return lax.rem(s[0] - jnp.where(chip < s[0], chip, chip + 1) + chips, chips) - 1

    def fixed(*shape):
        return pl.BlockSpec(shape, lambda b, s: (0,) * len(shape))

    block = pl.BlockSpec((rows, width), lambda b, s: (b, 0))
    return pl.pallas_call(
        others_kernel,
        grid_spec=pltpu.PrefetchScalarGridSpec(
            num_scalar_prefetch=1,
            grid=(others * CORES,),
            in_specs=[
                pl.BlockSpec((1, rows, width), lambda b, s: (slot(b, s), lax.rem(b, CORES), 0)),
                block,
                pl.BlockSpec((1, 2 * NS, rows), lambda b, s: (b, 0, 0)),
                fixed(*rates.shape),
                fixed(*gain.shape),
            ],
            out_specs=[block, pl.BlockSpec((1, NS, width), lambda b, s: (b // CORES, 0, 0))],
            scratch_shapes=work_shapes(rows, width),
        ),
        out_shape=[
            jax.ShapeDtypeStruct((others * CORES * rows, width), jnp.bfloat16),
            jax.ShapeDtypeStruct((others, NS, width), jnp.float32),
        ],
        compiler_params=params,
        cost_estimate=pl.CostEstimate(flops=4 * 10**9, bytes_accessed=1 << 21, transcendentals=0),
        name="scan_others",
    )(place, stream, steps, maps, rates, gain)


def carried_kernel(
    places_ref, part_own_ref, part_come_ref, sums_own_ref, sums_come_ref,
    maps_own_ref, maps_come_ref, last_own_ref, last_come_ref, rates_ref, carries_ref,
    out_ref, state_ref, wide_ref, begin_ref, spread_ref, sums_ref,
):
    block = pl.program_id(0)
    rows, width = out_ref.shape
    chip = block // CORES
    here = chip == places_ref[0]

    @pl.when(block == 0)
    def _():
        state_ref[...] = jnp.zeros_like(state_ref)

        def compose(row, nothing):
            follow(carries_ref.at[row], rates_ref, state_ref)
            return nothing

        lax.fori_loop(0, places_ref[1], compose, 0)
        for n in range(NS):
            wide_ref[n * SUBLANES : (n + 1) * SUBLANES, :] = jnp.broadcast_to(
                rates_ref[n : n + 1, :], (SUBLANES, width)
            )

    @pl.when((block > 0) & (lax.rem(block, CORES) == 0))
    def _():
        before = jnp.where(chip - 1 == places_ref[0], last_own_ref[...], last_come_ref[0])
        state_ref[...] = state_ref[...] + before

    state = state_ref[...]
    for n in range(NS):
        begin_ref[n * NS : (n + 1) * NS, :] = jnp.broadcast_to(
            state[n : n + 1, :], (NS, width)
        ).astype(jnp.bfloat16)
    maps = jnp.where(here, maps_own_ref[0], maps_come_ref[0])
    maps = jnp.concatenate([maps, jnp.zeros((LANES - 2 * NS, rows), jnp.float32)], axis=0).T
    for n in range(NS):
        spread_ref[:, n * LANES : (n + 1) * LANES] = jnp.broadcast_to(
            maps[:, NS + n : NS + n + 1], (rows, LANES)
        ).astype(jnp.bfloat16)
    sums = jnp.where(here, sums_own_ref[...], sums_come_ref[...]).astype(jnp.float32)
    sums_ref[...] = sums
    state_ref[...] = jnp.exp2(rates_ref[...] * sums[rows - 1 :, :]) * state
    chunk, several = CORES * LANES, 4

    def some(index, nothing):
        near = pl.ds(pl.multiple_of(index * NS, NS), NS)
        for item in range(width // chunk):
            lanes = slice(item * chunk, (item + 1) * chunk)
            part = jnp.where(here, part_own_ref[near, lanes], part_come_ref[near, lanes])
            total = part.astype(jnp.float32)
            sums = sums_ref[near, lanes].reshape(NS // SUBLANES, SUBLANES, chunk)
            for first in range(0, NS, several):
                terms = []
                for n in range(first, first + several):
                    rate = wide_ref[n * SUBLANES : (n + 1) * SUBLANES, lanes]
                    decay = jnp.exp2(sums * rate[None]).reshape(NS, chunk).astype(jnp.bfloat16)
                    out_of = spread_ref[near, n * LANES : (n + 1) * LANES]
                    out_of = jnp.concatenate([out_of] * (chunk // LANES), axis=1)
                    terms.append(decay * begin_ref[n * NS : (n + 1) * NS, lanes] * out_of)
                four = (terms[0] + terms[1]) + (terms[2] + terms[3])
                total = total + four.astype(jnp.float32)
            out_ref[near, lanes] = total.astype(jnp.bfloat16)
        return nothing

    lax.fori_loop(0, rows // NS, some, 0)


def add_carried(places, parts, sums, maps, lasts, rates, carries):
    blocks_come, _, rows = maps[1].shape
    chips = blocks_come // CORES + 1
    width = rates.shape[1]

    def core(b):
        return lax.rem(b, CORES)

    def order(b, s):
        chip = b // CORES
        return jnp.minimum(
            jnp.where(chip < s[0], b, jnp.maximum(b - CORES, 0)), blocks_come - 1
        )

    def before(b, s):
        chip = jnp.maximum(b // CORES - 1, 0)
        return jnp.minimum(jnp.where(chip < s[0], chip, jnp.maximum(chip - 1, 0)), chips - 2)

    def fixed(*shape):
        return pl.BlockSpec(shape, lambda b, s: (0,) * len(shape))

    own = pl.BlockSpec((rows, width), lambda b, s: (core(b), 0))
    come = pl.BlockSpec((rows, width), lambda b, s: (order(b, s), 0))
    return pl.pallas_call(
        carried_kernel,
        grid_spec=pltpu.PrefetchScalarGridSpec(
            num_scalar_prefetch=1,
            grid=(chips * CORES,),
            in_specs=[
                own,
                come,
                own,
                come,
                pl.BlockSpec((1, 2 * NS, rows), lambda b, s: (core(b), 0, 0)),
                pl.BlockSpec((1, 2 * NS, rows), lambda b, s: (order(b, s), 0, 0)),
                fixed(NS, width),
                pl.BlockSpec((1, NS, width), lambda b, s: (before(b, s), 0, 0)),
                fixed(*rates.shape),
                fixed(*carries.shape),
            ],
            out_specs=pl.BlockSpec((rows, width), lambda b, s: (b, 0)),
            scratch_shapes=[
                pltpu.VMEM((NS, width), jnp.float32),
                pltpu.VMEM((NS * SUBLANES, width), jnp.float32),
                pltpu.VMEM((NS * NS, width), jnp.bfloat16),
                pltpu.VMEM((rows, NS * LANES), jnp.bfloat16),
                pltpu.VMEM((rows, width), jnp.float32),
            ],
        ),
        out_shape=jax.ShapeDtypeStruct((chips * CORES * rows, width), jnp.bfloat16),
        compiler_params=params,
        name="add_carried",
    )(places, *parts, *sums, *maps, *lasts, rates, carries)


def local(
    queries, keys, values, doc_lengths, rank_in, bc_weight, rank_out, dt_bias, a_log, skip_gain
):
    devices = lax.axis_size("seq")
    chips = devices // CORES
    targets = lax.axis_size("chan")
    seq_place = lax.axis_index("seq").astype(jnp.int32)
    chan_place = lax.axis_index("chan").astype(jnp.int32)
    chip, core = seq_place // CORES, lax.rem(seq_place, CORES)
    place = jnp.stack([chip, core])
    width = queries.shape[2] // devices
    wide = max(HEAD_SIZE, keys.shape[2] // devices)

    def other(device):
        return device + 1 - 2 * (device % CORES)

    swap = [(device, other(device)) for device in range(devices)]
    near = [(device, device + CORES) for device in range(devices - CORES)]
    far = [(device, other(device + CORES)) for device in range(devices - CORES)]

    def onward(chips_on):
        return [(device, (device + chips_on * CORES) % devices) for device in range(devices)]

    parts = select_heads(keys[0], values[0], chips, wide)
    routes = (near, near, far, far)
    from_near, last_near, from_far, last_far = (
        lax.ppermute(part, "seq", route) for part, route in zip(parts, routes)
    )
    both_queries, both_keys, both_values = (
        (array[0], lax.ppermute(array[0], "seq", swap)) for array in (queries, keys, values)
    )

    first = seq_place * width
    logs = lax.dynamic_slice_in_dim(a_log, first, width, 0)
    rates = (-LOG2E * jnp.exp(logs)).T
    cols = lax.dynamic_slice_in_dim(rank_out, first, width, 1)
    bias = lax.dynamic_slice_in_dim(dt_bias, first, width, 0)[None]
    gain = lax.dynamic_slice_in_dim(skip_gain, first, width, 0)[None]

    asked = (place, doc_lengths, both_queries, both_keys, both_values)
    sent, *earlier = attend(
        *asked, (from_near, from_far), rank_in, bc_weight.T, 1, None, (rates, cols, bias, gain)
    )
    stayed, low, maps = attend(*asked, (last_near, last_far), rank_in, bc_weight.T, 0, earlier, ())
    come = [lax.ppermute(sent[step], "seq", onward(step + 1)) for step in range(chips - 1)]
    low_own = low_and_maps(low, maps, *lax.ppermute((low, maps), "seq", swap))
    low_come = [lax.ppermute(low_own, "seq", onward(step + 1)) for step in range(chips - 1)]
    got_sent = lax.ppermute(sent, "seq", swap)
    got_stayed = lax.ppermute(stayed, "seq", swap)
    attn_rows = join_heads(sent, stayed, got_sent, got_stayed)

    part_own, sums_own, maps_own, state, total = scan_own(stayed, low_own, cols, bias, rates, gain)
    come, low_come = jnp.stack(come), jnp.stack(low_come)
    steps, sums_come, maps_come, carry = step_sizes(
        place, come, low_come, cols, bias, rates, state, total, targets, attn_rows
    )
    carries = lax.all_to_all(carry, "chan", split_axis=0, concat_axis=0, tiled=True)
    part_come, last_come = scan_others(place, come, steps, maps_come, rates, gain)
    ssm_rows = add_carried(
        jnp.stack([chip, chan_place]), (part_own, part_come), (sums_own, sums_come),
        (maps_own, maps_come), (state, last_come), rates, carries,
    )
    return (attn_rows[None], ssm_rows[None])


def solution(mesh):
    return jax.shard_map(
        local,
        mesh=mesh,
        in_specs=(
            P("chan", "seq", None),
            P("chan", "seq", None),
            P("chan", "seq", None),
            P("chan", None),
            P(),
            P(),
            P(),
            P(),
            P(),
            P(),
        ),
        out_specs=(P("chan", "seq", None), P("chan", None, "seq")),
        check_vma=False,
    )
```

```python
import functools
import math

import jax
import jax.numpy as jnp
from jax import lax
from jax.experimental import pallas as pl
from jax.experimental.pallas import tpu as pltpu
from jax.sharding import PartitionSpec as P

QUERY_HEADS = 32
KEY_VALUE_HEADS = 8
HEAD_SIZE = 128
GROUP = QUERY_HEADS // KEY_VALUE_HEADS
NS = 16
RANK = 256
CORES = 2
LANES = 128
SUBLANES = 8
MAPS = 4 * NS
LOG2E = 1.4426950408889634

masked_fill = -1e30
params = pltpu.CompilerParams(vmem_limit_bytes=60 << 20)


def split(value):
    coarse = value.astype(jnp.bfloat16)
    return coarse, (value - coarse.astype(jnp.float32)).astype(jnp.bfloat16)


def run_copies(pairs, sems):
    copies = [
        pltpu.make_async_copy(source, target, sems.at[i]) for i, (source, target) in enumerate(pairs)
    ]
    for copy in copies:
        copy.start()
    for copy in copies:
        copy.wait()


def columns_of(ref, index, size):
    return ref.at[:, pl.ds(pl.multiple_of(index * size, LANES), size)]


def heads_kernel(key_ref, value_ref, *refs):
    near_ref, near_last_ref, far_ref, far_last_ref, sems = refs
    place = lax.axis_index("seq")
    chip, core = place // CORES, lax.rem(place, CORES)
    others, _, _, wide = near_ref.shape
    halves = key_ref.shape[1] // wide // (others + 1)
    pairs = []
    for target, last, which in ((near_ref, near_last_ref, core), (far_ref, far_last_ref, 1 - core)):
        for step in range(others + 1):
            owner = lax.rem(chip + 2 + step, others + 1)
            index = owner * halves + (which if halves == CORES else 0)
            place_in = target.at[step] if step < others else last.at[0]
            for kind, source in enumerate((key_ref, value_ref)):
                pairs.append((columns_of(source, index, wide), place_in.at[kind]))
    run_copies(pairs, sems)


def select_heads(keys, values, chips, wide):
    part = jax.ShapeDtypeStruct((chips - 1, 2, keys.shape[0], wide), keys.dtype)
    last = jax.ShapeDtypeStruct((1, 2, keys.shape[0], wide), keys.dtype)
    return pl.pallas_call(
        heads_kernel,
        in_specs=[pl.BlockSpec(memory_space=pl.ANY)] * 2,
        out_shape=[part, last, part, last],
        scratch_shapes=[pltpu.SemaphoreType.DMA((4 * chips,))],
        compiler_params=params,
        name="select_heads",
    )(keys, values)


def join_kernel(sent_ref, stayed_ref, got_sent_ref, got_stayed_ref, out_ref, sems):
    place = lax.axis_index("seq")
    core, chip = lax.rem(place, CORES), place // CORES
    rows = out_ref.shape[0]
    others, _, width = sent_ref.shape
    here = pl.ds(pl.multiple_of(core * rows, rows), rows)
    pairs = []
    for first, rest, which in (
        (stayed_ref, sent_ref, core), (got_stayed_ref, got_sent_ref, 1 - core)
    ):
        for step in range(others + 1):
            source = first.at[0, here, :] if step == 0 else rest.at[step - 1, here, :]
            owner = lax.rem(chip + step, others + 1)
            pairs.append((source, columns_of(out_ref, owner * CORES + which, width)))
    run_copies(pairs, sems)


def join_heads(sent, stayed, got_sent, got_stayed):
    others, rows, width = sent.shape
    return pl.pallas_call(
        join_kernel,
        in_specs=[pl.BlockSpec(memory_space=pl.ANY)] * 4,
        out_shape=jax.ShapeDtypeStruct(
            (rows // CORES, (others + 1) * CORES * width), sent.dtype
        ),
        scratch_shapes=[pltpu.SemaphoreType.DMA((CORES * (others + 1),))],
        compiler_params=params,
        name="join_heads",
    )(sent, stayed, got_sent, got_stayed)


def attend_kernel(
    place_ref, doc_ref, mine_ref, theirs_ref, own_key_ref, own_value_ref, swap_key_ref,
    swap_value_ref, near_ref, far_ref, rank_ref, map_ref, *rest, after,
):
    earlier = rest[0] if len(rest) > 3 + after else None
    out_ref, part_ref, mask_ref = rest[-3:]
    step = pl.program_id(0)
    rows = mine_ref.shape[0]
    group = mine_ref.shape[1] // HEAD_SIZE
    chip, core = place_ref[0], place_ref[1]
    first_core = core == 0

    def above(shape):
        row = lax.rem(lax.broadcasted_iota(jnp.int32, shape, 0), rows)
        return lax.broadcasted_iota(jnp.int32, shape, 1) > row

    @pl.when(step == 0)
    def _():
        part_ref[...] = jnp.zeros_like(part_ref) if earlier is None else earlier[...]
        own = chip * CORES + core
        swapped = chip * CORES + 1 - core
        near, far = own - CORES, swapped - CORES
        lane = lax.broadcasted_iota(jnp.int32, (rows, rows), 1)
        row = lax.broadcasted_iota(jnp.int32, (rows, rows), 0)
        for item, (place, before, middle) in enumerate(
            (
                (own, near, jnp.where(first_core, far, swapped)),
                (swapped, far, jnp.where(first_core, own, near)),
            )
        ):
            query_pos = place * rows + row
            start = jnp.zeros((rows, rows), jnp.int32)
            bound = jnp.int32(0)
            for doc in range(doc_ref.shape[1]):
                bound = bound + doc_ref[0, doc]
                start = jnp.where(query_pos >= bound, bound, start)
            ends = jnp.where(lane > row, before, place) * rows + lane
            mask_ref[item, :, :rows] = jnp.where(
                (ends >= start) & (ends <= query_pos), 0.0, masked_fill
            )
            mask_ref[item, :, rows:] = jnp.where(
                middle * rows + lane >= start, 0.0, masked_fill
            )

    scale = LOG2E / math.sqrt(HEAD_SIZE)
    ones = jnp.ones((3 * rows, HEAD_SIZE), jnp.bfloat16)

    def windows(kind):
        own = (own_key_ref, own_value_ref)[kind][...]
        swapped = (swap_key_ref, swap_value_ref)[kind][...]
        near, far = near_ref[0, kind], far_ref[0, kind]
        return (
            jnp.concatenate([near, own, jnp.where(first_core, far, swapped)], axis=0),
            jnp.concatenate([far, swapped, jnp.where(first_core, own, near)], axis=0),
        )

    scores = []
    for keys, query in zip(windows(0), (mine_ref[...], theirs_ref[...])):
        stacked = jnp.concatenate(
            [query[:, i * HEAD_SIZE : (i + 1) * HEAD_SIZE] for i in range(group)], axis=0
        )
        scores.append(
            lax.dot_general(
                stacked, keys, (((1,), (1,)), ((), ())), preferred_element_type=jnp.float32
            )
        )
    outputs = []
    before = above((group * rows, rows))
    for item, (values, score) in enumerate(zip(windows(1), scores)):
        fill = mask_ref[item]
        ends = jnp.where(before, score[:, :rows], score[:, rows : 2 * rows])
        kept = jnp.concatenate([ends, score[:, 2 * rows :]], axis=1)
        kept = jnp.concatenate(
            [kept[i * rows : (i + 1) * rows, :] + fill for i in range(group)], axis=0
        )
        peak = jnp.max(kept, axis=1, keepdims=True)
        raw = jnp.exp2((kept - peak) * scale).astype(jnp.bfloat16)
        ends = raw[:, :rows]
        none = jnp.zeros_like(ends)
        spread = jnp.concatenate(
            [jnp.where(before, ends, none), jnp.where(before, none, ends), raw[:, rows:]], axis=1
        )
        both = jnp.dot(
            spread, jnp.concatenate([values, ones], axis=1), preferred_element_type=jnp.float32
        )
        mixed = both[:, :HEAD_SIZE] * pl.reciprocal(both[:, HEAD_SIZE:])
        mixed = mixed.astype(jnp.bfloat16)
        outputs.append(
            jnp.concatenate([mixed[i * rows : (i + 1) * rows, :] for i in range(group)], axis=1)
        )
    stream = jnp.concatenate(
        [
            jnp.where(first_core, outputs[0], outputs[1]),
            jnp.where(first_core, outputs[1], outputs[0]),
        ],
        axis=0,
    )
    out_ref[0] = stream
    both = CORES * rows
    part_ref[:both, :] += jnp.dot(stream, rank_ref[...], preferred_element_type=jnp.float32)
    part_ref[both:, :] += lax.dot_general(
        map_ref[...], stream, (((1,), (1,)), ((), ())), preferred_element_type=jnp.float32
    )


def attend(place, doc_lengths, queries, keys, values, blocks, rank_in, map_rows, first, earlier, after):
    mine, theirs = queries
    count, _, rows, columns = blocks[0].shape
    heads = columns // HEAD_SIZE
    chips = lax.axis_size("seq") // CORES
    width = mine.shape[1] // (chips * CORES)
    wide = width // heads
    halves = keys[0].shape[1] // columns // chips

    def owner(j, s):
        return lax.rem(s[0] + first + j // heads, chips)

    def column(j, s):
        return (owner(j, s) * CORES + s[1]) * heads + lax.rem(j, heads)

    def key_column(j, s):
        return column(j, s) if halves == CORES else owner(j, s) * heads + lax.rem(j, heads)

    query = pl.BlockSpec((rows, wide), lambda j, s: (0, column(j, s)))
    here = pl.BlockSpec((rows, HEAD_SIZE), lambda j, s: (0, key_column(j, s)))
    block = pl.BlockSpec(
        (1, 2, rows, HEAD_SIZE), lambda j, s: (j // heads, 0, 0, lax.rem(j, heads))
    )
    part_shape = (CORES * rows + 2 * NS, RANK)
    part = pl.BlockSpec(part_shape, lambda j, s: (0, 0))
    return pl.pallas_call(
        functools.partial(attend_kernel, after=len(after)),
        grid_spec=pltpu.PrefetchScalarGridSpec(
            num_scalar_prefetch=1,
            grid=(count * heads,),
            in_specs=[pl.BlockSpec(memory_space=pltpu.SMEM), query, query]
            + [here] * 4
            + [block] * 2
            + [
                pl.BlockSpec((wide, RANK), lambda j, s: (column(j, s), 0)),
                pl.BlockSpec((2 * NS, wide), lambda j, s: (0, column(j, s))),
            ]
            + [part] * len(earlier)
            + [pl.BlockSpec(memory_space=pl.ANY)] * len(after),
            out_specs=[
                pl.BlockSpec(
                    (1, CORES * rows, wide), lambda j, s: (j // heads, 0, lax.rem(j, heads))
                ),
                part,
            ],
            scratch_shapes=[pltpu.VMEM((2, rows, 2 * rows), jnp.float32)],
        ),
        out_shape=[
            jax.ShapeDtypeStruct((count, CORES * rows, width), jnp.bfloat16),
            jax.ShapeDtypeStruct(part_shape, jnp.float32),
        ],
        compiler_params=params,
        cost_estimate=pl.CostEstimate(flops=1, bytes_accessed=1, transcendentals=0),
        name="attend",
    )(
        place, doc_lengths, mine, theirs, keys[0], values[0], keys[1], values[1], *blocks,
        rank_in, map_rows, *earlier, *after,
    )


def low_kernel(mine_ref, theirs_ref, out_ref):
    rows = mine_ref.shape[0] - 2 * NS
    total = mine_ref[...] + theirs_ref[...]
    out_ref[:rows, :] = total[:rows, :].astype(jnp.bfloat16)
    out_ref[rows:, :] = jnp.concatenate(split(total[rows:, :]), axis=0)


def low_and_maps(mine, theirs):
    return pl.pallas_call(
        low_kernel,
        out_shape=jax.ShapeDtypeStruct((mine.shape[0] + 2 * NS, RANK), jnp.bfloat16),
        compiler_params=params,
        cost_estimate=pl.CostEstimate(flops=1, bytes_accessed=1, transcendentals=0),
        name="low_and_maps",
    )(mine, theirs)


def softplus(value):
    small = jnp.exp(-jnp.abs(value))
    tail = jnp.where(small < 0.00390625, small * (1.0 - 0.5 * small), jnp.log(1.0 + small))
    return jnp.maximum(value, 0.0) + tail


def add_states(rates_ref, state_ref, total_ref, states, totals):
    state_ref[...] = jnp.exp2(rates_ref[...] * totals) * state_ref[...] + states
    total_ref[...] = total_ref[...] + totals


def sums_within(steps):
    rows = steps.shape[0]
    at = lax.broadcasted_iota(jnp.int32, (rows, rows), 0)
    of = lax.broadcasted_iota(jnp.int32, (rows, rows), 1)
    upto = jnp.where(of <= at, 1.0, 0.0).astype(jnp.bfloat16)
    return jnp.dot(upto, steps, preferred_element_type=jnp.float32)


def step_kernel(
    place_ref, stream_ref, low_ref, map_ref, cols_ref, bias_ref, rates_ref, *rest
):
    own_state_ref, own_total_ref = rest[:2]
    steps_ref, sums_ref, maps_ref, carry_ref, state_ref, total_ref, wide_ref, turn_ref = rest[3:]
    block = pl.program_id(0)
    rows, width = stream_ref.shape[1:]

    @pl.when(block == 0)
    def _():
        state_ref[...] = jnp.zeros_like(state_ref)
        total_ref[...] = jnp.zeros_like(total_ref)
        for n in range(NS):
            wide_ref[n * SUBLANES : (n + 1) * SUBLANES, :] = jnp.broadcast_to(
                rates_ref[n : n + 1, :], (SUBLANES, width)
            )

    @pl.when(block == place_ref[0] * CORES)
    def _():
        add_states(rates_ref, state_ref, total_ref, own_state_ref[...], own_total_ref[...])

    maps = map_ref[0].astype(jnp.float32)
    maps = maps[: 2 * NS, :] + maps[2 * NS :, :]
    maps_ref[0] = maps
    logits = jnp.dot(low_ref[0], cols_ref[...], preferred_element_type=jnp.float32)
    steps = softplus(logits + bias_ref[...]).astype(jnp.bfloat16)
    steps_ref[...] = steps
    push = steps * stream_ref[0]
    within = sums_within(steps)
    sums_ref[...] = within.astype(jnp.bfloat16)
    whole = within[rows - 1 :, :]
    left = whole - within
    some, chunk, several = rows // 2, CORES * LANES, 4
    state_row = lax.broadcasted_iota(jnp.int32, (NS, some), 0)
    for first in range(0, rows, some):
        span = slice(first, first + some)
        chosen = [
            jnp.concatenate(
                [
                    jnp.where(state_row == m, maps[:NS, span], 0.0).astype(jnp.bfloat16)
                    for m in range(n, n + several)
                ],
                axis=1,
            )
            for n in range(0, NS, several)
        ]
        for item in range(width // chunk):
            lanes = slice(item * chunk, (item + 1) * chunk)
            left_here = left[span, lanes].reshape(some // SUBLANES, SUBLANES, chunk)
            push_here = push[span, lanes]
            added = state_ref[:, lanes]
            if first == 0:
                added = jnp.exp2(rates_ref[:, lanes] * whole[:, lanes]) * added
            for n in range(0, NS, several):
                pushed = []
                for m in range(n, n + several):
                    rate = wide_ref[m * SUBLANES : (m + 1) * SUBLANES, lanes]
                    decay = jnp.exp2(left_here * rate[None]).reshape(some, chunk)
                    pushed.append(decay.astype(jnp.bfloat16) * push_here)
                added = added + jnp.dot(
                    chosen[n // several],
                    jnp.concatenate(pushed, axis=0),
                    preferred_element_type=jnp.float32,
                )
            state_ref[:, lanes] = added
    total_ref[...] = total_ref[...] + whole

    count = pl.num_programs(0)

    @pl.when(block == count - 1)
    def _():
        @pl.when(place_ref[0] * CORES == count)
        def _():
            add_states(rates_ref, state_ref, total_ref, own_state_ref[...], own_total_ref[...])

        write_carry(carry_ref.at[0], state_ref[...], total_ref[...], turn_ref)
        for target in range(1, carry_ref.shape[0]):
            carry_ref[target] = carry_ref[0]


def step_sizes(place, stream, lows, cols, bias, rates, state, total, targets, after):
    others = stream.shape[0]
    chips = others + 1
    rows, width = stream.shape[1] // CORES, stream.shape[2]
    map_row = CORES * rows // MAPS
    blocks = others * CORES
    carry = (targets, (width // LANES + 1) * NS, LANES)

    def slot(b, s):
        chip = b // CORES
        return lax.rem(s[0] - jnp.where(chip < s[0], chip, chip + 1) + chips, chips) - 1

    def core(b):
        return lax.rem(b, CORES)

    def fixed(*shape):
        return pl.BlockSpec(shape, lambda b, s: (0,) * len(shape))

    return pl.pallas_call(
        step_kernel,
        grid_spec=pltpu.PrefetchScalarGridSpec(
            num_scalar_prefetch=1,
            grid=(blocks,),
            in_specs=[
                pl.BlockSpec((1, rows, width), lambda b, s: (slot(b, s), core(b), 0)),
                pl.BlockSpec((1, rows, RANK), lambda b, s: (slot(b, s), core(b), 0)),
                pl.BlockSpec((1, MAPS, rows), lambda b, s: (slot(b, s), map_row, core(b))),
                fixed(*cols.shape),
                fixed(*bias.shape),
                fixed(*rates.shape),
                fixed(*state.shape),
                fixed(*total.shape),
                pl.BlockSpec(memory_space=pl.ANY),
            ],
            out_specs=[
                pl.BlockSpec((rows, width), lambda b, s: (b, 0)),
                pl.BlockSpec((rows, width), lambda b, s: (b, 0)),
                pl.BlockSpec((1, 2 * NS, rows), lambda b, s: (b, 0, 0)),
                fixed(*carry),
            ],
            scratch_shapes=[
                pltpu.VMEM((NS, width), jnp.float32),
                pltpu.VMEM((1, width), jnp.float32),
                pltpu.VMEM((NS * SUBLANES, width), jnp.float32),
                pltpu.VMEM((SUBLANES, LANES), jnp.float32),
            ],
        ),
        out_shape=[
            jax.ShapeDtypeStruct((blocks * rows, width), jnp.bfloat16),
            jax.ShapeDtypeStruct((blocks * rows, width), jnp.bfloat16),
            jax.ShapeDtypeStruct((blocks, 2 * NS, rows), jnp.float32),
            jax.ShapeDtypeStruct(carry, jnp.bfloat16),
        ],
        compiler_params=params,
        name="step_sizes",
    )(place, stream, lows, lows, cols, bias, rates, state, total, after)


def write_carry(out_ref, state, total, turn_ref):
    tile = state.shape[1] // LANES
    turn_ref[...] = jnp.zeros_like(turn_ref)
    for item in range(tile):
        lanes = slice(item * LANES, (item + 1) * LANES)
        turn_ref[item : item + 1, :] = total[:, lanes]
        out_ref[item * NS : (item + 1) * NS, :] = state[:, lanes].astype(jnp.bfloat16)
    out_ref[tile * NS :, :] = jnp.concatenate(split(turn_ref[...]), axis=0)


def follow(carry_ref, rates_ref, state_ref):
    tile = state_ref.shape[1] // LANES
    sums = carry_ref[tile * NS :, :].astype(jnp.float32)
    sums = sums[:SUBLANES, :] + sums[SUBLANES:, :]
    for item in range(tile):
        lanes = slice(item * LANES, (item + 1) * LANES)
        decay = jnp.exp2(rates_ref[:, lanes] * sums[item : item + 1, :])
        added = carry_ref[item * NS : (item + 1) * NS, :].astype(jnp.float32)
        state_ref[:, lanes] = decay * state_ref[:, lanes] + added
    return sums


def scan_blocks(stream_ref, steps_ref, maps, rates_ref, gain_ref, out_ref, state_ref, work_refs):
    out_of_ref, *hist_refs = work_refs
    rows, width = steps_ref.shape
    source = lax.broadcasted_iota(jnp.int32, (LANES, NS * NS), 0)
    column = lax.rem(lax.broadcasted_iota(jnp.int32, (LANES, NS * NS), 1), NS)
    token = lax.rem(lax.broadcasted_iota(jnp.int32, (rows, NS * NS), 0), NS)
    slot = lax.broadcasted_iota(jnp.int32, (rows, NS * NS), 1) // NS
    turned = jnp.concatenate(
        [maps, jnp.zeros((LANES - 2 * NS, rows), jnp.float32)], axis=0
    ).T.astype(jnp.bfloat16)
    pick = jnp.where(source == NS + column, 1.0, 0.0).astype(jnp.bfloat16)
    spread = jnp.dot(turned, pick, preferred_element_type=jnp.float32)
    out_of_ref[...] = jnp.where(token == slot, spread, 0.0).astype(jnp.bfloat16)
    map_in = maps[:NS, :]
    half = width // 2

    def finish(first, hist_ref):
        here = pl.ds(first, NS)
        mixed = jnp.dot(out_of_ref[here, :], hist_ref[...], preferred_element_type=jnp.float32)
        direct = gain_ref[...] * stream_ref[0, here, :].astype(jnp.float32)
        out_ref[here, :] = (mixed + direct).astype(jnp.bfloat16)

    def advance(first, hist_ref):
        here = pl.ds(first, NS)
        into = pltpu.roll(map_in, lax.rem(rows - first, rows), 1)
        for lanes in (slice(0, half), slice(half, width)):
            state = state_ref[:, lanes]
            rates = rates_ref[:, lanes]
            steps = steps_ref[here, lanes].astype(jnp.float32)
            push = steps * stream_ref[0, here, lanes].astype(jnp.float32)
            for near in range(NS):
                this = slice(near, near + 1)
                state = jnp.exp2(rates * steps[this, :]) * state + into[:, this] * push[this, :]
                hist_ref[near * NS : (near + 1) * NS, lanes] = state.astype(jnp.bfloat16)
            state_ref[:, lanes] = state

    def pair(index, nothing):
        first = pl.multiple_of(index * 2 * NS, 2 * NS)
        advance(first, hist_refs[0])
        finish(first, hist_refs[0])
        second = pl.multiple_of(first + NS, NS)
        advance(second, hist_refs[1])
        finish(second, hist_refs[1])
        return nothing

    lax.fori_loop(0, rows // (2 * NS), pair, 0)


def work_shapes(rows, width):
    return [
        pltpu.VMEM((rows, NS * NS), jnp.bfloat16),
        pltpu.VMEM((NS * NS, width), jnp.bfloat16),
        pltpu.VMEM((NS * NS, width), jnp.bfloat16),
    ]


def own_kernel(
    stream_ref, low_ref, map_ref, cols_ref, bias_ref, rates_ref, gain_ref,
    out_ref, sums_ref, maps_ref, state_ref, total_ref, steps_ref, *work_refs
):
    rows = steps_ref.shape[0]

    @pl.when(pl.program_id(0) == 0)
    def _():
        state_ref[...] = jnp.zeros_like(state_ref)
        total_ref[...] = jnp.zeros_like(total_ref)

    maps = map_ref[...].astype(jnp.float32)
    maps = maps[: 2 * NS, :] + maps[2 * NS :, :]
    maps_ref[0] = maps
    logits = jnp.dot(low_ref[...], cols_ref[...], preferred_element_type=jnp.float32)
    steps = softplus(logits + bias_ref[...]).astype(jnp.bfloat16)
    steps_ref[...] = steps
    within = sums_within(steps)
    sums_ref[...] = within.astype(jnp.bfloat16)
    total_ref[...] = total_ref[...] + within[rows - 1 :, :]
    scan_blocks(stream_ref, steps_ref, maps, rates_ref, gain_ref, out_ref, state_ref, work_refs)


def scan_own(stream, lows, cols, bias, rates, gain):
    rows, width = stream.shape[1] // CORES, stream.shape[2]
    map_row = CORES * rows // MAPS

    def fixed(*shape):
        return pl.BlockSpec(shape, lambda b: (0,) * len(shape))

    block = pl.BlockSpec((rows, width), lambda b: (b, 0))
    return pl.pallas_call(
        own_kernel,
        grid=(CORES,),
        in_specs=[
            pl.BlockSpec((1, rows, width), lambda b: (0, b, 0)),
            pl.BlockSpec((rows, RANK), lambda b: (b, 0)),
            pl.BlockSpec((MAPS, rows), lambda b: (map_row, b)),
            fixed(*cols.shape),
            fixed(*bias.shape),
            fixed(*rates.shape),
            fixed(*gain.shape),
        ],
        out_specs=[
            block,
            block,
            pl.BlockSpec((1, 2 * NS, rows), lambda b: (b, 0, 0)),
            fixed(NS, width),
            fixed(1, width),
        ],
        out_shape=[
            jax.ShapeDtypeStruct((CORES * rows, width), jnp.bfloat16),
            jax.ShapeDtypeStruct((CORES * rows, width), jnp.bfloat16),
            jax.ShapeDtypeStruct((CORES, 2 * NS, rows), jnp.float32),
            jax.ShapeDtypeStruct((NS, width), jnp.float32),
            jax.ShapeDtypeStruct((1, width), jnp.float32),
        ],
        scratch_shapes=[pltpu.VMEM((rows, width), jnp.bfloat16)] + work_shapes(rows, width),
        compiler_params=params,
        cost_estimate=pl.CostEstimate(flops=4 * 10**9, bytes_accessed=1 << 21, transcendentals=0),
        name="scan_own",
    )(stream, lows, lows, cols, bias, rates, gain)


def others_kernel(
    place_ref, stream_ref, steps_ref, maps_ref, rates_ref, gain_ref, out_ref, last_ref, *work_refs
):
    @pl.when(lax.rem(pl.program_id(0), CORES) == 0)
    def _():
        last_ref[...] = jnp.zeros_like(last_ref)

    scan_blocks(
        stream_ref, steps_ref, maps_ref[0], rates_ref, gain_ref, out_ref, last_ref.at[0], work_refs
    )


def scan_others(place, stream, steps, maps, rates, gain):
    others = stream.shape[0]
    chips = others + 1
    rows, width = stream.shape[1] // CORES, stream.shape[2]

    def slot(b, s):
        chip = b // CORES
        return lax.rem(s[0] - jnp.where(chip < s[0], chip, chip + 1) + chips, chips) - 1

    def fixed(*shape):
        return pl.BlockSpec(shape, lambda b, s: (0,) * len(shape))

    block = pl.BlockSpec((rows, width), lambda b, s: (b, 0))
    return pl.pallas_call(
        others_kernel,
        grid_spec=pltpu.PrefetchScalarGridSpec(
            num_scalar_prefetch=1,
            grid=(others * CORES,),
            in_specs=[
                pl.BlockSpec((1, rows, width), lambda b, s: (slot(b, s), lax.rem(b, CORES), 0)),
                block,
                pl.BlockSpec((1, 2 * NS, rows), lambda b, s: (b, 0, 0)),
                fixed(*rates.shape),
                fixed(*gain.shape),
            ],
            out_specs=[block, pl.BlockSpec((1, NS, width), lambda b, s: (b // CORES, 0, 0))],
            scratch_shapes=work_shapes(rows, width),
        ),
        out_shape=[
            jax.ShapeDtypeStruct((others * CORES * rows, width), jnp.bfloat16),
            jax.ShapeDtypeStruct((others, NS, width), jnp.float32),
        ],
        compiler_params=params,
        cost_estimate=pl.CostEstimate(flops=4 * 10**9, bytes_accessed=1 << 21, transcendentals=0),
        name="scan_others",
    )(place, stream, steps, maps, rates, gain)


def carried_kernel(
    places_ref, part_own_ref, part_come_ref, sums_own_ref, sums_come_ref,
    maps_own_ref, maps_come_ref, last_own_ref, last_come_ref, rates_ref, carries_ref,
    out_ref, state_ref, wide_ref, begin_ref, spread_ref, sums_ref,
):
    block = pl.program_id(0)
    rows, width = out_ref.shape
    chip = block // CORES
    here = chip == places_ref[0]

    @pl.when(block == 0)
    def _():
        state_ref[...] = jnp.zeros_like(state_ref)

        def compose(row, nothing):
            follow(carries_ref.at[row], rates_ref, state_ref)
            return nothing

        lax.fori_loop(0, places_ref[1], compose, 0)
        for n in range(NS):
            wide_ref[n * SUBLANES : (n + 1) * SUBLANES, :] = jnp.broadcast_to(
                rates_ref[n : n + 1, :] * (-1.0 / LOG2E), (SUBLANES, width)
            )

    @pl.when((block > 0) & (lax.rem(block, CORES) == 0))
    def _():
        before = jnp.where(chip - 1 == places_ref[0], last_own_ref[...], last_come_ref[0])
        state_ref[...] = state_ref[...] + before

    state = state_ref[...]
    for n in range(NS):
        begin_ref[n * NS : (n + 1) * NS, :] = jnp.broadcast_to(
            state[n : n + 1, :], (NS, width)
        ).astype(jnp.bfloat16)
    maps = jnp.where(here, maps_own_ref[0], maps_come_ref[0])
    maps = jnp.concatenate([maps, jnp.zeros((LANES - 2 * NS, rows), jnp.float32)], axis=0).T
    for n in range(NS):
        spread_ref[:, n * LANES : (n + 1) * LANES] = jnp.broadcast_to(
            maps[:, NS + n : NS + n + 1], (rows, LANES)
        ).astype(jnp.bfloat16)
    sums = jnp.where(here, sums_own_ref[...], sums_come_ref[...]).astype(jnp.float32)
    sums_ref[...] = sums
    state_ref[...] = jnp.exp2(rates_ref[...] * sums[rows - 1 :, :]) * state
    chunk, several = CORES * LANES, 4

    def some(index, nothing):
        near = pl.ds(pl.multiple_of(index * NS, NS), NS)
        for item in range(width // chunk):
            lanes = slice(item * chunk, (item + 1) * chunk)
            part = jnp.where(here, part_own_ref[near, lanes], part_come_ref[near, lanes])
            total = part.astype(jnp.float32)
            sums = sums_ref[near, lanes].reshape(NS // SUBLANES, SUBLANES, chunk)
            for first in range(0, NS, several):
                terms = []
                for n in range(first, first + several):
                    rate = wide_ref[n * SUBLANES : (n + 1) * SUBLANES, lanes]
                    decay = pl.reciprocal(lax.logistic(sums * rate[None]), approx=True) - 1.0
                    decay = decay.reshape(NS, chunk).astype(jnp.bfloat16)
                    out_of = spread_ref[near, n * LANES : (n + 1) * LANES]
                    out_of = jnp.concatenate([out_of] * (chunk // LANES), axis=1)
                    terms.append(decay * begin_ref[n * NS : (n + 1) * NS, lanes] * out_of)
                four = (terms[0] + terms[1]) + (terms[2] + terms[3])
                total = total + four.astype(jnp.float32)
            out_ref[near, lanes] = total.astype(jnp.bfloat16)
        return nothing

    lax.fori_loop(0, rows // NS, some, 0)


def add_carried(places, parts, sums, maps, lasts, rates, carries):
    blocks_come, _, rows = maps[1].shape
    chips = blocks_come // CORES + 1
    width = rates.shape[1]

    def core(b):
        return lax.rem(b, CORES)

    def order(b, s):
        chip = b // CORES
        return jnp.minimum(
            jnp.where(chip < s[0], b, jnp.maximum(b - CORES, 0)), blocks_come - 1
        )

    def before(b, s):
        chip = jnp.maximum(b // CORES - 1, 0)
        return jnp.minimum(jnp.where(chip < s[0], chip, jnp.maximum(chip - 1, 0)), chips - 2)

    def fixed(*shape):
        return pl.BlockSpec(shape, lambda b, s: (0,) * len(shape))

    own = pl.BlockSpec((rows, width), lambda b, s: (core(b), 0))
    come = pl.BlockSpec((rows, width), lambda b, s: (order(b, s), 0))
    return pl.pallas_call(
        carried_kernel,
        grid_spec=pltpu.PrefetchScalarGridSpec(
            num_scalar_prefetch=1,
            grid=(chips * CORES,),
            in_specs=[
                own,
                come,
                own,
                come,
                pl.BlockSpec((1, 2 * NS, rows), lambda b, s: (core(b), 0, 0)),
                pl.BlockSpec((1, 2 * NS, rows), lambda b, s: (order(b, s), 0, 0)),
                fixed(NS, width),
                pl.BlockSpec((1, NS, width), lambda b, s: (before(b, s), 0, 0)),
                fixed(*rates.shape),
                fixed(*carries.shape),
            ],
            out_specs=pl.BlockSpec((rows, width), lambda b, s: (b, 0)),
            scratch_shapes=[
                pltpu.VMEM((NS, width), jnp.float32),
                pltpu.VMEM((NS * SUBLANES, width), jnp.float32),
                pltpu.VMEM((NS * NS, width), jnp.bfloat16),
                pltpu.VMEM((rows, NS * LANES), jnp.bfloat16),
                pltpu.VMEM((rows, width), jnp.float32),
            ],
        ),
        out_shape=jax.ShapeDtypeStruct((chips * CORES * rows, width), jnp.bfloat16),
        compiler_params=params,
        name="add_carried",
    )(places, *parts, *sums, *maps, *lasts, rates, carries)


def local(
    queries, keys, values, doc_lengths, rank_in, bc_weight, rank_out, dt_bias, a_log, skip_gain
):
    devices = lax.axis_size("seq")
    chips = devices // CORES
    targets = lax.axis_size("chan")
    seq_place = lax.axis_index("seq").astype(jnp.int32)
    chan_place = lax.axis_index("chan").astype(jnp.int32)
    chip, core = seq_place // CORES, lax.rem(seq_place, CORES)
    place = jnp.stack([chip, core])
    width = queries.shape[2] // devices
    wide = max(HEAD_SIZE, keys.shape[2] // devices)

    def other(device):
        return device + 1 - 2 * (device % CORES)

    swap = [(device, other(device)) for device in range(devices)]
    near = [(device, device + CORES) for device in range(devices - CORES)]
    far = [(device, other(device + CORES)) for device in range(devices - CORES)]

    def onward(chips_on):
        return [(device, (device + chips_on * CORES) % devices) for device in range(devices)]

    parts = select_heads(keys[0], values[0], chips, wide)
    routes = (near, near, far, far)
    from_near, last_near, from_far, last_far = (
        lax.ppermute(part, "seq", route) for part, route in zip(parts, routes)
    )
    both_queries, both_keys, both_values = (
        (array[0], lax.ppermute(array[0], "seq", swap)) for array in (queries, keys, values)
    )

    first = seq_place * width
    logs = lax.dynamic_slice_in_dim(a_log, first, width, 0)
    rates = (-LOG2E * jnp.exp(logs)).T
    cols = lax.dynamic_slice_in_dim(rank_out, first, width, 1)
    bias = lax.dynamic_slice_in_dim(dt_bias, first, width, 0)[None]
    gain = lax.dynamic_slice_in_dim(skip_gain, first, width, 0)[None]

    asked = (place, doc_lengths, both_queries, both_keys, both_values)
    sent, *earlier = attend(
        *asked, (from_near, from_far), rank_in, bc_weight.T, 1, (), (rates, cols, bias, gain)
    )
    stayed, part = attend(*asked, (last_near, last_far), rank_in, bc_weight.T, 0, earlier, ())
    come = [lax.ppermute(sent[step], "seq", onward(step + 1)) for step in range(chips - 1)]
    low_own = low_and_maps(part, lax.ppermute(part, "seq", swap))
    low_come = [lax.ppermute(low_own, "seq", onward(step + 1)) for step in range(chips - 1)]
    got_sent = lax.ppermute(sent, "seq", swap)
    got_stayed = lax.ppermute(stayed, "seq", swap)
    attn_rows = join_heads(sent, stayed, got_sent, got_stayed)

    part_own, sums_own, maps_own, state, total = scan_own(stayed, low_own, cols, bias, rates, gain)
    come, low_come = jnp.stack(come), jnp.stack(low_come)
    steps, sums_come, maps_come, carry = step_sizes(
        place, come, low_come, cols, bias, rates, state, total, targets, attn_rows
    )
    carries = lax.all_to_all(carry, "chan", split_axis=0, concat_axis=0, tiled=True)
    part_come, last_come = scan_others(place, come, steps, maps_come, rates, gain)
    ssm_rows = add_carried(
        jnp.stack([chip, chan_place]), (part_own, part_come), (sums_own, sums_come),
        (maps_own, maps_come), (state, last_come), rates, carries,
    )
    return (attn_rows[None], ssm_rows[None])


def solution(mesh):
    return jax.shard_map(
        local,
        mesh=mesh,
        in_specs=(
            P("chan", "seq", None),
            P("chan", "seq", None),
            P("chan", "seq", None),
            P("chan", None),
            P(),
            P(),
            P(),
            P(),
            P(),
            P(),
        ),
        out_specs=(P("chan", "seq", None), P("chan", None, "seq")),
        check_vma=False,
    )
```

```python
import functools
import math

import jax
import jax.numpy as jnp
from jax import lax
from jax.experimental import pallas as pl
from jax.experimental.pallas import tpu as pltpu
from jax.sharding import PartitionSpec as P

QUERY_HEADS = 32
KEY_VALUE_HEADS = 8
HEAD_SIZE = 128
GROUP = QUERY_HEADS // KEY_VALUE_HEADS
NS = 16
RANK = 256
CORES = 2
LANES = 128
SUBLANES = 8
MAPS = 4 * NS
LOG2E = 1.4426950408889634

masked_fill = -1e30
scale = LOG2E / math.sqrt(HEAD_SIZE)
params = pltpu.CompilerParams(vmem_limit_bytes=60 << 20)


def split(value):
    coarse = value.astype(jnp.bfloat16)
    return coarse, (value - coarse.astype(jnp.float32)).astype(jnp.bfloat16)


def run_copies(pairs, sems):
    copies = [
        pltpu.make_async_copy(source, target, sems.at[i]) for i, (source, target) in enumerate(pairs)
    ]
    for copy in copies:
        copy.start()
    for copy in copies:
        copy.wait()


def columns_of(ref, index, size):
    return ref.at[:, pl.ds(pl.multiple_of(index * size, LANES), size)]


def heads_kernel(key_ref, value_ref, own_ref, their_ref, sems):
    core = lax.rem(lax.axis_index("seq"), CORES)
    wide = own_ref.shape[3]
    halves = key_ref.shape[1] // wide // own_ref.shape[0]
    pairs = []
    for target, which in ((own_ref, core), (their_ref, 1 - core)):
        for chip in range(own_ref.shape[0]):
            index = chip * halves + (which if halves == CORES else 0)
            for kind, source in enumerate((key_ref, value_ref)):
                pairs.append((columns_of(source, index, wide), target.at[chip, kind]))
    run_copies(pairs, sems)


def select_heads(keys, values, chips, wide):
    shape = jax.ShapeDtypeStruct((chips, 2, keys.shape[0], wide), keys.dtype)
    return pl.pallas_call(
        heads_kernel,
        in_specs=[pl.BlockSpec(memory_space=pl.ANY)] * 2,
        out_shape=[shape, shape],
        scratch_shapes=[pltpu.SemaphoreType.DMA((4 * chips,))],
        compiler_params=params,
        name="select_heads",
    )(keys, values)


def join_kernel(sent_ref, stayed_ref, got_sent_ref, got_stayed_ref, out_ref, sems):
    place = lax.axis_index("seq")
    core, chip = lax.rem(place, CORES), place // CORES
    rows = out_ref.shape[0]
    others, _, width = sent_ref.shape
    here = pl.ds(pl.multiple_of(core * rows, rows), rows)
    pairs = []
    for first, rest, which in (
        (stayed_ref, sent_ref, core), (got_stayed_ref, got_sent_ref, 1 - core)
    ):
        for step in range(others + 1):
            source = first.at[0, here, :] if step == 0 else rest.at[step - 1, here, :]
            owner = lax.rem(chip + step, others + 1)
            pairs.append((source, columns_of(out_ref, owner * CORES + which, width)))
    run_copies(pairs, sems)


def join_heads(sent, stayed, got_sent, got_stayed):
    others, rows, width = sent.shape
    return pl.pallas_call(
        join_kernel,
        in_specs=[pl.BlockSpec(memory_space=pl.ANY)] * 4,
        out_shape=jax.ShapeDtypeStruct(
            (rows // CORES, (others + 1) * CORES * width), sent.dtype
        ),
        scratch_shapes=[pltpu.SemaphoreType.DMA((CORES * (others + 1),))],
        compiler_params=params,
        name="join_heads",
    )(sent, stayed, got_sent, got_stayed)


def stacked_queries(query, group):
    return jnp.concatenate(
        [query[:, i * HEAD_SIZE : (i + 1) * HEAD_SIZE] for i in range(group)], axis=0
    )


def side_by_side(value, group):
    rows = value.shape[0] // group
    return jnp.concatenate([value[i * rows : (i + 1) * rows, :] for i in range(group)], axis=1)


def doc_starts(doc_ref, query_pos):
    start = jnp.zeros(query_pos.shape, jnp.int32)
    bound = jnp.int32(0)
    for doc in range(doc_ref.shape[1]):
        bound = bound + doc_ref[0, doc]
        start = jnp.where(query_pos >= bound, bound, start)
    return start


def write_masks(doc_ref, mask_ref, places, blocks):
    rows = mask_ref.shape[1]
    shape = (rows, 2 * rows)
    row = lax.broadcasted_iota(jnp.int32, shape, 0)
    lane = lax.broadcasted_iota(jnp.int32, shape, 1)
    for item, (place, (first, second)) in enumerate(zip(places, blocks)):
        query_pos = place * rows + row
        key_pos = jnp.where(lane < rows, first, second - 1) * rows + lane
        allowed = (key_pos >= doc_starts(doc_ref, query_pos)) & (key_pos <= query_pos)
        mask_ref[item] = jnp.where(allowed, 0.0, masked_fill)


def scores_of(query, keys, fill, group):
    rows = query.shape[0]
    scores = lax.dot_general(
        stacked_queries(query, group), keys, (((1,), (1,)), ((), ())),
        preferred_element_type=jnp.float32,
    )
    return jnp.concatenate(
        [scores[i * rows : (i + 1) * rows, :] * scale + fill for i in range(group)], axis=0
    )


def weighted(raw, values):
    ones = jnp.ones((values.shape[0], HEAD_SIZE), jnp.bfloat16)
    both = jnp.dot(
        raw.astype(jnp.bfloat16), jnp.concatenate([values, ones], axis=1),
        preferred_element_type=jnp.float32,
    )
    return both[:, :HEAD_SIZE], both[:, HEAD_SIZE:]


def near_kernel(
    place_ref, doc_ref, mine_ref, theirs_ref, own_ref, swap_ref, *rest
):
    out_ref, level_ref, mask_ref = rest[-3:]
    step = pl.program_id(0)
    rows = mine_ref.shape[0]
    group = mine_ref.shape[1] // HEAD_SIZE
    own = place_ref[0] * CORES + place_ref[1]
    swapped = place_ref[0] * CORES + 1 - place_ref[1]

    @pl.when(step == 0)
    def _():
        write_masks(doc_ref, mask_ref, (own, swapped), ((own, swapped),) * 2)
        level_ref[...] = jnp.zeros_like(level_ref)

    keys = jnp.concatenate([own_ref[0, 0], swap_ref[0, 0]], axis=0)
    values = jnp.concatenate([own_ref[0, 1], swap_ref[0, 1]], axis=0)
    lane = lax.broadcasted_iota(jnp.int32, (rows, LANES), 1)
    scores = [
        scores_of(query, keys, mask_ref[item], group)
        for item, query in enumerate((mine_ref[...], theirs_ref[...]))
    ]
    for item, score in enumerate(scores):
        peak = jnp.max(score, axis=1, keepdims=True)
        mixed, total = weighted(jnp.exp2(score - peak), values)
        out_ref[0, item] = side_by_side((mixed / total).astype(jnp.bfloat16), group)
        level = peak + jnp.log2(total)
        for i in range(group):
            level_ref[item] = jnp.where(
                lane == step * group + i, level[i * rows : (i + 1) * rows, :], level_ref[item]
            )


def far_kernel(
    place_ref, doc_ref, mine_ref, theirs_ref, near_ref, far_ref, mixed_ref, level_ref,
    rank_ref, map_ref, send_ref, stay_ref, part_ref, mask_ref, *, chips,
):
    step = pl.program_id(0)
    rows = mine_ref.shape[0]
    group = mine_ref.shape[1] // HEAD_SIZE
    first_core = place_ref[1] == 0
    own = place_ref[0] * CORES + place_ref[1]
    swapped = place_ref[0] * CORES + 1 - place_ref[1]

    @pl.when(step == 0)
    def _():
        behind = (own - CORES, swapped - CORES)
        write_masks(doc_ref, mask_ref, (own, swapped), (behind,) * 2)
        part_ref[...] = jnp.zeros_like(part_ref)

    keys = jnp.concatenate([near_ref[0, 0], far_ref[0, 0]], axis=0)
    values = jnp.concatenate([near_ref[0, 1], far_ref[0, 1]], axis=0)
    lane = lax.broadcasted_iota(jnp.int32, (rows, LANES), 1)
    scores = [
        scores_of(query, keys, mask_ref[item], group)
        for item, query in enumerate((mine_ref[...], theirs_ref[...]))
    ]
    outputs = []
    for item, score in enumerate(scores):
        level = jnp.concatenate(
            [
                jnp.max(
                    jnp.where(lane == step * group + i, level_ref[item], 2.0 * masked_fill),
                    axis=1,
                    keepdims=True,
                )
                for i in range(group)
            ],
            axis=0,
        )
        peak = jnp.maximum(jnp.max(score, axis=1, keepdims=True), level)
        mixed, total = weighted(jnp.exp2(score - peak), values)
        share = jnp.exp2(level - peak)
        before = stacked_queries(mixed_ref[0, item], group).astype(jnp.float32)
        mixed = (before * share + mixed) * pl.reciprocal(total + share)
        outputs.append(side_by_side(mixed.astype(jnp.bfloat16), group))
    stream = jnp.concatenate(
        [
            jnp.where(first_core, outputs[0], outputs[1]),
            jnp.where(first_core, outputs[1], outputs[0]),
        ],
        axis=0,
    )
    last = step >= pl.num_programs(0) - pl.num_programs(0) // chips

    @pl.when(last)
    def _():
        stay_ref[0] = stream

    @pl.when(jnp.logical_not(last))
    def _():
        send_ref[0] = stream

    both = CORES * rows
    part_ref[:both, :] += jnp.dot(stream, rank_ref[...], preferred_element_type=jnp.float32)
    part_ref[both:, :] += lax.dot_general(
        map_ref[...], stream, (((1,), (1,)), ((), ())), preferred_element_type=jnp.float32
    )


class Heads:
    def __init__(self, queries, block):
        self.chips, _, self.rows, columns = block.shape
        self.heads = columns // HEAD_SIZE
        self.width = queries.shape[1] // (self.chips * CORES)
        self.wide = self.width // self.heads
        self.steps = self.chips * self.heads

    def owner(self, j, s):
        return lax.rem(s[0] + 1 + j // self.heads, self.chips)

    def column(self, j, s):
        return (self.owner(j, s) * CORES + s[1]) * self.heads + lax.rem(j, self.heads)

    def query(self):
        return pl.BlockSpec((self.rows, self.wide), lambda j, s: (0, self.column(j, s)))

    def keys(self):
        return pl.BlockSpec(
            (1, 2, self.rows, HEAD_SIZE),
            lambda j, s: (self.owner(j, s), 0, 0, lax.rem(j, self.heads)),
        )

    def mixed(self):
        return pl.BlockSpec((1, 2, self.rows, self.wide), lambda j, s: (j, 0, 0, 0))

    def level(self):
        return pl.BlockSpec((2, self.rows, LANES), lambda j, s: (0, 0, 0))


def attend_near(place, doc_lengths, queries, blocks, after):
    plan = Heads(queries[0], blocks[0])
    return pl.pallas_call(
        near_kernel,
        grid_spec=pltpu.PrefetchScalarGridSpec(
            num_scalar_prefetch=1,
            grid=(plan.steps,),
            in_specs=[pl.BlockSpec(memory_space=pltpu.SMEM)]
            + [plan.query()] * 2
            + [plan.keys()] * 2
            + [pl.BlockSpec(memory_space=pl.ANY)] * len(after),
            out_specs=[plan.mixed(), plan.level()],
            scratch_shapes=[pltpu.VMEM((2, plan.rows, 2 * plan.rows), jnp.float32)],
        ),
        out_shape=[
            jax.ShapeDtypeStruct((plan.steps, 2, plan.rows, plan.wide), jnp.bfloat16),
            jax.ShapeDtypeStruct((2, plan.rows, LANES), jnp.float32),
        ],
        compiler_params=params,
        cost_estimate=pl.CostEstimate(flops=5 * 10**9, bytes_accessed=1 << 22, transcendentals=0),
        name="attend_near",
    )(place, doc_lengths, *queries, *blocks, *after)


def attend_far(place, doc_lengths, queries, blocks, near, rank_in, map_rows):
    plan = Heads(queries[0], blocks[0])
    chips, heads, rows, wide = plan.chips, plan.heads, plan.rows, plan.wide
    part = (CORES * rows + 2 * NS, RANK)

    def sent(j, s):
        at = jnp.minimum(j, (chips - 1) * heads - 1)
        return (at // heads, 0, lax.rem(at, heads))

    return pl.pallas_call(
        functools.partial(far_kernel, chips=chips),
        grid_spec=pltpu.PrefetchScalarGridSpec(
            num_scalar_prefetch=1,
            grid=(plan.steps,),
            in_specs=[pl.BlockSpec(memory_space=pltpu.SMEM)]
            + [plan.query()] * 2
            + [plan.keys()] * 2
            + [
                plan.mixed(),
                plan.level(),
                pl.BlockSpec((wide, RANK), lambda j, s: (plan.column(j, s), 0)),
                pl.BlockSpec((2 * NS, wide), lambda j, s: (0, plan.column(j, s))),
            ],
            out_specs=[
                pl.BlockSpec((1, CORES * rows, wide), sent),
                pl.BlockSpec(
                    (1, CORES * rows, wide),
                    lambda j, s: (0, 0, jnp.maximum(j - (chips - 1) * heads, 0)),
                ),
                pl.BlockSpec(part, lambda j, s: (0, 0)),
            ],
            scratch_shapes=[pltpu.VMEM((2, rows, 2 * rows), jnp.float32)],
        ),
        out_shape=[
            jax.ShapeDtypeStruct((chips - 1, CORES * rows, plan.width), jnp.bfloat16),
            jax.ShapeDtypeStruct((1, CORES * rows, plan.width), jnp.bfloat16),
            jax.ShapeDtypeStruct(part, jnp.float32),
        ],
        compiler_params=params,
        cost_estimate=pl.CostEstimate(flops=5 * 10**9, bytes_accessed=1 << 22, transcendentals=0),
        name="attend_far",
    )(place, doc_lengths, *queries, *blocks, *near, rank_in, map_rows)


def low_kernel(mine_ref, theirs_ref, out_ref):
    rows = mine_ref.shape[0] - 2 * NS
    total = mine_ref[...] + theirs_ref[...]
    out_ref[:rows, :] = total[:rows, :].astype(jnp.bfloat16)
    out_ref[rows:, :] = jnp.concatenate(split(total[rows:, :]), axis=0)


def low_and_maps(mine, theirs):
    return pl.pallas_call(
        low_kernel,
        out_shape=jax.ShapeDtypeStruct((mine.shape[0] + 2 * NS, RANK), jnp.bfloat16),
        compiler_params=params,
        cost_estimate=pl.CostEstimate(flops=1, bytes_accessed=1, transcendentals=0),
        name="low_and_maps",
    )(mine, theirs)


def softplus(value):
    small = jnp.exp(-jnp.abs(value))
    tail = jnp.where(small < 0.00390625, small * (1.0 - 0.5 * small), jnp.log(1.0 + small))
    return jnp.maximum(value, 0.0) + tail


def add_states(rates_ref, state_ref, total_ref, states, totals):
    state_ref[...] = jnp.exp2(rates_ref[...] * totals) * state_ref[...] + states
    total_ref[...] = total_ref[...] + totals


def sums_within(steps):
    rows = steps.shape[0]
    at = lax.broadcasted_iota(jnp.int32, (rows, rows), 0)
    of = lax.broadcasted_iota(jnp.int32, (rows, rows), 1)
    upto = jnp.where(of <= at, 1.0, 0.0).astype(jnp.bfloat16)
    return jnp.dot(upto, steps, preferred_element_type=jnp.float32)


def step_kernel(
    place_ref, stream_ref, low_ref, map_ref, cols_ref, bias_ref, rates_ref, *rest
):
    own_state_ref, own_total_ref = rest[:2]
    steps_ref, sums_ref, maps_ref, carry_ref, state_ref, total_ref, wide_ref, turn_ref = rest[3:]
    block = pl.program_id(0)
    rows, width = stream_ref.shape[1:]

    @pl.when(block == 0)
    def _():
        state_ref[...] = jnp.zeros_like(state_ref)
        total_ref[...] = jnp.zeros_like(total_ref)
        for n in range(NS):
            wide_ref[n * SUBLANES : (n + 1) * SUBLANES, :] = jnp.broadcast_to(
                rates_ref[n : n + 1, :], (SUBLANES, width)
            )

    @pl.when(block == place_ref[0] * CORES)
    def _():
        add_states(rates_ref, state_ref, total_ref, own_state_ref[...], own_total_ref[...])

    maps = map_ref[0].astype(jnp.float32)
    maps = maps[: 2 * NS, :] + maps[2 * NS :, :]
    maps_ref[0] = maps
    logits = jnp.dot(low_ref[0], cols_ref[...], preferred_element_type=jnp.float32)
    steps = softplus(logits + bias_ref[...]).astype(jnp.bfloat16)
    steps_ref[...] = steps
    push = steps * stream_ref[0]
    within = sums_within(steps)
    sums_ref[...] = within.astype(jnp.bfloat16)
    whole = within[rows - 1 :, :]
    left = whole - within
    some, chunk, several = rows // 2, CORES * LANES, 4
    state_row = lax.broadcasted_iota(jnp.int32, (NS, some), 0)
    for first in range(0, rows, some):
        span = slice(first, first + some)
        chosen = [
            jnp.concatenate(
                [
                    jnp.where(state_row == m, maps[:NS, span], 0.0).astype(jnp.bfloat16)
                    for m in range(n, n + several)
                ],
                axis=1,
            )
            for n in range(0, NS, several)
        ]
        for item in range(width // chunk):
            lanes = slice(item * chunk, (item + 1) * chunk)
            left_here = left[span, lanes].reshape(some // SUBLANES, SUBLANES, chunk)
            push_here = push[span, lanes]
            added = state_ref[:, lanes]
            if first == 0:
                added = jnp.exp2(rates_ref[:, lanes] * whole[:, lanes]) * added
            for n in range(0, NS, several):
                pushed = []
                for m in range(n, n + several):
                    rate = wide_ref[m * SUBLANES : (m + 1) * SUBLANES, lanes]
                    decay = jnp.exp2(left_here * rate[None]).reshape(some, chunk)
                    pushed.append(decay.astype(jnp.bfloat16) * push_here)
                added = added + jnp.dot(
                    chosen[n // several],
                    jnp.concatenate(pushed, axis=0),
                    preferred_element_type=jnp.float32,
                )
            state_ref[:, lanes] = added
    total_ref[...] = total_ref[...] + whole

    count = pl.num_programs(0)

    @pl.when(block == count - 1)
    def _():
        @pl.when(place_ref[0] * CORES == count)
        def _():
            add_states(rates_ref, state_ref, total_ref, own_state_ref[...], own_total_ref[...])

        write_carry(carry_ref.at[0], state_ref[...], total_ref[...], turn_ref)
        for target in range(1, carry_ref.shape[0]):
            carry_ref[target] = carry_ref[0]


def step_sizes(place, stream, lows, cols, bias, rates, state, total, targets, after):
    others = stream.shape[0]
    chips = others + 1
    rows, width = stream.shape[1] // CORES, stream.shape[2]
    map_row = CORES * rows // MAPS
    blocks = others * CORES
    carry = (targets, (width // LANES + 1) * NS, LANES)

    def slot(b, s):
        chip = b // CORES
        return lax.rem(s[0] - jnp.where(chip < s[0], chip, chip + 1) + chips, chips) - 1

    def core(b):
        return lax.rem(b, CORES)

    def fixed(*shape):
        return pl.BlockSpec(shape, lambda b, s: (0,) * len(shape))

    return pl.pallas_call(
        step_kernel,
        grid_spec=pltpu.PrefetchScalarGridSpec(
            num_scalar_prefetch=1,
            grid=(blocks,),
            in_specs=[
                pl.BlockSpec((1, rows, width), lambda b, s: (slot(b, s), core(b), 0)),
                pl.BlockSpec((1, rows, RANK), lambda b, s: (slot(b, s), core(b), 0)),
                pl.BlockSpec((1, MAPS, rows), lambda b, s: (slot(b, s), map_row, core(b))),
                fixed(*cols.shape),
                fixed(*bias.shape),
                fixed(*rates.shape),
                fixed(*state.shape),
                fixed(*total.shape),
                pl.BlockSpec(memory_space=pl.ANY),
            ],
            out_specs=[
                pl.BlockSpec((rows, width), lambda b, s: (b, 0)),
                pl.BlockSpec((rows, width), lambda b, s: (b, 0)),
                pl.BlockSpec((1, 2 * NS, rows), lambda b, s: (b, 0, 0)),
                fixed(*carry),
            ],
            scratch_shapes=[
                pltpu.VMEM((NS, width), jnp.float32),
                pltpu.VMEM((1, width), jnp.float32),
                pltpu.VMEM((NS * SUBLANES, width), jnp.float32),
                pltpu.VMEM((SUBLANES, LANES), jnp.float32),
            ],
        ),
        out_shape=[
            jax.ShapeDtypeStruct((blocks * rows, width), jnp.bfloat16),
            jax.ShapeDtypeStruct((blocks * rows, width), jnp.bfloat16),
            jax.ShapeDtypeStruct((blocks, 2 * NS, rows), jnp.float32),
            jax.ShapeDtypeStruct(carry, jnp.bfloat16),
        ],
        compiler_params=params,
        name="step_sizes",
    )(place, stream, lows, lows, cols, bias, rates, state, total, after)


def write_carry(out_ref, state, total, turn_ref):
    tile = state.shape[1] // LANES
    turn_ref[...] = jnp.zeros_like(turn_ref)
    for item in range(tile):
        lanes = slice(item * LANES, (item + 1) * LANES)
        turn_ref[item : item + 1, :] = total[:, lanes]
        out_ref[item * NS : (item + 1) * NS, :] = state[:, lanes].astype(jnp.bfloat16)
    out_ref[tile * NS :, :] = jnp.concatenate(split(turn_ref[...]), axis=0)


def follow(carry_ref, rates_ref, state_ref):
    tile = state_ref.shape[1] // LANES
    sums = carry_ref[tile * NS :, :].astype(jnp.float32)
    sums = sums[:SUBLANES, :] + sums[SUBLANES:, :]
    for item in range(tile):
        lanes = slice(item * LANES, (item + 1) * LANES)
        decay = jnp.exp2(rates_ref[:, lanes] * sums[item : item + 1, :])
        added = carry_ref[item * NS : (item + 1) * NS, :].astype(jnp.float32)
        state_ref[:, lanes] = decay * state_ref[:, lanes] + added
    return sums


def scan_blocks(stream_ref, steps_ref, maps, rates_ref, gain_ref, out_ref, state_ref, work_refs):
    out_of_ref, *hist_refs = work_refs
    rows, width = steps_ref.shape
    source = lax.broadcasted_iota(jnp.int32, (LANES, NS * NS), 0)
    column = lax.rem(lax.broadcasted_iota(jnp.int32, (LANES, NS * NS), 1), NS)
    token = lax.rem(lax.broadcasted_iota(jnp.int32, (rows, NS * NS), 0), NS)
    slot = lax.broadcasted_iota(jnp.int32, (rows, NS * NS), 1) // NS
    turned = jnp.concatenate(
        [maps, jnp.zeros((LANES - 2 * NS, rows), jnp.float32)], axis=0
    ).T.astype(jnp.bfloat16)
    pick = jnp.where(source == NS + column, 1.0, 0.0).astype(jnp.bfloat16)
    spread = jnp.dot(turned, pick, preferred_element_type=jnp.float32)
    out_of_ref[...] = jnp.where(token == slot, spread, 0.0).astype(jnp.bfloat16)
    map_in = maps[:NS, :]
    half = width // 2

    def finish(first, hist_ref):
        here = pl.ds(first, NS)
        mixed = jnp.dot(out_of_ref[here, :], hist_ref[...], preferred_element_type=jnp.float32)
        direct = gain_ref[...] * stream_ref[0, here, :].astype(jnp.float32)
        out_ref[here, :] = (mixed + direct).astype(jnp.bfloat16)

    def advance(first, hist_ref):
        here = pl.ds(first, NS)
        into = pltpu.roll(map_in, lax.rem(rows - first, rows), 1)
        for lanes in (slice(0, half), slice(half, width)):
            state = state_ref[:, lanes]
            rates = rates_ref[:, lanes]
            steps = steps_ref[here, lanes].astype(jnp.float32)
            push = steps * stream_ref[0, here, lanes].astype(jnp.float32)
            for near in range(NS):
                this = slice(near, near + 1)
                state = jnp.exp2(rates * steps[this, :]) * state + into[:, this] * push[this, :]
                hist_ref[near * NS : (near + 1) * NS, lanes] = state.astype(jnp.bfloat16)
            state_ref[:, lanes] = state

    def pair(index, nothing):
        first = pl.multiple_of(index * 2 * NS, 2 * NS)
        advance(first, hist_refs[0])
        finish(first, hist_refs[0])
        second = pl.multiple_of(first + NS, NS)
        advance(second, hist_refs[1])
        finish(second, hist_refs[1])
        return nothing

    lax.fori_loop(0, rows // (2 * NS), pair, 0)


def work_shapes(rows, width):
    return [
        pltpu.VMEM((rows, NS * NS), jnp.bfloat16),
        pltpu.VMEM((NS * NS, width), jnp.bfloat16),
        pltpu.VMEM((NS * NS, width), jnp.bfloat16),
    ]


def own_kernel(
    stream_ref, low_ref, map_ref, cols_ref, bias_ref, rates_ref, gain_ref,
    out_ref, sums_ref, maps_ref, state_ref, total_ref, steps_ref, *work_refs
):
    rows = steps_ref.shape[0]

    @pl.when(pl.program_id(0) == 0)
    def _():
        state_ref[...] = jnp.zeros_like(state_ref)
        total_ref[...] = jnp.zeros_like(total_ref)

    maps = map_ref[...].astype(jnp.float32)
    maps = maps[: 2 * NS, :] + maps[2 * NS :, :]
    maps_ref[0] = maps
    logits = jnp.dot(low_ref[...], cols_ref[...], preferred_element_type=jnp.float32)
    steps = softplus(logits + bias_ref[...]).astype(jnp.bfloat16)
    steps_ref[...] = steps
    within = sums_within(steps)
    sums_ref[...] = within.astype(jnp.bfloat16)
    total_ref[...] = total_ref[...] + within[rows - 1 :, :]
    scan_blocks(stream_ref, steps_ref, maps, rates_ref, gain_ref, out_ref, state_ref, work_refs)


def scan_own(stream, lows, cols, bias, rates, gain):
    rows, width = stream.shape[1] // CORES, stream.shape[2]
    map_row = CORES * rows // MAPS

    def fixed(*shape):
        return pl.BlockSpec(shape, lambda b: (0,) * len(shape))

    block = pl.BlockSpec((rows, width), lambda b: (b, 0))
    return pl.pallas_call(
        own_kernel,
        grid=(CORES,),
        in_specs=[
            pl.BlockSpec((1, rows, width), lambda b: (0, b, 0)),
            pl.BlockSpec((rows, RANK), lambda b: (b, 0)),
            pl.BlockSpec((MAPS, rows), lambda b: (map_row, b)),
            fixed(*cols.shape),
            fixed(*bias.shape),
            fixed(*rates.shape),
            fixed(*gain.shape),
        ],
        out_specs=[
            block,
            block,
            pl.BlockSpec((1, 2 * NS, rows), lambda b: (b, 0, 0)),
            fixed(NS, width),
            fixed(1, width),
        ],
        out_shape=[
            jax.ShapeDtypeStruct((CORES * rows, width), jnp.bfloat16),
            jax.ShapeDtypeStruct((CORES * rows, width), jnp.bfloat16),
            jax.ShapeDtypeStruct((CORES, 2 * NS, rows), jnp.float32),
            jax.ShapeDtypeStruct((NS, width), jnp.float32),
            jax.ShapeDtypeStruct((1, width), jnp.float32),
        ],
        scratch_shapes=[pltpu.VMEM((rows, width), jnp.bfloat16)] + work_shapes(rows, width),
        compiler_params=params,
        cost_estimate=pl.CostEstimate(flops=4 * 10**9, bytes_accessed=1 << 21, transcendentals=0),
        name="scan_own",
    )(stream, lows, lows, cols, bias, rates, gain)


def others_kernel(
    place_ref, stream_ref, steps_ref, maps_ref, rates_ref, gain_ref, out_ref, last_ref, *work_refs
):
    @pl.when(lax.rem(pl.program_id(0), CORES) == 0)
    def _():
        last_ref[...] = jnp.zeros_like(last_ref)

    scan_blocks(
        stream_ref, steps_ref, maps_ref[0], rates_ref, gain_ref, out_ref, last_ref.at[0], work_refs
    )


def scan_others(place, stream, steps, maps, rates, gain):
    others = stream.shape[0]
    chips = others + 1
    rows, width = stream.shape[1] // CORES, stream.shape[2]

    def slot(b, s):
        chip = b // CORES
        return lax.rem(s[0] - jnp.where(chip < s[0], chip, chip + 1) + chips, chips) - 1

    def fixed(*shape):
        return pl.BlockSpec(shape, lambda b, s: (0,) * len(shape))

    block = pl.BlockSpec((rows, width), lambda b, s: (b, 0))
    return pl.pallas_call(
        others_kernel,
        grid_spec=pltpu.PrefetchScalarGridSpec(
            num_scalar_prefetch=1,
            grid=(others * CORES,),
            in_specs=[
                pl.BlockSpec((1, rows, width), lambda b, s: (slot(b, s), lax.rem(b, CORES), 0)),
                block,
                pl.BlockSpec((1, 2 * NS, rows), lambda b, s: (b, 0, 0)),
                fixed(*rates.shape),
                fixed(*gain.shape),
            ],
            out_specs=[block, pl.BlockSpec((1, NS, width), lambda b, s: (b // CORES, 0, 0))],
            scratch_shapes=work_shapes(rows, width),
        ),
        out_shape=[
            jax.ShapeDtypeStruct((others * CORES * rows, width), jnp.bfloat16),
            jax.ShapeDtypeStruct((others, NS, width), jnp.float32),
        ],
        compiler_params=params,
        cost_estimate=pl.CostEstimate(flops=4 * 10**9, bytes_accessed=1 << 21, transcendentals=0),
        name="scan_others",
    )(place, stream, steps, maps, rates, gain)


def carried_kernel(
    places_ref, part_own_ref, part_come_ref, sums_own_ref, sums_come_ref,
    maps_own_ref, maps_come_ref, last_own_ref, last_come_ref, rates_ref, carries_ref,
    out_ref, state_ref, wide_ref, begin_ref, spread_ref, sums_ref,
):
    block = pl.program_id(0)
    rows, width = out_ref.shape
    chip = block // CORES
    here = chip == places_ref[0]

    @pl.when(block == 0)
    def _():
        state_ref[...] = jnp.zeros_like(state_ref)

        def compose(row, nothing):
            follow(carries_ref.at[row], rates_ref, state_ref)
            return nothing

        lax.fori_loop(0, places_ref[1], compose, 0)
        for n in range(NS):
            wide_ref[n * SUBLANES : (n + 1) * SUBLANES, :] = jnp.broadcast_to(
                rates_ref[n : n + 1, :], (SUBLANES, width)
            )

    @pl.when((block > 0) & (lax.rem(block, CORES) == 0))
    def _():
        before = jnp.where(chip - 1 == places_ref[0], last_own_ref[...], last_come_ref[0])
        state_ref[...] = state_ref[...] + before

    state = state_ref[...]
    for n in range(NS):
        begin_ref[n * NS : (n + 1) * NS, :] = jnp.broadcast_to(
            state[n : n + 1, :], (NS, width)
        ).astype(jnp.bfloat16)
    maps = jnp.where(here, maps_own_ref[0], maps_come_ref[0])
    maps = jnp.concatenate([maps, jnp.zeros((LANES - 2 * NS, rows), jnp.float32)], axis=0).T
    for n in range(NS):
        spread_ref[:, n * LANES : (n + 1) * LANES] = jnp.broadcast_to(
            maps[:, NS + n : NS + n + 1], (rows, LANES)
        ).astype(jnp.bfloat16)
    sums = jnp.where(here, sums_own_ref[...], sums_come_ref[...]).astype(jnp.float32)
    sums_ref[...] = sums
    state_ref[...] = jnp.exp2(rates_ref[...] * sums[rows - 1 :, :]) * state
    chunk, several = CORES * LANES, 4

    def some(index, nothing):
        near = pl.ds(pl.multiple_of(index * NS, NS), NS)
        for item in range(width // chunk):
            lanes = slice(item * chunk, (item + 1) * chunk)
            part = jnp.where(here, part_own_ref[near, lanes], part_come_ref[near, lanes])
            total = part.astype(jnp.float32)
            sums = sums_ref[near, lanes].reshape(NS // SUBLANES, SUBLANES, chunk)
            for first in range(0, NS, several):
                terms = []
                for n in range(first, first + several):
                    rate = wide_ref[n * SUBLANES : (n + 1) * SUBLANES, lanes]
                    decay = jnp.exp2(sums * rate[None]).reshape(NS, chunk).astype(jnp.bfloat16)
                    out_of = spread_ref[near, n * LANES : (n + 1) * LANES]
                    out_of = jnp.concatenate([out_of] * (chunk // LANES), axis=1)
                    terms.append(decay * begin_ref[n * NS : (n + 1) * NS, lanes] * out_of)
                four = (terms[0] + terms[1]) + (terms[2] + terms[3])
                total = total + four.astype(jnp.float32)
            out_ref[near, lanes] = total.astype(jnp.bfloat16)
        return nothing

    lax.fori_loop(0, rows // NS, some, 0)


def add_carried(places, parts, sums, maps, lasts, rates, carries):
    blocks_come, _, rows = maps[1].shape
    chips = blocks_come // CORES + 1
    width = rates.shape[1]

    def core(b):
        return lax.rem(b, CORES)

    def order(b, s):
        chip = b // CORES
        return jnp.minimum(
            jnp.where(chip < s[0], b, jnp.maximum(b - CORES, 0)), blocks_come - 1
        )

    def before(b, s):
        chip = jnp.maximum(b // CORES - 1, 0)
        return jnp.minimum(jnp.where(chip < s[0], chip, jnp.maximum(chip - 1, 0)), chips - 2)

    def fixed(*shape):
        return pl.BlockSpec(shape, lambda b, s: (0,) * len(shape))

    own = pl.BlockSpec((rows, width), lambda b, s: (core(b), 0))
    come = pl.BlockSpec((rows, width), lambda b, s: (order(b, s), 0))
    return pl.pallas_call(
        carried_kernel,
        grid_spec=pltpu.PrefetchScalarGridSpec(
            num_scalar_prefetch=1,
            grid=(chips * CORES,),
            in_specs=[
                own,
                come,
                own,
                come,
                pl.BlockSpec((1, 2 * NS, rows), lambda b, s: (core(b), 0, 0)),
                pl.BlockSpec((1, 2 * NS, rows), lambda b, s: (order(b, s), 0, 0)),
                fixed(NS, width),
                pl.BlockSpec((1, NS, width), lambda b, s: (before(b, s), 0, 0)),
                fixed(*rates.shape),
                fixed(*carries.shape),
            ],
            out_specs=pl.BlockSpec((rows, width), lambda b, s: (b, 0)),
            scratch_shapes=[
                pltpu.VMEM((NS, width), jnp.float32),
                pltpu.VMEM((NS * SUBLANES, width), jnp.float32),
                pltpu.VMEM((NS * NS, width), jnp.bfloat16),
                pltpu.VMEM((rows, NS * LANES), jnp.bfloat16),
                pltpu.VMEM((rows, width), jnp.float32),
            ],
        ),
        out_shape=jax.ShapeDtypeStruct((chips * CORES * rows, width), jnp.bfloat16),
        compiler_params=params,
        name="add_carried",
    )(places, *parts, *sums, *maps, *lasts, rates, carries)


def local(
    queries, keys, values, doc_lengths, rank_in, bc_weight, rank_out, dt_bias, a_log, skip_gain
):
    devices = lax.axis_size("seq")
    chips = devices // CORES
    targets = lax.axis_size("chan")
    seq_place = lax.axis_index("seq").astype(jnp.int32)
    chan_place = lax.axis_index("chan").astype(jnp.int32)
    chip, core = seq_place // CORES, lax.rem(seq_place, CORES)
    place = jnp.stack([chip, core])
    width = queries.shape[2] // devices
    wide = max(HEAD_SIZE, keys.shape[2] // devices)

    def other(device):
        return device + 1 - 2 * (device % CORES)

    swap = [(device, other(device)) for device in range(devices)]
    near = [(device, device + CORES) for device in range(devices - CORES)]
    far = [(device, other(device + CORES)) for device in range(devices - CORES)]

    def onward(chips_on):
        return [(device, (device + chips_on * CORES) % devices) for device in range(devices)]

    own, theirs = select_heads(keys[0], values[0], chips, wide)
    from_near = lax.ppermute(own, "seq", near)
    from_far = lax.ppermute(theirs, "seq", far)
    swapped = lax.ppermute(theirs, "seq", swap)
    their_queries = lax.ppermute(queries[0], "seq", swap)

    first = seq_place * width
    logs = lax.dynamic_slice_in_dim(a_log, first, width, 0)
    rates = (-LOG2E * jnp.exp(logs)).T
    cols = lax.dynamic_slice_in_dim(rank_out, first, width, 1)
    bias = lax.dynamic_slice_in_dim(dt_bias, first, width, 0)[None]
    gain = lax.dynamic_slice_in_dim(skip_gain, first, width, 0)[None]

    asked = (place, doc_lengths, (queries[0], their_queries))
    mixed = attend_near(*asked, (own, swapped), (rates, cols, bias, gain))
    sent, stayed, part = attend_far(*asked, (from_near, from_far), mixed, rank_in, bc_weight.T)
    come = [lax.ppermute(sent[step], "seq", onward(step + 1)) for step in range(chips - 1)]
    low_own = low_and_maps(part, lax.ppermute(part, "seq", swap))
    low_come = [lax.ppermute(low_own, "seq", onward(step + 1)) for step in range(chips - 1)]
    got_sent = lax.ppermute(sent, "seq", swap)
    got_stayed = lax.ppermute(stayed, "seq", swap)
    attn_rows = join_heads(sent, stayed, got_sent, got_stayed)

    part_own, sums_own, maps_own, state, total = scan_own(stayed, low_own, cols, bias, rates, gain)
    come, low_come = jnp.stack(come), jnp.stack(low_come)
    steps, sums_come, maps_come, carry = step_sizes(
        place, come, low_come, cols, bias, rates, state, total, targets, attn_rows
    )
    carries = lax.all_to_all(carry, "chan", split_axis=0, concat_axis=0, tiled=True)
    part_come, last_come = scan_others(place, come, steps, maps_come, rates, gain)
    ssm_rows = add_carried(
        jnp.stack([chip, chan_place]), (part_own, part_come), (sums_own, sums_come),
        (maps_own, maps_come), (state, last_come), rates, carries,
    )
    return (attn_rows[None], ssm_rows[None])


def solution(mesh):
    return jax.shard_map(
        local,
        mesh=mesh,
        in_specs=(
            P("chan", "seq", None),
            P("chan", "seq", None),
            P("chan", "seq", None),
            P("chan", None),
            P(),
            P(),
            P(),
            P(),
            P(),
            P(),
        ),
        out_specs=(P("chan", "seq", None), P("chan", None, "seq")),
        check_vma=False,
    )
```

```python
import functools
import math

import jax
import jax.numpy as jnp
from jax import lax
from jax.experimental import pallas as pl
from jax.experimental.pallas import tpu as pltpu
from jax.sharding import PartitionSpec as P

QUERY_HEADS = 32
KEY_VALUE_HEADS = 8
HEAD_SIZE = 128
GROUP = QUERY_HEADS // KEY_VALUE_HEADS
NS = 16
RANK = 256
CORES = 2
LANES = 128
SUBLANES = 8
MAPS = 2 * NS
LOG2E = 1.4426950408889634

masked_fill = -1e30
params = pltpu.CompilerParams(vmem_limit_bytes=60 << 20)


def split(value):
    coarse = value.astype(jnp.bfloat16)
    return coarse, (value - coarse.astype(jnp.float32)).astype(jnp.bfloat16)


def run_copies(pairs, sems):
    copies = [
        pltpu.make_async_copy(source, target, sems.at[i]) for i, (source, target) in enumerate(pairs)
    ]
    for copy in copies:
        copy.start()
    for copy in copies:
        copy.wait()


def columns_of(ref, index, size):
    return ref.at[:, pl.ds(pl.multiple_of(index * size, LANES), size)]


def heads_kernel(key_ref, value_ref, own_ref, their_ref, sems):
    core = lax.rem(lax.axis_index("seq"), CORES)
    wide = own_ref.shape[3]
    halves = key_ref.shape[1] // wide // own_ref.shape[0]
    pairs = []
    for target, which in ((own_ref, core), (their_ref, 1 - core)):
        for chip in range(own_ref.shape[0]):
            index = chip * halves + (which if halves == CORES else 0)
            for kind, source in enumerate((key_ref, value_ref)):
                pairs.append((columns_of(source, index, wide), target.at[chip, kind]))
    run_copies(pairs, sems)


def select_heads(keys, values, chips, wide):
    shape = jax.ShapeDtypeStruct((chips, 2, keys.shape[0], wide), keys.dtype)
    return pl.pallas_call(
        heads_kernel,
        in_specs=[pl.BlockSpec(memory_space=pl.ANY)] * 2,
        out_shape=[shape, shape],
        scratch_shapes=[pltpu.SemaphoreType.DMA((4 * chips,))],
        compiler_params=params,
        name="select_heads",
    )(keys, values)


def join_kernel(sent_ref, stayed_ref, got_sent_ref, got_stayed_ref, out_ref, sems):
    place = lax.axis_index("seq")
    core, chip = lax.rem(place, CORES), place // CORES
    rows = out_ref.shape[0]
    others, _, width = sent_ref.shape
    here = pl.ds(pl.multiple_of(core * rows, rows), rows)
    pairs = []
    for first, rest, which in (
        (stayed_ref, sent_ref, core), (got_stayed_ref, got_sent_ref, 1 - core)
    ):
        for step in range(others + 1):
            source = first.at[0, here, :] if step == 0 else rest.at[step - 1, here, :]
            owner = lax.rem(chip + step, others + 1)
            pairs.append((source, columns_of(out_ref, owner * CORES + which, width)))
    run_copies(pairs, sems)


def join_heads(sent, stayed, got_sent, got_stayed):
    others, rows, width = sent.shape
    return pl.pallas_call(
        join_kernel,
        in_specs=[pl.BlockSpec(memory_space=pl.ANY)] * 4,
        out_shape=jax.ShapeDtypeStruct(
            (rows // CORES, (others + 1) * CORES * width), sent.dtype
        ),
        scratch_shapes=[pltpu.SemaphoreType.DMA((CORES * (others + 1),))],
        compiler_params=params,
        name="join_heads",
    )(sent, stayed, got_sent, got_stayed)


def attend_kernel(
    place_ref, doc_ref, mine_ref, theirs_ref, own_ref, swap_ref, near_ref, far_ref,
    rank_ref, map_ref, *rest, chips,
):
    send_ref, stay_ref, part_ref, mask_ref = rest[-4:]
    step = pl.program_id(0)
    rows = mine_ref.shape[0]
    group = mine_ref.shape[1] // HEAD_SIZE
    chip, core = place_ref[0], place_ref[1]
    first_core = core == 0

    def above(shape):
        row = lax.rem(lax.broadcasted_iota(jnp.int32, shape, 0), rows)
        return lax.broadcasted_iota(jnp.int32, shape, 1) > row

    @pl.when(step == 0)
    def _():
        part_ref[...] = jnp.zeros_like(part_ref)
        own = chip * CORES + core
        swapped = chip * CORES + 1 - core
        near, far = own - CORES, swapped - CORES
        lane = lax.broadcasted_iota(jnp.int32, (rows, rows), 1)
        row = lax.broadcasted_iota(jnp.int32, (rows, rows), 0)
        for item, (place, before, middle) in enumerate(
            (
                (own, near, jnp.where(first_core, far, swapped)),
                (swapped, far, jnp.where(first_core, own, near)),
            )
        ):
            query_pos = place * rows + row
            start = jnp.zeros((rows, rows), jnp.int32)
            bound = jnp.int32(0)
            for doc in range(doc_ref.shape[1]):
                bound = bound + doc_ref[0, doc]
                start = jnp.where(query_pos >= bound, bound, start)
            ends = jnp.where(lane > row, before, place) * rows + lane
            mask_ref[item, :, :rows] = jnp.where(
                (ends >= start) & (ends <= query_pos), 0.0, masked_fill
            )
            mask_ref[item, :, rows:] = jnp.where(
                middle * rows + lane >= start, 0.0, masked_fill
            )

    scale = LOG2E / math.sqrt(HEAD_SIZE)
    ones = jnp.ones((3 * rows, HEAD_SIZE), jnp.bfloat16)

    def windows(kind):
        own, swapped = own_ref[0, kind], swap_ref[0, kind]
        near, far = near_ref[0, kind], far_ref[0, kind]
        return (
            jnp.concatenate([near, own, jnp.where(first_core, far, swapped)], axis=0),
            jnp.concatenate([far, swapped, jnp.where(first_core, own, near)], axis=0),
        )

    scores = []
    for keys, query in zip(windows(0), (mine_ref[...], theirs_ref[...])):
        stacked = jnp.concatenate(
            [query[:, i * HEAD_SIZE : (i + 1) * HEAD_SIZE] for i in range(group)], axis=0
        )
        scores.append(
            lax.dot_general(
                stacked, keys, (((1,), (1,)), ((), ())), preferred_element_type=jnp.float32
            )
        )
    outputs = []
    before = above((group * rows, rows))
    for item, (values, score) in enumerate(zip(windows(1), scores)):
        fill = mask_ref[item]
        ends = jnp.where(before, score[:, :rows], score[:, rows : 2 * rows])
        kept = jnp.concatenate([ends, score[:, 2 * rows :]], axis=1)
        kept = jnp.concatenate(
            [kept[i * rows : (i + 1) * rows, :] + fill for i in range(group)], axis=0
        )
        peak = jnp.max(kept, axis=1, keepdims=True)
        raw = jnp.exp2((kept - peak) * scale).astype(jnp.bfloat16)
        ends = raw[:, :rows]
        none = jnp.zeros_like(ends)
        spread = jnp.concatenate(
            [jnp.where(before, ends, none), jnp.where(before, none, ends), raw[:, rows:]], axis=1
        )
        both = jnp.dot(
            spread, jnp.concatenate([values, ones], axis=1), preferred_element_type=jnp.float32
        )
        mixed = both[:, :HEAD_SIZE] * pl.reciprocal(both[:, HEAD_SIZE:])
        mixed = mixed.astype(jnp.bfloat16)
        outputs.append(
            jnp.concatenate([mixed[i * rows : (i + 1) * rows, :] for i in range(group)], axis=1)
        )
    stream = jnp.concatenate(
        [
            jnp.where(first_core, outputs[0], outputs[1]),
            jnp.where(first_core, outputs[1], outputs[0]),
        ],
        axis=0,
    )
    last = step >= pl.num_programs(0) - pl.num_programs(0) // chips

    @pl.when(last)
    def _():
        stay_ref[0] = stream

    @pl.when(jnp.logical_not(last))
    def _():
        send_ref[0] = stream

    both = CORES * rows
    part_ref[:both, :] += jnp.dot(stream, rank_ref[...], preferred_element_type=jnp.float32)
    part_ref[both:, :] += lax.dot_general(
        map_ref[...], stream, (((1,), (1,)), ((), ())), preferred_element_type=jnp.float32
    )


def attend(place, doc_lengths, queries, blocks, rank_in, map_rows, after):
    mine, theirs = queries
    chips, _, rows, columns = blocks[0].shape
    heads = columns // HEAD_SIZE
    width = mine.shape[1] // (chips * CORES)
    wide = width // heads

    def owner(j, s):
        return lax.rem(s[0] + 1 + j // heads, chips)

    def column(j, s):
        return (owner(j, s) * CORES + s[1]) * heads + lax.rem(j, heads)

    def sent(j, s):
        at = jnp.minimum(j, (chips - 1) * heads - 1)
        return (at // heads, 0, lax.rem(at, heads))

    query = pl.BlockSpec((rows, wide), lambda j, s: (0, column(j, s)))
    block = pl.BlockSpec(
        (1, 2, rows, HEAD_SIZE), lambda j, s: (owner(j, s), 0, 0, lax.rem(j, heads))
    )
    return pl.pallas_call(
        functools.partial(attend_kernel, chips=chips),
        grid_spec=pltpu.PrefetchScalarGridSpec(
            num_scalar_prefetch=1,
            grid=(chips * heads,),
            in_specs=[pl.BlockSpec(memory_space=pltpu.SMEM), query, query]
            + [block] * 4
            + [
                pl.BlockSpec((wide, RANK), lambda j, s: (column(j, s), 0)),
                pl.BlockSpec((2 * NS, wide), lambda j, s: (0, column(j, s))),
            ]
            + [pl.BlockSpec(memory_space=pl.ANY)] * len(after),
            out_specs=[
                pl.BlockSpec((1, CORES * rows, wide), sent),
                pl.BlockSpec(
                    (1, CORES * rows, wide),
                    lambda j, s: (0, 0, jnp.maximum(j - (chips - 1) * heads, 0)),
                ),
                pl.BlockSpec((CORES * rows + 2 * NS, RANK), lambda j, s: (0, 0)),
            ],
            scratch_shapes=[pltpu.VMEM((2, rows, 2 * rows), jnp.float32)],
        ),
        out_shape=[
            jax.ShapeDtypeStruct((chips - 1, CORES * rows, width), jnp.bfloat16),
            jax.ShapeDtypeStruct((1, CORES * rows, width), jnp.bfloat16),
            jax.ShapeDtypeStruct((CORES * rows + 2 * NS, RANK), jnp.float32),
        ],
        compiler_params=params,
        cost_estimate=pl.CostEstimate(flops=5 * 10**9, bytes_accessed=1 << 22, transcendentals=0),
        name="attend",
    )(place, doc_lengths, mine, theirs, *blocks, rank_in, map_rows, *after)


def low_kernel(mine_ref, theirs_ref, out_ref):
    out_ref[...] = (mine_ref[...] + theirs_ref[...]).astype(jnp.bfloat16)


def low_and_maps(mine, theirs):
    return pl.pallas_call(
        low_kernel,
        out_shape=jax.ShapeDtypeStruct(mine.shape, jnp.bfloat16),
        compiler_params=params,
        cost_estimate=pl.CostEstimate(flops=1, bytes_accessed=1, transcendentals=0),
        name="low_and_maps",
    )(mine, theirs)


def softplus(value):
    small = jnp.exp(-jnp.abs(value))
    tail = jnp.where(small < 0.00390625, small * (1.0 - 0.5 * small), jnp.log(1.0 + small))
    return jnp.maximum(value, 0.0) + tail


def add_states(rates_ref, state_ref, total_ref, states, totals):
    state_ref[...] = jnp.exp2(rates_ref[...] * totals) * state_ref[...] + states
    total_ref[...] = total_ref[...] + totals


def sums_within(steps):
    rows = steps.shape[0]
    at = lax.broadcasted_iota(jnp.int32, (rows, rows), 0)
    of = lax.broadcasted_iota(jnp.int32, (rows, rows), 1)
    upto = jnp.where(of <= at, 1.0, 0.0).astype(jnp.bfloat16)
    return jnp.dot(upto, steps, preferred_element_type=jnp.float32)


def step_kernel(
    place_ref, stream_ref, low_ref, map_ref, cols_ref, bias_ref, rates_ref, *rest
):
    own_state_ref, own_total_ref = rest[:2]
    steps_ref, sums_ref, maps_ref, carry_ref, state_ref, total_ref, wide_ref, turn_ref = rest[3:]
    block = pl.program_id(0)
    rows, width = stream_ref.shape[1:]

    @pl.when(block == 0)
    def _():
        state_ref[...] = jnp.zeros_like(state_ref)
        total_ref[...] = jnp.zeros_like(total_ref)
        for n in range(NS):
            wide_ref[n * SUBLANES : (n + 1) * SUBLANES, :] = jnp.broadcast_to(
                rates_ref[n : n + 1, :], (SUBLANES, width)
            )

    @pl.when(block == place_ref[0] * CORES)
    def _():
        add_states(rates_ref, state_ref, total_ref, own_state_ref[...], own_total_ref[...])

    maps = map_ref[0].astype(jnp.float32)
    maps_ref[0] = maps
    logits = jnp.dot(low_ref[0], cols_ref[...], preferred_element_type=jnp.float32)
    steps = softplus(logits + bias_ref[...]).astype(jnp.bfloat16)
    steps_ref[...] = steps
    push = steps * stream_ref[0]
    within = sums_within(steps)
    sums_ref[...] = within.astype(jnp.bfloat16)
    whole = within[rows - 1 :, :]
    left = whole - within
    some, chunk, several = rows // 2, CORES * LANES, 4
    state_row = lax.broadcasted_iota(jnp.int32, (NS, some), 0)
    for first in range(0, rows, some):
        span = slice(first, first + some)
        chosen = [
            jnp.concatenate(
                [
                    jnp.where(state_row == m, maps[:NS, span], 0.0).astype(jnp.bfloat16)
                    for m in range(n, n + several)
                ],
                axis=1,
            )
            for n in range(0, NS, several)
        ]
        for item in range(width // chunk):
            lanes = slice(item * chunk, (item + 1) * chunk)
            left_here = left[span, lanes].reshape(some // SUBLANES, SUBLANES, chunk)
            push_here = push[span, lanes]
            added = state_ref[:, lanes]
            if first == 0:
                added = jnp.exp2(rates_ref[:, lanes] * whole[:, lanes]) * added
            for n in range(0, NS, several):
                pushed = []
                for m in range(n, n + several):
                    rate = wide_ref[m * SUBLANES : (m + 1) * SUBLANES, lanes]
                    decay = jnp.exp2(left_here * rate[None]).reshape(some, chunk)
                    pushed.append(decay.astype(jnp.bfloat16) * push_here)
                added = added + jnp.dot(
                    chosen[n // several],
                    jnp.concatenate(pushed, axis=0),
                    preferred_element_type=jnp.float32,
                )
            state_ref[:, lanes] = added
    total_ref[...] = total_ref[...] + whole

    count = pl.num_programs(0)

    @pl.when(block == count - 1)
    def _():
        @pl.when(place_ref[0] * CORES == count)
        def _():
            add_states(rates_ref, state_ref, total_ref, own_state_ref[...], own_total_ref[...])

        write_carry(carry_ref.at[0], state_ref[...], total_ref[...], turn_ref)
        for target in range(1, carry_ref.shape[0]):
            carry_ref[target] = carry_ref[0]


def step_sizes(place, stream, lows, cols, bias, rates, state, total, targets, after):
    others = stream.shape[0]
    chips = others + 1
    rows, width = stream.shape[1] // CORES, stream.shape[2]
    map_row = CORES * rows // MAPS
    blocks = others * CORES
    carry = (targets, (width // LANES + 1) * NS, LANES)

    def slot(b, s):
        chip = b // CORES
        return lax.rem(s[0] - jnp.where(chip < s[0], chip, chip + 1) + chips, chips) - 1

    def core(b):
        return lax.rem(b, CORES)

    def fixed(*shape):
        return pl.BlockSpec(shape, lambda b, s: (0,) * len(shape))

    return pl.pallas_call(
        step_kernel,
        grid_spec=pltpu.PrefetchScalarGridSpec(
            num_scalar_prefetch=1,
            grid=(blocks,),
            in_specs=[
                pl.BlockSpec((1, rows, width), lambda b, s: (slot(b, s), core(b), 0)),
                pl.BlockSpec((1, rows, RANK), lambda b, s: (slot(b, s), core(b), 0)),
                pl.BlockSpec((1, MAPS, rows), lambda b, s: (slot(b, s), map_row, core(b))),
                fixed(*cols.shape),
                fixed(*bias.shape),
                fixed(*rates.shape),
                fixed(*state.shape),
                fixed(*total.shape),
                pl.BlockSpec(memory_space=pl.ANY),
            ],
            out_specs=[
                pl.BlockSpec((rows, width), lambda b, s: (b, 0)),
                pl.BlockSpec((rows, width), lambda b, s: (b, 0)),
                pl.BlockSpec((1, 2 * NS, rows), lambda b, s: (b, 0, 0)),
                fixed(*carry),
            ],
            scratch_shapes=[
                pltpu.VMEM((NS, width), jnp.float32),
                pltpu.VMEM((1, width), jnp.float32),
                pltpu.VMEM((NS * SUBLANES, width), jnp.float32),
                pltpu.VMEM((SUBLANES, LANES), jnp.float32),
            ],
        ),
        out_shape=[
            jax.ShapeDtypeStruct((blocks * rows, width), jnp.bfloat16),
            jax.ShapeDtypeStruct((blocks * rows, width), jnp.bfloat16),
            jax.ShapeDtypeStruct((blocks, 2 * NS, rows), jnp.float32),
            jax.ShapeDtypeStruct(carry, jnp.bfloat16),
        ],
        compiler_params=params,
        name="step_sizes",
    )(place, stream, lows, lows, cols, bias, rates, state, total, after)


def write_carry(out_ref, state, total, turn_ref):
    tile = state.shape[1] // LANES
    turn_ref[...] = jnp.zeros_like(turn_ref)
    for item in range(tile):
        lanes = slice(item * LANES, (item + 1) * LANES)
        turn_ref[item : item + 1, :] = total[:, lanes]
        out_ref[item * NS : (item + 1) * NS, :] = state[:, lanes].astype(jnp.bfloat16)
    out_ref[tile * NS :, :] = jnp.concatenate(split(turn_ref[...]), axis=0)


def follow(carry_ref, rates_ref, state_ref):
    tile = state_ref.shape[1] // LANES
    sums = carry_ref[tile * NS :, :].astype(jnp.float32)
    sums = sums[:SUBLANES, :] + sums[SUBLANES:, :]
    for item in range(tile):
        lanes = slice(item * LANES, (item + 1) * LANES)
        decay = jnp.exp2(rates_ref[:, lanes] * sums[item : item + 1, :])
        added = carry_ref[item * NS : (item + 1) * NS, :].astype(jnp.float32)
        state_ref[:, lanes] = decay * state_ref[:, lanes] + added
    return sums


def scan_blocks(stream_ref, steps_ref, maps, rates_ref, gain_ref, out_ref, state_ref, work_refs):
    out_of_ref, *hist_refs = work_refs
    rows, width = steps_ref.shape
    source = lax.broadcasted_iota(jnp.int32, (LANES, NS * NS), 0)
    column = lax.rem(lax.broadcasted_iota(jnp.int32, (LANES, NS * NS), 1), NS)
    token = lax.rem(lax.broadcasted_iota(jnp.int32, (rows, NS * NS), 0), NS)
    slot = lax.broadcasted_iota(jnp.int32, (rows, NS * NS), 1) // NS
    turned = jnp.concatenate(
        [maps, jnp.zeros((LANES - 2 * NS, rows), jnp.float32)], axis=0
    ).T.astype(jnp.bfloat16)
    pick = jnp.where(source == NS + column, 1.0, 0.0).astype(jnp.bfloat16)
    spread = jnp.dot(turned, pick, preferred_element_type=jnp.float32)
    out_of_ref[...] = jnp.where(token == slot, spread, 0.0).astype(jnp.bfloat16)
    map_in = maps[:NS, :]
    half = width // 2

    def finish(first, hist_ref):
        here = pl.ds(first, NS)
        mixed = jnp.dot(out_of_ref[here, :], hist_ref[...], preferred_element_type=jnp.float32)
        direct = gain_ref[...] * stream_ref[0, here, :].astype(jnp.float32)
        out_ref[here, :] = (mixed + direct).astype(jnp.bfloat16)

    def advance(first, hist_ref):
        here = pl.ds(first, NS)
        into = pltpu.roll(map_in, lax.rem(rows - first, rows), 1)
        for lanes in (slice(0, half), slice(half, width)):
            state = state_ref[:, lanes]
            rates = rates_ref[:, lanes]
            steps = steps_ref[here, lanes].astype(jnp.float32)
            push = steps * stream_ref[0, here, lanes].astype(jnp.float32)
            for near in range(NS):
                this = slice(near, near + 1)
                state = jnp.exp2(rates * steps[this, :]) * state + into[:, this] * push[this, :]
                hist_ref[near * NS : (near + 1) * NS, lanes] = state.astype(jnp.bfloat16)
            state_ref[:, lanes] = state

    def at(group):
        return pl.multiple_of(group * NS, NS)

    def pair(index, nothing):
        finish(at(2 * index), hist_refs[1])
        advance(at(2 * index + 1), hist_refs[0])
        finish(at(2 * index + 1), hist_refs[0])
        advance(at(2 * index + 2), hist_refs[1])
        return nothing

    groups = rows // NS
    advance(0, hist_refs[1])
    lax.fori_loop(0, groups // 2 - 1, pair, 0)
    finish(rows - 2 * NS, hist_refs[1])
    advance(rows - NS, hist_refs[0])
    finish(rows - NS, hist_refs[0])


def work_shapes(rows, width):
    return [
        pltpu.VMEM((rows, NS * NS), jnp.bfloat16),
        pltpu.VMEM((NS * NS, width), jnp.bfloat16),
        pltpu.VMEM((NS * NS, width), jnp.bfloat16),
    ]


def own_kernel(
    stream_ref, low_ref, map_ref, cols_ref, bias_ref, rates_ref, gain_ref,
    out_ref, sums_ref, maps_ref, state_ref, total_ref, steps_ref, *work_refs
):
    rows = steps_ref.shape[0]

    @pl.when(pl.program_id(0) == 0)
    def _():
        state_ref[...] = jnp.zeros_like(state_ref)
        total_ref[...] = jnp.zeros_like(total_ref)

    maps = map_ref[...].astype(jnp.float32)
    maps_ref[0] = maps
    logits = jnp.dot(low_ref[...], cols_ref[...], preferred_element_type=jnp.float32)
    steps = softplus(logits + bias_ref[...]).astype(jnp.bfloat16)
    steps_ref[...] = steps
    within = sums_within(steps)
    sums_ref[...] = within.astype(jnp.bfloat16)
    total_ref[...] = total_ref[...] + within[rows - 1 :, :]
    scan_blocks(stream_ref, steps_ref, maps, rates_ref, gain_ref, out_ref, state_ref, work_refs)


def scan_own(stream, lows, cols, bias, rates, gain):
    rows, width = stream.shape[1] // CORES, stream.shape[2]
    map_row = CORES * rows // MAPS

    def fixed(*shape):
        return pl.BlockSpec(shape, lambda b: (0,) * len(shape))

    block = pl.BlockSpec((rows, width), lambda b: (b, 0))
    return pl.pallas_call(
        own_kernel,
        grid=(CORES,),
        in_specs=[
            pl.BlockSpec((1, rows, width), lambda b: (0, b, 0)),
            pl.BlockSpec((rows, RANK), lambda b: (b, 0)),
            pl.BlockSpec((MAPS, rows), lambda b: (map_row, b)),
            fixed(*cols.shape),
            fixed(*bias.shape),
            fixed(*rates.shape),
            fixed(*gain.shape),
        ],
        out_specs=[
            block,
            block,
            pl.BlockSpec((1, 2 * NS, rows), lambda b: (b, 0, 0)),
            fixed(NS, width),
            fixed(1, width),
        ],
        out_shape=[
            jax.ShapeDtypeStruct((CORES * rows, width), jnp.bfloat16),
            jax.ShapeDtypeStruct((CORES * rows, width), jnp.bfloat16),
            jax.ShapeDtypeStruct((CORES, 2 * NS, rows), jnp.float32),
            jax.ShapeDtypeStruct((NS, width), jnp.float32),
            jax.ShapeDtypeStruct((1, width), jnp.float32),
        ],
        scratch_shapes=[pltpu.VMEM((rows, width), jnp.bfloat16)] + work_shapes(rows, width),
        compiler_params=params,
        cost_estimate=pl.CostEstimate(flops=4 * 10**9, bytes_accessed=1 << 21, transcendentals=0),
        name="scan_own",
    )(stream, lows, lows, cols, bias, rates, gain)


def others_kernel(
    place_ref, stream_ref, steps_ref, maps_ref, rates_ref, gain_ref, out_ref, last_ref, *work_refs
):
    @pl.when(lax.rem(pl.program_id(0), CORES) == 0)
    def _():
        last_ref[...] = jnp.zeros_like(last_ref)

    scan_blocks(
        stream_ref, steps_ref, maps_ref[0], rates_ref, gain_ref, out_ref, last_ref.at[0], work_refs
    )


def scan_others(place, stream, steps, maps, rates, gain):
    others = stream.shape[0]
    chips = others + 1
    rows, width = stream.shape[1] // CORES, stream.shape[2]

    def slot(b, s):
        chip = b // CORES
        return lax.rem(s[0] - jnp.where(chip < s[0], chip, chip + 1) + chips, chips) - 1

    def fixed(*shape):
        return pl.BlockSpec(shape, lambda b, s: (0,) * len(shape))

    block = pl.BlockSpec((rows, width), lambda b, s: (b, 0))
    return pl.pallas_call(
        others_kernel,
        grid_spec=pltpu.PrefetchScalarGridSpec(
            num_scalar_prefetch=1,
            grid=(others * CORES,),
            in_specs=[
                pl.BlockSpec((1, rows, width), lambda b, s: (slot(b, s), lax.rem(b, CORES), 0)),
                block,
                pl.BlockSpec((1, 2 * NS, rows), lambda b, s: (b, 0, 0)),
                fixed(*rates.shape),
                fixed(*gain.shape),
            ],
            out_specs=[block, pl.BlockSpec((1, NS, width), lambda b, s: (b // CORES, 0, 0))],
            scratch_shapes=work_shapes(rows, width),
        ),
        out_shape=[
            jax.ShapeDtypeStruct((others * CORES * rows, width), jnp.bfloat16),
            jax.ShapeDtypeStruct((others, NS, width), jnp.float32),
        ],
        compiler_params=params,
        cost_estimate=pl.CostEstimate(flops=4 * 10**9, bytes_accessed=1 << 21, transcendentals=0),
        name="scan_others",
    )(place, stream, steps, maps, rates, gain)


def carried_kernel(
    places_ref, part_own_ref, part_come_ref, sums_own_ref, sums_come_ref,
    maps_own_ref, maps_come_ref, last_own_ref, last_come_ref, rates_ref, carries_ref,
    out_ref, state_ref, wide_ref, begin_ref, spread_ref, sums_ref,
):
    block = pl.program_id(0)
    rows, width = out_ref.shape
    chip = block // CORES
    here = chip == places_ref[0]

    @pl.when(block == 0)
    def _():
        state_ref[...] = jnp.zeros_like(state_ref)

        def compose(row, nothing):
            follow(carries_ref.at[row], rates_ref, state_ref)
            return nothing

        lax.fori_loop(0, places_ref[1], compose, 0)
        for n in range(NS):
            wide_ref[n * NS : (n + 1) * NS, :] = jnp.broadcast_to(
                rates_ref[n : n + 1, :], (NS, width)
            ).astype(jnp.bfloat16)

    @pl.when((block > 0) & (lax.rem(block, CORES) == 0))
    def _():
        before = jnp.where(chip - 1 == places_ref[0], last_own_ref[...], last_come_ref[0])
        state_ref[...] = state_ref[...] + before

    state = state_ref[...]
    for n in range(NS):
        begin_ref[n * NS : (n + 1) * NS, :] = jnp.broadcast_to(
            state[n : n + 1, :], (NS, width)
        ).astype(jnp.bfloat16)
    maps = jnp.where(here, maps_own_ref[0], maps_come_ref[0])
    maps = jnp.concatenate([maps, jnp.zeros((LANES - 2 * NS, rows), jnp.float32)], axis=0).T
    for n in range(NS):
        spread_ref[:, n * LANES : (n + 1) * LANES] = jnp.broadcast_to(
            maps[:, NS + n : NS + n + 1], (rows, LANES)
        ).astype(jnp.bfloat16)
    sums = jnp.where(here, sums_own_ref[...], sums_come_ref[...])
    sums_ref[...] = sums
    last = sums[rows - NS :, :].astype(jnp.float32)[NS - 1 :, :]
    state_ref[...] = jnp.exp2(rates_ref[...] * last) * state
    chunk, several = CORES * LANES, 4

    def some(index, nothing):
        near = pl.ds(pl.multiple_of(index * NS, NS), NS)
        for item in range(width // chunk):
            lanes = slice(item * chunk, (item + 1) * chunk)
            part = jnp.where(here, part_own_ref[near, lanes], part_come_ref[near, lanes])
            total = part.astype(jnp.float32)
            sums = sums_ref[near, lanes]
            for first in range(0, NS, several):
                terms = []
                for n in range(first, first + several):
                    decay = jnp.exp2(sums * wide_ref[n * NS : (n + 1) * NS, lanes])
                    out_of = spread_ref[near, n * LANES : (n + 1) * LANES]
                    out_of = jnp.concatenate([out_of] * (chunk // LANES), axis=1)
                    terms.append(decay * begin_ref[n * NS : (n + 1) * NS, lanes] * out_of)
                four = (terms[0] + terms[1]) + (terms[2] + terms[3])
                total = total + four.astype(jnp.float32)
            out_ref[near, lanes] = total.astype(jnp.bfloat16)
        return nothing

    lax.fori_loop(0, rows // NS, some, 0)


def add_carried(places, parts, sums, maps, lasts, rates, carries):
    blocks_come, _, rows = maps[1].shape
    chips = blocks_come // CORES + 1
    width = rates.shape[1]

    def core(b):
        return lax.rem(b, CORES)

    def order(b, s):
        chip = b // CORES
        return jnp.minimum(
            jnp.where(chip < s[0], b, jnp.maximum(b - CORES, 0)), blocks_come - 1
        )

    def before(b, s):
        chip = jnp.maximum(b // CORES - 1, 0)
        return jnp.minimum(jnp.where(chip < s[0], chip, jnp.maximum(chip - 1, 0)), chips - 2)

    def fixed(*shape):
        return pl.BlockSpec(shape, lambda b, s: (0,) * len(shape))

    own = pl.BlockSpec((rows, width), lambda b, s: (core(b), 0))
    come = pl.BlockSpec((rows, width), lambda b, s: (order(b, s), 0))
    return pl.pallas_call(
        carried_kernel,
        grid_spec=pltpu.PrefetchScalarGridSpec(
            num_scalar_prefetch=1,
            grid=(chips * CORES,),
            in_specs=[
                own,
                come,
                own,
                come,
                pl.BlockSpec((1, 2 * NS, rows), lambda b, s: (core(b), 0, 0)),
                pl.BlockSpec((1, 2 * NS, rows), lambda b, s: (order(b, s), 0, 0)),
                fixed(NS, width),
                pl.BlockSpec((1, NS, width), lambda b, s: (before(b, s), 0, 0)),
                fixed(*rates.shape),
                fixed(*carries.shape),
            ],
            out_specs=pl.BlockSpec((rows, width), lambda b, s: (b, 0)),
            scratch_shapes=[
                pltpu.VMEM((NS, width), jnp.float32),
                pltpu.VMEM((NS * NS, width), jnp.bfloat16),
                pltpu.VMEM((NS * NS, width), jnp.bfloat16),
                pltpu.VMEM((rows, NS * LANES), jnp.bfloat16),
                pltpu.VMEM((rows, width), jnp.bfloat16),
            ],
        ),
        out_shape=jax.ShapeDtypeStruct((chips * CORES * rows, width), jnp.bfloat16),
        compiler_params=params,
        name="add_carried",
    )(places, *parts, *sums, *maps, *lasts, rates, carries)


def local(
    queries, keys, values, doc_lengths, rank_in, bc_weight, rank_out, dt_bias, a_log, skip_gain
):
    devices = lax.axis_size("seq")
    chips = devices // CORES
    targets = lax.axis_size("chan")
    seq_place = lax.axis_index("seq").astype(jnp.int32)
    chan_place = lax.axis_index("chan").astype(jnp.int32)
    chip, core = seq_place // CORES, lax.rem(seq_place, CORES)
    place = jnp.stack([chip, core])
    width = queries.shape[2] // devices
    wide = max(HEAD_SIZE, keys.shape[2] // devices)

    def other(device):
        return device + 1 - 2 * (device % CORES)

    swap = [(device, other(device)) for device in range(devices)]
    near = [(device, device + CORES) for device in range(devices - CORES)]
    far = [(device, other(device + CORES)) for device in range(devices - CORES)]

    def onward(chips_on):
        return [(device, (device + chips_on * CORES) % devices) for device in range(devices)]

    own, theirs = select_heads(keys[0], values[0], chips, wide)
    from_near = lax.ppermute(own, "seq", near)
    from_far = lax.ppermute(theirs, "seq", far)
    swapped = lax.ppermute(theirs, "seq", swap)
    queries_after, _ = lax.optimization_barrier((queries[0], own))
    their_queries = lax.ppermute(queries_after, "seq", swap)
    blocks = (own, swapped, from_near, from_far)

    first = seq_place * width
    logs = lax.dynamic_slice_in_dim(a_log, first, width, 0)
    rates = (-LOG2E * jnp.exp(logs)).T
    cols = lax.dynamic_slice_in_dim(rank_out, first, width, 1)
    bias = lax.dynamic_slice_in_dim(dt_bias, first, width, 0)[None]
    gain = lax.dynamic_slice_in_dim(skip_gain, first, width, 0)[None]

    sent, stayed, part = attend(
        place, doc_lengths, (queries[0], their_queries), blocks, rank_in, bc_weight.T,
        (rates, cols, bias, gain),
    )
    come = [lax.ppermute(sent[step], "seq", onward(step + 1)) for step in range(chips - 1)]
    low_own = low_and_maps(part, lax.ppermute(part, "seq", swap))
    low_come = [lax.ppermute(low_own, "seq", onward(step + 1)) for step in range(chips - 1)]
    got_sent = lax.ppermute(sent, "seq", swap)
    got_stayed = lax.ppermute(stayed, "seq", swap)
    attn_rows = join_heads(sent, stayed, got_sent, got_stayed)

    part_own, sums_own, maps_own, state, total = scan_own(stayed, low_own, cols, bias, rates, gain)
    come, low_come = jnp.stack(come), jnp.stack(low_come)
    steps, sums_come, maps_come, carry = step_sizes(
        place, come, low_come, cols, bias, rates, state, total, targets, attn_rows
    )
    carries = lax.all_to_all(carry, "chan", split_axis=0, concat_axis=0, tiled=True)
    part_come, last_come = scan_others(place, come, steps, maps_come, rates, gain)
    ssm_rows = add_carried(
        jnp.stack([chip, chan_place]), (part_own, part_come), (sums_own, sums_come),
        (maps_own, maps_come), (state, last_come), rates, carries,
    )
    return (attn_rows[None], ssm_rows[None])


def solution(mesh):
    return jax.shard_map(
        local,
        mesh=mesh,
        in_specs=(
            P("chan", "seq", None),
            P("chan", "seq", None),
            P("chan", "seq", None),
            P("chan", None),
            P(),
            P(),
            P(),
            P(),
            P(),
            P(),
        ),
        out_specs=(P("chan", "seq", None), P("chan", None, "seq")),
        check_vma=False,
    )
```

```python
import functools
import math

import jax
import jax.numpy as jnp
from jax import lax
from jax.experimental import pallas as pl
from jax.experimental.pallas import tpu as pltpu
from jax.sharding import PartitionSpec as P

QUERY_HEADS = 32
KEY_VALUE_HEADS = 8
HEAD_SIZE = 128
GROUP = QUERY_HEADS // KEY_VALUE_HEADS
NS = 16
RANK = 256
CORES = 2
LANES = 128
SUBLANES = 8
MAPS = 2 * NS
LOG2E = 1.4426950408889634

masked_fill = -1e30
params = pltpu.CompilerParams(vmem_limit_bytes=60 << 20)


def split(value):
    coarse = value.astype(jnp.bfloat16)
    return coarse, (value - coarse.astype(jnp.float32)).astype(jnp.bfloat16)


def run_copies(pairs, sems):
    copies = [
        pltpu.make_async_copy(source, target, sems.at[i]) for i, (source, target) in enumerate(pairs)
    ]
    for copy in copies:
        copy.start()
    for copy in copies:
        copy.wait()


def columns_of(ref, index, size):
    return ref.at[:, pl.ds(pl.multiple_of(index * size, LANES), size)]


def heads_kernel(key_ref, value_ref, own_ref, their_ref, sems):
    core = lax.rem(lax.axis_index("seq"), CORES)
    wide = own_ref.shape[3]
    halves = key_ref.shape[1] // wide // own_ref.shape[0]
    pairs = []
    for target, which in ((own_ref, core), (their_ref, 1 - core)):
        for chip in range(own_ref.shape[0]):
            index = chip * halves + (which if halves == CORES else 0)
            for kind, source in enumerate((key_ref, value_ref)):
                pairs.append((columns_of(source, index, wide), target.at[chip, kind]))
    run_copies(pairs, sems)


def select_heads(keys, values, chips, wide):
    shape = jax.ShapeDtypeStruct((chips, 2, keys.shape[0], wide), keys.dtype)
    return pl.pallas_call(
        heads_kernel,
        in_specs=[pl.BlockSpec(memory_space=pl.ANY)] * 2,
        out_shape=[shape, shape],
        scratch_shapes=[pltpu.SemaphoreType.DMA((4 * chips,))],
        compiler_params=params,
        name="select_heads",
    )(keys, values)


def join_kernel(sent_ref, stayed_ref, got_sent_ref, got_stayed_ref, out_ref, sems):
    place = lax.axis_index("seq")
    core, chip = lax.rem(place, CORES), place // CORES
    rows = out_ref.shape[0]
    others, _, width = sent_ref.shape
    here = pl.ds(pl.multiple_of(core * rows, rows), rows)
    pairs = []
    for first, rest, which in (
        (stayed_ref, sent_ref, core), (got_stayed_ref, got_sent_ref, 1 - core)
    ):
        for step in range(others + 1):
            source = first.at[0, here, :] if step == 0 else rest.at[step - 1, here, :]
            owner = lax.rem(chip + step, others + 1)
            pairs.append((source, columns_of(out_ref, owner * CORES + which, width)))
    run_copies(pairs, sems)


def join_heads(sent, stayed, got_sent, got_stayed):
    others, rows, width = sent.shape
    return pl.pallas_call(
        join_kernel,
        in_specs=[pl.BlockSpec(memory_space=pl.ANY)] * 4,
        out_shape=jax.ShapeDtypeStruct(
            (rows // CORES, (others + 1) * CORES * width), sent.dtype
        ),
        scratch_shapes=[pltpu.SemaphoreType.DMA((CORES * (others + 1),))],
        compiler_params=params,
        name="join_heads",
    )(sent, stayed, got_sent, got_stayed)


def attend_kernel(
    place_ref, doc_ref, mine_ref, theirs_ref, own_ref, swap_ref, near_ref, far_ref,
    rank_ref, map_ref, *rest, chips,
):
    send_ref, stay_ref, part_ref, mask_ref = rest[-4:]
    step = pl.program_id(0)
    rows = mine_ref.shape[0]
    group = mine_ref.shape[1] // HEAD_SIZE
    chip, core = place_ref[0], place_ref[1]
    first_core = core == 0

    def above(shape):
        row = lax.rem(lax.broadcasted_iota(jnp.int32, shape, 0), rows)
        return lax.broadcasted_iota(jnp.int32, shape, 1) > row

    @pl.when(step == 0)
    def _():
        part_ref[...] = jnp.zeros_like(part_ref)
        own = chip * CORES + core
        swapped = chip * CORES + 1 - core
        near, far = own - CORES, swapped - CORES
        lane = lax.broadcasted_iota(jnp.int32, (rows, rows), 1)
        row = lax.broadcasted_iota(jnp.int32, (rows, rows), 0)
        for item, (place, before, middle) in enumerate(
            (
                (own, near, jnp.where(first_core, far, swapped)),
                (swapped, far, jnp.where(first_core, own, near)),
            )
        ):
            query_pos = place * rows + row
            start = jnp.zeros((rows, rows), jnp.int32)
            bound = jnp.int32(0)
            for doc in range(doc_ref.shape[1]):
                bound = bound + doc_ref[0, doc]
                start = jnp.where(query_pos >= bound, bound, start)
            ends = jnp.where(lane > row, before, place) * rows + lane
            mask_ref[item, :, :rows] = jnp.where(
                (ends >= start) & (ends <= query_pos), 0.0, masked_fill
            )
            mask_ref[item, :, rows:] = jnp.where(
                middle * rows + lane >= start, 0.0, masked_fill
            )

    scale = LOG2E / math.sqrt(HEAD_SIZE)
    ones = jnp.ones((3 * rows, HEAD_SIZE), jnp.bfloat16)

    def windows(kind):
        own, swapped = own_ref[0, kind], swap_ref[0, kind]
        near, far = near_ref[0, kind], far_ref[0, kind]
        return (
            jnp.concatenate([near, own, jnp.where(first_core, far, swapped)], axis=0),
            jnp.concatenate([far, swapped, jnp.where(first_core, own, near)], axis=0),
        )

    scores = []
    for keys, query in zip(windows(0), (mine_ref[...], theirs_ref[...])):
        stacked = jnp.concatenate(
            [query[:, i * HEAD_SIZE : (i + 1) * HEAD_SIZE] for i in range(group)], axis=0
        )
        scores.append(
            lax.dot_general(
                stacked, keys, (((1,), (1,)), ((), ())), preferred_element_type=jnp.float32
            )
        )
    outputs = []
    before = above((group * rows, rows))
    for item, (values, score) in enumerate(zip(windows(1), scores)):
        fill = mask_ref[item]
        ends = jnp.where(before, score[:, :rows], score[:, rows : 2 * rows])
        kept = jnp.concatenate([ends, score[:, 2 * rows :]], axis=1)
        kept = jnp.concatenate(
            [kept[i * rows : (i + 1) * rows, :] + fill for i in range(group)], axis=0
        )
        peak = jnp.max(kept, axis=1, keepdims=True)
        raw = jnp.exp2((kept - peak) * scale).astype(jnp.bfloat16)
        ends = raw[:, :rows]
        none = jnp.zeros_like(ends)
        spread = jnp.concatenate(
            [jnp.where(before, ends, none), jnp.where(before, none, ends), raw[:, rows:]], axis=1
        )
        both = jnp.dot(
            spread, jnp.concatenate([values, ones], axis=1), preferred_element_type=jnp.float32
        )
        mixed = both[:, :HEAD_SIZE] * pl.reciprocal(both[:, HEAD_SIZE:])
        mixed = mixed.astype(jnp.bfloat16)
        outputs.append(
            jnp.concatenate([mixed[i * rows : (i + 1) * rows, :] for i in range(group)], axis=1)
        )
    stream = jnp.concatenate(
        [
            jnp.where(first_core, outputs[0], outputs[1]),
            jnp.where(first_core, outputs[1], outputs[0]),
        ],
        axis=0,
    )
    last = step >= pl.num_programs(0) - pl.num_programs(0) // chips

    @pl.when(last)
    def _():
        stay_ref[0] = stream

    @pl.when(jnp.logical_not(last))
    def _():
        send_ref[0] = stream

    both = CORES * rows
    part_ref[:both, :] += jnp.dot(stream, rank_ref[...], preferred_element_type=jnp.float32)
    part_ref[both:, :] += lax.dot_general(
        map_ref[...], stream, (((1,), (1,)), ((), ())), preferred_element_type=jnp.float32
    )


def attend(place, doc_lengths, queries, blocks, rank_in, map_rows, after):
    mine, theirs = queries
    chips, _, rows, columns = blocks[0].shape
    heads = columns // HEAD_SIZE
    width = mine.shape[1] // (chips * CORES)
    wide = width // heads

    def owner(j, s):
        return lax.rem(s[0] + 1 + j // heads, chips)

    def column(j, s):
        return (owner(j, s) * CORES + s[1]) * heads + lax.rem(j, heads)

    def sent(j, s):
        at = jnp.minimum(j, (chips - 1) * heads - 1)
        return (at // heads, 0, lax.rem(at, heads))

    query = pl.BlockSpec((rows, wide), lambda j, s: (0, column(j, s)))
    block = pl.BlockSpec(
        (1, 2, rows, HEAD_SIZE), lambda j, s: (owner(j, s), 0, 0, lax.rem(j, heads))
    )
    return pl.pallas_call(
        functools.partial(attend_kernel, chips=chips),
        grid_spec=pltpu.PrefetchScalarGridSpec(
            num_scalar_prefetch=1,
            grid=(chips * heads,),
            in_specs=[pl.BlockSpec(memory_space=pltpu.SMEM), query, query]
            + [block] * 4
            + [
                pl.BlockSpec((wide, RANK), lambda j, s: (column(j, s), 0)),
                pl.BlockSpec((2 * NS, wide), lambda j, s: (0, column(j, s))),
            ]
            + [pl.BlockSpec(memory_space=pl.ANY)] * len(after),
            out_specs=[
                pl.BlockSpec((1, CORES * rows, wide), sent),
                pl.BlockSpec(
                    (1, CORES * rows, wide),
                    lambda j, s: (0, 0, jnp.maximum(j - (chips - 1) * heads, 0)),
                ),
                pl.BlockSpec((CORES * rows + 2 * NS, RANK), lambda j, s: (0, 0)),
            ],
            scratch_shapes=[pltpu.VMEM((2, rows, 2 * rows), jnp.float32)],
        ),
        out_shape=[
            jax.ShapeDtypeStruct((chips - 1, CORES * rows, width), jnp.bfloat16),
            jax.ShapeDtypeStruct((1, CORES * rows, width), jnp.bfloat16),
            jax.ShapeDtypeStruct((CORES * rows + 2 * NS, RANK), jnp.float32),
        ],
        compiler_params=params,
        cost_estimate=pl.CostEstimate(flops=5 * 10**9, bytes_accessed=1 << 22, transcendentals=0),
        name="attend",
    )(place, doc_lengths, mine, theirs, *blocks, rank_in, map_rows, *after)


def low_kernel(mine_ref, theirs_ref, out_ref):
    out_ref[...] = (mine_ref[...] + theirs_ref[...]).astype(jnp.bfloat16)


def low_and_maps(mine, theirs):
    return pl.pallas_call(
        low_kernel,
        out_shape=jax.ShapeDtypeStruct(mine.shape, jnp.bfloat16),
        compiler_params=params,
        cost_estimate=pl.CostEstimate(flops=1, bytes_accessed=1, transcendentals=0),
        name="low_and_maps",
    )(mine, theirs)


def softplus(value):
    small = jnp.exp(-jnp.abs(value))
    tail = jnp.where(small < 0.00390625, small * (1.0 - 0.5 * small), jnp.log(1.0 + small))
    return jnp.maximum(value, 0.0) + tail


def add_states(rates_ref, state_ref, total_ref, states, totals):
    state_ref[...] = jnp.exp2(rates_ref[...] * totals) * state_ref[...] + states
    total_ref[...] = total_ref[...] + totals


def sums_within(steps):
    rows = steps.shape[0]
    at = lax.broadcasted_iota(jnp.int32, (rows, rows), 0)
    of = lax.broadcasted_iota(jnp.int32, (rows, rows), 1)
    upto = jnp.where(of <= at, 1.0, 0.0).astype(jnp.bfloat16)
    return jnp.dot(upto, steps, preferred_element_type=jnp.float32)


def write_carry(out_ref, state, total, turn_ref):
    tile = state.shape[1] // LANES
    turn_ref[...] = jnp.zeros_like(turn_ref)
    for item in range(tile):
        lanes = slice(item * LANES, (item + 1) * LANES)
        turn_ref[item : item + 1, :] = total[:, lanes]
        out_ref[item * NS : (item + 1) * NS, :] = state[:, lanes].astype(jnp.bfloat16)
    out_ref[tile * NS :, :] = jnp.concatenate(split(turn_ref[...]), axis=0)


def follow(carry_ref, rates_ref, state_ref):
    tile = state_ref.shape[1] // LANES
    sums = carry_ref[tile * NS :, :].astype(jnp.float32)
    sums = sums[:SUBLANES, :] + sums[SUBLANES:, :]
    for item in range(tile):
        lanes = slice(item * LANES, (item + 1) * LANES)
        decay = jnp.exp2(rates_ref[:, lanes] * sums[item : item + 1, :])
        added = carry_ref[item * NS : (item + 1) * NS, :].astype(jnp.float32)
        state_ref[:, lanes] = decay * state_ref[:, lanes] + added
    return sums


def scan_blocks(stream_ref, steps_ref, maps, rates_ref, gain_ref, out_ref, state_ref, work_refs):
    out_of_ref, *hist_refs = work_refs
    rows, width = steps_ref.shape
    source = lax.broadcasted_iota(jnp.int32, (LANES, NS * NS), 0)
    column = lax.rem(lax.broadcasted_iota(jnp.int32, (LANES, NS * NS), 1), NS)
    token = lax.rem(lax.broadcasted_iota(jnp.int32, (rows, NS * NS), 0), NS)
    slot = lax.broadcasted_iota(jnp.int32, (rows, NS * NS), 1) // NS
    turned = jnp.concatenate(
        [maps, jnp.zeros((LANES - 2 * NS, rows), jnp.float32)], axis=0
    ).T.astype(jnp.bfloat16)
    pick = jnp.where(source == NS + column, 1.0, 0.0).astype(jnp.bfloat16)
    spread = jnp.dot(turned, pick, preferred_element_type=jnp.float32)
    out_of_ref[...] = jnp.where(token == slot, spread, 0.0).astype(jnp.bfloat16)
    map_in = maps[:NS, :]
    half = width // 2

    def finish(first, hist_ref):
        here = pl.ds(first, NS)
        mixed = jnp.dot(out_of_ref[here, :], hist_ref[...], preferred_element_type=jnp.float32)
        direct = gain_ref[...] * stream_ref[0, here, :].astype(jnp.float32)
        out_ref[here, :] = (mixed + direct).astype(jnp.bfloat16)

    def advance(first, hist_ref):
        here = pl.ds(first, NS)
        into = pltpu.roll(map_in, lax.rem(rows - first, rows), 1)
        for lanes in (slice(0, half), slice(half, width)):
            state = state_ref[:, lanes]
            rates = rates_ref[:, lanes]
            steps = steps_ref[here, lanes].astype(jnp.float32)
            push = steps * stream_ref[0, here, lanes].astype(jnp.float32)
            for near in range(NS):
                this = slice(near, near + 1)
                state = jnp.exp2(rates * steps[this, :]) * state + into[:, this] * push[this, :]
                hist_ref[near * NS : (near + 1) * NS, lanes] = state.astype(jnp.bfloat16)
            state_ref[:, lanes] = state

    def at(group):
        return pl.multiple_of(group * NS, NS)

    def pair(index, nothing):
        finish(at(2 * index), hist_refs[1])
        advance(at(2 * index + 1), hist_refs[0])
        finish(at(2 * index + 1), hist_refs[0])
        advance(at(2 * index + 2), hist_refs[1])
        return nothing

    groups = rows // NS
    advance(0, hist_refs[1])
    lax.fori_loop(0, groups // 2 - 1, pair, 0)
    finish(rows - 2 * NS, hist_refs[1])
    advance(rows - NS, hist_refs[0])
    finish(rows - NS, hist_refs[0])


def work_shapes(rows, width):
    return [
        pltpu.VMEM((rows, NS * NS), jnp.bfloat16),
        pltpu.VMEM((NS * NS, width), jnp.bfloat16),
        pltpu.VMEM((NS * NS, width), jnp.bfloat16),
    ]


def tokens_kernel(
    place_ref, stream_ref, low_ref, map_ref, cols_ref, bias_ref, rates_ref, gain_ref, *rest, carried
):
    if carried:
        own_last_ref, own_total_ref, _, *rest = rest
    out_ref, sums_ref, maps_ref, last_ref, total_ref, *rest = rest
    if carried:
        carry_ref, *rest = rest
    steps_ref, run_state_ref, run_total_ref, turn_ref, *work_refs = rest
    block = pl.program_id(0)
    rows = steps_ref.shape[0]
    first_core = lax.rem(block, CORES) == 0

    @pl.when(first_core)
    def _():
        last_ref[...] = jnp.zeros_like(last_ref)
        total_ref[...] = jnp.zeros_like(total_ref)

    def place_own():
        add_states(rates_ref, run_state_ref, run_total_ref, own_last_ref[0], own_total_ref[0])

    if carried:

        @pl.when(block == 0)
        def _():
            run_state_ref[...] = jnp.zeros_like(run_state_ref)
            run_total_ref[...] = jnp.zeros_like(run_total_ref)

        pl.when(block == place_ref[0] * CORES)(place_own)

    maps = map_ref[0].astype(jnp.float32)
    maps_ref[0] = maps
    logits = jnp.dot(low_ref[0], cols_ref[...], preferred_element_type=jnp.float32)
    steps = softplus(logits + bias_ref[...]).astype(jnp.bfloat16)
    steps_ref[...] = steps
    within = sums_within(steps)
    sums_ref[...] = within.astype(jnp.bfloat16)
    total_ref[0] = total_ref[0] + within[rows - 1 :, :]
    scan_blocks(
        stream_ref, steps_ref, maps, rates_ref, gain_ref, out_ref, last_ref.at[0], work_refs
    )
    if carried:
        count = pl.num_programs(0)

        @pl.when(jnp.logical_not(first_core))
        def _():
            add_states(rates_ref, run_state_ref, run_total_ref, last_ref[0], total_ref[0])

        @pl.when(block == count - 1)
        def _():
            pl.when(place_ref[0] * CORES == count)(place_own)
            write_carry(carry_ref.at[0], run_state_ref[...], run_total_ref[...], turn_ref)
            for target in range(1, carry_ref.shape[0]):
                carry_ref[target] = carry_ref[0]


def scan_tokens(place, stream, lows, cols, bias, rates, gain, own, targets, after):
    count = stream.shape[0]
    chips = count + 1
    rows, width = stream.shape[1] // CORES, stream.shape[2]
    map_row = CORES * rows // MAPS
    blocks = count * CORES
    carried = own is not None
    carry = (targets, (width // LANES + 1) * NS, LANES)

    def slot(b, s):
        chip = b // CORES
        if not carried:
            return chip
        return lax.rem(s[0] - jnp.where(chip < s[0], chip, chip + 1) + chips, chips) - 1

    def core(b):
        return lax.rem(b, CORES)

    def fixed(*shape):
        return pl.BlockSpec(shape, lambda b, s: (0,) * len(shape))

    block = pl.BlockSpec((rows, width), lambda b, s: (b, 0))
    in_specs = [
        pl.BlockSpec((1, rows, width), lambda b, s: (slot(b, s), core(b), 0)),
        pl.BlockSpec((1, rows, RANK), lambda b, s: (slot(b, s), core(b), 0)),
        pl.BlockSpec((1, MAPS, rows), lambda b, s: (slot(b, s), map_row, core(b))),
        fixed(*cols.shape),
        fixed(*bias.shape),
        fixed(*rates.shape),
        fixed(*gain.shape),
    ]
    out_specs = [
        block,
        block,
        pl.BlockSpec((1, 2 * NS, rows), lambda b, s: (b, 0, 0)),
        pl.BlockSpec((1, NS, width), lambda b, s: (b // CORES, 0, 0)),
        pl.BlockSpec((1, 1, width), lambda b, s: (b // CORES, 0, 0)),
    ]
    out_shape = [
        jax.ShapeDtypeStruct((blocks * rows, width), jnp.bfloat16),
        jax.ShapeDtypeStruct((blocks * rows, width), jnp.bfloat16),
        jax.ShapeDtypeStruct((blocks, 2 * NS, rows), jnp.float32),
        jax.ShapeDtypeStruct((count, NS, width), jnp.float32),
        jax.ShapeDtypeStruct((count, 1, width), jnp.float32),
    ]
    more = []
    if carried:
        more = [*own, after]
        in_specs += [fixed(1, NS, width), fixed(1, 1, width), pl.BlockSpec(memory_space=pl.ANY)]
        out_specs.append(fixed(*carry))
        out_shape.append(jax.ShapeDtypeStruct(carry, jnp.bfloat16))
    return pl.pallas_call(
        functools.partial(tokens_kernel, carried=carried),
        grid_spec=pltpu.PrefetchScalarGridSpec(
            num_scalar_prefetch=1,
            grid=(blocks,),
            in_specs=in_specs,
            out_specs=out_specs,
            scratch_shapes=[
                pltpu.VMEM((rows, width), jnp.bfloat16),
                pltpu.VMEM((NS, width), jnp.float32),
                pltpu.VMEM((1, width), jnp.float32),
                pltpu.VMEM((SUBLANES, LANES), jnp.float32),
            ]
            + work_shapes(rows, width),
        ),
        out_shape=out_shape,
        compiler_params=params,
        cost_estimate=pl.CostEstimate(flops=4 * 10**9, bytes_accessed=1 << 21, transcendentals=0),
        name="scan_tokens",
    )(place, stream, lows, lows, cols, bias, rates, gain, *more)


def write_rates(wide_ref, rates_ref):
    width = rates_ref.shape[1]
    for n in range(NS):
        wide_ref[n * NS : (n + 1) * NS, :] = jnp.broadcast_to(
            rates_ref[n : n + 1, :], (NS, width)
        ).astype(jnp.bfloat16)


def write_spread(spread_ref, maps):
    rows = maps.shape[1]
    maps = jnp.concatenate([maps, jnp.zeros((LANES - 2 * NS, rows), jnp.float32)], axis=0).T
    for n in range(NS):
        spread_ref[:, n * LANES : (n + 1) * LANES] = jnp.broadcast_to(
            maps[:, NS + n : NS + n + 1], (rows, LANES)
        ).astype(jnp.bfloat16)


def factor(sums, wide_ref, spread_ref, near, n, lanes):
    out_of = spread_ref[near, n * LANES : (n + 1) * LANES]
    copies = (lanes.stop - lanes.start) // LANES
    decay = jnp.exp2(sums * wide_ref[n * NS : (n + 1) * NS, lanes])
    return decay * jnp.concatenate([out_of] * copies, axis=1)


def factors_kernel(sums_ref, maps_ref, rates_ref, out_ref, wide_ref, spread_ref):
    rows, width = sums_ref.shape
    step = pl.program_id(0)
    parts = spread_ref.shape[0] // rows

    @pl.when(step == 0)
    def _():
        write_rates(wide_ref, rates_ref)

    @pl.when(lax.rem(step, parts) == 0)
    def _():
        write_spread(spread_ref, maps_ref[0])

    chunk = CORES * LANES

    def some(index, nothing):
        start = pl.multiple_of(index * NS, NS)
        near = pl.ds(pl.multiple_of(lax.rem(step, parts) * rows + start, NS), NS)
        for item in range(width // chunk):
            lanes = slice(item * chunk, (item + 1) * chunk)
            sums = sums_ref[pl.ds(start, NS), lanes]
            for n in range(NS):
                to = pl.ds(pl.multiple_of(start * NS + n * NS, NS), NS)
                out_ref[to, lanes] = factor(sums, wide_ref, spread_ref, near, n, lanes)
        return nothing

    lax.fori_loop(0, rows // NS, some, 0)


def make_factors(sums, maps, rates):
    rows, width = sums.shape[0] // maps.shape[0], sums.shape[1]
    parts = 2
    some = rows // parts
    return pl.pallas_call(
        factors_kernel,
        grid=(maps.shape[0] * parts,),
        in_specs=[
            pl.BlockSpec((some, width), lambda b: (b, 0)),
            pl.BlockSpec((1, 2 * NS, rows), lambda b: (b // parts, 0, 0)),
            pl.BlockSpec((NS, width), lambda b: (0, 0)),
        ],
        out_specs=pl.BlockSpec((some * NS, width), lambda b: (b, 0)),
        out_shape=jax.ShapeDtypeStruct((sums.shape[0] * NS, width), jnp.bfloat16),
        scratch_shapes=[
            pltpu.VMEM((NS * NS, width), jnp.bfloat16),
            pltpu.VMEM((rows, NS * LANES), jnp.bfloat16),
        ],
        compiler_params=params,
        cost_estimate=pl.CostEstimate(flops=3 * 10**9, bytes_accessed=1 << 23, transcendentals=0),
        name="make_factors",
    )(sums, maps, rates)


def carried_kernel(
    places_ref, part_own_ref, part_come_ref, factors_ref, sums_own_ref, sums_come_ref, maps_ref,
    last_own_ref, total_own_ref, last_come_ref, total_come_ref, rates_ref, carries_ref,
    out_ref, state_ref, starts_ref, total_ref, wide_ref, begin_ref, spread_ref,
):
    block = pl.program_id(0)
    rows, width = out_ref.shape
    others = last_come_ref.shape[0]
    chip = places_ref[0]
    first_core = lax.rem(block, CORES) == 0
    own = block >= others * CORES

    @pl.when(block == 0)
    def _():
        state_ref[...] = jnp.zeros_like(state_ref)

        def compose(row, nothing):
            follow(carries_ref.at[row], rates_ref, state_ref)
            return nothing

        lax.fori_loop(0, places_ref[1], compose, 0)
        write_rates(wide_ref, rates_ref)

        def place_own():
            starts_ref[others] = state_ref[...]
            add_states(rates_ref, state_ref, total_ref, last_own_ref[0], total_own_ref[0])

        total_ref[...] = jnp.zeros_like(total_ref)
        for other in range(others):
            pl.when(chip == other)(place_own)
            starts_ref[other] = state_ref[...]
            add_states(
                rates_ref, state_ref, total_ref, last_come_ref[other], total_come_ref[other]
            )
        pl.when(chip == others)(place_own)

    @pl.when(first_core)
    def _():
        state_ref[...] = starts_ref[block // CORES]

    state = state_ref[...]
    for n in range(NS):
        begin_ref[n * NS : (n + 1) * NS, :] = jnp.broadcast_to(
            state[n : n + 1, :], (NS, width)
        ).astype(jnp.bfloat16)
    sums = jnp.where(own, sums_own_ref[...], sums_come_ref[rows - NS :, :])
    last = sums.astype(jnp.float32)[NS - 1 :, :]
    state_ref[...] = jnp.exp2(rates_ref[...] * last) * state
    chunk, several = CORES * LANES, 4

    def add_up(part_ref, near, lanes, factor_of):
        total = part_ref[near, lanes].astype(jnp.float32)
        for first in range(0, NS, several):
            terms = [
                factor_of(n) * begin_ref[n * NS : (n + 1) * NS, lanes]
                for n in range(first, first + several)
            ]
            four = (terms[0] + terms[1]) + (terms[2] + terms[3])
            total = total + four.astype(jnp.float32)
        out_ref[near, lanes] = total.astype(jnp.bfloat16)

    @pl.when(own)
    def _():
        def some(index, nothing):
            start = pl.multiple_of(index * NS, NS)
            for item in range(width // chunk):
                lanes = slice(item * chunk, (item + 1) * chunk)
                add_up(
                    part_own_ref, pl.ds(start, NS), lanes,
                    lambda n: factors_ref[
                        pl.ds(pl.multiple_of(start * NS + n * NS, NS), NS), lanes
                    ],
                )
            return nothing

        lax.fori_loop(0, rows // NS, some, 0)

    @pl.when(jnp.logical_not(own))
    def _():
        write_spread(spread_ref, maps_ref[0])

        def some(index, nothing):
            near = pl.ds(pl.multiple_of(index * NS, NS), NS)
            for item in range(width // chunk):
                lanes = slice(item * chunk, (item + 1) * chunk)
                sums = sums_come_ref[near, lanes]
                add_up(
                    part_come_ref, near, lanes,
                    lambda n: factor(sums, wide_ref, spread_ref, near, n, lanes),
                )
            return nothing

        lax.fori_loop(0, rows // NS, some, 0)


def add_carried(places, own, come, factors, rates, carries):
    part_own, sums_own, _, last_own, total_own = own
    part_come, sums_come, maps, last_come, total_come = come
    others, _, width = last_come.shape
    rows = part_own.shape[0] // CORES
    chips = others + 1

    def core(b):
        return lax.rem(b, CORES)

    def other(b, s):
        return jnp.minimum(b, others * CORES - 1)

    def mine(b, s):
        return jnp.maximum(b - others * CORES, 0)

    def out(b, s):
        place = b // CORES
        chip = jnp.where(
            place == others, s[0], jnp.where(place < s[0], place, place + 1)
        )
        return (chip * CORES + core(b), 0)

    def fixed(*shape):
        return pl.BlockSpec(shape, lambda b, s: (0,) * len(shape))

    last_rows = rows // NS
    return pl.pallas_call(
        carried_kernel,
        grid_spec=pltpu.PrefetchScalarGridSpec(
            num_scalar_prefetch=1,
            grid=(chips * CORES,),
            in_specs=[
                pl.BlockSpec((rows, width), lambda b, s: (mine(b, s), 0)),
                pl.BlockSpec((rows, width), lambda b, s: (other(b, s), 0)),
                pl.BlockSpec((rows * NS, width), lambda b, s: (mine(b, s), 0)),
                pl.BlockSpec((NS, width), lambda b, s: ((mine(b, s) + 1) * last_rows - 1, 0)),
                pl.BlockSpec((rows, width), lambda b, s: (other(b, s), 0)),
                pl.BlockSpec((1, 2 * NS, rows), lambda b, s: (other(b, s), 0, 0)),
                fixed(*last_own.shape),
                fixed(*total_own.shape),
                fixed(*last_come.shape),
                fixed(*total_come.shape),
                fixed(*rates.shape),
                fixed(*carries.shape),
            ],
            out_specs=pl.BlockSpec((rows, width), out),
            scratch_shapes=[
                pltpu.VMEM((NS, width), jnp.float32),
                pltpu.VMEM((chips, NS, width), jnp.float32),
                pltpu.VMEM((1, width), jnp.float32),
                pltpu.VMEM((NS * NS, width), jnp.bfloat16),
                pltpu.VMEM((NS * NS, width), jnp.bfloat16),
                pltpu.VMEM((rows, NS * LANES), jnp.bfloat16),
            ],
        ),
        out_shape=jax.ShapeDtypeStruct((chips * CORES * rows, width), jnp.bfloat16),
        compiler_params=params,
        name="add_carried",
    )(
        places, part_own, part_come, factors, sums_own, sums_come, maps, last_own, total_own,
        last_come, total_come, rates, carries,
    )


def local(
    queries, keys, values, doc_lengths, rank_in, bc_weight, rank_out, dt_bias, a_log, skip_gain
):
    devices = lax.axis_size("seq")
    chips = devices // CORES
    targets = lax.axis_size("chan")
    seq_place = lax.axis_index("seq").astype(jnp.int32)
    chan_place = lax.axis_index("chan").astype(jnp.int32)
    chip, core = seq_place // CORES, lax.rem(seq_place, CORES)
    place = jnp.stack([chip, core])
    width = queries.shape[2] // devices
    wide = max(HEAD_SIZE, keys.shape[2] // devices)

    def other(device):
        return device + 1 - 2 * (device % CORES)

    swap = [(device, other(device)) for device in range(devices)]
    near = [(device, device + CORES) for device in range(devices - CORES)]
    far = [(device, other(device + CORES)) for device in range(devices - CORES)]

    def onward(chips_on):
        return [(device, (device + chips_on * CORES) % devices) for device in range(devices)]

    own, theirs = select_heads(keys[0], values[0], chips, wide)
    from_near = lax.ppermute(own, "seq", near)
    from_far = lax.ppermute(theirs, "seq", far)
    swapped = lax.ppermute(theirs, "seq", swap)
    queries_after, _ = lax.optimization_barrier((queries[0], own))
    their_queries = lax.ppermute(queries_after, "seq", swap)
    blocks = (own, swapped, from_near, from_far)

    first = seq_place * width
    logs = lax.dynamic_slice_in_dim(a_log, first, width, 0)
    rates = (-LOG2E * jnp.exp(logs)).T
    cols = lax.dynamic_slice_in_dim(rank_out, first, width, 1)
    bias = lax.dynamic_slice_in_dim(dt_bias, first, width, 0)[None]
    gain = lax.dynamic_slice_in_dim(skip_gain, first, width, 0)[None]

    sent, stayed, part = attend(
        place, doc_lengths, (queries[0], their_queries), blocks, rank_in, bc_weight.T,
        (rates, cols, bias, gain),
    )
    come = [lax.ppermute(sent[step], "seq", onward(step + 1)) for step in range(chips - 1)]
    low_own = low_and_maps(part, lax.ppermute(part, "seq", swap))
    low_come = [lax.ppermute(low_own, "seq", onward(step + 1)) for step in range(chips - 1)]
    got_sent = lax.ppermute(sent, "seq", swap)
    got_stayed = lax.ppermute(stayed, "seq", swap)
    attn_rows = join_heads(sent, stayed, got_sent, got_stayed)

    given = (cols, bias, rates, gain)
    own = scan_tokens(place, stayed, low_own[None], *given, None, targets, None)
    *come, carry = scan_tokens(
        place, jnp.stack(come), jnp.stack(low_come), *given, own[3:], targets, attn_rows
    )
    carries = lax.all_to_all(carry, "chan", split_axis=0, concat_axis=0, tiled=True)
    factors = make_factors(own[1], own[2], rates)
    ssm_rows = add_carried(
        jnp.stack([chip, chan_place]), own, come, factors, rates, carries
    )
    return (attn_rows[None], ssm_rows[None])


def solution(mesh):
    return jax.shard_map(
        local,
        mesh=mesh,
        in_specs=(
            P("chan", "seq", None),
            P("chan", "seq", None),
            P("chan", "seq", None),
            P("chan", None),
            P(),
            P(),
            P(),
            P(),
            P(),
            P(),
        ),
        out_specs=(P("chan", "seq", None), P("chan", None, "seq")),
        check_vma=False,
    )
```

```python
import functools
import math

import jax
import jax.numpy as jnp
from jax import lax
from jax.experimental import pallas as pl
from jax.experimental.pallas import tpu as pltpu
from jax.sharding import PartitionSpec as P

QUERY_HEADS = 32
KEY_VALUE_HEADS = 8
HEAD_SIZE = 128
GROUP = QUERY_HEADS // KEY_VALUE_HEADS
NS = 16
RANK = 256
CORES = 2
LANES = 128
SUBLANES = 8
MAPS = 2 * NS
LOG2E = 1.4426950408889634

masked_fill = -1e30
params = pltpu.CompilerParams(vmem_limit_bytes=60 << 20)
less = pltpu.CompilerParams(vmem_limit_bytes=40 << 20)


def split(value):
    coarse = value.astype(jnp.bfloat16)
    return coarse, (value - coarse.astype(jnp.float32)).astype(jnp.bfloat16)


def run_copies(pairs, sems):
    copies = [
        pltpu.make_async_copy(source, target, sems.at[i]) for i, (source, target) in enumerate(pairs)
    ]
    for copy in copies:
        copy.start()
    for copy in copies:
        copy.wait()


def columns_of(ref, index, size):
    return ref.at[:, pl.ds(pl.multiple_of(index * size, LANES), size)]


def heads_kernel(key_ref, value_ref, own_ref, their_ref, sems):
    core = lax.rem(lax.axis_index("seq"), CORES)
    wide = own_ref.shape[3]
    halves = key_ref.shape[1] // wide // own_ref.shape[0]
    pairs = []
    for target, which in ((own_ref, core), (their_ref, 1 - core)):
        for chip in range(own_ref.shape[0]):
            index = chip * halves + (which if halves == CORES else 0)
            for kind, source in enumerate((key_ref, value_ref)):
                pairs.append((columns_of(source, index, wide), target.at[chip, kind]))
    run_copies(pairs, sems)


def select_heads(keys, values, chips, wide):
    shape = jax.ShapeDtypeStruct((chips, 2, keys.shape[0], wide), keys.dtype)
    return pl.pallas_call(
        heads_kernel,
        in_specs=[pl.BlockSpec(memory_space=pl.ANY)] * 2,
        out_shape=[shape, shape],
        scratch_shapes=[pltpu.SemaphoreType.DMA((4 * chips,))],
        compiler_params=params,
        name="select_heads",
    )(keys, values)


def join_kernel(sent_ref, stayed_ref, got_sent_ref, got_stayed_ref, out_ref, sems):
    place = lax.axis_index("seq")
    core, chip = lax.rem(place, CORES), place // CORES
    rows = out_ref.shape[0]
    others, _, width = sent_ref.shape
    here = pl.ds(pl.multiple_of(core * rows, rows), rows)
    pairs = []
    for first, rest, which in (
        (stayed_ref, sent_ref, core), (got_stayed_ref, got_sent_ref, 1 - core)
    ):
        for step in range(others + 1):
            source = first.at[0, here, :] if step == 0 else rest.at[step - 1, here, :]
            owner = lax.rem(chip + step, others + 1)
            pairs.append((source, columns_of(out_ref, owner * CORES + which, width)))
    run_copies(pairs, sems)


def join_heads(sent, stayed, got_sent, got_stayed):
    others, rows, width = sent.shape
    return pl.pallas_call(
        join_kernel,
        in_specs=[pl.BlockSpec(memory_space=pl.ANY)] * 4,
        out_shape=jax.ShapeDtypeStruct(
            (rows // CORES, (others + 1) * CORES * width), sent.dtype
        ),
        scratch_shapes=[pltpu.SemaphoreType.DMA((CORES * (others + 1),))],
        compiler_params=params,
        name="join_heads",
    )(sent, stayed, got_sent, got_stayed)


def attend_kernel(
    place_ref, doc_ref, mine_ref, theirs_ref, own_ref, swap_ref, near_ref, far_ref,
    rank_ref, map_ref, *rest, chips,
):
    send_ref, stay_ref, part_ref, mask_ref = rest[-4:]
    step = pl.program_id(0)
    rows = mine_ref.shape[0]
    group = mine_ref.shape[1] // HEAD_SIZE
    chip, core = place_ref[0], place_ref[1]
    first_core = core == 0

    def above(shape):
        row = lax.rem(lax.broadcasted_iota(jnp.int32, shape, 0), rows)
        return lax.broadcasted_iota(jnp.int32, shape, 1) > row

    @pl.when(step == 0)
    def _():
        part_ref[...] = jnp.zeros_like(part_ref)
        own = chip * CORES + core
        swapped = chip * CORES + 1 - core
        near, far = own - CORES, swapped - CORES
        lane = lax.broadcasted_iota(jnp.int32, (rows, rows), 1)
        row = lax.broadcasted_iota(jnp.int32, (rows, rows), 0)
        for item, (place, before, middle) in enumerate(
            (
                (own, near, jnp.where(first_core, far, swapped)),
                (swapped, far, jnp.where(first_core, own, near)),
            )
        ):
            query_pos = place * rows + row
            start = jnp.zeros((rows, rows), jnp.int32)
            bound = jnp.int32(0)
            for doc in range(doc_ref.shape[1]):
                bound = bound + doc_ref[0, doc]
                start = jnp.where(query_pos >= bound, bound, start)
            ends = jnp.where(lane > row, before, place) * rows + lane
            mask_ref[item, :, :rows] = jnp.where(
                (ends >= start) & (ends <= query_pos), 0.0, masked_fill
            )
            mask_ref[item, :, rows:] = jnp.where(
                middle * rows + lane >= start, 0.0, masked_fill
            )

    scale = LOG2E / math.sqrt(HEAD_SIZE)
    ones = jnp.ones((3 * rows, HEAD_SIZE), jnp.bfloat16)

    def windows(kind):
        own, swapped = own_ref[0, kind], swap_ref[0, kind]
        near, far = near_ref[0, kind], far_ref[0, kind]
        return (
            jnp.concatenate([near, own, jnp.where(first_core, far, swapped)], axis=0),
            jnp.concatenate([far, swapped, jnp.where(first_core, own, near)], axis=0),
        )

    scores = []
    for keys, query in zip(windows(0), (mine_ref[...], theirs_ref[...])):
        stacked = jnp.concatenate(
            [query[:, i * HEAD_SIZE : (i + 1) * HEAD_SIZE] for i in range(group)], axis=0
        )
        scores.append(
            lax.dot_general(
                stacked, keys, (((1,), (1,)), ((), ())), preferred_element_type=jnp.float32
            )
        )
    outputs = []
    before = above((group * rows, rows))
    for item, (values, score) in enumerate(zip(windows(1), scores)):
        fill = mask_ref[item]
        ends = jnp.where(before, score[:, :rows], score[:, rows : 2 * rows])
        kept = jnp.concatenate([ends, score[:, 2 * rows :]], axis=1)
        kept = jnp.concatenate(
            [kept[i * rows : (i + 1) * rows, :] + fill for i in range(group)], axis=0
        )
        peak = jnp.max(kept, axis=1, keepdims=True)
        raw = jnp.exp2((kept - peak) * scale).astype(jnp.bfloat16)
        ends = raw[:, :rows]
        none = jnp.zeros_like(ends)
        spread = jnp.concatenate(
            [jnp.where(before, ends, none), jnp.where(before, none, ends), raw[:, rows:]], axis=1
        )
        both = jnp.dot(
            spread, jnp.concatenate([values, ones], axis=1), preferred_element_type=jnp.float32
        )
        mixed = both[:, :HEAD_SIZE] * pl.reciprocal(both[:, HEAD_SIZE:])
        mixed = mixed.astype(jnp.bfloat16)
        outputs.append(
            jnp.concatenate([mixed[i * rows : (i + 1) * rows, :] for i in range(group)], axis=1)
        )
    stream = jnp.concatenate(
        [
            jnp.where(first_core, outputs[0], outputs[1]),
            jnp.where(first_core, outputs[1], outputs[0]),
        ],
        axis=0,
    )
    last = step >= pl.num_programs(0) - pl.num_programs(0) // chips

    @pl.when(last)
    def _():
        stay_ref[0] = stream

    @pl.when(jnp.logical_not(last))
    def _():
        send_ref[0] = stream

    both = CORES * rows
    part_ref[:both, :] += jnp.dot(stream, rank_ref[...], preferred_element_type=jnp.float32)
    part_ref[both:, :] += lax.dot_general(
        map_ref[...], stream, (((1,), (1,)), ((), ())), preferred_element_type=jnp.float32
    )


def attend(place, doc_lengths, queries, blocks, rank_in, map_rows, after):
    mine, theirs = queries
    chips, _, rows, columns = blocks[0].shape
    heads = columns // HEAD_SIZE
    width = mine.shape[1] // (chips * CORES)
    wide = width // heads

    def owner(j, s):
        return lax.rem(s[0] + 1 + j // heads, chips)

    def column(j, s):
        return (owner(j, s) * CORES + s[1]) * heads + lax.rem(j, heads)

    def sent(j, s):
        at = jnp.minimum(j, (chips - 1) * heads - 1)
        return (at // heads, 0, lax.rem(at, heads))

    query = pl.BlockSpec((rows, wide), lambda j, s: (0, column(j, s)))
    block = pl.BlockSpec(
        (1, 2, rows, HEAD_SIZE), lambda j, s: (owner(j, s), 0, 0, lax.rem(j, heads))
    )
    return pl.pallas_call(
        functools.partial(attend_kernel, chips=chips),
        grid_spec=pltpu.PrefetchScalarGridSpec(
            num_scalar_prefetch=1,
            grid=(chips * heads,),
            in_specs=[pl.BlockSpec(memory_space=pltpu.SMEM), query, query]
            + [block] * 4
            + [
                pl.BlockSpec((wide, RANK), lambda j, s: (column(j, s), 0)),
                pl.BlockSpec((2 * NS, wide), lambda j, s: (0, column(j, s))),
            ]
            + [pl.BlockSpec(memory_space=pl.ANY)] * len(after),
            out_specs=[
                pl.BlockSpec((1, CORES * rows, wide), sent),
                pl.BlockSpec(
                    (1, CORES * rows, wide),
                    lambda j, s: (0, 0, jnp.maximum(j - (chips - 1) * heads, 0)),
                ),
                pl.BlockSpec((CORES * rows + 2 * NS, RANK), lambda j, s: (0, 0)),
            ],
            scratch_shapes=[pltpu.VMEM((2, rows, 2 * rows), jnp.float32)],
        ),
        out_shape=[
            jax.ShapeDtypeStruct((chips - 1, CORES * rows, width), jnp.bfloat16),
            jax.ShapeDtypeStruct((1, CORES * rows, width), jnp.bfloat16),
            jax.ShapeDtypeStruct((CORES * rows + 2 * NS, RANK), jnp.float32),
        ],
        compiler_params=params,
        cost_estimate=pl.CostEstimate(flops=5 * 10**9, bytes_accessed=1 << 22, transcendentals=0),
        name="attend",
    )(place, doc_lengths, mine, theirs, *blocks, rank_in, map_rows, *after)


def low_kernel(mine_ref, theirs_ref, out_ref):
    out_ref[...] = (mine_ref[...] + theirs_ref[...]).astype(jnp.bfloat16)


def low_and_maps(mine, theirs):
    return pl.pallas_call(
        low_kernel,
        out_shape=jax.ShapeDtypeStruct(mine.shape, jnp.bfloat16),
        compiler_params=params,
        cost_estimate=pl.CostEstimate(flops=1, bytes_accessed=1, transcendentals=0),
        name="low_and_maps",
    )(mine, theirs)


def softplus(value):
    small = jnp.exp(-jnp.abs(value))
    tail = jnp.where(small < 0.00390625, small * (1.0 - 0.5 * small), jnp.log(1.0 + small))
    return jnp.maximum(value, 0.0) + tail


def add_states(rates_ref, state_ref, total_ref, states, totals):
    state_ref[...] = jnp.exp2(rates_ref[...] * totals) * state_ref[...] + states
    total_ref[...] = total_ref[...] + totals


def sums_within(steps):
    rows = steps.shape[0]
    at = lax.broadcasted_iota(jnp.int32, (rows, rows), 0)
    of = lax.broadcasted_iota(jnp.int32, (rows, rows), 1)
    upto = jnp.where(of <= at, 1.0, 0.0).astype(jnp.bfloat16)
    return jnp.dot(upto, steps, preferred_element_type=jnp.float32)


def step_kernel(
    place_ref, stream_ref, low_ref, cols_ref, bias_ref, rates_ref, *rest
):
    own_state_ref, own_total_ref = rest[:2]
    steps_ref, sums_ref, maps_ref, carry_ref, state_ref, total_ref, wide_ref, turn_ref = rest[2:]
    block = pl.program_id(0)
    others, both, width = stream_ref.shape
    rows = both // CORES
    chip = block // CORES
    slot = lax.rem(
        place_ref[0] - jnp.where(chip < place_ref[0], chip, chip + 1) + others + 1, others + 1
    ) - 1
    here = pl.ds(pl.multiple_of(lax.rem(block, CORES) * rows, rows), rows)
    stream = stream_ref[slot, here, :]

    @pl.when(block == 0)
    def _():
        state_ref[...] = jnp.zeros_like(state_ref)
        total_ref[...] = jnp.zeros_like(total_ref)
        for n in range(NS):
            wide_ref[n * NS : (n + 1) * NS, :] = jnp.broadcast_to(
                rates_ref[n : n + 1, :], (NS, width)
            ).astype(jnp.bfloat16)

    @pl.when(block == place_ref[0] * CORES)
    def _():
        add_states(rates_ref, state_ref, total_ref, own_state_ref[...], own_total_ref[...])

    maps = low_ref[slot, both:, here].astype(jnp.float32)
    maps_ref[0] = maps
    logits = jnp.dot(low_ref[slot, here, :], cols_ref[...], preferred_element_type=jnp.float32)
    steps = softplus(logits + bias_ref[...]).astype(jnp.bfloat16)
    steps_ref[...] = steps
    push = steps * stream
    within = sums_within(steps)
    sums_ref[...] = within.astype(jnp.bfloat16)
    whole = within[rows - 1 :, :]
    left = (whole - within).astype(jnp.bfloat16)
    some, chunk, several = rows // 2, CORES * LANES, 4
    state_row = lax.broadcasted_iota(jnp.int32, (NS, some), 0)
    for first in range(0, rows, some):
        span = slice(first, first + some)
        chosen = [
            jnp.concatenate(
                [
                    jnp.where(state_row == m, maps[:NS, span], 0.0).astype(jnp.bfloat16)
                    for m in range(n, n + several)
                ],
                axis=1,
            )
            for n in range(0, NS, several)
        ]
        for item in range(width // chunk):
            lanes = slice(item * chunk, (item + 1) * chunk)
            left_here = left[span, lanes].reshape(some // NS, NS, chunk)
            push_here = push[span, lanes].reshape(some // NS, NS, chunk)
            added = state_ref[:, lanes]
            if first == 0:
                added = jnp.exp2(rates_ref[:, lanes] * whole[:, lanes]) * added
            for n in range(0, NS, several):
                pushed = []
                for m in range(n, n + several):
                    decay = jnp.exp2(left_here * wide_ref[m * NS : (m + 1) * NS, lanes][None])
                    pushed.append((decay * push_here).reshape(some, chunk))
                added = added + jnp.dot(
                    chosen[n // several],
                    jnp.concatenate(pushed, axis=0),
                    preferred_element_type=jnp.float32,
                )
            state_ref[:, lanes] = added
    total_ref[...] = total_ref[...] + whole

    count = pl.num_programs(0)

    @pl.when(block == count - 1)
    def _():
        @pl.when(place_ref[0] * CORES == count)
        def _():
            add_states(rates_ref, state_ref, total_ref, own_state_ref[...], own_total_ref[...])

        write_carry(carry_ref.at[0], state_ref[...], total_ref[...], turn_ref)
        for target in range(1, carry_ref.shape[0]):
            carry_ref[target] = carry_ref[0]


def step_sizes(place, stream, lows, cols, bias, rates, state, total, targets):
    others = stream.shape[0]
    rows, width = stream.shape[1] // CORES, stream.shape[2]
    blocks = others * CORES
    carry = (targets, (width // LANES + 1) * NS, LANES)

    def fixed(*shape):
        return pl.BlockSpec(shape, lambda b, s: (0,) * len(shape))

    return pl.pallas_call(
        step_kernel,
        grid_spec=pltpu.PrefetchScalarGridSpec(
            num_scalar_prefetch=1,
            grid=(blocks,),
            in_specs=[
                pl.BlockSpec(memory_space=pltpu.VMEM),
                pl.BlockSpec(memory_space=pltpu.VMEM),
                fixed(*cols.shape),
                fixed(*bias.shape),
                fixed(*rates.shape),
                fixed(*state.shape),
                fixed(*total.shape),
            ],
            out_specs=[
                pl.BlockSpec((rows, width), lambda b, s: (b, 0)),
                pl.BlockSpec((rows, width), lambda b, s: (b, 0)),
                pl.BlockSpec((1, 2 * NS, rows), lambda b, s: (b, 0, 0)),
                fixed(*carry),
            ],
            scratch_shapes=[
                pltpu.VMEM((NS, width), jnp.float32),
                pltpu.VMEM((1, width), jnp.float32),
                pltpu.VMEM((NS * NS, width), jnp.bfloat16),
                pltpu.VMEM((SUBLANES, LANES), jnp.float32),
            ],
        ),
        out_shape=[
            jax.ShapeDtypeStruct((blocks * rows, width), jnp.bfloat16),
            jax.ShapeDtypeStruct((blocks * rows, width), jnp.bfloat16),
            jax.ShapeDtypeStruct((blocks, 2 * NS, rows), jnp.float32),
            jax.ShapeDtypeStruct(carry, jnp.bfloat16),
        ],
        compiler_params=less,
        name="step_sizes",
    )(place, stream, lows, cols, bias, rates, state, total)


def write_carry(out_ref, state, total, turn_ref):
    tile = state.shape[1] // LANES
    turn_ref[...] = jnp.zeros_like(turn_ref)
    for item in range(tile):
        lanes = slice(item * LANES, (item + 1) * LANES)
        turn_ref[item : item + 1, :] = total[:, lanes]
        out_ref[item * NS : (item + 1) * NS, :] = state[:, lanes].astype(jnp.bfloat16)
    out_ref[tile * NS :, :] = jnp.concatenate(split(turn_ref[...]), axis=0)


def follow(carry_ref, rates_ref, state_ref):
    tile = state_ref.shape[1] // LANES
    sums = carry_ref[tile * NS :, :].astype(jnp.float32)
    sums = sums[:SUBLANES, :] + sums[SUBLANES:, :]
    for item in range(tile):
        lanes = slice(item * LANES, (item + 1) * LANES)
        decay = jnp.exp2(rates_ref[:, lanes] * sums[item : item + 1, :])
        added = carry_ref[item * NS : (item + 1) * NS, :].astype(jnp.float32)
        state_ref[:, lanes] = decay * state_ref[:, lanes] + added
    return sums


def scan_blocks(stream_ref, steps_ref, maps, rates_ref, gain_ref, out_ref, state_ref, work_refs):
    out_of_ref, *hist_refs = work_refs
    rows, width = steps_ref.shape
    source = lax.broadcasted_iota(jnp.int32, (LANES, NS * NS), 0)
    column = lax.rem(lax.broadcasted_iota(jnp.int32, (LANES, NS * NS), 1), NS)
    token = lax.rem(lax.broadcasted_iota(jnp.int32, (rows, NS * NS), 0), NS)
    slot = lax.broadcasted_iota(jnp.int32, (rows, NS * NS), 1) // NS
    turned = jnp.concatenate(
        [maps, jnp.zeros((LANES - 2 * NS, rows), jnp.float32)], axis=0
    ).T.astype(jnp.bfloat16)
    pick = jnp.where(source == NS + column, 1.0, 0.0).astype(jnp.bfloat16)
    spread = jnp.dot(turned, pick, preferred_element_type=jnp.float32)
    out_of_ref[...] = jnp.where(token == slot, spread, 0.0).astype(jnp.bfloat16)
    map_in = maps[:NS, :]
    half = width // 2

    def finish(first, hist_ref):
        here = pl.ds(first, NS)
        mixed = jnp.dot(out_of_ref[here, :], hist_ref[...], preferred_element_type=jnp.float32)
        direct = gain_ref[...] * stream_ref[0, here, :].astype(jnp.float32)
        out_ref[here, :] = (mixed + direct).astype(jnp.bfloat16)

    def advance(first, hist_ref):
        here = pl.ds(first, NS)
        into = pltpu.roll(map_in, lax.rem(rows - first, rows), 1)
        for lanes in (slice(0, half), slice(half, width)):
            state = state_ref[:, lanes]
            rates = rates_ref[:, lanes]
            steps = steps_ref[here, lanes].astype(jnp.float32)
            push = steps * stream_ref[0, here, lanes].astype(jnp.float32)
            for near in range(NS):
                this = slice(near, near + 1)
                state = jnp.exp2(rates * steps[this, :]) * state + into[:, this] * push[this, :]
                hist_ref[near * NS : (near + 1) * NS, lanes] = state.astype(jnp.bfloat16)
            state_ref[:, lanes] = state

    def at(group):
        return pl.multiple_of(group * NS, NS)

    def pair(index, nothing):
        finish(at(2 * index), hist_refs[1])
        advance(at(2 * index + 1), hist_refs[0])
        finish(at(2 * index + 1), hist_refs[0])
        advance(at(2 * index + 2), hist_refs[1])
        return nothing

    groups = rows // NS
    advance(0, hist_refs[1])
    lax.fori_loop(0, groups // 2 - 1, pair, 0)
    finish(rows - 2 * NS, hist_refs[1])
    advance(rows - NS, hist_refs[0])
    finish(rows - NS, hist_refs[0])


def work_shapes(rows, width):
    return [
        pltpu.VMEM((rows, NS * NS), jnp.bfloat16),
        pltpu.VMEM((NS * NS, width), jnp.bfloat16),
        pltpu.VMEM((NS * NS, width), jnp.bfloat16),
    ]


def own_kernel(
    stream_ref, low_ref, map_ref, cols_ref, bias_ref, rates_ref, gain_ref,
    out_ref, sums_ref, maps_ref, state_ref, total_ref, steps_ref, *work_refs
):
    rows = steps_ref.shape[0]

    @pl.when(pl.program_id(0) == 0)
    def _():
        state_ref[...] = jnp.zeros_like(state_ref)
        total_ref[...] = jnp.zeros_like(total_ref)

    maps = map_ref[...].astype(jnp.float32)
    maps_ref[0] = maps
    logits = jnp.dot(low_ref[...], cols_ref[...], preferred_element_type=jnp.float32)
    steps = softplus(logits + bias_ref[...]).astype(jnp.bfloat16)
    steps_ref[...] = steps
    within = sums_within(steps)
    sums_ref[...] = within.astype(jnp.bfloat16)
    total_ref[...] = total_ref[...] + within[rows - 1 :, :]
    scan_blocks(stream_ref, steps_ref, maps, rates_ref, gain_ref, out_ref, state_ref, work_refs)


def scan_own(stream, lows, cols, bias, rates, gain):
    rows, width = stream.shape[1] // CORES, stream.shape[2]
    map_row = CORES * rows // MAPS

    def fixed(*shape):
        return pl.BlockSpec(shape, lambda b: (0,) * len(shape))

    block = pl.BlockSpec((rows, width), lambda b: (b, 0))
    return pl.pallas_call(
        own_kernel,
        grid=(CORES,),
        in_specs=[
            pl.BlockSpec((1, rows, width), lambda b: (0, b, 0)),
            pl.BlockSpec((rows, RANK), lambda b: (b, 0)),
            pl.BlockSpec((MAPS, rows), lambda b: (map_row, b)),
            fixed(*cols.shape),
            fixed(*bias.shape),
            fixed(*rates.shape),
            fixed(*gain.shape),
        ],
        out_specs=[
            block,
            block,
            pl.BlockSpec((1, 2 * NS, rows), lambda b: (b, 0, 0)),
            fixed(NS, width),
            fixed(1, width),
        ],
        out_shape=[
            jax.ShapeDtypeStruct((CORES * rows, width), jnp.bfloat16),
            jax.ShapeDtypeStruct((CORES * rows, width), jnp.bfloat16),
            jax.ShapeDtypeStruct((CORES, 2 * NS, rows), jnp.float32),
            jax.ShapeDtypeStruct((NS, width), jnp.float32),
            jax.ShapeDtypeStruct((1, width), jnp.float32),
        ],
        scratch_shapes=[pltpu.VMEM((rows, width), jnp.bfloat16)] + work_shapes(rows, width),
        compiler_params=less,
        cost_estimate=pl.CostEstimate(flops=4 * 10**9, bytes_accessed=1 << 21, transcendentals=0),
        name="scan_own",
    )(stream, lows, lows, cols, bias, rates, gain)


def others_kernel(
    place_ref, stream_ref, steps_ref, maps_ref, rates_ref, gain_ref, out_ref, last_ref, *work_refs
):
    @pl.when(lax.rem(pl.program_id(0), CORES) == 0)
    def _():
        last_ref[...] = jnp.zeros_like(last_ref)

    scan_blocks(
        stream_ref, steps_ref, maps_ref[0], rates_ref, gain_ref, out_ref, last_ref.at[0], work_refs
    )


def scan_others(place, stream, steps, maps, rates, gain):
    others = stream.shape[0]
    chips = others + 1
    rows, width = stream.shape[1] // CORES, stream.shape[2]

    def slot(b, s):
        chip = b // CORES
        return lax.rem(s[0] - jnp.where(chip < s[0], chip, chip + 1) + chips, chips) - 1

    def fixed(*shape):
        return pl.BlockSpec(shape, lambda b, s: (0,) * len(shape))

    block = pl.BlockSpec((rows, width), lambda b, s: (b, 0))
    return pl.pallas_call(
        others_kernel,
        grid_spec=pltpu.PrefetchScalarGridSpec(
            num_scalar_prefetch=1,
            grid=(others * CORES,),
            in_specs=[
                pl.BlockSpec((1, rows, width), lambda b, s: (slot(b, s), lax.rem(b, CORES), 0)),
                block,
                pl.BlockSpec((1, 2 * NS, rows), lambda b, s: (b, 0, 0)),
                fixed(*rates.shape),
                fixed(*gain.shape),
            ],
            out_specs=[block, pl.BlockSpec((1, NS, width), lambda b, s: (b // CORES, 0, 0))],
            scratch_shapes=work_shapes(rows, width),
        ),
        out_shape=[
            jax.ShapeDtypeStruct((others * CORES * rows, width), jnp.bfloat16),
            jax.ShapeDtypeStruct((others, NS, width), jnp.float32),
        ],
        compiler_params=less,
        cost_estimate=pl.CostEstimate(flops=4 * 10**9, bytes_accessed=1 << 21, transcendentals=0),
        name="scan_others",
    )(place, stream, steps, maps, rates, gain)


def carried_kernel(
    places_ref, part_own_ref, part_come_ref, sums_own_ref, sums_come_ref,
    maps_own_ref, maps_come_ref, last_own_ref, last_come_ref, rates_ref, carries_ref,
    out_ref, state_ref, wide_ref, begin_ref, spread_ref, sums_ref,
):
    block = pl.program_id(0)
    rows, width = out_ref.shape
    chip = block // CORES
    here = chip == places_ref[0]

    @pl.when(block == 0)
    def _():
        state_ref[...] = jnp.zeros_like(state_ref)

        def compose(row, nothing):
            follow(carries_ref.at[row], rates_ref, state_ref)
            return nothing

        lax.fori_loop(0, lax.axis_index("chan"), compose, 0)
        for n in range(NS):
            wide_ref[n * NS : (n + 1) * NS, :] = jnp.broadcast_to(
                rates_ref[n : n + 1, :], (NS, width)
            ).astype(jnp.bfloat16)

    @pl.when((block > 0) & (lax.rem(block, CORES) == 0))
    def _():
        before = jnp.where(chip - 1 == places_ref[0], last_own_ref[...], last_come_ref[0])
        state_ref[...] = state_ref[...] + before

    state = state_ref[...]
    for n in range(NS):
        begin_ref[n * NS : (n + 1) * NS, :] = jnp.broadcast_to(
            state[n : n + 1, :], (NS, width)
        ).astype(jnp.bfloat16)
    maps = jnp.where(here, maps_own_ref[0], maps_come_ref[0])
    maps = jnp.concatenate([maps, jnp.zeros((LANES - 2 * NS, rows), jnp.float32)], axis=0).T
    for n in range(NS):
        spread_ref[:, n * LANES : (n + 1) * LANES] = jnp.broadcast_to(
            maps[:, NS + n : NS + n + 1], (rows, LANES)
        ).astype(jnp.bfloat16)
    sums = jnp.where(here, sums_own_ref[...], sums_come_ref[...])
    sums_ref[...] = sums
    last = sums[rows - NS :, :].astype(jnp.float32)[NS - 1 :, :]
    state_ref[...] = jnp.exp2(rates_ref[...] * last) * state
    chunk, several = CORES * LANES, 4

    def some(index, nothing):
        near = pl.ds(pl.multiple_of(index * NS, NS), NS)
        for item in range(width // chunk):
            lanes = slice(item * chunk, (item + 1) * chunk)
            part = jnp.where(here, part_own_ref[near, lanes], part_come_ref[near, lanes])
            total = part.astype(jnp.float32)
            sums = sums_ref[near, lanes]
            for first in range(0, NS, several):
                terms = []
                for n in range(first, first + several):
                    decay = jnp.exp2(sums * wide_ref[n * NS : (n + 1) * NS, lanes])
                    out_of = spread_ref[near, n * LANES : (n + 1) * LANES]
                    out_of = jnp.concatenate([out_of] * (chunk // LANES), axis=1)
                    terms.append(decay * begin_ref[n * NS : (n + 1) * NS, lanes] * out_of)
                four = (terms[0] + terms[1]) + (terms[2] + terms[3])
                total = total + four.astype(jnp.float32)
            out_ref[near, lanes] = total.astype(jnp.bfloat16)
        return nothing

    lax.fori_loop(0, rows // NS, some, 0)


def add_carried(places, parts, sums, maps, lasts, rates, carries):
    blocks_come, _, rows = maps[1].shape
    chips = blocks_come // CORES + 1
    width = rates.shape[1]

    def core(b):
        return lax.rem(b, CORES)

    def order(b, s):
        chip = b // CORES
        return jnp.minimum(
            jnp.where(chip < s[0], b, jnp.maximum(b - CORES, 0)), blocks_come - 1
        )

    def before(b, s):
        chip = jnp.maximum(b // CORES - 1, 0)
        return jnp.minimum(jnp.where(chip < s[0], chip, jnp.maximum(chip - 1, 0)), chips - 2)

    def fixed(*shape):
        return pl.BlockSpec(shape, lambda b, s: (0,) * len(shape))

    own = pl.BlockSpec((rows, width), lambda b, s: (core(b), 0))
    come = pl.BlockSpec((rows, width), lambda b, s: (order(b, s), 0))
    return pl.pallas_call(
        carried_kernel,
        grid_spec=pltpu.PrefetchScalarGridSpec(
            num_scalar_prefetch=1,
            grid=(chips * CORES,),
            in_specs=[
                own,
                come,
                own,
                come,
                pl.BlockSpec((1, 2 * NS, rows), lambda b, s: (core(b), 0, 0)),
                pl.BlockSpec((1, 2 * NS, rows), lambda b, s: (order(b, s), 0, 0)),
                fixed(NS, width),
                pl.BlockSpec((1, NS, width), lambda b, s: (before(b, s), 0, 0)),
                fixed(*rates.shape),
                pl.BlockSpec(memory_space=pltpu.VMEM),
            ],
            out_specs=pl.BlockSpec((rows, width), lambda b, s: (b, 0)),
            scratch_shapes=[
                pltpu.VMEM((NS, width), jnp.float32),
                pltpu.VMEM((NS * NS, width), jnp.bfloat16),
                pltpu.VMEM((NS * NS, width), jnp.bfloat16),
                pltpu.VMEM((rows, NS * LANES), jnp.bfloat16),
                pltpu.VMEM((rows, width), jnp.bfloat16),
            ],
        ),
        out_shape=jax.ShapeDtypeStruct((chips * CORES * rows, width), jnp.bfloat16),
        compiler_params=less,
        name="add_carried",
    )(places, *parts, *sums, *maps, *lasts, rates, carries)


def local(
    queries, keys, values, doc_lengths, rank_in, bc_weight, rank_out, dt_bias, a_log, skip_gain
):
    devices = lax.axis_size("seq")
    chips = devices // CORES
    targets = lax.axis_size("chan")
    seq_place = lax.axis_index("seq").astype(jnp.int32)
    chip, core = seq_place // CORES, lax.rem(seq_place, CORES)
    place = jnp.stack([chip, core])
    width = queries.shape[2] // devices
    wide = max(HEAD_SIZE, keys.shape[2] // devices)

    def other(device):
        return device + 1 - 2 * (device % CORES)

    swap = [(device, other(device)) for device in range(devices)]
    near = [(device, device + CORES) for device in range(devices - CORES)]
    far = [(device, other(device + CORES)) for device in range(devices - CORES)]

    def onward(chips_on):
        return [(device, (device + chips_on * CORES) % devices) for device in range(devices)]

    own, theirs = select_heads(keys[0], values[0], chips, wide)
    from_near = lax.ppermute(own, "seq", near)
    from_far = lax.ppermute(theirs, "seq", far)
    swapped = lax.ppermute(theirs, "seq", swap)
    queries_after, swapped = lax.optimization_barrier((queries[0], swapped))
    their_queries = lax.ppermute(queries_after, "seq", swap)
    blocks = (own, swapped, from_near, from_far)

    first = seq_place * width
    logs = lax.dynamic_slice_in_dim(a_log, first, width, 0)
    rates = (-LOG2E * jnp.exp(logs)).T
    cols = lax.dynamic_slice_in_dim(rank_out, first, width, 1)
    bias = lax.dynamic_slice_in_dim(dt_bias, first, width, 0)[None]
    gain = lax.dynamic_slice_in_dim(skip_gain, first, width, 0)[None]

    sent, stayed, part = attend(
        place, doc_lengths, (queries[0], their_queries), blocks, rank_in, bc_weight.T,
        (rates, cols, bias, gain),
    )
    come = [lax.ppermute(sent[step], "seq", onward(step + 1)) for step in range(chips - 1)]
    low_own = low_and_maps(part, lax.ppermute(part, "seq", swap))
    low_come = [lax.ppermute(low_own, "seq", onward(step + 1)) for step in range(chips - 1)]
    got_sent = lax.ppermute(sent, "seq", swap)
    got_stayed = lax.ppermute(stayed, "seq", swap)
    attn_rows = join_heads(sent, stayed, got_sent, got_stayed)

    part_own, sums_own, maps_own, state, total = scan_own(stayed, low_own, cols, bias, rates, gain)
    come, low_come = jnp.stack(come), jnp.stack(low_come)
    state, attn_rows = lax.optimization_barrier((state, attn_rows))
    steps, sums_come, maps_come, carry = step_sizes(
        place, come, low_come, cols, bias, rates, state, total, targets
    )
    carries = lax.all_to_all(carry, "chan", split_axis=0, concat_axis=0, tiled=True)
    part_come, last_come = scan_others(place, come, steps, maps_come, rates, gain)
    ssm_rows = add_carried(
        place, (part_own, part_come), (sums_own, sums_come),
        (maps_own, maps_come), (state, last_come), rates, carries,
    )
    return (attn_rows[None], ssm_rows[None])


def solution(mesh):
    return jax.shard_map(
        local,
        mesh=mesh,
        in_specs=(
            P("chan", "seq", None),
            P("chan", "seq", None),
            P("chan", "seq", None),
            P("chan", None),
            P(),
            P(),
            P(),
            P(),
            P(),
            P(),
        ),
        out_specs=(P("chan", "seq", None), P("chan", None, "seq")),
        check_vma=False,
    )
```

```python
import functools
import math

import jax
import jax.numpy as jnp
from jax import lax
from jax.experimental import pallas as pl
from jax.experimental.pallas import tpu as pltpu
from jax.sharding import PartitionSpec as P

QUERY_HEADS = 32
KEY_VALUE_HEADS = 8
HEAD_SIZE = 128
GROUP = QUERY_HEADS // KEY_VALUE_HEADS
NS = 16
RANK = 256
CORES = 2
LANES = 128
SUBLANES = 8
MAPS = 2 * NS
LOG2E = 1.4426950408889634

masked_fill = -1e30
params = pltpu.CompilerParams(vmem_limit_bytes=60 << 20)


def split(value):
    coarse = value.astype(jnp.bfloat16)
    return coarse, (value - coarse.astype(jnp.float32)).astype(jnp.bfloat16)


def run_copies(pairs, sems):
    copies = [
        pltpu.make_async_copy(source, target, sems.at[i]) for i, (source, target) in enumerate(pairs)
    ]
    for copy in copies:
        copy.start()
    for copy in copies:
        copy.wait()


def columns_of(ref, index, size):
    return ref.at[:, pl.ds(pl.multiple_of(index * size, LANES), size)]


def heads_kernel(key_ref, value_ref, own_ref, their_ref, sems):
    core = lax.rem(lax.axis_index("seq"), CORES)
    wide = own_ref.shape[3]
    halves = key_ref.shape[1] // wide // own_ref.shape[0]
    pairs = []
    for target, which in ((own_ref, core), (their_ref, 1 - core)):
        for chip in range(own_ref.shape[0]):
            index = chip * halves + (which if halves == CORES else 0)
            for kind, source in enumerate((key_ref, value_ref)):
                pairs.append((columns_of(source, index, wide), target.at[chip, kind]))
    run_copies(pairs, sems)


def select_heads(keys, values, chips, wide):
    shape = jax.ShapeDtypeStruct((chips, 2, keys.shape[0], wide), keys.dtype)
    return pl.pallas_call(
        heads_kernel,
        in_specs=[pl.BlockSpec(memory_space=pl.ANY)] * 2,
        out_shape=[shape, shape],
        scratch_shapes=[pltpu.SemaphoreType.DMA((4 * chips,))],
        compiler_params=params,
        name="select_heads",
    )(keys, values)


def join_kernel(sent_ref, stayed_ref, got_sent_ref, got_stayed_ref, out_ref, sems):
    place = lax.axis_index("seq")
    core, chip = lax.rem(place, CORES), place // CORES
    rows = out_ref.shape[0]
    others, _, width = sent_ref.shape
    here = pl.ds(pl.multiple_of(core * rows, rows), rows)
    pairs = []
    for first, rest, which in (
        (stayed_ref, sent_ref, core), (got_stayed_ref, got_sent_ref, 1 - core)
    ):
        for step in range(others + 1):
            source = first.at[0, here, :] if step == 0 else rest.at[step - 1, here, :]
            owner = lax.rem(chip + step, others + 1)
            pairs.append((source, columns_of(out_ref, owner * CORES + which, width)))
    run_copies(pairs, sems)


def join_heads(sent, stayed, got_sent, got_stayed):
    others, rows, width = sent.shape
    return pl.pallas_call(
        join_kernel,
        in_specs=[pl.BlockSpec(memory_space=pl.ANY)] * 4,
        out_shape=jax.ShapeDtypeStruct(
            (rows // CORES, (others + 1) * CORES * width), sent.dtype
        ),
        scratch_shapes=[pltpu.SemaphoreType.DMA((CORES * (others + 1),))],
        compiler_params=params,
        name="join_heads",
    )(sent, stayed, got_sent, got_stayed)


def attend_kernel(
    place_ref, doc_ref, mine_ref, theirs_ref, own_ref, swap_ref, near_ref, far_ref,
    rank_ref, map_ref, *rest, chips,
):
    send_ref, stay_ref, part_ref, mask_ref = rest[-4:]
    step = pl.program_id(0)
    rows = mine_ref.shape[0]
    group = mine_ref.shape[1] // HEAD_SIZE
    chip, core = place_ref[0], place_ref[1]
    first_core = core == 0

    def above(shape):
        row = lax.rem(lax.broadcasted_iota(jnp.int32, shape, 0), rows)
        return lax.broadcasted_iota(jnp.int32, shape, 1) > row

    @pl.when(step == 0)
    def _():
        part_ref[...] = jnp.zeros_like(part_ref)
        own = chip * CORES + core
        swapped = chip * CORES + 1 - core
        near, far = own - CORES, swapped - CORES
        lane = lax.broadcasted_iota(jnp.int32, (rows, rows), 1)
        row = lax.broadcasted_iota(jnp.int32, (rows, rows), 0)
        for item, (place, before, middle) in enumerate(
            (
                (own, near, jnp.where(first_core, far, swapped)),
                (swapped, far, jnp.where(first_core, own, near)),
            )
        ):
            query_pos = place * rows + row
            start = jnp.zeros((rows, rows), jnp.int32)
            bound = jnp.int32(0)
            for doc in range(doc_ref.shape[1]):
                bound = bound + doc_ref[0, doc]
                start = jnp.where(query_pos >= bound, bound, start)
            ends = jnp.where(lane > row, before, place) * rows + lane
            mask_ref[item, :, :rows] = jnp.where(
                (ends >= start) & (ends <= query_pos), 0.0, masked_fill
            )
            mask_ref[item, :, rows:] = jnp.where(
                middle * rows + lane >= start, 0.0, masked_fill
            )

    scale = LOG2E / math.sqrt(HEAD_SIZE)
    ones = jnp.ones((3 * rows, HEAD_SIZE), jnp.bfloat16)

    def windows(kind):
        own, swapped = own_ref[0, kind], swap_ref[0, kind]
        near, far = near_ref[0, kind], far_ref[0, kind]
        return (
            jnp.concatenate([near, own, jnp.where(first_core, far, swapped)], axis=0),
            jnp.concatenate([far, swapped, jnp.where(first_core, own, near)], axis=0),
        )

    scores = []
    for keys, query in zip(windows(0), (mine_ref[...], theirs_ref[...])):
        stacked = jnp.concatenate(
            [query[:, i * HEAD_SIZE : (i + 1) * HEAD_SIZE] for i in range(group)], axis=0
        )
        scores.append(
            lax.dot_general(
                stacked, keys, (((1,), (1,)), ((), ())), preferred_element_type=jnp.float32
            )
        )
    outputs = []
    before = above((group * rows, rows))
    for item, (values, score) in enumerate(zip(windows(1), scores)):
        fill = mask_ref[item]
        ends = jnp.where(before, score[:, :rows], score[:, rows : 2 * rows])
        kept = jnp.concatenate([ends, score[:, 2 * rows :]], axis=1)
        kept = jnp.concatenate(
            [kept[i * rows : (i + 1) * rows, :] + fill for i in range(group)], axis=0
        )
        peak = jnp.max(kept, axis=1, keepdims=True)
        raw = jnp.exp2((kept - peak) * scale).astype(jnp.bfloat16)
        ends = raw[:, :rows]
        none = jnp.zeros_like(ends)
        spread = jnp.concatenate(
            [jnp.where(before, ends, none), jnp.where(before, none, ends), raw[:, rows:]], axis=1
        )
        both = jnp.dot(
            spread, jnp.concatenate([values, ones], axis=1), preferred_element_type=jnp.float32
        )
        mixed = both[:, :HEAD_SIZE] * pl.reciprocal(both[:, HEAD_SIZE:])
        mixed = mixed.astype(jnp.bfloat16)
        outputs.append(
            jnp.concatenate([mixed[i * rows : (i + 1) * rows, :] for i in range(group)], axis=1)
        )
    stream = jnp.concatenate(
        [
            jnp.where(first_core, outputs[0], outputs[1]),
            jnp.where(first_core, outputs[1], outputs[0]),
        ],
        axis=0,
    )
    last = step >= pl.num_programs(0) - pl.num_programs(0) // chips

    @pl.when(last)
    def _():
        stay_ref[0] = stream

    @pl.when(jnp.logical_not(last))
    def _():
        send_ref[0] = stream

    both = CORES * rows
    part_ref[:both, :] += jnp.dot(stream, rank_ref[...], preferred_element_type=jnp.float32)
    part_ref[both:, :] += lax.dot_general(
        map_ref[...], stream, (((1,), (1,)), ((), ())), preferred_element_type=jnp.float32
    )


def attend(place, doc_lengths, queries, blocks, rank_in, map_rows, after):
    mine, theirs = queries
    chips, _, rows, columns = blocks[0].shape
    heads = columns // HEAD_SIZE
    width = mine.shape[1] // (chips * CORES)
    wide = width // heads

    def owner(j, s):
        return lax.rem(s[0] + 1 + j // heads, chips)

    def column(j, s):
        return (owner(j, s) * CORES + s[1]) * heads + lax.rem(j, heads)

    def sent(j, s):
        at = jnp.minimum(j, (chips - 1) * heads - 1)
        return (at // heads, 0, lax.rem(at, heads))

    query = pl.BlockSpec((rows, wide), lambda j, s: (0, column(j, s)))
    block = pl.BlockSpec(
        (1, 2, rows, HEAD_SIZE), lambda j, s: (owner(j, s), 0, 0, lax.rem(j, heads))
    )
    return pl.pallas_call(
        functools.partial(attend_kernel, chips=chips),
        grid_spec=pltpu.PrefetchScalarGridSpec(
            num_scalar_prefetch=1,
            grid=(chips * heads,),
            in_specs=[pl.BlockSpec(memory_space=pltpu.SMEM), query, query]
            + [block] * 4
            + [
                pl.BlockSpec((wide, RANK), lambda j, s: (column(j, s), 0)),
                pl.BlockSpec((2 * NS, wide), lambda j, s: (0, column(j, s))),
            ]
            + [pl.BlockSpec(memory_space=pl.ANY)] * len(after),
            out_specs=[
                pl.BlockSpec((1, CORES * rows, wide), sent),
                pl.BlockSpec(
                    (1, CORES * rows, wide),
                    lambda j, s: (0, 0, jnp.maximum(j - (chips - 1) * heads, 0)),
                ),
                pl.BlockSpec((CORES * rows + 2 * NS, RANK), lambda j, s: (0, 0)),
            ],
            scratch_shapes=[pltpu.VMEM((2, rows, 2 * rows), jnp.float32)],
        ),
        out_shape=[
            jax.ShapeDtypeStruct((chips - 1, CORES * rows, width), jnp.bfloat16),
            jax.ShapeDtypeStruct((1, CORES * rows, width), jnp.bfloat16),
            jax.ShapeDtypeStruct((CORES * rows + 2 * NS, RANK), jnp.float32),
        ],
        compiler_params=params,
        cost_estimate=pl.CostEstimate(flops=5 * 10**9, bytes_accessed=1 << 22, transcendentals=0),
        name="attend",
    )(place, doc_lengths, mine, theirs, *blocks, rank_in, map_rows, *after)


def low_kernel(mine_ref, theirs_ref, out_ref):
    out_ref[...] = (mine_ref[...] + theirs_ref[...]).astype(jnp.bfloat16)


def low_and_maps(mine, theirs):
    return pl.pallas_call(
        low_kernel,
        out_shape=jax.ShapeDtypeStruct(mine.shape, jnp.bfloat16),
        compiler_params=params,
        cost_estimate=pl.CostEstimate(flops=1, bytes_accessed=1, transcendentals=0),
        name="low_and_maps",
    )(mine, theirs)


def softplus(value):
    small = jnp.exp(-jnp.abs(value))
    tail = jnp.where(small < 0.00390625, small * (1.0 - 0.5 * small), jnp.log(1.0 + small))
    return jnp.maximum(value, 0.0) + tail


def add_states(rates_ref, state_ref, total_ref, states, totals):
    state_ref[...] = jnp.exp2(rates_ref[...] * totals) * state_ref[...] + states
    total_ref[...] = total_ref[...] + totals


def sums_within(steps):
    rows = steps.shape[0]
    at = lax.broadcasted_iota(jnp.int32, (rows, rows), 0)
    of = lax.broadcasted_iota(jnp.int32, (rows, rows), 1)
    upto = jnp.where(of <= at, 1.0, 0.0).astype(jnp.bfloat16)
    return jnp.dot(upto, steps, preferred_element_type=jnp.float32)


def step_kernel(
    place_ref, stream_ref, low_ref, map_ref, cols_ref, bias_ref, rates_ref, *rest
):
    own_state_ref, own_total_ref = rest[:2]
    steps_ref, sums_ref, maps_ref, carry_ref, state_ref, total_ref, wide_ref, turn_ref = rest[5:]
    block = pl.program_id(0)
    rows, width = stream_ref.shape[1:]

    @pl.when(block == 0)
    def _():
        state_ref[...] = jnp.zeros_like(state_ref)
        total_ref[...] = jnp.zeros_like(total_ref)
        for n in range(NS):
            wide_ref[n * NS : (n + 1) * NS, :] = jnp.broadcast_to(
                rates_ref[n : n + 1, :], (NS, width)
            ).astype(jnp.bfloat16)

    @pl.when(block == place_ref[0] * CORES)
    def _():
        add_states(rates_ref, state_ref, total_ref, own_state_ref[...], own_total_ref[...])

    maps = map_ref[0].astype(jnp.float32)
    maps_ref[0] = maps
    logits = jnp.dot(low_ref[0], cols_ref[...], preferred_element_type=jnp.float32)
    steps = softplus(logits + bias_ref[...]).astype(jnp.bfloat16)
    steps_ref[...] = steps
    push = steps * stream_ref[0]
    within = sums_within(steps)
    sums_ref[...] = within.astype(jnp.bfloat16)
    whole = within[rows - 1 :, :]
    left = (whole - within).astype(jnp.bfloat16)
    some, chunk, several = rows // 2, CORES * LANES, 4
    state_row = lax.broadcasted_iota(jnp.int32, (NS, some), 0)
    for first in range(0, rows, some):
        span = slice(first, first + some)
        chosen = [
            jnp.concatenate(
                [
                    jnp.where(state_row == m, maps[:NS, span], 0.0).astype(jnp.bfloat16)
                    for m in range(n, n + several)
                ],
                axis=1,
            )
            for n in range(0, NS, several)
        ]
        for item in range(width // chunk):
            lanes = slice(item * chunk, (item + 1) * chunk)
            left_here = left[span, lanes].reshape(some // NS, NS, chunk)
            push_here = push[span, lanes].reshape(some // NS, NS, chunk)
            added = state_ref[:, lanes]
            if first == 0:
                added = jnp.exp2(rates_ref[:, lanes] * whole[:, lanes]) * added
            for n in range(0, NS, several):
                pushed = []
                for m in range(n, n + several):
                    decay = jnp.exp2(left_here * wide_ref[m * NS : (m + 1) * NS, lanes][None])
                    pushed.append((decay * push_here).reshape(some, chunk))
                added = added + jnp.dot(
                    chosen[n // several],
                    jnp.concatenate(pushed, axis=0),
                    preferred_element_type=jnp.float32,
                )
            state_ref[:, lanes] = added
    total_ref[...] = total_ref[...] + whole

    count = pl.num_programs(0)

    @pl.when(block == count - 1)
    def _():
        @pl.when(place_ref[0] * CORES == count)
        def _():
            add_states(rates_ref, state_ref, total_ref, own_state_ref[...], own_total_ref[...])

        write_carry(carry_ref.at[0], state_ref[...], total_ref[...], turn_ref)
        for target in range(1, carry_ref.shape[0]):
            carry_ref[target] = carry_ref[0]


def step_sizes(place, stream, lows, cols, bias, rates, state, total, targets, after, sums, maps):
    others = stream.shape[0]
    chips = others + 1
    rows, width = stream.shape[1] // CORES, stream.shape[2]
    map_row = CORES * rows // MAPS
    blocks = others * CORES
    carry = (targets, (width // LANES + 1) * NS, LANES)

    def slot(b, s):
        chip = b // CORES
        return lax.rem(s[0] - jnp.where(chip < s[0], chip, chip + 1) + chips, chips) - 1

    def core(b):
        return lax.rem(b, CORES)

    def in_row(b, s):
        return jnp.where(b // CORES < s[0], b, b + CORES)

    def fixed(*shape):
        return pl.BlockSpec(shape, lambda b, s: (0,) * len(shape))

    return pl.pallas_call(
        step_kernel,
        grid_spec=pltpu.PrefetchScalarGridSpec(
            num_scalar_prefetch=1,
            grid=(blocks,),
            in_specs=[
                pl.BlockSpec((1, rows, width), lambda b, s: (slot(b, s), core(b), 0)),
                pl.BlockSpec((1, rows, RANK), lambda b, s: (slot(b, s), core(b), 0)),
                pl.BlockSpec((1, MAPS, rows), lambda b, s: (slot(b, s), map_row, core(b))),
                fixed(*cols.shape),
                fixed(*bias.shape),
                fixed(*rates.shape),
                fixed(*state.shape),
                fixed(*total.shape),
            ]
            + [pl.BlockSpec(memory_space=pl.ANY)] * 3,
            out_specs=[
                pl.BlockSpec((rows, width), lambda b, s: (b, 0)),
                pl.BlockSpec((rows, width), lambda b, s: (in_row(b, s), 0)),
                pl.BlockSpec((1, 2 * NS, rows), lambda b, s: (in_row(b, s), 0, 0)),
                fixed(*carry),
            ],
            scratch_shapes=[
                pltpu.VMEM((NS, width), jnp.float32),
                pltpu.VMEM((1, width), jnp.float32),
                pltpu.VMEM((NS * NS, width), jnp.bfloat16),
                pltpu.VMEM((SUBLANES, LANES), jnp.float32),
            ],
        ),
        out_shape=[
            jax.ShapeDtypeStruct((blocks * rows, width), jnp.bfloat16),
            jax.ShapeDtypeStruct(sums.shape, sums.dtype),
            jax.ShapeDtypeStruct(maps.shape, maps.dtype),
            jax.ShapeDtypeStruct(carry, jnp.bfloat16),
        ],
        input_output_aliases={10: 1, 11: 2},
        compiler_params=params,
        name="step_sizes",
    )(place, stream, lows, lows, cols, bias, rates, state, total, after, sums, maps)


def write_carry(out_ref, state, total, turn_ref):
    tile = state.shape[1] // LANES
    turn_ref[...] = jnp.zeros_like(turn_ref)
    for item in range(tile):
        lanes = slice(item * LANES, (item + 1) * LANES)
        turn_ref[item : item + 1, :] = total[:, lanes]
        out_ref[item * NS : (item + 1) * NS, :] = state[:, lanes].astype(jnp.bfloat16)
    out_ref[tile * NS :, :] = jnp.concatenate(split(turn_ref[...]), axis=0)


def follow(carry_ref, rates_ref, state_ref):
    tile = state_ref.shape[1] // LANES
    sums = carry_ref[tile * NS :, :].astype(jnp.float32)
    sums = sums[:SUBLANES, :] + sums[SUBLANES:, :]
    for item in range(tile):
        lanes = slice(item * LANES, (item + 1) * LANES)
        decay = jnp.exp2(rates_ref[:, lanes] * sums[item : item + 1, :])
        added = carry_ref[item * NS : (item + 1) * NS, :].astype(jnp.float32)
        state_ref[:, lanes] = decay * state_ref[:, lanes] + added
    return sums


def scan_blocks(stream_ref, steps_ref, maps, rates_ref, gain_ref, out_ref, state_ref, work_refs):
    out_of_ref, *hist_refs = work_refs
    rows, width = steps_ref.shape
    source = lax.broadcasted_iota(jnp.int32, (LANES, NS * NS), 0)
    column = lax.rem(lax.broadcasted_iota(jnp.int32, (LANES, NS * NS), 1), NS)
    token = lax.rem(lax.broadcasted_iota(jnp.int32, (rows, NS * NS), 0), NS)
    slot = lax.broadcasted_iota(jnp.int32, (rows, NS * NS), 1) // NS
    turned = jnp.concatenate(
        [maps, jnp.zeros((LANES - 2 * NS, rows), jnp.float32)], axis=0
    ).T.astype(jnp.bfloat16)
    pick = jnp.where(source == NS + column, 1.0, 0.0).astype(jnp.bfloat16)
    spread = jnp.dot(turned, pick, preferred_element_type=jnp.float32)
    out_of_ref[...] = jnp.where(token == slot, spread, 0.0).astype(jnp.bfloat16)
    map_in = maps[:NS, :]
    half = width // 2

    def finish(first, hist_ref):
        here = pl.ds(first, NS)
        mixed = jnp.dot(out_of_ref[here, :], hist_ref[...], preferred_element_type=jnp.float32)
        direct = gain_ref[...] * stream_ref[0, here, :].astype(jnp.float32)
        out_ref[here, :] = (mixed + direct).astype(jnp.bfloat16)

    def advance(first, hist_ref):
        here = pl.ds(first, NS)
        into = pltpu.roll(map_in, lax.rem(rows - first, rows), 1)
        for lanes in (slice(0, half), slice(half, width)):
            state = state_ref[:, lanes]
            rates = rates_ref[:, lanes]
            steps = steps_ref[here, lanes].astype(jnp.float32)
            push = steps * stream_ref[0, here, lanes].astype(jnp.float32)
            for near in range(NS):
                this = slice(near, near + 1)
                state = jnp.exp2(rates * steps[this, :]) * state + into[:, this] * push[this, :]
                hist_ref[near * NS : (near + 1) * NS, lanes] = state.astype(jnp.bfloat16)
            state_ref[:, lanes] = state

    def at(group):
        return pl.multiple_of(group * NS, NS)

    def pair(index, nothing):
        finish(at(2 * index), hist_refs[1])
        advance(at(2 * index + 1), hist_refs[0])
        finish(at(2 * index + 1), hist_refs[0])
        advance(at(2 * index + 2), hist_refs[1])
        return nothing

    groups = rows // NS
    advance(0, hist_refs[1])
    lax.fori_loop(0, groups // 2 - 1, pair, 0)
    finish(rows - 2 * NS, hist_refs[1])
    advance(rows - NS, hist_refs[0])
    finish(rows - NS, hist_refs[0])


def work_shapes(rows, width):
    return [
        pltpu.VMEM((rows, NS * NS), jnp.bfloat16),
        pltpu.VMEM((NS * NS, width), jnp.bfloat16),
        pltpu.VMEM((NS * NS, width), jnp.bfloat16),
    ]


def own_kernel(
    place_ref, stream_ref, low_ref, map_ref, cols_ref, bias_ref, rates_ref, gain_ref,
    out_ref, sums_ref, maps_ref, state_ref, total_ref, steps_ref, *work_refs
):
    rows = steps_ref.shape[0]

    @pl.when(pl.program_id(0) == 0)
    def _():
        state_ref[...] = jnp.zeros_like(state_ref)
        total_ref[...] = jnp.zeros_like(total_ref)

    maps = map_ref[...].astype(jnp.float32)
    maps_ref[0] = maps
    logits = jnp.dot(low_ref[...], cols_ref[...], preferred_element_type=jnp.float32)
    steps = softplus(logits + bias_ref[...]).astype(jnp.bfloat16)
    steps_ref[...] = steps
    within = sums_within(steps)
    sums_ref[...] = within.astype(jnp.bfloat16)
    total_ref[...] = total_ref[...] + within[rows - 1 :, :]
    scan_blocks(stream_ref, steps_ref, maps, rates_ref, gain_ref, out_ref, state_ref, work_refs)


def scan_own(place, stream, lows, cols, bias, rates, gain):
    rows, width = stream.shape[1] // CORES, stream.shape[2]
    map_row = CORES * rows // MAPS

    blocks = lax.axis_size("seq")

    def in_row(b, s):
        return s[0] * CORES + b

    def fixed(*shape):
        return pl.BlockSpec(shape, lambda b, s: (0,) * len(shape))

    block = pl.BlockSpec((rows, width), lambda b, s: (in_row(b, s), 0))
    return pl.pallas_call(
        own_kernel,
        grid_spec=pltpu.PrefetchScalarGridSpec(
            num_scalar_prefetch=1,
            grid=(CORES,),
            in_specs=[
                pl.BlockSpec((1, rows, width), lambda b, s: (0, b, 0)),
                pl.BlockSpec((rows, RANK), lambda b, s: (b, 0)),
                pl.BlockSpec((MAPS, rows), lambda b, s: (map_row, b)),
                fixed(*cols.shape),
                fixed(*bias.shape),
                fixed(*rates.shape),
                fixed(*gain.shape),
            ],
            out_specs=[
                block,
                block,
                pl.BlockSpec((1, 2 * NS, rows), lambda b, s: (in_row(b, s), 0, 0)),
                fixed(NS, width),
                fixed(1, width),
            ],
            scratch_shapes=[pltpu.VMEM((rows, width), jnp.bfloat16)] + work_shapes(rows, width),
        ),
        out_shape=[
            jax.ShapeDtypeStruct((blocks * rows, width), jnp.bfloat16),
            jax.ShapeDtypeStruct((blocks * rows, width), jnp.bfloat16),
            jax.ShapeDtypeStruct((blocks, 2 * NS, rows), jnp.float32),
            jax.ShapeDtypeStruct((NS, width), jnp.float32),
            jax.ShapeDtypeStruct((1, width), jnp.float32),
        ],
        compiler_params=params,
        cost_estimate=pl.CostEstimate(flops=4 * 10**9, bytes_accessed=1 << 21, transcendentals=0),
        name="scan_own",
    )(place, stream, lows, lows, cols, bias, rates, gain)


def others_kernel(
    place_ref, stream_ref, steps_ref, maps_ref, rates_ref, gain_ref, part_ref, out_ref, last_ref,
    *work_refs
):
    del part_ref

    @pl.when(lax.rem(pl.program_id(0), CORES) == 0)
    def _():
        last_ref[...] = jnp.zeros_like(last_ref)

    scan_blocks(
        stream_ref, steps_ref, maps_ref[0], rates_ref, gain_ref, out_ref, last_ref.at[0], work_refs
    )


def scan_others(place, stream, steps, maps, rates, gain, part):
    others = stream.shape[0]
    chips = others + 1
    rows, width = stream.shape[1] // CORES, stream.shape[2]

    def slot(b, s):
        chip = b // CORES
        return lax.rem(s[0] - jnp.where(chip < s[0], chip, chip + 1) + chips, chips) - 1

    def in_row(b, s):
        return jnp.where(b // CORES < s[0], b, b + CORES)

    def fixed(*shape):
        return pl.BlockSpec(shape, lambda b, s: (0,) * len(shape))

    return pl.pallas_call(
        others_kernel,
        grid_spec=pltpu.PrefetchScalarGridSpec(
            num_scalar_prefetch=1,
            grid=(others * CORES,),
            in_specs=[
                pl.BlockSpec((1, rows, width), lambda b, s: (slot(b, s), lax.rem(b, CORES), 0)),
                pl.BlockSpec((rows, width), lambda b, s: (b, 0)),
                pl.BlockSpec((1, 2 * NS, rows), lambda b, s: (in_row(b, s), 0, 0)),
                fixed(*rates.shape),
                fixed(*gain.shape),
                pl.BlockSpec(memory_space=pl.ANY),
            ],
            out_specs=[
                pl.BlockSpec((rows, width), lambda b, s: (in_row(b, s), 0)),
                pl.BlockSpec((1, NS, width), lambda b, s: (b // CORES, 0, 0)),
            ],
            scratch_shapes=work_shapes(rows, width),
        ),
        out_shape=[
            jax.ShapeDtypeStruct(part.shape, part.dtype),
            jax.ShapeDtypeStruct((others, NS, width), jnp.float32),
        ],
        input_output_aliases={6: 0},
        compiler_params=params,
        cost_estimate=pl.CostEstimate(flops=4 * 10**9, bytes_accessed=1 << 21, transcendentals=0),
        name="scan_others",
    )(place, stream, steps, maps, rates, gain, part)


def carried_kernel(
    place_ref, part_ref, sums_ref, maps_ref, last_own_ref, last_come_ref, rates_ref, carries_ref,
    out_ref, state_ref, wide_ref, begin_ref, spread_ref,
):
    block = pl.program_id(0)
    rows, width = out_ref.shape
    chip = block // CORES

    @pl.when(block == 0)
    def _():
        state_ref[...] = jnp.zeros_like(state_ref)

        def compose(row, nothing):
            follow(carries_ref.at[row], rates_ref, state_ref)
            return nothing

        lax.fori_loop(0, lax.axis_index("chan"), compose, 0)
        for n in range(NS):
            wide_ref[n * NS : (n + 1) * NS, :] = jnp.broadcast_to(
                rates_ref[n : n + 1, :], (NS, width)
            ).astype(jnp.bfloat16)

    @pl.when((block > 0) & (lax.rem(block, CORES) == 0))
    def _():
        before = jnp.where(chip - 1 == place_ref[0], last_own_ref[...], last_come_ref[0])
        state_ref[...] = state_ref[...] + before

    state = state_ref[...]
    for n in range(NS):
        begin_ref[n * NS : (n + 1) * NS, :] = jnp.broadcast_to(
            state[n : n + 1, :], (NS, width)
        ).astype(jnp.bfloat16)
    maps = jnp.concatenate([maps_ref[0], jnp.zeros((LANES - 2 * NS, rows), jnp.float32)], axis=0).T
    for n in range(NS):
        spread_ref[:, n * LANES : (n + 1) * LANES] = jnp.broadcast_to(
            maps[:, NS + n : NS + n + 1], (rows, LANES)
        ).astype(jnp.bfloat16)
    last = sums_ref[rows - NS :, :].astype(jnp.float32)[NS - 1 :, :]
    state_ref[...] = jnp.exp2(rates_ref[...] * last) * state
    chunk, several = CORES * LANES, 4

    def some(index, nothing):
        near = pl.ds(pl.multiple_of(index * NS, NS), NS)
        for item in range(width // chunk):
            lanes = slice(item * chunk, (item + 1) * chunk)
            total = part_ref[near, lanes].astype(jnp.float32)
            sums = sums_ref[near, lanes]
            for first in range(0, NS, several):
                terms = []
                for n in range(first, first + several):
                    decay = jnp.exp2(sums * wide_ref[n * NS : (n + 1) * NS, lanes])
                    out_of = spread_ref[near, n * LANES : (n + 1) * LANES]
                    out_of = jnp.concatenate([out_of] * (chunk // LANES), axis=1)
                    terms.append(decay * begin_ref[n * NS : (n + 1) * NS, lanes] * out_of)
                four = (terms[0] + terms[1]) + (terms[2] + terms[3])
                total = total + four.astype(jnp.float32)
            out_ref[near, lanes] = total.astype(jnp.bfloat16)
        return nothing

    lax.fori_loop(0, rows // NS, some, 0)


def add_carried(place, part, sums, maps, lasts, rates, carries):
    blocks, _, rows = maps.shape
    others = lasts[1].shape[0]
    width = rates.shape[1]

    def before(b, s):
        chip = jnp.maximum(b // CORES - 1, 0)
        return jnp.minimum(jnp.where(chip < s[0], chip, jnp.maximum(chip - 1, 0)), others - 1)

    def fixed(*shape):
        return pl.BlockSpec(shape, lambda b, s: (0,) * len(shape))

    block = pl.BlockSpec((rows, width), lambda b, s: (b, 0))
    return pl.pallas_call(
        carried_kernel,
        grid_spec=pltpu.PrefetchScalarGridSpec(
            num_scalar_prefetch=1,
            grid=(blocks,),
            in_specs=[
                block,
                block,
                pl.BlockSpec((1, 2 * NS, rows), lambda b, s: (b, 0, 0)),
                fixed(NS, width),
                pl.BlockSpec((1, NS, width), lambda b, s: (before(b, s), 0, 0)),
                fixed(*rates.shape),
                fixed(*carries.shape),
            ],
            out_specs=block,
            scratch_shapes=[
                pltpu.VMEM((NS, width), jnp.float32),
                pltpu.VMEM((NS * NS, width), jnp.bfloat16),
                pltpu.VMEM((NS * NS, width), jnp.bfloat16),
                pltpu.VMEM((rows, NS * LANES), jnp.bfloat16),
            ],
        ),
        out_shape=jax.ShapeDtypeStruct(part.shape, jnp.bfloat16),
        compiler_params=params,
        name="add_carried",
    )(place, part, sums, maps, *lasts, rates, carries)


def local(
    queries, keys, values, doc_lengths, rank_in, bc_weight, rank_out, dt_bias, a_log, skip_gain
):
    devices = lax.axis_size("seq")
    chips = devices // CORES
    targets = lax.axis_size("chan")
    seq_place = lax.axis_index("seq").astype(jnp.int32)
    chip, core = seq_place // CORES, lax.rem(seq_place, CORES)
    place = jnp.stack([chip, core])
    width = queries.shape[2] // devices
    wide = max(HEAD_SIZE, keys.shape[2] // devices)

    def other(device):
        return device + 1 - 2 * (device % CORES)

    swap = [(device, other(device)) for device in range(devices)]
    near = [(device, device + CORES) for device in range(devices - CORES)]
    far = [(device, other(device + CORES)) for device in range(devices - CORES)]

    def onward(chips_on):
        return [(device, (device + chips_on * CORES) % devices) for device in range(devices)]

    own, theirs = select_heads(keys[0], values[0], chips, wide)
    from_near = lax.ppermute(own, "seq", near)
    from_far = lax.ppermute(theirs, "seq", far)
    swapped = lax.ppermute(theirs, "seq", swap)
    queries_after, _ = lax.optimization_barrier((queries[0], own))
    their_queries = lax.ppermute(queries_after, "seq", swap)
    blocks = (own, swapped, from_near, from_far)

    first = seq_place * width
    logs = lax.dynamic_slice_in_dim(a_log, first, width, 0)
    rates = (-LOG2E * jnp.exp(logs)).T
    cols = lax.dynamic_slice_in_dim(rank_out, first, width, 1)
    bias = lax.dynamic_slice_in_dim(dt_bias, first, width, 0)[None]
    gain = lax.dynamic_slice_in_dim(skip_gain, first, width, 0)[None]

    sent, stayed, part = attend(
        place, doc_lengths, (queries[0], their_queries), blocks, rank_in, bc_weight.T,
        (rates, cols, bias, gain),
    )
    come = [lax.ppermute(sent[step], "seq", onward(step + 1)) for step in range(chips - 1)]
    low_own = low_and_maps(part, lax.ppermute(part, "seq", swap))
    low_come = [lax.ppermute(low_own, "seq", onward(step + 1)) for step in range(chips - 1)]
    got_sent = lax.ppermute(sent, "seq", swap)
    got_stayed = lax.ppermute(stayed, "seq", swap)
    attn_rows = join_heads(sent, stayed, got_sent, got_stayed)

    part, sums, maps, state, total = scan_own(place, stayed, low_own, cols, bias, rates, gain)
    come, low_come = jnp.stack(come), jnp.stack(low_come)
    steps, sums, maps, carry = step_sizes(
        place, come, low_come, cols, bias, rates, state, total, targets, attn_rows, sums, maps
    )
    carries = lax.all_to_all(carry, "chan", split_axis=0, concat_axis=0, tiled=True)
    part, last_come = scan_others(place, come, steps, maps, rates, gain, part)
    ssm_rows = add_carried(place, part, sums, maps, (state, last_come), rates, carries)
    return (attn_rows[None], ssm_rows[None])


def solution(mesh):
    return jax.shard_map(
        local,
        mesh=mesh,
        in_specs=(
            P("chan", "seq", None),
            P("chan", "seq", None),
            P("chan", "seq", None),
            P("chan", None),
            P(),
            P(),
            P(),
            P(),
            P(),
            P(),
        ),
        out_specs=(P("chan", "seq", None), P("chan", None, "seq")),
        check_vma=False,
    )
```

```python
import functools
import math

import jax
import jax.numpy as jnp
from jax import lax
from jax.experimental import pallas as pl
from jax.experimental.pallas import tpu as pltpu
from jax.sharding import PartitionSpec as P

QUERY_HEADS = 32
KEY_VALUE_HEADS = 8
HEAD_SIZE = 128
GROUP = QUERY_HEADS // KEY_VALUE_HEADS
NS = 16
RANK = 256
CORES = 2
LANES = 128
SUBLANES = 8
MAPS = 2 * NS
LOG2E = 1.4426950408889634

masked_fill = -1e30
params = pltpu.CompilerParams(vmem_limit_bytes=60 << 20)


def split(value):
    coarse = value.astype(jnp.bfloat16)
    return coarse, (value - coarse.astype(jnp.float32)).astype(jnp.bfloat16)


def run_copies(pairs, sems):
    copies = [
        pltpu.make_async_copy(source, target, sems.at[i]) for i, (source, target) in enumerate(pairs)
    ]
    for copy in copies:
        copy.start()
    for copy in copies:
        copy.wait()


def columns_of(ref, index, size):
    return ref.at[:, pl.ds(pl.multiple_of(index * size, LANES), size)]


def heads_kernel(key_ref, value_ref, own_ref, their_ref, own_held, their_held, in_sems, out_sems):
    core = lax.rem(lax.axis_index("seq"), CORES)
    wide = own_ref.shape[3]
    halves = key_ref.shape[1] // wide // own_ref.shape[0]
    arriving, leaving = [], []
    for target, held, which in ((own_ref, own_held, core), (their_ref, their_held, 1 - core)):
        for chip in range(own_ref.shape[0]):
            index = chip * halves + (which if halves == CORES else 0)
            for kind, source in enumerate((key_ref, value_ref)):
                at, place = len(arriving), held.at[chip, kind]
                arriving.append(
                    pltpu.make_async_copy(columns_of(source, index, wide), place, in_sems.at[at])
                )
                leaving.append(
                    pltpu.make_async_copy(place, target.at[chip, kind], out_sems.at[at])
                )
    for copy in arriving:
        copy.start()
    for copy, onward in zip(arriving, leaving):
        copy.wait()
        onward.start()
    for onward in leaving:
        onward.wait()


def select_heads(keys, values, chips, wide):
    shape = (chips, 2, keys.shape[0], wide)
    return pl.pallas_call(
        heads_kernel,
        in_specs=[pl.BlockSpec(memory_space=pl.ANY)] * 2,
        out_specs=[pl.BlockSpec(memory_space=pl.ANY)] * 2,
        out_shape=[jax.ShapeDtypeStruct(shape, keys.dtype)] * 2,
        scratch_shapes=[pltpu.VMEM(shape, keys.dtype)] * 2
        + [pltpu.SemaphoreType.DMA((4 * chips,))] * 2,
        compiler_params=params,
        name="select_heads",
    )(keys, values)


def join_kernel(sent_ref, stayed_ref, got_sent_ref, got_stayed_ref, out_ref, sems):
    place = lax.axis_index("seq")
    core, chip = lax.rem(place, CORES), place // CORES
    rows = out_ref.shape[0]
    others, _, width = sent_ref.shape
    here = pl.ds(pl.multiple_of(core * rows, rows), rows)
    pairs = []
    for first, rest, which in (
        (stayed_ref, sent_ref, core), (got_stayed_ref, got_sent_ref, 1 - core)
    ):
        for step in range(others + 1):
            source = first.at[0, here, :] if step == 0 else rest.at[step - 1, here, :]
            owner = lax.rem(chip + step, others + 1)
            pairs.append((source, columns_of(out_ref, owner * CORES + which, width)))
    run_copies(pairs, sems)


def join_heads(sent, stayed, got_sent, got_stayed):
    others, rows, width = sent.shape
    return pl.pallas_call(
        join_kernel,
        in_specs=[pl.BlockSpec(memory_space=pl.ANY)] * 4,
        out_shape=jax.ShapeDtypeStruct(
            (rows // CORES, (others + 1) * CORES * width), sent.dtype
        ),
        scratch_shapes=[pltpu.SemaphoreType.DMA((CORES * (others + 1),))],
        compiler_params=params,
        name="join_heads",
    )(sent, stayed, got_sent, got_stayed)


def attend_kernel(
    place_ref, doc_ref, mine_ref, theirs_ref, own_ref, swap_ref, near_ref, far_ref,
    rank_ref, map_ref, *rest, chips,
):
    send_ref, stay_ref, part_ref, mask_ref = rest[-4:]
    step = pl.program_id(0)
    rows = mine_ref.shape[0]
    group = mine_ref.shape[1] // HEAD_SIZE
    chip, core = place_ref[0], place_ref[1]
    first_core = core == 0

    def above(shape):
        row = lax.rem(lax.broadcasted_iota(jnp.int32, shape, 0), rows)
        return lax.broadcasted_iota(jnp.int32, shape, 1) > row

    @pl.when(step == 0)
    def _():
        part_ref[...] = jnp.zeros_like(part_ref)
        own = chip * CORES + core
        swapped = chip * CORES + 1 - core
        near, far = own - CORES, swapped - CORES
        lane = lax.broadcasted_iota(jnp.int32, (rows, rows), 1)
        row = lax.broadcasted_iota(jnp.int32, (rows, rows), 0)
        for item, (place, before, middle) in enumerate(
            (
                (own, near, jnp.where(first_core, far, swapped)),
                (swapped, far, jnp.where(first_core, own, near)),
            )
        ):
            query_pos = place * rows + row
            start = jnp.zeros((rows, rows), jnp.int32)
            bound = jnp.int32(0)
            for doc in range(doc_ref.shape[1]):
                bound = bound + doc_ref[0, doc]
                start = jnp.where(query_pos >= bound, bound, start)
            ends = jnp.where(lane > row, before, place) * rows + lane
            mask_ref[item, :, :rows] = jnp.where(
                (ends >= start) & (ends <= query_pos), 0.0, masked_fill
            )
            mask_ref[item, :, rows:] = jnp.where(
                middle * rows + lane >= start, 0.0, masked_fill
            )

    scale = LOG2E / math.sqrt(HEAD_SIZE)
    ones = jnp.ones((4 * rows, HEAD_SIZE), jnp.bfloat16)

    def all_blocks(kind):
        refs = (near_ref, far_ref, own_ref, swap_ref)
        return jnp.concatenate([ref[0, kind] for ref in refs], axis=0)

    stacked = jnp.concatenate(
        [
            query_ref[:, i * HEAD_SIZE : (i + 1) * HEAD_SIZE]
            for query_ref in (mine_ref, theirs_ref)
            for i in range(group)
        ],
        axis=0,
    )
    scores = lax.dot_general(
        stacked, all_blocks(0), (((1,), (1,)), ((), ())), preferred_element_type=jnp.float32
    )
    shape = (group * rows, rows)
    before = above(shape)
    none = jnp.zeros(shape, jnp.bfloat16)
    spreads = []
    for item in range(CORES):
        score = scores[item * group * rows : (item + 1) * group * rows, :]
        near, far, own, swapped = (score[:, i * rows : (i + 1) * rows] for i in range(4))
        if item == 0:
            ends, middle = jnp.where(before, near, own), jnp.where(first_core, far, swapped)
        else:
            ends, middle = jnp.where(before, far, swapped), jnp.where(first_core, own, near)
        fill = mask_ref[item]
        kept = jnp.concatenate([ends, middle], axis=1)
        kept = jnp.concatenate(
            [kept[i * rows : (i + 1) * rows, :] + fill for i in range(group)], axis=0
        )
        peak = jnp.max(kept, axis=1, keepdims=True)
        raw = jnp.exp2((kept - peak) * scale).astype(jnp.bfloat16)
        ends, middle = raw[:, :rows], raw[:, rows:]
        old, new = jnp.where(before, ends, none), jnp.where(before, none, ends)
        if_first = jnp.where(first_core, middle, none)
        if_second = jnp.where(first_core, none, middle)
        spreads.append(
            jnp.concatenate(
                [old, if_first, new, if_second] if item == 0 else [if_second, old, if_first, new],
                axis=1,
            )
        )
    both = jnp.dot(
        jnp.concatenate(spreads, axis=0),
        jnp.concatenate([all_blocks(1), ones], axis=1),
        preferred_element_type=jnp.float32,
    )
    mixed = (both[:, :HEAD_SIZE] * pl.reciprocal(both[:, HEAD_SIZE:])).astype(jnp.bfloat16)
    outputs = [
        jnp.concatenate(
            [mixed[(item * group + i) * rows : (item * group + i + 1) * rows, :] for i in range(group)],
            axis=1,
        )
        for item in range(CORES)
    ]
    stream = jnp.concatenate(
        [
            jnp.where(first_core, outputs[0], outputs[1]),
            jnp.where(first_core, outputs[1], outputs[0]),
        ],
        axis=0,
    )
    last = step >= pl.num_programs(0) - pl.num_programs(0) // chips

    @pl.when(last)
    def _():
        stay_ref[0] = stream

    @pl.when(jnp.logical_not(last))
    def _():
        send_ref[0] = stream

    both = CORES * rows
    part_ref[:both, :] += jnp.dot(stream, rank_ref[...], preferred_element_type=jnp.float32)
    part_ref[both:, :] += lax.dot_general(
        map_ref[...], stream, (((1,), (1,)), ((), ())), preferred_element_type=jnp.float32
    )


def attend(place, doc_lengths, queries, blocks, rank_in, map_rows, after):
    mine, theirs = queries
    chips, _, rows, columns = blocks[0].shape
    heads = columns // HEAD_SIZE
    width = mine.shape[1] // (chips * CORES)
    wide = width // heads

    def owner(j, s):
        return lax.rem(s[0] + 1 + j // heads, chips)

    def column(j, s):
        return (owner(j, s) * CORES + s[1]) * heads + lax.rem(j, heads)

    def sent(j, s):
        at = jnp.minimum(j, (chips - 1) * heads - 1)
        return (at // heads, 0, lax.rem(at, heads))

    query = pl.BlockSpec((rows, wide), lambda j, s: (0, column(j, s)))
    block = pl.BlockSpec(
        (1, 2, rows, HEAD_SIZE), lambda j, s: (owner(j, s), 0, 0, lax.rem(j, heads))
    )
    return pl.pallas_call(
        functools.partial(attend_kernel, chips=chips),
        grid_spec=pltpu.PrefetchScalarGridSpec(
            num_scalar_prefetch=1,
            grid=(chips * heads,),
            in_specs=[pl.BlockSpec(memory_space=pltpu.SMEM), query, query]
            + [block] * 4
            + [
                pl.BlockSpec((wide, RANK), lambda j, s: (column(j, s), 0)),
                pl.BlockSpec((2 * NS, wide), lambda j, s: (0, column(j, s))),
            ]
            + [pl.BlockSpec(memory_space=pl.ANY)] * len(after),
            out_specs=[
                pl.BlockSpec((1, CORES * rows, wide), sent),
                pl.BlockSpec(
                    (1, CORES * rows, wide),
                    lambda j, s: (0, 0, jnp.maximum(j - (chips - 1) * heads, 0)),
                ),
                pl.BlockSpec((CORES * rows + 2 * NS, RANK), lambda j, s: (0, 0)),
            ],
            scratch_shapes=[pltpu.VMEM((2, rows, 2 * rows), jnp.float32)],
        ),
        out_shape=[
            jax.ShapeDtypeStruct((chips - 1, CORES * rows, width), jnp.bfloat16),
            jax.ShapeDtypeStruct((1, CORES * rows, width), jnp.bfloat16),
            jax.ShapeDtypeStruct((CORES * rows + 2 * NS, RANK), jnp.float32),
        ],
        compiler_params=params,
        cost_estimate=pl.CostEstimate(flops=5 * 10**9, bytes_accessed=1 << 22, transcendentals=0),
        name="attend",
    )(place, doc_lengths, mine, theirs, *blocks, rank_in, map_rows, *after)


def low_kernel(mine_ref, theirs_ref, out_ref):
    out_ref[...] = (mine_ref[...] + theirs_ref[...]).astype(jnp.bfloat16)


def low_and_maps(mine, theirs):
    return pl.pallas_call(
        low_kernel,
        out_shape=jax.ShapeDtypeStruct(mine.shape, jnp.bfloat16),
        compiler_params=params,
        cost_estimate=pl.CostEstimate(flops=1, bytes_accessed=1, transcendentals=0),
        name="low_and_maps",
    )(mine, theirs)


def softplus(value):
    small = jnp.exp(-jnp.abs(value))
    tail = jnp.where(small < 0.00390625, small * (1.0 - 0.5 * small), jnp.log(1.0 + small))
    return jnp.maximum(value, 0.0) + tail


def add_states(rates_ref, state_ref, total_ref, states, totals):
    state_ref[...] = jnp.exp2(rates_ref[...] * totals) * state_ref[...] + states
    total_ref[...] = total_ref[...] + totals


def sums_within(steps):
    rows = steps.shape[0]
    at = lax.broadcasted_iota(jnp.int32, (rows, rows), 0)
    of = lax.broadcasted_iota(jnp.int32, (rows, rows), 1)
    upto = jnp.where(of <= at, 1.0, 0.0).astype(jnp.bfloat16)
    return jnp.dot(upto, steps, preferred_element_type=jnp.float32)


def step_kernel(
    place_ref, stream_ref, low_ref, map_ref, cols_ref, bias_ref, rates_ref, *rest
):
    own_state_ref, own_total_ref = rest[:2]
    steps_ref, sums_ref, maps_ref, carry_ref, state_ref, total_ref, wide_ref, turn_ref = rest[5:]
    block = pl.program_id(0)
    rows, width = stream_ref.shape[1:]

    @pl.when(block == 0)
    def _():
        state_ref[...] = jnp.zeros_like(state_ref)
        total_ref[...] = jnp.zeros_like(total_ref)
        for n in range(NS):
            wide_ref[n * NS : (n + 1) * NS, :] = jnp.broadcast_to(
                rates_ref[n : n + 1, :], (NS, width)
            ).astype(jnp.bfloat16)

    @pl.when(block == place_ref[0] * CORES)
    def _():
        add_states(rates_ref, state_ref, total_ref, own_state_ref[...], own_total_ref[...])

    maps = map_ref[0].astype(jnp.float32)
    maps_ref[0] = maps
    logits = jnp.dot(low_ref[0], cols_ref[...], preferred_element_type=jnp.float32)
    steps = softplus(logits + bias_ref[...]).astype(jnp.bfloat16)
    steps_ref[...] = steps
    push = steps * stream_ref[0]
    within = sums_within(steps)
    sums_ref[...] = within.astype(jnp.bfloat16)
    whole = within[rows - 1 :, :]
    left = (whole - within).astype(jnp.bfloat16)
    some, chunk, several = rows // 2, CORES * LANES, 4
    state_row = lax.broadcasted_iota(jnp.int32, (NS, some), 0)
    for first in range(0, rows, some):
        span = slice(first, first + some)
        chosen = [
            jnp.concatenate(
                [
                    jnp.where(state_row == m, maps[:NS, span], 0.0).astype(jnp.bfloat16)
                    for m in range(n, n + several)
                ],
                axis=1,
            )
            for n in range(0, NS, several)
        ]
        for item in range(width // chunk):
            lanes = slice(item * chunk, (item + 1) * chunk)
            left_here = left[span, lanes].reshape(some // NS, NS, chunk)
            push_here = push[span, lanes].reshape(some // NS, NS, chunk)
            added = state_ref[:, lanes]
            if first == 0:
                added = jnp.exp2(rates_ref[:, lanes] * whole[:, lanes]) * added
            for n in range(0, NS, several):
                pushed = []
                for m in range(n, n + several):
                    decay = jnp.exp2(left_here * wide_ref[m * NS : (m + 1) * NS, lanes][None])
                    pushed.append((decay * push_here).reshape(some, chunk))
                added = added + jnp.dot(
                    chosen[n // several],
                    jnp.concatenate(pushed, axis=0),
                    preferred_element_type=jnp.float32,
                )
            state_ref[:, lanes] = added
    total_ref[...] = total_ref[...] + whole

    count = pl.num_programs(0)

    @pl.when(block == count - 1)
    def _():
        @pl.when(place_ref[0] * CORES == count)
        def _():
            add_states(rates_ref, state_ref, total_ref, own_state_ref[...], own_total_ref[...])

        write_carry(carry_ref.at[0], state_ref[...], total_ref[...], turn_ref)
        for target in range(1, carry_ref.shape[0]):
            carry_ref[target] = carry_ref[0]


def step_sizes(place, stream, lows, cols, bias, rates, state, total, targets, after, sums, maps):
    others = stream.shape[0]
    chips = others + 1
    rows, width = stream.shape[1] // CORES, stream.shape[2]
    map_row = CORES * rows // MAPS
    blocks = others * CORES
    carry = (targets, (width // LANES + 1) * NS, LANES)

    def slot(b, s):
        chip = b // CORES
        return lax.rem(s[0] - jnp.where(chip < s[0], chip, chip + 1) + chips, chips) - 1

    def core(b):
        return lax.rem(b, CORES)

    def in_row(b, s):
        return jnp.where(b // CORES < s[0], b, b + CORES)

    def fixed(*shape):
        return pl.BlockSpec(shape, lambda b, s: (0,) * len(shape))

    return pl.pallas_call(
        step_kernel,
        grid_spec=pltpu.PrefetchScalarGridSpec(
            num_scalar_prefetch=1,
            grid=(blocks,),
            in_specs=[
                pl.BlockSpec((1, rows, width), lambda b, s: (slot(b, s), core(b), 0)),
                pl.BlockSpec((1, rows, RANK), lambda b, s: (slot(b, s), core(b), 0)),
                pl.BlockSpec((1, MAPS, rows), lambda b, s: (slot(b, s), map_row, core(b))),
                fixed(*cols.shape),
                fixed(*bias.shape),
                fixed(*rates.shape),
                fixed(*state.shape),
                fixed(*total.shape),
            ]
            + [pl.BlockSpec(memory_space=pl.ANY)] * 3,
            out_specs=[
                pl.BlockSpec((rows, width), lambda b, s: (b, 0)),
                pl.BlockSpec((rows, width), lambda b, s: (in_row(b, s), 0)),
                pl.BlockSpec((1, 2 * NS, rows), lambda b, s: (in_row(b, s), 0, 0)),
                fixed(*carry),
            ],
            scratch_shapes=[
                pltpu.VMEM((NS, width), jnp.float32),
                pltpu.VMEM((1, width), jnp.float32),
                pltpu.VMEM((NS * NS, width), jnp.bfloat16),
                pltpu.VMEM((SUBLANES, LANES), jnp.float32),
            ],
        ),
        out_shape=[
            jax.ShapeDtypeStruct((blocks * rows, width), jnp.bfloat16),
            jax.ShapeDtypeStruct(sums.shape, sums.dtype),
            jax.ShapeDtypeStruct(maps.shape, maps.dtype),
            jax.ShapeDtypeStruct(carry, jnp.bfloat16),
        ],
        input_output_aliases={10: 1, 11: 2},
        compiler_params=params,
        name="step_sizes",
    )(place, stream, lows, lows, cols, bias, rates, state, total, after, sums, maps)


def write_carry(out_ref, state, total, turn_ref):
    tile = state.shape[1] // LANES
    turn_ref[...] = jnp.zeros_like(turn_ref)
    for item in range(tile):
        lanes = slice(item * LANES, (item + 1) * LANES)
        turn_ref[item : item + 1, :] = total[:, lanes]
        out_ref[item * NS : (item + 1) * NS, :] = state[:, lanes].astype(jnp.bfloat16)
    out_ref[tile * NS :, :] = jnp.concatenate(split(turn_ref[...]), axis=0)


def follow(carry_ref, rates_ref, state_ref):
    tile = state_ref.shape[1] // LANES
    sums = carry_ref[tile * NS :, :].astype(jnp.float32)
    sums = sums[:SUBLANES, :] + sums[SUBLANES:, :]
    for item in range(tile):
        lanes = slice(item * LANES, (item + 1) * LANES)
        decay = jnp.exp2(rates_ref[:, lanes] * sums[item : item + 1, :])
        added = carry_ref[item * NS : (item + 1) * NS, :].astype(jnp.float32)
        state_ref[:, lanes] = decay * state_ref[:, lanes] + added
    return sums


def scan_blocks(stream_ref, steps_ref, maps, rates_ref, gain_ref, out_ref, state_ref, work_refs):
    out_of_ref, *hist_refs = work_refs
    rows, width = steps_ref.shape
    source = lax.broadcasted_iota(jnp.int32, (LANES, NS * NS), 0)
    column = lax.rem(lax.broadcasted_iota(jnp.int32, (LANES, NS * NS), 1), NS)
    token = lax.rem(lax.broadcasted_iota(jnp.int32, (rows, NS * NS), 0), NS)
    slot = lax.broadcasted_iota(jnp.int32, (rows, NS * NS), 1) // NS
    turned = jnp.concatenate(
        [maps, jnp.zeros((LANES - 2 * NS, rows), jnp.float32)], axis=0
    ).T.astype(jnp.bfloat16)
    pick = jnp.where(source == NS + column, 1.0, 0.0).astype(jnp.bfloat16)
    spread = jnp.dot(turned, pick, preferred_element_type=jnp.float32)
    out_of_ref[...] = jnp.where(token == slot, spread, 0.0).astype(jnp.bfloat16)
    map_in = maps[:NS, :]
    half = width // 2

    def finish(first, hist_ref):
        here = pl.ds(first, NS)
        mixed = jnp.dot(out_of_ref[here, :], hist_ref[...], preferred_element_type=jnp.float32)
        direct = gain_ref[...] * stream_ref[0, here, :].astype(jnp.float32)
        out_ref[here, :] = (mixed + direct).astype(jnp.bfloat16)

    def advance(first, hist_ref):
        here = pl.ds(first, NS)
        into = pltpu.roll(map_in, lax.rem(rows - first, rows), 1)
        for lanes in (slice(0, half), slice(half, width)):
            state = state_ref[:, lanes]
            rates = rates_ref[:, lanes]
            steps = steps_ref[here, lanes].astype(jnp.float32)
            push = steps * stream_ref[0, here, lanes].astype(jnp.float32)
            for near in range(NS):
                this = slice(near, near + 1)
                state = jnp.exp2(rates * steps[this, :]) * state + into[:, this] * push[this, :]
                hist_ref[near * NS : (near + 1) * NS, lanes] = state.astype(jnp.bfloat16)
            state_ref[:, lanes] = state

    def at(group):
        return pl.multiple_of(group * NS, NS)

    def pair(index, nothing):
        finish(at(2 * index), hist_refs[1])
        advance(at(2 * index + 1), hist_refs[0])
        finish(at(2 * index + 1), hist_refs[0])
        advance(at(2 * index + 2), hist_refs[1])
        return nothing

    groups = rows // NS
    advance(0, hist_refs[1])
    lax.fori_loop(0, groups // 2 - 1, pair, 0)
    finish(rows - 2 * NS, hist_refs[1])
    advance(rows - NS, hist_refs[0])
    finish(rows - NS, hist_refs[0])


def work_shapes(rows, width):
    return [
        pltpu.VMEM((rows, NS * NS), jnp.bfloat16),
        pltpu.VMEM((NS * NS, width), jnp.bfloat16),
        pltpu.VMEM((NS * NS, width), jnp.bfloat16),
    ]


def own_kernel(
    place_ref, stream_ref, low_ref, map_ref, cols_ref, bias_ref, rates_ref, gain_ref,
    out_ref, sums_ref, maps_ref, state_ref, total_ref, steps_ref, *work_refs
):
    rows = steps_ref.shape[0]

    @pl.when(pl.program_id(0) == 0)
    def _():
        state_ref[...] = jnp.zeros_like(state_ref)
        total_ref[...] = jnp.zeros_like(total_ref)

    maps = map_ref[...].astype(jnp.float32)
    maps_ref[0] = maps
    logits = jnp.dot(low_ref[...], cols_ref[...], preferred_element_type=jnp.float32)
    steps = softplus(logits + bias_ref[...]).astype(jnp.bfloat16)
    steps_ref[...] = steps
    within = sums_within(steps)
    sums_ref[...] = within.astype(jnp.bfloat16)
    total_ref[...] = total_ref[...] + within[rows - 1 :, :]
    scan_blocks(stream_ref, steps_ref, maps, rates_ref, gain_ref, out_ref, state_ref, work_refs)


def scan_own(place, stream, lows, cols, bias, rates, gain):
    rows, width = stream.shape[1] // CORES, stream.shape[2]
    map_row = CORES * rows // MAPS

    blocks = lax.axis_size("seq")

    def in_row(b, s):
        return s[0] * CORES + b

    def fixed(*shape):
        return pl.BlockSpec(shape, lambda b, s: (0,) * len(shape))

    block = pl.BlockSpec((rows, width), lambda b, s: (in_row(b, s), 0))
    return pl.pallas_call(
        own_kernel,
        grid_spec=pltpu.PrefetchScalarGridSpec(
            num_scalar_prefetch=1,
            grid=(CORES,),
            in_specs=[
                pl.BlockSpec((1, rows, width), lambda b, s: (0, b, 0)),
                pl.BlockSpec((rows, RANK), lambda b, s: (b, 0)),
                pl.BlockSpec((MAPS, rows), lambda b, s: (map_row, b)),
                fixed(*cols.shape),
                fixed(*bias.shape),
                fixed(*rates.shape),
                fixed(*gain.shape),
            ],
            out_specs=[
                block,
                block,
                pl.BlockSpec((1, 2 * NS, rows), lambda b, s: (in_row(b, s), 0, 0)),
                fixed(NS, width),
                fixed(1, width),
            ],
            scratch_shapes=[pltpu.VMEM((rows, width), jnp.bfloat16)] + work_shapes(rows, width),
        ),
        out_shape=[
            jax.ShapeDtypeStruct((blocks * rows, width), jnp.bfloat16),
            jax.ShapeDtypeStruct((blocks * rows, width), jnp.bfloat16),
            jax.ShapeDtypeStruct((blocks, 2 * NS, rows), jnp.float32),
            jax.ShapeDtypeStruct((NS, width), jnp.float32),
            jax.ShapeDtypeStruct((1, width), jnp.float32),
        ],
        compiler_params=params,
        cost_estimate=pl.CostEstimate(flops=4 * 10**9, bytes_accessed=1 << 21, transcendentals=0),
        name="scan_own",
    )(place, stream, lows, lows, cols, bias, rates, gain)


def others_kernel(
    place_ref, stream_ref, steps_ref, maps_ref, rates_ref, gain_ref, part_ref, out_ref, last_ref,
    *work_refs
):
    del part_ref

    @pl.when(lax.rem(pl.program_id(0), CORES) == 0)
    def _():
        last_ref[...] = jnp.zeros_like(last_ref)

    scan_blocks(
        stream_ref, steps_ref, maps_ref[0], rates_ref, gain_ref, out_ref, last_ref.at[0], work_refs
    )


def scan_others(place, stream, steps, maps, rates, gain, part):
    others = stream.shape[0]
    chips = others + 1
    rows, width = stream.shape[1] // CORES, stream.shape[2]

    def slot(b, s):
        chip = b // CORES
        return lax.rem(s[0] - jnp.where(chip < s[0], chip, chip + 1) + chips, chips) - 1

    def in_row(b, s):
        return jnp.where(b // CORES < s[0], b, b + CORES)

    def fixed(*shape):
        return pl.BlockSpec(shape, lambda b, s: (0,) * len(shape))

    return pl.pallas_call(
        others_kernel,
        grid_spec=pltpu.PrefetchScalarGridSpec(
            num_scalar_prefetch=1,
            grid=(others * CORES,),
            in_specs=[
                pl.BlockSpec((1, rows, width), lambda b, s: (slot(b, s), lax.rem(b, CORES), 0)),
                pl.BlockSpec((rows, width), lambda b, s: (b, 0)),
                pl.BlockSpec((1, 2 * NS, rows), lambda b, s: (in_row(b, s), 0, 0)),
                fixed(*rates.shape),
                fixed(*gain.shape),
                pl.BlockSpec(memory_space=pl.ANY),
            ],
            out_specs=[
                pl.BlockSpec((rows, width), lambda b, s: (in_row(b, s), 0)),
                pl.BlockSpec((1, NS, width), lambda b, s: (b // CORES, 0, 0)),
            ],
            scratch_shapes=work_shapes(rows, width),
        ),
        out_shape=[
            jax.ShapeDtypeStruct(part.shape, part.dtype),
            jax.ShapeDtypeStruct((others, NS, width), jnp.float32),
        ],
        input_output_aliases={6: 0},
        compiler_params=params,
        cost_estimate=pl.CostEstimate(flops=4 * 10**9, bytes_accessed=1 << 21, transcendentals=0),
        name="scan_others",
    )(place, stream, steps, maps, rates, gain, part)


def carried_kernel(
    place_ref, part_ref, sums_ref, maps_ref, last_own_ref, last_come_ref, rates_ref, carries_ref,
    out_ref, state_ref, wide_ref, begin_ref, spread_ref,
):
    block = pl.program_id(0)
    rows, width = out_ref.shape
    chip = block // CORES

    @pl.when(block == 0)
    def _():
        state_ref[...] = jnp.zeros_like(state_ref)

        def compose(row, nothing):
            follow(carries_ref.at[row], rates_ref, state_ref)
            return nothing

        lax.fori_loop(0, lax.axis_index("chan"), compose, 0)
        for n in range(NS):
            wide_ref[n * NS : (n + 1) * NS, :] = jnp.broadcast_to(
                rates_ref[n : n + 1, :], (NS, width)
            ).astype(jnp.bfloat16)

    @pl.when((block > 0) & (lax.rem(block, CORES) == 0))
    def _():
        before = jnp.where(chip - 1 == place_ref[0], last_own_ref[...], last_come_ref[0])
        state_ref[...] = state_ref[...] + before

    state = state_ref[...]
    for n in range(NS):
        begin_ref[n * NS : (n + 1) * NS, :] = jnp.broadcast_to(
            state[n : n + 1, :], (NS, width)
        ).astype(jnp.bfloat16)
    maps = jnp.concatenate([maps_ref[0], jnp.zeros((LANES - 2 * NS, rows), jnp.float32)], axis=0).T
    for n in range(NS):
        spread_ref[:, n * LANES : (n + 1) * LANES] = jnp.broadcast_to(
            maps[:, NS + n : NS + n + 1], (rows, LANES)
        ).astype(jnp.bfloat16)
    last = sums_ref[rows - NS :, :].astype(jnp.float32)[NS - 1 :, :]
    state_ref[...] = jnp.exp2(rates_ref[...] * last) * state
    chunk, several = CORES * LANES, 4

    def some(index, nothing):
        near = pl.ds(pl.multiple_of(index * NS, NS), NS)
        for item in range(width // chunk):
            lanes = slice(item * chunk, (item + 1) * chunk)
            total = part_ref[near, lanes].astype(jnp.float32)
            sums = sums_ref[near, lanes]
            for first in range(0, NS, several):
                terms = []
                for n in range(first, first + several):
                    decay = jnp.exp2(sums * wide_ref[n * NS : (n + 1) * NS, lanes])
                    out_of = spread_ref[near, n * LANES : (n + 1) * LANES]
                    out_of = jnp.concatenate([out_of] * (chunk // LANES), axis=1)
                    terms.append(decay * begin_ref[n * NS : (n + 1) * NS, lanes] * out_of)
                four = (terms[0] + terms[1]) + (terms[2] + terms[3])
                total = total + four.astype(jnp.float32)
            out_ref[near, lanes] = total.astype(jnp.bfloat16)
        return nothing

    lax.fori_loop(0, rows // NS, some, 0)


def add_carried(place, part, sums, maps, lasts, rates, carries):
    blocks, _, rows = maps.shape
    others = lasts[1].shape[0]
    width = rates.shape[1]

    def before(b, s):
        chip = jnp.maximum(b // CORES - 1, 0)
        return jnp.minimum(jnp.where(chip < s[0], chip, jnp.maximum(chip - 1, 0)), others - 1)

    def fixed(*shape):
        return pl.BlockSpec(shape, lambda b, s: (0,) * len(shape))

    block = pl.BlockSpec((rows, width), lambda b, s: (b, 0))
    return pl.pallas_call(
        carried_kernel,
        grid_spec=pltpu.PrefetchScalarGridSpec(
            num_scalar_prefetch=1,
            grid=(blocks,),
            in_specs=[
                block,
                block,
                pl.BlockSpec((1, 2 * NS, rows), lambda b, s: (b, 0, 0)),
                fixed(NS, width),
                pl.BlockSpec((1, NS, width), lambda b, s: (before(b, s), 0, 0)),
                fixed(*rates.shape),
                fixed(*carries.shape),
            ],
            out_specs=block,
            scratch_shapes=[
                pltpu.VMEM((NS, width), jnp.float32),
                pltpu.VMEM((NS * NS, width), jnp.bfloat16),
                pltpu.VMEM((NS * NS, width), jnp.bfloat16),
                pltpu.VMEM((rows, NS * LANES), jnp.bfloat16),
            ],
        ),
        out_shape=jax.ShapeDtypeStruct(part.shape, jnp.bfloat16),
        compiler_params=params,
        name="add_carried",
    )(place, part, sums, maps, *lasts, rates, carries)


def local(
    queries, keys, values, doc_lengths, rank_in, bc_weight, rank_out, dt_bias, a_log, skip_gain
):
    devices = lax.axis_size("seq")
    chips = devices // CORES
    targets = lax.axis_size("chan")
    seq_place = lax.axis_index("seq").astype(jnp.int32)
    chip, core = seq_place // CORES, lax.rem(seq_place, CORES)
    place = jnp.stack([chip, core])
    width = queries.shape[2] // devices
    wide = max(HEAD_SIZE, keys.shape[2] // devices)

    def other(device):
        return device + 1 - 2 * (device % CORES)

    swap = [(device, other(device)) for device in range(devices)]
    near = [(device, device + CORES) for device in range(devices - CORES)]
    far = [(device, other(device + CORES)) for device in range(devices - CORES)]

    def onward(chips_on):
        return [(device, (device + chips_on * CORES) % devices) for device in range(devices)]

    own, theirs = select_heads(keys[0], values[0], chips, wide)
    from_near = lax.ppermute(own, "seq", near)
    from_far = lax.ppermute(theirs, "seq", far)
    swapped = lax.ppermute(theirs, "seq", swap)
    queries_after, _ = lax.optimization_barrier((queries[0], own))
    their_queries = lax.ppermute(queries_after, "seq", swap)
    blocks = (own, swapped, from_near, from_far)

    first = seq_place * width
    logs = lax.dynamic_slice_in_dim(a_log, first, width, 0)
    rates = (-LOG2E * jnp.exp(logs)).T
    cols = lax.dynamic_slice_in_dim(rank_out, first, width, 1)
    bias = lax.dynamic_slice_in_dim(dt_bias, first, width, 0)[None]
    gain = lax.dynamic_slice_in_dim(skip_gain, first, width, 0)[None]

    sent, stayed, part = attend(
        place, doc_lengths, (queries[0], their_queries), blocks, rank_in, bc_weight.T,
        (rates, cols, bias, gain),
    )
    come = [lax.ppermute(sent[step], "seq", onward(step + 1)) for step in range(chips - 1)]
    low_own = low_and_maps(part, lax.ppermute(part, "seq", swap))
    low_come = [lax.ppermute(low_own, "seq", onward(step + 1)) for step in range(chips - 1)]
    got_sent = lax.ppermute(sent, "seq", swap)
    got_stayed = lax.ppermute(stayed, "seq", swap)
    attn_rows = join_heads(sent, stayed, got_sent, got_stayed)

    part, sums, maps, state, total = scan_own(place, stayed, low_own, cols, bias, rates, gain)
    come, low_come = jnp.stack(come), jnp.stack(low_come)
    steps, sums, maps, carry = step_sizes(
        place, come, low_come, cols, bias, rates, state, total, targets, attn_rows, sums, maps
    )
    carries = lax.all_to_all(carry, "chan", split_axis=0, concat_axis=0, tiled=True)
    part, last_come = scan_others(place, come, steps, maps, rates, gain, part)
    ssm_rows = add_carried(place, part, sums, maps, (state, last_come), rates, carries)
    return (attn_rows[None], ssm_rows[None])


def solution(mesh):
    return jax.shard_map(
        local,
        mesh=mesh,
        in_specs=(
            P("chan", "seq", None),
            P("chan", "seq", None),
            P("chan", "seq", None),
            P("chan", None),
            P(),
            P(),
            P(),
            P(),
            P(),
            P(),
        ),
        out_specs=(P("chan", "seq", None), P("chan", None, "seq")),
        check_vma=False,
    )
```

```python
import functools
import math

import jax
import jax.numpy as jnp
from jax import lax
from jax.experimental import pallas as pl
from jax.experimental.pallas import tpu as pltpu
from jax.sharding import PartitionSpec as P

QUERY_HEADS = 32
KEY_VALUE_HEADS = 8
HEAD_SIZE = 128
GROUP = QUERY_HEADS // KEY_VALUE_HEADS
NS = 16
RANK = 256
CORES = 2
LANES = 128
SUBLANES = 8
MAPS = 2 * NS
LOG2E = 1.4426950408889634

masked_fill = -1e30
params = pltpu.CompilerParams(vmem_limit_bytes=60 << 20)


def split(value):
    coarse = value.astype(jnp.bfloat16)
    return coarse, (value - coarse.astype(jnp.float32)).astype(jnp.bfloat16)


def run_copies(pairs, sems):
    copies = [
        pltpu.make_async_copy(source, target, sems.at[i]) for i, (source, target) in enumerate(pairs)
    ]
    for copy in copies:
        copy.start()
    for copy in copies:
        copy.wait()


def columns_of(ref, index, size):
    return ref.at[:, pl.ds(pl.multiple_of(index * size, LANES), size)]


def heads_kernel(key_ref, value_ref, own_ref, their_ref, sems):
    core = lax.rem(lax.axis_index("seq"), CORES)
    wide = own_ref.shape[3]
    halves = key_ref.shape[1] // wide // own_ref.shape[0]
    pairs = []
    for target, which in ((own_ref, core), (their_ref, 1 - core)):
        for chip in range(own_ref.shape[0]):
            index = chip * halves + (which if halves == CORES else 0)
            for kind, source in enumerate((key_ref, value_ref)):
                pairs.append((columns_of(source, index, wide), target.at[chip, kind]))
    run_copies(pairs, sems)


def select_heads(keys, values, chips, wide):
    shape = jax.ShapeDtypeStruct((chips, 2, keys.shape[0], wide), keys.dtype)
    return pl.pallas_call(
        heads_kernel,
        in_specs=[pl.BlockSpec(memory_space=pl.ANY)] * 2,
        out_shape=[shape, shape],
        scratch_shapes=[pltpu.SemaphoreType.DMA((4 * chips,))],
        compiler_params=params,
        name="select_heads",
    )(keys, values)


def join_kernel(sent_ref, stayed_ref, got_sent_ref, got_stayed_ref, out_ref, sems):
    place = lax.axis_index("seq")
    core, chip = lax.rem(place, CORES), place // CORES
    rows = out_ref.shape[0]
    others, _, width = sent_ref.shape
    here = pl.ds(pl.multiple_of(core * rows, rows), rows)
    pairs = []
    for first, rest, which in (
        (stayed_ref, sent_ref, core), (got_stayed_ref, got_sent_ref, 1 - core)
    ):
        for step in range(others + 1):
            source = first.at[0, here, :] if step == 0 else rest.at[step - 1, here, :]
            owner = lax.rem(chip + step, others + 1)
            pairs.append((source, columns_of(out_ref, owner * CORES + which, width)))
    run_copies(pairs, sems)


def join_heads(sent, stayed, got_sent, got_stayed):
    others, rows, width = sent.shape
    return pl.pallas_call(
        join_kernel,
        in_specs=[pl.BlockSpec(memory_space=pl.ANY)] * 4,
        out_shape=jax.ShapeDtypeStruct(
            (rows // CORES, (others + 1) * CORES * width), sent.dtype
        ),
        scratch_shapes=[pltpu.SemaphoreType.DMA((CORES * (others + 1),))],
        compiler_params=params,
        name="join_heads",
    )(sent, stayed, got_sent, got_stayed)


def attend_kernel(
    place_ref, doc_ref, mine_ref, theirs_ref, own_ref, swap_ref, near_ref, far_ref,
    rank_ref, map_ref, *rest, chips,
):
    send_ref, stay_ref, part_ref, mask_ref = rest[-4:]
    step = pl.program_id(0)
    rows = mine_ref.shape[0]
    group = mine_ref.shape[1] // HEAD_SIZE
    chip, core = place_ref[0], place_ref[1]
    first_core = core == 0

    def below(shape):
        column = lax.rem(lax.broadcasted_iota(jnp.int32, shape, 1), rows)
        return lax.broadcasted_iota(jnp.int32, shape, 0) > column

    @pl.when(step == 0)
    def _():
        part_ref[...] = jnp.zeros_like(part_ref)
        own = chip * CORES + core
        swapped = chip * CORES + 1 - core
        near, far = own - CORES, swapped - CORES
        query = lax.broadcasted_iota(jnp.int32, (rows, rows), 1)
        key = lax.broadcasted_iota(jnp.int32, (rows, rows), 0)
        for item, (place, before, middle) in enumerate(
            (
                (own, near, jnp.where(first_core, far, swapped)),
                (swapped, far, jnp.where(first_core, own, near)),
            )
        ):
            query_pos = place * rows + query
            start = jnp.zeros((rows, rows), jnp.int32)
            bound = jnp.int32(0)
            for doc in range(doc_ref.shape[1]):
                bound = bound + doc_ref[0, doc]
                start = jnp.where(query_pos >= bound, bound, start)
            ends = jnp.where(key > query, before, place) * rows + key
            mask_ref[item, :rows, :] = jnp.where(
                (ends >= start) & (ends <= query_pos), 0.0, masked_fill
            )
            mask_ref[item, rows:, :] = jnp.where(
                middle * rows + key >= start, 0.0, masked_fill
            )

    scale = LOG2E / math.sqrt(HEAD_SIZE)

    def windows(kind):
        own, swapped = own_ref[0, kind], swap_ref[0, kind]
        near, far = near_ref[0, kind], far_ref[0, kind]
        return (
            jnp.concatenate([near, own, jnp.where(first_core, far, swapped)], axis=0),
            jnp.concatenate([far, swapped, jnp.where(first_core, own, near)], axis=0),
        )

    scores = []
    for keys, query in zip(windows(0), (mine_ref[...], theirs_ref[...])):
        stacked = jnp.concatenate(
            [query[:, i * HEAD_SIZE : (i + 1) * HEAD_SIZE] for i in range(group)], axis=0
        )
        scores.append(
            lax.dot_general(
                keys, stacked, (((1,), (1,)), ((), ())), preferred_element_type=jnp.float32
            )
        )
    outputs = []
    before = below((rows, group * rows))
    none = jnp.zeros((rows, group * rows), jnp.bfloat16)
    for item, (values, score) in enumerate(zip(windows(1), scores)):
        fill = mask_ref[item]
        ends = jnp.where(before, score[:rows, :], score[rows : 2 * rows, :])
        kept = jnp.concatenate([ends, score[2 * rows :, :]], axis=0)
        kept = kept + jnp.concatenate([fill] * group, axis=1)
        peak = jnp.max(kept, axis=0, keepdims=True)
        raw = jnp.exp2((kept - peak) * scale)
        share = pl.reciprocal(jnp.sum(raw, axis=0, keepdims=True))
        raw = raw.astype(jnp.bfloat16)
        ends = raw[:rows, :]
        spread = jnp.concatenate(
            [jnp.where(before, ends, none), jnp.where(before, none, ends), raw[rows:, :]], axis=0
        )
        mixed = lax.dot_general(
            values, spread, (((0,), (0,)), ((), ())), preferred_element_type=jnp.float32
        )
        mixed = mixed * share
        outputs.append(
            jnp.concatenate(
                [mixed[:, i * rows : (i + 1) * rows].T.astype(jnp.bfloat16) for i in range(group)],
                axis=1,
            )
        )
    stream = jnp.concatenate(
        [
            jnp.where(first_core, outputs[0], outputs[1]),
            jnp.where(first_core, outputs[1], outputs[0]),
        ],
        axis=0,
    )
    last = step >= pl.num_programs(0) - pl.num_programs(0) // chips

    @pl.when(last)
    def _():
        stay_ref[0] = stream

    @pl.when(jnp.logical_not(last))
    def _():
        send_ref[0] = stream

    both = CORES * rows
    part_ref[:both, :] += jnp.dot(stream, rank_ref[...], preferred_element_type=jnp.float32)
    part_ref[both:, :] += lax.dot_general(
        map_ref[...], stream, (((1,), (1,)), ((), ())), preferred_element_type=jnp.float32
    )


def attend(place, doc_lengths, queries, blocks, rank_in, map_rows, after):
    mine, theirs = queries
    chips, _, rows, columns = blocks[0].shape
    heads = columns // HEAD_SIZE
    width = mine.shape[1] // (chips * CORES)
    wide = width // heads

    def owner(j, s):
        return lax.rem(s[0] + 1 + j // heads, chips)

    def column(j, s):
        return (owner(j, s) * CORES + s[1]) * heads + lax.rem(j, heads)

    def sent(j, s):
        at = jnp.minimum(j, (chips - 1) * heads - 1)
        return (at // heads, 0, lax.rem(at, heads))

    query = pl.BlockSpec((rows, wide), lambda j, s: (0, column(j, s)))
    block = pl.BlockSpec(
        (1, 2, rows, HEAD_SIZE), lambda j, s: (owner(j, s), 0, 0, lax.rem(j, heads))
    )
    return pl.pallas_call(
        functools.partial(attend_kernel, chips=chips),
        grid_spec=pltpu.PrefetchScalarGridSpec(
            num_scalar_prefetch=1,
            grid=(chips * heads,),
            in_specs=[pl.BlockSpec(memory_space=pltpu.SMEM), query, query]
            + [block] * 4
            + [
                pl.BlockSpec((wide, RANK), lambda j, s: (column(j, s), 0)),
                pl.BlockSpec((2 * NS, wide), lambda j, s: (0, column(j, s))),
            ]
            + [pl.BlockSpec(memory_space=pl.ANY)] * len(after),
            out_specs=[
                pl.BlockSpec((1, CORES * rows, wide), sent),
                pl.BlockSpec(
                    (1, CORES * rows, wide),
                    lambda j, s: (0, 0, jnp.maximum(j - (chips - 1) * heads, 0)),
                ),
                pl.BlockSpec((CORES * rows + 2 * NS, RANK), lambda j, s: (0, 0)),
            ],
            scratch_shapes=[pltpu.VMEM((2, 2 * rows, rows), jnp.float32)],
        ),
        out_shape=[
            jax.ShapeDtypeStruct((chips - 1, CORES * rows, width), jnp.bfloat16),
            jax.ShapeDtypeStruct((1, CORES * rows, width), jnp.bfloat16),
            jax.ShapeDtypeStruct((CORES * rows + 2 * NS, RANK), jnp.float32),
        ],
        compiler_params=params,
        cost_estimate=pl.CostEstimate(flops=5 * 10**9, bytes_accessed=1 << 22, transcendentals=0),
        name="attend",
    )(place, doc_lengths, mine, theirs, *blocks, rank_in, map_rows, *after)


def low_kernel(mine_ref, theirs_ref, out_ref):
    out_ref[...] = (mine_ref[...] + theirs_ref[...]).astype(jnp.bfloat16)


def low_and_maps(mine, theirs):
    return pl.pallas_call(
        low_kernel,
        out_shape=jax.ShapeDtypeStruct(mine.shape, jnp.bfloat16),
        compiler_params=params,
        cost_estimate=pl.CostEstimate(flops=1, bytes_accessed=1, transcendentals=0),
        name="low_and_maps",
    )(mine, theirs)


def softplus(value):
    small = jnp.exp(-jnp.abs(value))
    tail = jnp.where(small < 0.00390625, small * (1.0 - 0.5 * small), jnp.log(1.0 + small))
    return jnp.maximum(value, 0.0) + tail


def add_states(rates_ref, state_ref, total_ref, states, totals):
    state_ref[...] = jnp.exp2(rates_ref[...] * totals) * state_ref[...] + states
    total_ref[...] = total_ref[...] + totals


def sums_within(steps):
    rows = steps.shape[0]
    at = lax.broadcasted_iota(jnp.int32, (rows, rows), 0)
    of = lax.broadcasted_iota(jnp.int32, (rows, rows), 1)
    upto = jnp.where(of <= at, 1.0, 0.0).astype(jnp.bfloat16)
    return jnp.dot(upto, steps, preferred_element_type=jnp.float32)


def step_kernel(
    place_ref, stream_ref, low_ref, map_ref, cols_ref, bias_ref, rates_ref, *rest
):
    own_state_ref, own_total_ref = rest[:2]
    steps_ref, sums_ref, maps_ref, carry_ref, state_ref, total_ref, wide_ref, turn_ref = rest[5:]
    block = pl.program_id(0)
    rows, width = stream_ref.shape[1:]

    @pl.when(block == 0)
    def _():
        state_ref[...] = jnp.zeros_like(state_ref)
        total_ref[...] = jnp.zeros_like(total_ref)
        for n in range(NS):
            wide_ref[n * NS : (n + 1) * NS, :] = jnp.broadcast_to(
                rates_ref[n : n + 1, :], (NS, width)
            ).astype(jnp.bfloat16)

    @pl.when(block == place_ref[0] * CORES)
    def _():
        add_states(rates_ref, state_ref, total_ref, own_state_ref[...], own_total_ref[...])

    maps = map_ref[0].astype(jnp.float32)
    maps_ref[0] = maps
    logits = jnp.dot(low_ref[0], cols_ref[...], preferred_element_type=jnp.float32)
    steps = softplus(logits + bias_ref[...]).astype(jnp.bfloat16)
    steps_ref[...] = steps
    push = steps * stream_ref[0]
    within = sums_within(steps)
    sums_ref[...] = within.astype(jnp.bfloat16)
    whole = within[rows - 1 :, :]
    left = (whole - within).astype(jnp.bfloat16)
    some, chunk, several = rows // 2, CORES * LANES, 4
    state_row = lax.broadcasted_iota(jnp.int32, (NS, some), 0)
    for first in range(0, rows, some):
        span = slice(first, first + some)
        chosen = [
            jnp.concatenate(
                [
                    jnp.where(state_row == m, maps[:NS, span], 0.0).astype(jnp.bfloat16)
                    for m in range(n, n + several)
                ],
                axis=1,
            )
            for n in range(0, NS, several)
        ]
        for item in range(width // chunk):
            lanes = slice(item * chunk, (item + 1) * chunk)
            left_here = left[span, lanes].reshape(some // NS, NS, chunk)
            push_here = push[span, lanes].reshape(some // NS, NS, chunk)
            added = state_ref[:, lanes]
            if first == 0:
                added = jnp.exp2(rates_ref[:, lanes] * whole[:, lanes]) * added
            for n in range(0, NS, several):
                pushed = []
                for m in range(n, n + several):
                    decay = jnp.exp2(left_here * wide_ref[m * NS : (m + 1) * NS, lanes][None])
                    pushed.append((decay * push_here).reshape(some, chunk))
                added = added + jnp.dot(
                    chosen[n // several],
                    jnp.concatenate(pushed, axis=0),
                    preferred_element_type=jnp.float32,
                )
            state_ref[:, lanes] = added
    total_ref[...] = total_ref[...] + whole

    count = pl.num_programs(0)

    @pl.when(block == count - 1)
    def _():
        @pl.when(place_ref[0] * CORES == count)
        def _():
            add_states(rates_ref, state_ref, total_ref, own_state_ref[...], own_total_ref[...])

        write_carry(carry_ref.at[0], state_ref[...], total_ref[...], turn_ref)
        for target in range(1, carry_ref.shape[0]):
            carry_ref[target] = carry_ref[0]


def step_sizes(place, stream, lows, cols, bias, rates, state, total, targets, after, sums, maps):
    others = stream.shape[0]
    chips = others + 1
    rows, width = stream.shape[1] // CORES, stream.shape[2]
    map_row = CORES * rows // MAPS
    blocks = others * CORES
    carry = (targets, (width // LANES + 1) * NS, LANES)

    def slot(b, s):
        chip = b // CORES
        return lax.rem(s[0] - jnp.where(chip < s[0], chip, chip + 1) + chips, chips) - 1

    def core(b):
        return lax.rem(b, CORES)

    def in_row(b, s):
        return jnp.where(b // CORES < s[0], b, b + CORES)

    def fixed(*shape):
        return pl.BlockSpec(shape, lambda b, s: (0,) * len(shape))

    return pl.pallas_call(
        step_kernel,
        grid_spec=pltpu.PrefetchScalarGridSpec(
            num_scalar_prefetch=1,
            grid=(blocks,),
            in_specs=[
                pl.BlockSpec((1, rows, width), lambda b, s: (slot(b, s), core(b), 0)),
                pl.BlockSpec((1, rows, RANK), lambda b, s: (slot(b, s), core(b), 0)),
                pl.BlockSpec((1, MAPS, rows), lambda b, s: (slot(b, s), map_row, core(b))),
                fixed(*cols.shape),
                fixed(*bias.shape),
                fixed(*rates.shape),
                fixed(*state.shape),
                fixed(*total.shape),
            ]
            + [pl.BlockSpec(memory_space=pl.ANY)] * 3,
            out_specs=[
                pl.BlockSpec((rows, width), lambda b, s: (b, 0)),
                pl.BlockSpec((rows, width), lambda b, s: (in_row(b, s), 0)),
                pl.BlockSpec((1, 2 * NS, rows), lambda b, s: (in_row(b, s), 0, 0)),
                fixed(*carry),
            ],
            scratch_shapes=[
                pltpu.VMEM((NS, width), jnp.float32),
                pltpu.VMEM((1, width), jnp.float32),
                pltpu.VMEM((NS * NS, width), jnp.bfloat16),
                pltpu.VMEM((SUBLANES, LANES), jnp.float32),
            ],
        ),
        out_shape=[
            jax.ShapeDtypeStruct((blocks * rows, width), jnp.bfloat16),
            jax.ShapeDtypeStruct(sums.shape, sums.dtype),
            jax.ShapeDtypeStruct(maps.shape, maps.dtype),
            jax.ShapeDtypeStruct(carry, jnp.bfloat16),
        ],
        input_output_aliases={10: 1, 11: 2},
        compiler_params=params,
        name="step_sizes",
    )(place, stream, lows, lows, cols, bias, rates, state, total, after, sums, maps)


def write_carry(out_ref, state, total, turn_ref):
    tile = state.shape[1] // LANES
    turn_ref[...] = jnp.zeros_like(turn_ref)
    for item in range(tile):
        lanes = slice(item * LANES, (item + 1) * LANES)
        turn_ref[item : item + 1, :] = total[:, lanes]
        out_ref[item * NS : (item + 1) * NS, :] = state[:, lanes].astype(jnp.bfloat16)
    out_ref[tile * NS :, :] = jnp.concatenate(split(turn_ref[...]), axis=0)


def follow(carry_ref, rates_ref, state_ref):
    tile = state_ref.shape[1] // LANES
    sums = carry_ref[tile * NS :, :].astype(jnp.float32)
    sums = sums[:SUBLANES, :] + sums[SUBLANES:, :]
    for item in range(tile):
        lanes = slice(item * LANES, (item + 1) * LANES)
        decay = jnp.exp2(rates_ref[:, lanes] * sums[item : item + 1, :])
        added = carry_ref[item * NS : (item + 1) * NS, :].astype(jnp.float32)
        state_ref[:, lanes] = decay * state_ref[:, lanes] + added
    return sums


def scan_blocks(stream_ref, steps_ref, maps, rates_ref, gain_ref, out_ref, state_ref, work_refs):
    out_of_ref, *hist_refs = work_refs
    rows, width = steps_ref.shape
    source = lax.broadcasted_iota(jnp.int32, (LANES, NS * NS), 0)
    column = lax.rem(lax.broadcasted_iota(jnp.int32, (LANES, NS * NS), 1), NS)
    token = lax.rem(lax.broadcasted_iota(jnp.int32, (rows, NS * NS), 0), NS)
    slot = lax.broadcasted_iota(jnp.int32, (rows, NS * NS), 1) // NS
    turned = jnp.concatenate(
        [maps, jnp.zeros((LANES - 2 * NS, rows), jnp.float32)], axis=0
    ).T.astype(jnp.bfloat16)
    pick = jnp.where(source == NS + column, 1.0, 0.0).astype(jnp.bfloat16)
    spread = jnp.dot(turned, pick, preferred_element_type=jnp.float32)
    out_of_ref[...] = jnp.where(token == slot, spread, 0.0).astype(jnp.bfloat16)
    map_in = maps[:NS, :]
    half = width // 2

    def finish(first, hist_ref):
        here = pl.ds(first, NS)
        mixed = jnp.dot(out_of_ref[here, :], hist_ref[...], preferred_element_type=jnp.float32)
        direct = gain_ref[...] * stream_ref[0, here, :].astype(jnp.float32)
        out_ref[here, :] = (mixed + direct).astype(jnp.bfloat16)

    def advance(first, hist_ref):
        here = pl.ds(first, NS)
        into = pltpu.roll(map_in, lax.rem(rows - first, rows), 1)
        for lanes in (slice(0, half), slice(half, width)):
            state = state_ref[:, lanes]
            rates = rates_ref[:, lanes]
            steps = steps_ref[here, lanes].astype(jnp.float32)
            push = steps * stream_ref[0, here, lanes].astype(jnp.float32)
            for near in range(NS):
                this = slice(near, near + 1)
                state = jnp.exp2(rates * steps[this, :]) * state + into[:, this] * push[this, :]
                hist_ref[near * NS : (near + 1) * NS, lanes] = state.astype(jnp.bfloat16)
            state_ref[:, lanes] = state

    def at(group):
        return pl.multiple_of(group * NS, NS)

    def pair(index, nothing):
        finish(at(2 * index), hist_refs[1])
        advance(at(2 * index + 1), hist_refs[0])
        finish(at(2 * index + 1), hist_refs[0])
        advance(at(2 * index + 2), hist_refs[1])
        return nothing

    groups = rows // NS
    advance(0, hist_refs[1])
    lax.fori_loop(0, groups // 2 - 1, pair, 0)
    finish(rows - 2 * NS, hist_refs[1])
    advance(rows - NS, hist_refs[0])
    finish(rows - NS, hist_refs[0])


def work_shapes(rows, width):
    return [
        pltpu.VMEM((rows, NS * NS), jnp.bfloat16),
        pltpu.VMEM((NS * NS, width), jnp.bfloat16),
        pltpu.VMEM((NS * NS, width), jnp.bfloat16),
    ]


def own_kernel(
    place_ref, stream_ref, low_ref, map_ref, cols_ref, bias_ref, rates_ref, gain_ref,
    out_ref, sums_ref, maps_ref, state_ref, total_ref, steps_ref, *work_refs
):
    rows = steps_ref.shape[0]

    @pl.when(pl.program_id(0) == 0)
    def _():
        state_ref[...] = jnp.zeros_like(state_ref)
        total_ref[...] = jnp.zeros_like(total_ref)

    maps = map_ref[...].astype(jnp.float32)
    maps_ref[0] = maps
    logits = jnp.dot(low_ref[...], cols_ref[...], preferred_element_type=jnp.float32)
    steps = softplus(logits + bias_ref[...]).astype(jnp.bfloat16)
    steps_ref[...] = steps
    within = sums_within(steps)
    sums_ref[...] = within.astype(jnp.bfloat16)
    total_ref[...] = total_ref[...] + within[rows - 1 :, :]
    scan_blocks(stream_ref, steps_ref, maps, rates_ref, gain_ref, out_ref, state_ref, work_refs)


def scan_own(place, stream, lows, cols, bias, rates, gain):
    rows, width = stream.shape[1] // CORES, stream.shape[2]
    map_row = CORES * rows // MAPS

    blocks = lax.axis_size("seq")

    def in_row(b, s):
        return s[0] * CORES + b

    def fixed(*shape):
        return pl.BlockSpec(shape, lambda b, s: (0,) * len(shape))

    block = pl.BlockSpec((rows, width), lambda b, s: (in_row(b, s), 0))
    return pl.pallas_call(
        own_kernel,
        grid_spec=pltpu.PrefetchScalarGridSpec(
            num_scalar_prefetch=1,
            grid=(CORES,),
            in_specs=[
                pl.BlockSpec((1, rows, width), lambda b, s: (0, b, 0)),
                pl.BlockSpec((rows, RANK), lambda b, s: (b, 0)),
                pl.BlockSpec((MAPS, rows), lambda b, s: (map_row, b)),
                fixed(*cols.shape),
                fixed(*bias.shape),
                fixed(*rates.shape),
                fixed(*gain.shape),
            ],
            out_specs=[
                block,
                block,
                pl.BlockSpec((1, 2 * NS, rows), lambda b, s: (in_row(b, s), 0, 0)),
                fixed(NS, width),
                fixed(1, width),
            ],
            scratch_shapes=[pltpu.VMEM((rows, width), jnp.bfloat16)] + work_shapes(rows, width),
        ),
        out_shape=[
            jax.ShapeDtypeStruct((blocks * rows, width), jnp.bfloat16),
            jax.ShapeDtypeStruct((blocks * rows, width), jnp.bfloat16),
            jax.ShapeDtypeStruct((blocks, 2 * NS, rows), jnp.float32),
            jax.ShapeDtypeStruct((NS, width), jnp.float32),
            jax.ShapeDtypeStruct((1, width), jnp.float32),
        ],
        compiler_params=params,
        cost_estimate=pl.CostEstimate(flops=4 * 10**9, bytes_accessed=1 << 21, transcendentals=0),
        name="scan_own",
    )(place, stream, lows, lows, cols, bias, rates, gain)


def others_kernel(
    place_ref, stream_ref, steps_ref, maps_ref, rates_ref, gain_ref, part_ref, out_ref, last_ref,
    *work_refs
):
    del part_ref

    @pl.when(lax.rem(pl.program_id(0), CORES) == 0)
    def _():
        last_ref[...] = jnp.zeros_like(last_ref)

    scan_blocks(
        stream_ref, steps_ref, maps_ref[0], rates_ref, gain_ref, out_ref, last_ref.at[0], work_refs
    )


def scan_others(place, stream, steps, maps, rates, gain, part):
    others = stream.shape[0]
    chips = others + 1
    rows, width = stream.shape[1] // CORES, stream.shape[2]

    def slot(b, s):
        chip = b // CORES
        return lax.rem(s[0] - jnp.where(chip < s[0], chip, chip + 1) + chips, chips) - 1

    def in_row(b, s):
        return jnp.where(b // CORES < s[0], b, b + CORES)

    def fixed(*shape):
        return pl.BlockSpec(shape, lambda b, s: (0,) * len(shape))

    return pl.pallas_call(
        others_kernel,
        grid_spec=pltpu.PrefetchScalarGridSpec(
            num_scalar_prefetch=1,
            grid=(others * CORES,),
            in_specs=[
                pl.BlockSpec((1, rows, width), lambda b, s: (slot(b, s), lax.rem(b, CORES), 0)),
                pl.BlockSpec((rows, width), lambda b, s: (b, 0)),
                pl.BlockSpec((1, 2 * NS, rows), lambda b, s: (in_row(b, s), 0, 0)),
                fixed(*rates.shape),
                fixed(*gain.shape),
                pl.BlockSpec(memory_space=pl.ANY),
            ],
            out_specs=[
                pl.BlockSpec((rows, width), lambda b, s: (in_row(b, s), 0)),
                pl.BlockSpec((1, NS, width), lambda b, s: (b // CORES, 0, 0)),
            ],
            scratch_shapes=work_shapes(rows, width),
        ),
        out_shape=[
            jax.ShapeDtypeStruct(part.shape, part.dtype),
            jax.ShapeDtypeStruct((others, NS, width), jnp.float32),
        ],
        input_output_aliases={6: 0},
        compiler_params=params,
        cost_estimate=pl.CostEstimate(flops=4 * 10**9, bytes_accessed=1 << 21, transcendentals=0),
        name="scan_others",
    )(place, stream, steps, maps, rates, gain, part)


def carried_kernel(
    place_ref, part_ref, sums_ref, maps_ref, last_own_ref, last_come_ref, rates_ref, carries_ref,
    out_ref, state_ref, wide_ref, begin_ref, spread_ref,
):
    block = pl.program_id(0)
    rows, width = out_ref.shape
    chip = block // CORES

    @pl.when(block == 0)
    def _():
        state_ref[...] = jnp.zeros_like(state_ref)

        def compose(row, nothing):
            follow(carries_ref.at[row], rates_ref, state_ref)
            return nothing

        lax.fori_loop(0, lax.axis_index("chan"), compose, 0)
        for n in range(NS):
            wide_ref[n * NS : (n + 1) * NS, :] = jnp.broadcast_to(
                rates_ref[n : n + 1, :], (NS, width)
            ).astype(jnp.bfloat16)

    @pl.when((block > 0) & (lax.rem(block, CORES) == 0))
    def _():
        before = jnp.where(chip - 1 == place_ref[0], last_own_ref[...], last_come_ref[0])
        state_ref[...] = state_ref[...] + before

    state = state_ref[...]
    for n in range(NS):
        begin_ref[n * NS : (n + 1) * NS, :] = jnp.broadcast_to(
            state[n : n + 1, :], (NS, width)
        ).astype(jnp.bfloat16)
    maps = jnp.concatenate([maps_ref[0], jnp.zeros((LANES - 2 * NS, rows), jnp.float32)], axis=0).T
    for n in range(NS):
        spread_ref[:, n * LANES : (n + 1) * LANES] = jnp.broadcast_to(
            maps[:, NS + n : NS + n + 1], (rows, LANES)
        ).astype(jnp.bfloat16)
    last = sums_ref[rows - NS :, :].astype(jnp.float32)[NS - 1 :, :]
    state_ref[...] = jnp.exp2(rates_ref[...] * last) * state
    chunk, several = CORES * LANES, 4

    def some(index, nothing):
        near = pl.ds(pl.multiple_of(index * NS, NS), NS)
        for item in range(width // chunk):
            lanes = slice(item * chunk, (item + 1) * chunk)
            total = part_ref[near, lanes].astype(jnp.float32)
            sums = sums_ref[near, lanes]
            for first in range(0, NS, several):
                terms = []
                for n in range(first, first + several):
                    decay = jnp.exp2(sums * wide_ref[n * NS : (n + 1) * NS, lanes])
                    out_of = spread_ref[near, n * LANES : (n + 1) * LANES]
                    out_of = jnp.concatenate([out_of] * (chunk // LANES), axis=1)
                    terms.append(decay * begin_ref[n * NS : (n + 1) * NS, lanes] * out_of)
                four = (terms[0] + terms[1]) + (terms[2] + terms[3])
                total = total + four.astype(jnp.float32)
            out_ref[near, lanes] = total.astype(jnp.bfloat16)
        return nothing

    lax.fori_loop(0, rows // NS, some, 0)


def add_carried(place, part, sums, maps, lasts, rates, carries):
    blocks, _, rows = maps.shape
    others = lasts[1].shape[0]
    width = rates.shape[1]

    def before(b, s):
        chip = jnp.maximum(b // CORES - 1, 0)
        return jnp.minimum(jnp.where(chip < s[0], chip, jnp.maximum(chip - 1, 0)), others - 1)

    def fixed(*shape):
        return pl.BlockSpec(shape, lambda b, s: (0,) * len(shape))

    block = pl.BlockSpec((rows, width), lambda b, s: (b, 0))
    return pl.pallas_call(
        carried_kernel,
        grid_spec=pltpu.PrefetchScalarGridSpec(
            num_scalar_prefetch=1,
            grid=(blocks,),
            in_specs=[
                block,
                block,
                pl.BlockSpec((1, 2 * NS, rows), lambda b, s: (b, 0, 0)),
                fixed(NS, width),
                pl.BlockSpec((1, NS, width), lambda b, s: (before(b, s), 0, 0)),
                fixed(*rates.shape),
                fixed(*carries.shape),
            ],
            out_specs=block,
            scratch_shapes=[
                pltpu.VMEM((NS, width), jnp.float32),
                pltpu.VMEM((NS * NS, width), jnp.bfloat16),
                pltpu.VMEM((NS * NS, width), jnp.bfloat16),
                pltpu.VMEM((rows, NS * LANES), jnp.bfloat16),
            ],
        ),
        out_shape=jax.ShapeDtypeStruct(part.shape, jnp.bfloat16),
        compiler_params=params,
        name="add_carried",
    )(place, part, sums, maps, *lasts, rates, carries)


def local(
    queries, keys, values, doc_lengths, rank_in, bc_weight, rank_out, dt_bias, a_log, skip_gain
):
    devices = lax.axis_size("seq")
    chips = devices // CORES
    targets = lax.axis_size("chan")
    seq_place = lax.axis_index("seq").astype(jnp.int32)
    chip, core = seq_place // CORES, lax.rem(seq_place, CORES)
    place = jnp.stack([chip, core])
    width = queries.shape[2] // devices
    wide = max(HEAD_SIZE, keys.shape[2] // devices)

    def other(device):
        return device + 1 - 2 * (device % CORES)

    swap = [(device, other(device)) for device in range(devices)]
    near = [(device, device + CORES) for device in range(devices - CORES)]
    far = [(device, other(device + CORES)) for device in range(devices - CORES)]

    def onward(chips_on):
        return [(device, (device + chips_on * CORES) % devices) for device in range(devices)]

    own, theirs = select_heads(keys[0], values[0], chips, wide)
    from_near = lax.ppermute(own, "seq", near)
    from_far = lax.ppermute(theirs, "seq", far)
    swapped = lax.ppermute(theirs, "seq", swap)
    queries_after, _ = lax.optimization_barrier((queries[0], own))
    their_queries = lax.ppermute(queries_after, "seq", swap)
    blocks = (own, swapped, from_near, from_far)

    first = seq_place * width
    logs = lax.dynamic_slice_in_dim(a_log, first, width, 0)
    rates = (-LOG2E * jnp.exp(logs)).T
    cols = lax.dynamic_slice_in_dim(rank_out, first, width, 1)
    bias = lax.dynamic_slice_in_dim(dt_bias, first, width, 0)[None]
    gain = lax.dynamic_slice_in_dim(skip_gain, first, width, 0)[None]

    sent, stayed, part = attend(
        place, doc_lengths, (queries[0], their_queries), blocks, rank_in, bc_weight.T,
        (rates, cols, bias, gain),
    )
    come = [lax.ppermute(sent[step], "seq", onward(step + 1)) for step in range(chips - 1)]
    low_own = low_and_maps(part, lax.ppermute(part, "seq", swap))
    low_come = [lax.ppermute(low_own, "seq", onward(step + 1)) for step in range(chips - 1)]
    got_sent = lax.ppermute(sent, "seq", swap)
    got_stayed = lax.ppermute(stayed, "seq", swap)
    attn_rows = join_heads(sent, stayed, got_sent, got_stayed)

    part, sums, maps, state, total = scan_own(place, stayed, low_own, cols, bias, rates, gain)
    come, low_come = jnp.stack(come), jnp.stack(low_come)
    steps, sums, maps, carry = step_sizes(
        place, come, low_come, cols, bias, rates, state, total, targets, attn_rows, sums, maps
    )
    carries = lax.all_to_all(carry, "chan", split_axis=0, concat_axis=0, tiled=True)
    part, last_come = scan_others(place, come, steps, maps, rates, gain, part)
    ssm_rows = add_carried(place, part, sums, maps, (state, last_come), rates, carries)
    return (attn_rows[None], ssm_rows[None])


def solution(mesh):
    return jax.shard_map(
        local,
        mesh=mesh,
        in_specs=(
            P("chan", "seq", None),
            P("chan", "seq", None),
            P("chan", "seq", None),
            P("chan", None),
            P(),
            P(),
            P(),
            P(),
            P(),
            P(),
        ),
        out_specs=(P("chan", "seq", None), P("chan", None, "seq")),
        check_vma=False,
    )
```

```python
import functools
import math

import jax
import jax.numpy as jnp
from jax import lax
from jax.experimental import pallas as pl
from jax.experimental.pallas import tpu as pltpu
from jax.sharding import PartitionSpec as P

QUERY_HEADS = 32
KEY_VALUE_HEADS = 8
HEAD_SIZE = 128
GROUP = QUERY_HEADS // KEY_VALUE_HEADS
NS = 16
RANK = 256
CORES = 2
LANES = 128
SUBLANES = 8
MAPS = 2 * NS
LOG2E = 1.4426950408889634

masked_fill = -1e30
params = pltpu.CompilerParams(vmem_limit_bytes=60 << 20)


def split(value):
    coarse = value.astype(jnp.bfloat16)
    return coarse, (value - coarse.astype(jnp.float32)).astype(jnp.bfloat16)


def run_copies(pairs, sems):
    copies = [
        pltpu.make_async_copy(source, target, sems.at[i]) for i, (source, target) in enumerate(pairs)
    ]
    for copy in copies:
        copy.start()
    for copy in copies:
        copy.wait()


def columns_of(ref, index, size):
    return ref.at[:, pl.ds(pl.multiple_of(index * size, LANES), size)]


def heads_kernel(key_ref, value_ref, own_ref, their_ref, sems):
    core = lax.rem(lax.axis_index("seq"), CORES)
    wide = own_ref.shape[3]
    halves = key_ref.shape[1] // wide // own_ref.shape[0]
    pairs = []
    for target, which in ((own_ref, core), (their_ref, 1 - core)):
        for chip in range(own_ref.shape[0]):
            index = chip * halves + (which if halves == CORES else 0)
            for kind, source in enumerate((key_ref, value_ref)):
                pairs.append((columns_of(source, index, wide), target.at[chip, kind]))
    run_copies(pairs, sems)


def select_heads(keys, values, chips, wide):
    shape = jax.ShapeDtypeStruct((chips, 2, keys.shape[0], wide), keys.dtype)
    return pl.pallas_call(
        heads_kernel,
        in_specs=[pl.BlockSpec(memory_space=pl.ANY)] * 2,
        out_shape=[shape, shape],
        scratch_shapes=[pltpu.SemaphoreType.DMA((4 * chips,))],
        compiler_params=params,
        name="select_heads",
    )(keys, values)


def join_kernel(sent_ref, stayed_ref, got_sent_ref, got_stayed_ref, out_ref, sems):
    place = lax.axis_index("seq")
    core, chip = lax.rem(place, CORES), place // CORES
    rows = out_ref.shape[0]
    others, _, width = sent_ref.shape
    here = pl.ds(pl.multiple_of(core * rows, rows), rows)
    pairs = []
    for first, rest, which in (
        (stayed_ref, sent_ref, core), (got_stayed_ref, got_sent_ref, 1 - core)
    ):
        for step in range(others + 1):
            source = first.at[0, here, :] if step == 0 else rest.at[step - 1, here, :]
            owner = lax.rem(chip + step, others + 1)
            pairs.append((source, columns_of(out_ref, owner * CORES + which, width)))
    run_copies(pairs, sems)


def join_heads(sent, stayed, got_sent, got_stayed):
    others, rows, width = sent.shape
    return pl.pallas_call(
        join_kernel,
        in_specs=[pl.BlockSpec(memory_space=pl.ANY)] * 4,
        out_shape=jax.ShapeDtypeStruct(
            (rows // CORES, (others + 1) * CORES * width), sent.dtype
        ),
        scratch_shapes=[pltpu.SemaphoreType.DMA((CORES * (others + 1),))],
        compiler_params=params,
        name="join_heads",
    )(sent, stayed, got_sent, got_stayed)


def attend_kernel(
    place_ref, doc_ref, mine_ref, theirs_ref, own_ref, swap_ref, near_ref, far_ref,
    rank_ref, map_ref, *rest, chips,
):
    send_ref, stay_ref, part_ref, mask_ref = rest[-4:]
    step = pl.program_id(0)
    rows = mine_ref.shape[0]
    group = mine_ref.shape[1] // HEAD_SIZE
    chip, core = place_ref[0], place_ref[1]
    first_core = core == 0

    def below(shape):
        column = lax.rem(lax.broadcasted_iota(jnp.int32, shape, 1), rows)
        return lax.broadcasted_iota(jnp.int32, shape, 0) > column

    @pl.when(step == 0)
    def _():
        part_ref[...] = jnp.zeros_like(part_ref)
        own = chip * CORES + core
        swapped = chip * CORES + 1 - core
        near, far = own - CORES, swapped - CORES
        query = lax.broadcasted_iota(jnp.int32, (rows, rows), 1)
        key = lax.broadcasted_iota(jnp.int32, (rows, rows), 0)
        for item, (place, before, middle) in enumerate(
            (
                (own, near, jnp.where(first_core, far, swapped)),
                (swapped, far, jnp.where(first_core, own, near)),
            )
        ):
            query_pos = place * rows + query
            start = jnp.zeros((rows, rows), jnp.int32)
            bound = jnp.int32(0)
            for doc in range(doc_ref.shape[1]):
                bound = bound + doc_ref[0, doc]
                start = jnp.where(query_pos >= bound, bound, start)
            ends = jnp.where(key > query, before, place) * rows + key
            mask_ref[item, :rows, :] = jnp.where(
                (ends >= start) & (ends <= query_pos), 0.0, masked_fill
            )
            mask_ref[item, rows:, :] = jnp.where(
                middle * rows + key >= start, 0.0, masked_fill
            )

    scale = LOG2E / math.sqrt(HEAD_SIZE)

    def windows(kind):
        own, swapped = own_ref[0, kind], swap_ref[0, kind]
        near, far = near_ref[0, kind], far_ref[0, kind]
        return (
            jnp.concatenate([near, own, jnp.where(first_core, far, swapped)], axis=0),
            jnp.concatenate([far, swapped, jnp.where(first_core, own, near)], axis=0),
        )

    scores = []
    for keys, query in zip(windows(0), (mine_ref[...], theirs_ref[...])):
        stacked = jnp.concatenate(
            [query[:, i * HEAD_SIZE : (i + 1) * HEAD_SIZE] for i in range(group)], axis=0
        )
        scores.append(
            lax.dot_general(
                keys, stacked, (((1,), (1,)), ((), ())), preferred_element_type=jnp.float32
            )
        )
    outputs = []
    before = below((rows, group * rows))
    none = jnp.zeros((rows, group * rows), jnp.bfloat16)
    for item, (values, score) in enumerate(zip(windows(1), scores)):
        fill = mask_ref[item]
        ends = jnp.where(before, score[:rows, :], score[rows : 2 * rows, :])
        kept = jnp.concatenate([ends, score[2 * rows :, :]], axis=0)
        kept = kept + jnp.concatenate([fill] * group, axis=1)
        peak = jnp.max(kept, axis=0, keepdims=True)
        raw = jnp.exp2((kept - peak) * scale)
        share = pl.reciprocal(jnp.sum(raw, axis=0, keepdims=True))
        raw = raw.astype(jnp.bfloat16)
        ends = raw[:rows, :]
        spread = jnp.concatenate(
            [jnp.where(before, ends, none), jnp.where(before, none, ends), raw[rows:, :]], axis=0
        )
        mixed = lax.dot_general(
            values, spread, (((0,), (0,)), ((), ())), preferred_element_type=jnp.float32
        )
        mixed = mixed * share
        outputs.append(
            jnp.concatenate(
                [mixed[:, i * rows : (i + 1) * rows].T.astype(jnp.bfloat16) for i in range(group)],
                axis=1,
            )
        )
    stream = jnp.concatenate(
        [
            jnp.where(first_core, outputs[0], outputs[1]),
            jnp.where(first_core, outputs[1], outputs[0]),
        ],
        axis=0,
    )
    last = step >= pl.num_programs(0) - pl.num_programs(0) // chips

    @pl.when(last)
    def _():
        stay_ref[0] = stream

    @pl.when(jnp.logical_not(last))
    def _():
        send_ref[0] = stream

    both = CORES * rows
    part_ref[:both, :] += jnp.dot(stream, rank_ref[...], preferred_element_type=jnp.float32)
    part_ref[both:, :] += lax.dot_general(
        map_ref[...], stream, (((1,), (1,)), ((), ())), preferred_element_type=jnp.float32
    )


def attend(place, doc_lengths, queries, blocks, rank_in, map_rows, after):
    mine, theirs = queries
    chips, _, rows, columns = blocks[0].shape
    heads = columns // HEAD_SIZE
    width = mine.shape[1] // (chips * CORES)
    wide = width // heads

    def owner(j, s):
        return lax.rem(s[0] + 1 + j // heads, chips)

    def column(j, s):
        return (owner(j, s) * CORES + s[1]) * heads + lax.rem(j, heads)

    def sent(j, s):
        at = jnp.minimum(j, (chips - 1) * heads - 1)
        return (at // heads, 0, lax.rem(at, heads))

    query = pl.BlockSpec((rows, wide), lambda j, s: (0, column(j, s)))
    block = pl.BlockSpec(
        (1, 2, rows, HEAD_SIZE), lambda j, s: (owner(j, s), 0, 0, lax.rem(j, heads))
    )
    return pl.pallas_call(
        functools.partial(attend_kernel, chips=chips),
        grid_spec=pltpu.PrefetchScalarGridSpec(
            num_scalar_prefetch=1,
            grid=(chips * heads,),
            in_specs=[pl.BlockSpec(memory_space=pltpu.SMEM), query, query]
            + [block] * 4
            + [
                pl.BlockSpec((wide, RANK), lambda j, s: (column(j, s), 0)),
                pl.BlockSpec((2 * NS, wide), lambda j, s: (0, column(j, s))),
            ]
            + [pl.BlockSpec(memory_space=pl.ANY)] * len(after),
            out_specs=[
                pl.BlockSpec((1, CORES * rows, wide), sent),
                pl.BlockSpec(
                    (1, CORES * rows, wide),
                    lambda j, s: (0, 0, jnp.maximum(j - (chips - 1) * heads, 0)),
                ),
                pl.BlockSpec((CORES * rows + 2 * NS, RANK), lambda j, s: (0, 0)),
            ],
            scratch_shapes=[pltpu.VMEM((2, 2 * rows, rows), jnp.float32)],
        ),
        out_shape=[
            jax.ShapeDtypeStruct((chips - 1, CORES * rows, width), jnp.bfloat16),
            jax.ShapeDtypeStruct((1, CORES * rows, width), jnp.bfloat16),
            jax.ShapeDtypeStruct((CORES * rows + 2 * NS, RANK), jnp.float32),
        ],
        compiler_params=params,
        cost_estimate=pl.CostEstimate(flops=5 * 10**9, bytes_accessed=1 << 22, transcendentals=0),
        name="attend",
    )(place, doc_lengths, mine, theirs, *blocks, rank_in, map_rows, *after)


def low_kernel(mine_ref, theirs_ref, out_ref):
    out_ref[...] = (mine_ref[...] + theirs_ref[...]).astype(jnp.bfloat16)


def low_and_maps(mine, theirs):
    return pl.pallas_call(
        low_kernel,
        out_shape=jax.ShapeDtypeStruct(mine.shape, jnp.bfloat16),
        compiler_params=params,
        cost_estimate=pl.CostEstimate(flops=1, bytes_accessed=1, transcendentals=0),
        name="low_and_maps",
    )(mine, theirs)


def softplus(value):
    small = jnp.exp(-jnp.abs(value))
    tail = jnp.where(small < 0.00390625, small * (1.0 - 0.5 * small), jnp.log(1.0 + small))
    return jnp.maximum(value, 0.0) + tail


def add_states(rates_ref, state_ref, total_ref, states, totals):
    state_ref[...] = jnp.exp2(rates_ref[...] * totals) * state_ref[...] + states
    total_ref[...] = total_ref[...] + totals


def sums_within(steps):
    rows = steps.shape[0]
    at = lax.broadcasted_iota(jnp.int32, (rows, rows), 0)
    of = lax.broadcasted_iota(jnp.int32, (rows, rows), 1)
    upto = jnp.where(of <= at, 1.0, 0.0).astype(jnp.bfloat16)
    return jnp.dot(upto, steps, preferred_element_type=jnp.float32)


def step_kernel(
    place_ref, stream_ref, low_ref, map_ref, cols_ref, bias_ref, rates_ref, *rest
):
    own_state_ref, own_total_ref = rest[:2]
    steps_ref, sums_ref, maps_ref, carry_ref, state_ref, total_ref, wide_ref, turn_ref = rest[5:]
    block = pl.program_id(0)
    rows, width = stream_ref.shape[1:]

    @pl.when(block == 0)
    def _():
        state_ref[...] = jnp.zeros_like(state_ref)
        total_ref[...] = jnp.zeros_like(total_ref)
        for n in range(NS):
            wide_ref[n * NS : (n + 1) * NS, :] = jnp.broadcast_to(
                rates_ref[n : n + 1, :], (NS, width)
            ).astype(jnp.bfloat16)

    @pl.when(block == place_ref[0] * CORES)
    def _():
        add_states(rates_ref, state_ref, total_ref, own_state_ref[...], own_total_ref[...])

    maps = map_ref[0].astype(jnp.float32)
    maps_ref[0] = maps
    logits = jnp.dot(low_ref[0], cols_ref[...], preferred_element_type=jnp.float32)
    steps = softplus(logits + bias_ref[...]).astype(jnp.bfloat16)
    steps_ref[...] = steps
    push = steps * stream_ref[0]
    within = sums_within(steps)
    sums_ref[...] = within.astype(jnp.bfloat16)
    whole = within[rows - 1 :, :]
    left = (whole - within).astype(jnp.bfloat16)
    some, chunk, several = rows // 2, CORES * LANES, 4
    state_row = lax.broadcasted_iota(jnp.int32, (NS, some), 0)
    for first in range(0, rows, some):
        span = slice(first, first + some)
        chosen = [
            jnp.concatenate(
                [
                    jnp.where(state_row == m, maps[:NS, span], 0.0).astype(jnp.bfloat16)
                    for m in range(n, n + several)
                ],
                axis=1,
            )
            for n in range(0, NS, several)
        ]
        for item in range(width // chunk):
            lanes = slice(item * chunk, (item + 1) * chunk)
            left_here = left[span, lanes].reshape(some // NS, NS, chunk)
            push_here = push[span, lanes].reshape(some // NS, NS, chunk)
            added = state_ref[:, lanes]
            if first == 0:
                added = jnp.exp2(rates_ref[:, lanes] * whole[:, lanes]) * added
            for n in range(0, NS, several):
                pushed = []
                for m in range(n, n + several):
                    decay = jnp.exp2(left_here * wide_ref[m * NS : (m + 1) * NS, lanes][None])
                    pushed.append((decay * push_here).reshape(some, chunk))
                added = added + jnp.dot(
                    chosen[n // several],
                    jnp.concatenate(pushed, axis=0),
                    preferred_element_type=jnp.float32,
                )
            state_ref[:, lanes] = added
    total_ref[...] = total_ref[...] + whole

    count = pl.num_programs(0)

    @pl.when(block == count - 1)
    def _():
        @pl.when(place_ref[0] * CORES == count)
        def _():
            add_states(rates_ref, state_ref, total_ref, own_state_ref[...], own_total_ref[...])

        write_carry(carry_ref.at[0], state_ref[...], total_ref[...], turn_ref)
        for target in range(1, carry_ref.shape[0]):
            carry_ref[target] = carry_ref[0]


def step_sizes(place, stream, lows, cols, bias, rates, state, total, targets, after, sums, maps):
    others = stream.shape[0]
    chips = others + 1
    rows, width = stream.shape[1] // CORES, stream.shape[2]
    map_row = CORES * rows // MAPS
    blocks = others * CORES
    carry = (targets, (width // LANES + 1) * NS, LANES)

    def slot(b, s):
        chip = b // CORES
        return lax.rem(s[0] - jnp.where(chip < s[0], chip, chip + 1) + chips, chips) - 1

    def core(b):
        return lax.rem(b, CORES)

    def in_row(b, s):
        return jnp.where(b // CORES < s[0], b, b + CORES)

    def fixed(*shape):
        return pl.BlockSpec(shape, lambda b, s: (0,) * len(shape))

    return pl.pallas_call(
        step_kernel,
        grid_spec=pltpu.PrefetchScalarGridSpec(
            num_scalar_prefetch=1,
            grid=(blocks,),
            in_specs=[
                pl.BlockSpec((1, rows, width), lambda b, s: (slot(b, s), core(b), 0)),
                pl.BlockSpec((1, rows, RANK), lambda b, s: (slot(b, s), core(b), 0)),
                pl.BlockSpec((1, MAPS, rows), lambda b, s: (slot(b, s), map_row, core(b))),
                fixed(*cols.shape),
                fixed(*bias.shape),
                fixed(*rates.shape),
                fixed(*state.shape),
                fixed(*total.shape),
            ]
            + [pl.BlockSpec(memory_space=pl.ANY)] * 3,
            out_specs=[
                pl.BlockSpec((rows, width), lambda b, s: (b, 0)),
                pl.BlockSpec((rows, width), lambda b, s: (in_row(b, s), 0)),
                pl.BlockSpec((1, 2 * NS, rows), lambda b, s: (in_row(b, s), 0, 0)),
                fixed(*carry),
            ],
            scratch_shapes=[
                pltpu.VMEM((NS, width), jnp.float32),
                pltpu.VMEM((1, width), jnp.float32),
                pltpu.VMEM((NS * NS, width), jnp.bfloat16),
                pltpu.VMEM((SUBLANES, LANES), jnp.float32),
            ],
        ),
        out_shape=[
            jax.ShapeDtypeStruct((blocks * rows, width), jnp.bfloat16),
            jax.ShapeDtypeStruct(sums.shape, sums.dtype),
            jax.ShapeDtypeStruct(maps.shape, maps.dtype),
            jax.ShapeDtypeStruct(carry, jnp.bfloat16),
        ],
        input_output_aliases={10: 1, 11: 2},
        compiler_params=params,
        name="step_sizes",
    )(place, stream, lows, lows, cols, bias, rates, state, total, after, sums, maps)


def write_carry(out_ref, state, total, turn_ref):
    tile = state.shape[1] // LANES
    turn_ref[...] = jnp.zeros_like(turn_ref)
    for item in range(tile):
        lanes = slice(item * LANES, (item + 1) * LANES)
        turn_ref[item : item + 1, :] = total[:, lanes]
        out_ref[item * NS : (item + 1) * NS, :] = state[:, lanes].astype(jnp.bfloat16)
    out_ref[tile * NS :, :] = jnp.concatenate(split(turn_ref[...]), axis=0)


def follow(carry_ref, rates_ref, state_ref):
    tile = state_ref.shape[1] // LANES
    sums = carry_ref[tile * NS :, :].astype(jnp.float32)
    sums = sums[:SUBLANES, :] + sums[SUBLANES:, :]
    for item in range(tile):
        lanes = slice(item * LANES, (item + 1) * LANES)
        decay = jnp.exp2(rates_ref[:, lanes] * sums[item : item + 1, :])
        added = carry_ref[item * NS : (item + 1) * NS, :].astype(jnp.float32)
        state_ref[:, lanes] = decay * state_ref[:, lanes] + added
    return sums


def scan_blocks(stream_ref, steps_ref, maps, rates_ref, gain_ref, out_ref, state_ref, work_refs):
    out_of_ref, *hist_refs = work_refs
    rows, width = steps_ref.shape
    source = lax.broadcasted_iota(jnp.int32, (LANES, NS * NS), 0)
    column = lax.rem(lax.broadcasted_iota(jnp.int32, (LANES, NS * NS), 1), NS)
    token = lax.rem(lax.broadcasted_iota(jnp.int32, (rows, NS * NS), 0), NS)
    slot = lax.broadcasted_iota(jnp.int32, (rows, NS * NS), 1) // NS
    turned = jnp.concatenate(
        [maps, jnp.zeros((LANES - 2 * NS, rows), jnp.float32)], axis=0
    ).T.astype(jnp.bfloat16)
    pick = jnp.where(source == NS + column, 1.0, 0.0).astype(jnp.bfloat16)
    spread = jnp.dot(turned, pick, preferred_element_type=jnp.float32)
    out_of_ref[...] = jnp.where(token == slot, spread, 0.0).astype(jnp.bfloat16)
    map_in = maps[:NS, :]
    half = width // 2

    def finish(first, hist_ref):
        here = pl.ds(first, NS)
        mixed = jnp.dot(out_of_ref[here, :], hist_ref[...], preferred_element_type=jnp.float32)
        direct = gain_ref[...] * stream_ref[0, here, :].astype(jnp.float32)
        out_ref[here, :] = (mixed + direct).astype(jnp.bfloat16)

    def advance(first, hist_ref):
        here = pl.ds(first, NS)
        into = pltpu.roll(map_in, lax.rem(rows - first, rows), 1)
        for lanes in (slice(0, half), slice(half, width)):
            state = state_ref[:, lanes]
            rates = rates_ref[:, lanes]
            steps = steps_ref[here, lanes].astype(jnp.float32)
            push = steps * stream_ref[0, here, lanes].astype(jnp.float32)
            for near in range(NS):
                this = slice(near, near + 1)
                state = jnp.exp2(rates * steps[this, :]) * state + into[:, this] * push[this, :]
                hist_ref[near * NS : (near + 1) * NS, lanes] = state.astype(jnp.bfloat16)
            state_ref[:, lanes] = state

    def at(group):
        return pl.multiple_of(group * NS, NS)

    def pair(index, nothing):
        finish(at(2 * index), hist_refs[1])
        advance(at(2 * index + 1), hist_refs[0])
        finish(at(2 * index + 1), hist_refs[0])
        advance(at(2 * index + 2), hist_refs[1])
        return nothing

    groups = rows // NS
    advance(0, hist_refs[1])
    lax.fori_loop(0, groups // 2 - 1, pair, 0)
    finish(rows - 2 * NS, hist_refs[1])
    advance(rows - NS, hist_refs[0])
    finish(rows - NS, hist_refs[0])


def work_shapes(rows, width):
    return [
        pltpu.VMEM((rows, NS * NS), jnp.bfloat16),
        pltpu.VMEM((NS * NS, width), jnp.bfloat16),
        pltpu.VMEM((NS * NS, width), jnp.bfloat16),
    ]


def own_kernel(
    place_ref, stream_ref, low_ref, map_ref, cols_ref, bias_ref, rates_ref, gain_ref,
    out_ref, sums_ref, maps_ref, state_ref, total_ref, steps_ref, *work_refs
):
    rows = steps_ref.shape[0]

    @pl.when(pl.program_id(0) == 0)
    def _():
        state_ref[...] = jnp.zeros_like(state_ref)
        total_ref[...] = jnp.zeros_like(total_ref)

    maps = map_ref[...].astype(jnp.float32)
    maps_ref[0] = maps
    logits = jnp.dot(low_ref[...], cols_ref[...], preferred_element_type=jnp.float32)
    steps = softplus(logits + bias_ref[...]).astype(jnp.bfloat16)
    steps_ref[...] = steps
    within = sums_within(steps)
    sums_ref[...] = within.astype(jnp.bfloat16)
    total_ref[...] = total_ref[...] + within[rows - 1 :, :]
    scan_blocks(stream_ref, steps_ref, maps, rates_ref, gain_ref, out_ref, state_ref, work_refs)


def scan_own(place, stream, lows, cols, bias, rates, gain):
    rows, width = stream.shape[1] // CORES, stream.shape[2]
    map_row = CORES * rows // MAPS

    blocks = lax.axis_size("seq")

    def in_row(b, s):
        return s[0] * CORES + b

    def fixed(*shape):
        return pl.BlockSpec(shape, lambda b, s: (0,) * len(shape))

    block = pl.BlockSpec((rows, width), lambda b, s: (in_row(b, s), 0))
    return pl.pallas_call(
        own_kernel,
        grid_spec=pltpu.PrefetchScalarGridSpec(
            num_scalar_prefetch=1,
            grid=(CORES,),
            in_specs=[
                pl.BlockSpec((1, rows, width), lambda b, s: (0, b, 0)),
                pl.BlockSpec((rows, RANK), lambda b, s: (b, 0)),
                pl.BlockSpec((MAPS, rows), lambda b, s: (map_row, b)),
                fixed(*cols.shape),
                fixed(*bias.shape),
                fixed(*rates.shape),
                fixed(*gain.shape),
            ],
            out_specs=[
                block,
                block,
                pl.BlockSpec((1, 2 * NS, rows), lambda b, s: (in_row(b, s), 0, 0)),
                fixed(NS, width),
                fixed(1, width),
            ],
            scratch_shapes=[pltpu.VMEM((rows, width), jnp.bfloat16)] + work_shapes(rows, width),
        ),
        out_shape=[
            jax.ShapeDtypeStruct((blocks * rows, width), jnp.bfloat16),
            jax.ShapeDtypeStruct((blocks * rows, width), jnp.bfloat16),
            jax.ShapeDtypeStruct((blocks, 2 * NS, rows), jnp.float32),
            jax.ShapeDtypeStruct((NS, width), jnp.float32),
            jax.ShapeDtypeStruct((1, width), jnp.float32),
        ],
        compiler_params=params,
        cost_estimate=pl.CostEstimate(flops=4 * 10**9, bytes_accessed=1 << 21, transcendentals=0),
        name="scan_own",
    )(place, stream, lows, lows, cols, bias, rates, gain)


def others_kernel(
    place_ref, stream_ref, steps_ref, maps_ref, rates_ref, gain_ref, part_ref, out_ref, last_ref,
    *work_refs
):
    del part_ref

    @pl.when(lax.rem(pl.program_id(0), CORES) == 0)
    def _():
        last_ref[...] = jnp.zeros_like(last_ref)

    scan_blocks(
        stream_ref, steps_ref, maps_ref[0], rates_ref, gain_ref, out_ref, last_ref.at[0], work_refs
    )


def scan_others(place, stream, steps, maps, rates, gain, part):
    others = stream.shape[0]
    chips = others + 1
    rows, width = stream.shape[1] // CORES, stream.shape[2]

    def slot(b, s):
        chip = b // CORES
        return lax.rem(s[0] - jnp.where(chip < s[0], chip, chip + 1) + chips, chips) - 1

    def in_row(b, s):
        return jnp.where(b // CORES < s[0], b, b + CORES)

    def fixed(*shape):
        return pl.BlockSpec(shape, lambda b, s: (0,) * len(shape))

    return pl.pallas_call(
        others_kernel,
        grid_spec=pltpu.PrefetchScalarGridSpec(
            num_scalar_prefetch=1,
            grid=(others * CORES,),
            in_specs=[
                pl.BlockSpec((1, rows, width), lambda b, s: (slot(b, s), lax.rem(b, CORES), 0)),
                pl.BlockSpec((rows, width), lambda b, s: (b, 0)),
                pl.BlockSpec((1, 2 * NS, rows), lambda b, s: (in_row(b, s), 0, 0)),
                fixed(*rates.shape),
                fixed(*gain.shape),
                pl.BlockSpec(memory_space=pl.ANY),
            ],
            out_specs=[
                pl.BlockSpec((rows, width), lambda b, s: (in_row(b, s), 0)),
                pl.BlockSpec((1, NS, width), lambda b, s: (b // CORES, 0, 0)),
            ],
            scratch_shapes=work_shapes(rows, width),
        ),
        out_shape=[
            jax.ShapeDtypeStruct(part.shape, part.dtype),
            jax.ShapeDtypeStruct((others, NS, width), jnp.float32),
        ],
        input_output_aliases={6: 0},
        compiler_params=params,
        cost_estimate=pl.CostEstimate(flops=4 * 10**9, bytes_accessed=1 << 21, transcendentals=0),
        name="scan_others",
    )(place, stream, steps, maps, rates, gain, part)


def carried_kernel(
    place_ref, part_ref, sums_ref, maps_ref, last_own_ref, last_come_ref, rates_ref, carries_ref,
    out_ref, state_ref, wide_ref, begin_ref, spread_ref,
):
    block = pl.program_id(0)
    rows, width = out_ref.shape
    chip = block // CORES

    @pl.when(block == 0)
    def _():
        state_ref[...] = jnp.zeros_like(state_ref)

        def compose(row, nothing):
            follow(carries_ref.at[row], rates_ref, state_ref)
            return nothing

        lax.fori_loop(0, lax.axis_index("chan"), compose, 0)
        for n in range(NS):
            wide_ref[n * NS : (n + 1) * NS, :] = jnp.broadcast_to(
                rates_ref[n : n + 1, :], (NS, width)
            ).astype(jnp.bfloat16)

    @pl.when((block > 0) & (lax.rem(block, CORES) == 0))
    def _():
        before = jnp.where(chip - 1 == place_ref[0], last_own_ref[...], last_come_ref[0])
        state_ref[...] = state_ref[...] + before

    state = state_ref[...]
    for n in range(NS):
        begin_ref[n * NS : (n + 1) * NS, :] = jnp.broadcast_to(
            state[n : n + 1, :], (NS, width)
        ).astype(jnp.bfloat16)
    maps = jnp.concatenate([maps_ref[0], jnp.zeros((LANES - 2 * NS, rows), jnp.float32)], axis=0).T
    for n in range(NS):
        spread_ref[:, n * LANES : (n + 1) * LANES] = jnp.broadcast_to(
            maps[:, NS + n : NS + n + 1], (rows, LANES)
        ).astype(jnp.bfloat16)
    last = sums_ref[rows - NS :, :].astype(jnp.float32)[NS - 1 :, :]
    state_ref[...] = jnp.exp2(rates_ref[...] * last) * state
    chunk, several = CORES * LANES, 4

    def some(index, nothing):
        near = pl.ds(pl.multiple_of(index * NS, NS), NS)
        for item in range(width // chunk):
            lanes = slice(item * chunk, (item + 1) * chunk)
            total = part_ref[near, lanes].astype(jnp.float32)
            sums = sums_ref[near, lanes]
            for first in range(0, NS, several):
                terms = []
                for n in range(first, first + several):
                    decay = jnp.exp2(sums * wide_ref[n * NS : (n + 1) * NS, lanes])
                    out_of = spread_ref[near, n * LANES : (n + 1) * LANES]
                    out_of = jnp.concatenate([out_of] * (chunk // LANES), axis=1)
                    terms.append(decay * begin_ref[n * NS : (n + 1) * NS, lanes] * out_of)
                four = (terms[0] + terms[1]) + (terms[2] + terms[3])
                total = total + four.astype(jnp.float32)
            out_ref[near, lanes] = total.astype(jnp.bfloat16)
        return nothing

    lax.fori_loop(0, rows // NS, some, 0)


def add_carried(place, part, sums, maps, lasts, rates, carries):
    blocks, _, rows = maps.shape
    others = lasts[1].shape[0]
    width = rates.shape[1]

    def before(b, s):
        chip = jnp.maximum(b // CORES - 1, 0)
        return jnp.minimum(jnp.where(chip < s[0], chip, jnp.maximum(chip - 1, 0)), others - 1)

    def fixed(*shape):
        return pl.BlockSpec(shape, lambda b, s: (0,) * len(shape))

    block = pl.BlockSpec((rows, width), lambda b, s: (b, 0))
    return pl.pallas_call(
        carried_kernel,
        grid_spec=pltpu.PrefetchScalarGridSpec(
            num_scalar_prefetch=1,
            grid=(blocks,),
            in_specs=[
                block,
                block,
                pl.BlockSpec((1, 2 * NS, rows), lambda b, s: (b, 0, 0)),
                fixed(NS, width),
                pl.BlockSpec((1, NS, width), lambda b, s: (before(b, s), 0, 0)),
                fixed(*rates.shape),
                fixed(*carries.shape),
            ],
            out_specs=block,
            scratch_shapes=[
                pltpu.VMEM((NS, width), jnp.float32),
                pltpu.VMEM((NS * NS, width), jnp.bfloat16),
                pltpu.VMEM((NS * NS, width), jnp.bfloat16),
                pltpu.VMEM((rows, NS * LANES), jnp.bfloat16),
            ],
        ),
        out_shape=jax.ShapeDtypeStruct(part.shape, jnp.bfloat16),
        compiler_params=params,
        name="add_carried",
    )(place, part, sums, maps, *lasts, rates, carries)


def local(
    queries, keys, values, doc_lengths, rank_in, bc_weight, rank_out, dt_bias, a_log, skip_gain
):
    devices = lax.axis_size("seq")
    chips = devices // CORES
    targets = lax.axis_size("chan")
    seq_place = lax.axis_index("seq").astype(jnp.int32)
    chip, core = seq_place // CORES, lax.rem(seq_place, CORES)
    place = jnp.stack([chip, core])
    width = queries.shape[2] // devices
    wide = max(HEAD_SIZE, keys.shape[2] // devices)

    def other(device):
        return device + 1 - 2 * (device % CORES)

    swap = [(device, other(device)) for device in range(devices)]
    near = [(device, device + CORES) for device in range(devices - CORES)]
    far = [(device, other(device + CORES)) for device in range(devices - CORES)]

    def onward(chips_on):
        return [(device, (device + chips_on * CORES) % devices) for device in range(devices)]

    own, theirs = select_heads(keys[0], values[0], chips, wide)
    from_near = lax.ppermute(own, "seq", near)
    from_far = lax.ppermute(theirs, "seq", far)
    swapped = lax.ppermute(theirs, "seq", swap)
    queries_after, _ = lax.optimization_barrier((queries[0], own))
    their_queries = lax.ppermute(queries_after, "seq", swap)
    blocks = (own, swapped, from_near, from_far)

    first = seq_place * width
    logs = lax.dynamic_slice_in_dim(a_log, first, width, 0)
    rates = (-LOG2E * jnp.exp(logs)).T
    cols = lax.dynamic_slice_in_dim(rank_out, first, width, 1)
    bias = lax.dynamic_slice_in_dim(dt_bias, first, width, 0)[None]
    gain = lax.dynamic_slice_in_dim(skip_gain, first, width, 0)[None]

    sent, stayed, part = attend(
        place, doc_lengths, (queries[0], their_queries), blocks, rank_in, bc_weight.T,
        (rates, cols, bias, gain),
    )
    come = [lax.ppermute(sent[step], "seq", onward(step + 1)) for step in range(chips - 1)]
    low_own = low_and_maps(part, lax.ppermute(part, "seq", swap))
    low_come = [lax.ppermute(low_own, "seq", onward(step + 1)) for step in range(chips - 1)]
    got_sent = lax.ppermute(sent, "seq", swap)
    got_stayed = lax.ppermute(stayed, "seq", swap)
    *come, got_stayed = lax.optimization_barrier((*come, got_stayed))
    attn_rows = join_heads(sent, stayed, got_sent, got_stayed)

    part, sums, maps, state, total = scan_own(place, stayed, low_own, cols, bias, rates, gain)
    come, low_come = jnp.stack(come), jnp.stack(low_come)
    steps, sums, maps, carry = step_sizes(
        place, come, low_come, cols, bias, rates, state, total, targets, attn_rows, sums, maps
    )
    carries = lax.all_to_all(carry, "chan", split_axis=0, concat_axis=0, tiled=True)
    part, last_come = scan_others(place, come, steps, maps, rates, gain, part)
    ssm_rows = add_carried(place, part, sums, maps, (state, last_come), rates, carries)
    return (attn_rows[None], ssm_rows[None])


def solution(mesh):
    return jax.shard_map(
        local,
        mesh=mesh,
        in_specs=(
            P("chan", "seq", None),
            P("chan", "seq", None),
            P("chan", "seq", None),
            P("chan", None),
            P(),
            P(),
            P(),
            P(),
            P(),
            P(),
        ),
        out_specs=(P("chan", "seq", None), P("chan", None, "seq")),
        check_vma=False,
    )
```

```python
import functools
import math

import jax
import jax.numpy as jnp
from jax import lax
from jax.experimental import pallas as pl
from jax.experimental.pallas import tpu as pltpu
from jax.sharding import PartitionSpec as P

QUERY_HEADS = 32
KEY_VALUE_HEADS = 8
HEAD_SIZE = 128
GROUP = QUERY_HEADS // KEY_VALUE_HEADS
NS = 16
RANK = 256
CORES = 2
LANES = 128
SUBLANES = 8
MAPS = 2 * NS
LOG2E = 1.4426950408889634

masked_fill = -1e30
params = pltpu.CompilerParams(vmem_limit_bytes=60 << 20)
less = pltpu.CompilerParams(vmem_limit_bytes=16 << 20)


def split(value):
    coarse = value.astype(jnp.bfloat16)
    return coarse, (value - coarse.astype(jnp.float32)).astype(jnp.bfloat16)


def run_copies(pairs, sems):
    copies = [
        pltpu.make_async_copy(source, target, sems.at[i]) for i, (source, target) in enumerate(pairs)
    ]
    for copy in copies:
        copy.start()
    for copy in copies:
        copy.wait()


def columns_of(ref, index, size):
    return ref.at[:, pl.ds(pl.multiple_of(index * size, LANES), size)]


def heads_kernel(key_ref, value_ref, own_ref, their_ref, sems):
    core = lax.rem(lax.axis_index("seq"), CORES)
    wide = own_ref.shape[3]
    halves = key_ref.shape[1] // wide // own_ref.shape[0]
    pairs = []
    for target, which in ((own_ref, core), (their_ref, 1 - core)):
        for chip in range(own_ref.shape[0]):
            index = chip * halves + (which if halves == CORES else 0)
            for kind, source in enumerate((key_ref, value_ref)):
                pairs.append((columns_of(source, index, wide), target.at[chip, kind]))
    run_copies(pairs, sems)


def select_heads(keys, values, chips, wide):
    shape = jax.ShapeDtypeStruct((chips, 2, keys.shape[0], wide), keys.dtype)
    return pl.pallas_call(
        heads_kernel,
        in_specs=[pl.BlockSpec(memory_space=pl.ANY)] * 2,
        out_shape=[shape, shape],
        scratch_shapes=[pltpu.SemaphoreType.DMA((4 * chips,))],
        compiler_params=params,
        name="select_heads",
    )(keys, values)


def join_kernel(sent_ref, stayed_ref, got_sent_ref, got_stayed_ref, out_ref, sems):
    place = lax.axis_index("seq")
    core, chip = lax.rem(place, CORES), place // CORES
    rows = out_ref.shape[0]
    others, _, width = sent_ref.shape
    here = pl.ds(pl.multiple_of(core * rows, rows), rows)
    pairs = []
    for first, rest, which in (
        (stayed_ref, sent_ref, core), (got_stayed_ref, got_sent_ref, 1 - core)
    ):
        for step in range(others + 1):
            source = first.at[0, here, :] if step == 0 else rest.at[step - 1, here, :]
            owner = lax.rem(chip + step, others + 1)
            pairs.append((source, columns_of(out_ref, owner * CORES + which, width)))
    run_copies(pairs, sems)


def join_heads(sent, stayed, got_sent, got_stayed):
    others, rows, width = sent.shape
    return pl.pallas_call(
        join_kernel,
        in_specs=[pl.BlockSpec(memory_space=pl.ANY)] * 4,
        out_shape=jax.ShapeDtypeStruct(
            (rows // CORES, (others + 1) * CORES * width), sent.dtype
        ),
        scratch_shapes=[pltpu.SemaphoreType.DMA((CORES * (others + 1),))],
        compiler_params=less,
        name="join_heads",
    )(sent, stayed, got_sent, got_stayed)


def attend_kernel(
    place_ref, doc_ref, mine_ref, theirs_ref, own_ref, swap_ref, near_ref, far_ref,
    rank_ref, map_ref, *rest, chips,
):
    send_ref, stay_ref, part_ref, mask_ref = rest[-4:]
    step = pl.program_id(0)
    rows = mine_ref.shape[0]
    group = mine_ref.shape[1] // HEAD_SIZE
    chip, core = place_ref[0], place_ref[1]
    first_core = core == 0

    def below(shape):
        column = lax.rem(lax.broadcasted_iota(jnp.int32, shape, 1), rows)
        return lax.broadcasted_iota(jnp.int32, shape, 0) > column

    @pl.when(step == 0)
    def _():
        part_ref[...] = jnp.zeros_like(part_ref)
        own = chip * CORES + core
        swapped = chip * CORES + 1 - core
        near, far = own - CORES, swapped - CORES
        query = lax.broadcasted_iota(jnp.int32, (rows, rows), 1)
        key = lax.broadcasted_iota(jnp.int32, (rows, rows), 0)
        for item, (place, before, middle) in enumerate(
            (
                (own, near, jnp.where(first_core, far, swapped)),
                (swapped, far, jnp.where(first_core, own, near)),
            )
        ):
            query_pos = place * rows + query
            start = jnp.zeros((rows, rows), jnp.int32)
            bound = jnp.int32(0)
            for doc in range(doc_ref.shape[1]):
                bound = bound + doc_ref[0, doc]
                start = jnp.where(query_pos >= bound, bound, start)
            ends = jnp.where(key > query, before, place) * rows + key
            mask_ref[item, :rows, :] = jnp.where(
                (ends >= start) & (ends <= query_pos), 0.0, masked_fill
            )
            mask_ref[item, rows:, :] = jnp.where(
                middle * rows + key >= start, 0.0, masked_fill
            )

    scale = LOG2E / math.sqrt(HEAD_SIZE)

    def windows(kind):
        own, swapped = own_ref[0, kind], swap_ref[0, kind]
        near, far = near_ref[0, kind], far_ref[0, kind]
        return (
            jnp.concatenate([near, own, jnp.where(first_core, far, swapped)], axis=0),
            jnp.concatenate([far, swapped, jnp.where(first_core, own, near)], axis=0),
        )

    scores = []
    for keys, query in zip(windows(0), (mine_ref[...], theirs_ref[...])):
        stacked = jnp.concatenate(
            [query[:, i * HEAD_SIZE : (i + 1) * HEAD_SIZE] for i in range(group)], axis=0
        )
        scores.append(
            lax.dot_general(
                keys, stacked, (((1,), (1,)), ((), ())), preferred_element_type=jnp.float32
            )
        )
    outputs = []
    before = below((rows, group * rows))
    none = jnp.zeros((rows, group * rows), jnp.bfloat16)
    for item, (values, score) in enumerate(zip(windows(1), scores)):
        fill = mask_ref[item]
        ends = jnp.where(before, score[:rows, :], score[rows : 2 * rows, :])
        kept = jnp.concatenate([ends, score[2 * rows :, :]], axis=0)
        kept = kept + jnp.concatenate([fill] * group, axis=1)
        peak = jnp.max(kept, axis=0, keepdims=True)
        raw = jnp.exp2((kept - peak) * scale)
        share = pl.reciprocal(jnp.sum(raw, axis=0, keepdims=True))
        raw = raw.astype(jnp.bfloat16)
        ends = raw[:rows, :]
        spread = jnp.concatenate(
            [jnp.where(before, ends, none), jnp.where(before, none, ends), raw[rows:, :]], axis=0
        )
        mixed = lax.dot_general(
            values, spread, (((0,), (0,)), ((), ())), preferred_element_type=jnp.float32
        )
        mixed = mixed * share
        outputs.append(
            jnp.concatenate(
                [mixed[:, i * rows : (i + 1) * rows].T.astype(jnp.bfloat16) for i in range(group)],
                axis=1,
            )
        )
    stream = jnp.concatenate(
        [
            jnp.where(first_core, outputs[0], outputs[1]),
            jnp.where(first_core, outputs[1], outputs[0]),
        ],
        axis=0,
    )
    last = step >= pl.num_programs(0) - pl.num_programs(0) // chips

    @pl.when(last)
    def _():
        stay_ref[0] = stream

    @pl.when(jnp.logical_not(last))
    def _():
        send_ref[0] = stream

    both = CORES * rows
    part_ref[:both, :] += jnp.dot(stream, rank_ref[...], preferred_element_type=jnp.float32)
    part_ref[both:, :] += lax.dot_general(
        map_ref[...], stream, (((1,), (1,)), ((), ())), preferred_element_type=jnp.float32
    )


def attend(place, doc_lengths, queries, blocks, rank_in, map_rows, after):
    mine, theirs = queries
    chips, _, rows, columns = blocks[0].shape
    heads = columns // HEAD_SIZE
    width = mine.shape[1] // (chips * CORES)
    wide = width // heads

    def owner(j, s):
        return lax.rem(s[0] + 1 + j // heads, chips)

    def column(j, s):
        return (owner(j, s) * CORES + s[1]) * heads + lax.rem(j, heads)

    def sent(j, s):
        at = jnp.minimum(j, (chips - 1) * heads - 1)
        return (at // heads, 0, lax.rem(at, heads))

    query = pl.BlockSpec((rows, wide), lambda j, s: (0, column(j, s)))
    block = pl.BlockSpec(
        (1, 2, rows, HEAD_SIZE), lambda j, s: (owner(j, s), 0, 0, lax.rem(j, heads))
    )
    return pl.pallas_call(
        functools.partial(attend_kernel, chips=chips),
        grid_spec=pltpu.PrefetchScalarGridSpec(
            num_scalar_prefetch=1,
            grid=(chips * heads,),
            in_specs=[pl.BlockSpec(memory_space=pltpu.SMEM), query, query]
            + [block] * 4
            + [
                pl.BlockSpec((wide, RANK), lambda j, s: (column(j, s), 0)),
                pl.BlockSpec((2 * NS, wide), lambda j, s: (0, column(j, s))),
            ]
            + [pl.BlockSpec(memory_space=pl.ANY)] * len(after),
            out_specs=[
                pl.BlockSpec((1, CORES * rows, wide), sent),
                pl.BlockSpec(
                    (1, CORES * rows, wide),
                    lambda j, s: (0, 0, jnp.maximum(j - (chips - 1) * heads, 0)),
                ),
                pl.BlockSpec((CORES * rows + 2 * NS, RANK), lambda j, s: (0, 0)),
            ],
            scratch_shapes=[pltpu.VMEM((2, 2 * rows, rows), jnp.float32)],
        ),
        out_shape=[
            jax.ShapeDtypeStruct((chips - 1, CORES * rows, width), jnp.bfloat16),
            jax.ShapeDtypeStruct((1, CORES * rows, width), jnp.bfloat16),
            jax.ShapeDtypeStruct((CORES * rows + 2 * NS, RANK), jnp.float32),
        ],
        compiler_params=params,
        cost_estimate=pl.CostEstimate(flops=5 * 10**9, bytes_accessed=1 << 22, transcendentals=0),
        name="attend",
    )(place, doc_lengths, mine, theirs, *blocks, rank_in, map_rows, *after)


def low_kernel(mine_ref, theirs_ref, out_ref):
    out_ref[...] = (mine_ref[...] + theirs_ref[...]).astype(jnp.bfloat16)


def low_and_maps(mine, theirs):
    return pl.pallas_call(
        low_kernel,
        out_shape=jax.ShapeDtypeStruct(mine.shape, jnp.bfloat16),
        compiler_params=params,
        cost_estimate=pl.CostEstimate(flops=1, bytes_accessed=1, transcendentals=0),
        name="low_and_maps",
    )(mine, theirs)


def softplus(value):
    small = jnp.exp(-jnp.abs(value))
    tail = jnp.where(small < 0.00390625, small * (1.0 - 0.5 * small), jnp.log(1.0 + small))
    return jnp.maximum(value, 0.0) + tail


def add_states(rates_ref, state_ref, total_ref, states, totals):
    state_ref[...] = jnp.exp2(rates_ref[...] * totals) * state_ref[...] + states
    total_ref[...] = total_ref[...] + totals


def sums_within(steps):
    rows = steps.shape[0]
    at = lax.broadcasted_iota(jnp.int32, (rows, rows), 0)
    of = lax.broadcasted_iota(jnp.int32, (rows, rows), 1)
    upto = jnp.where(of <= at, 1.0, 0.0).astype(jnp.bfloat16)
    return jnp.dot(upto, steps, preferred_element_type=jnp.float32)


def step_kernel(
    place_ref, stream_ref, low_ref, map_ref, cols_ref, bias_ref, rates_ref, *rest
):
    own_state_ref, own_total_ref = rest[:2]
    steps_ref, sums_ref, maps_ref, carry_ref, state_ref, total_ref, wide_ref, turn_ref = rest[5:]
    block = pl.program_id(0)
    rows, width = stream_ref.shape[1:]

    @pl.when(block == 0)
    def _():
        state_ref[...] = jnp.zeros_like(state_ref)
        total_ref[...] = jnp.zeros_like(total_ref)
        for n in range(NS):
            wide_ref[n * NS : (n + 1) * NS, :] = jnp.broadcast_to(
                rates_ref[n : n + 1, :], (NS, width)
            ).astype(jnp.bfloat16)

    @pl.when(block == place_ref[0] * CORES)
    def _():
        add_states(rates_ref, state_ref, total_ref, own_state_ref[...], own_total_ref[...])

    maps = map_ref[0].astype(jnp.float32)
    maps_ref[0] = maps
    logits = jnp.dot(low_ref[0], cols_ref[...], preferred_element_type=jnp.float32)
    steps = softplus(logits + bias_ref[...]).astype(jnp.bfloat16)
    steps_ref[...] = steps
    push = steps * stream_ref[0]
    within = sums_within(steps)
    sums_ref[...] = within.astype(jnp.bfloat16)
    whole = within[rows - 1 :, :]
    left = (whole - within).astype(jnp.bfloat16)
    some, chunk, several = rows // 2, CORES * LANES, 4
    state_row = lax.broadcasted_iota(jnp.int32, (NS, some), 0)
    for first in range(0, rows, some):
        span = slice(first, first + some)
        chosen = [
            jnp.concatenate(
                [
                    jnp.where(state_row == m, maps[:NS, span], 0.0).astype(jnp.bfloat16)
                    for m in range(n, n + several)
                ],
                axis=1,
            )
            for n in range(0, NS, several)
        ]
        for item in range(width // chunk):
            lanes = slice(item * chunk, (item + 1) * chunk)
            left_here = left[span, lanes].reshape(some // NS, NS, chunk)
            push_here = push[span, lanes].reshape(some // NS, NS, chunk)
            added = state_ref[:, lanes]
            if first == 0:
                added = jnp.exp2(rates_ref[:, lanes] * whole[:, lanes]) * added
            for n in range(0, NS, several):
                pushed = []
                for m in range(n, n + several):
                    decay = jnp.exp2(left_here * wide_ref[m * NS : (m + 1) * NS, lanes][None])
                    pushed.append((decay * push_here).reshape(some, chunk))
                added = added + jnp.dot(
                    chosen[n // several],
                    jnp.concatenate(pushed, axis=0),
                    preferred_element_type=jnp.float32,
                )
            state_ref[:, lanes] = added
    total_ref[...] = total_ref[...] + whole

    count = pl.num_programs(0)

    @pl.when(block == count - 1)
    def _():
        @pl.when(place_ref[0] * CORES == count)
        def _():
            add_states(rates_ref, state_ref, total_ref, own_state_ref[...], own_total_ref[...])

        write_carry(carry_ref.at[0], state_ref[...], total_ref[...], turn_ref)
        for target in range(1, carry_ref.shape[0]):
            carry_ref[target] = carry_ref[0]


def step_sizes(place, stream, lows, cols, bias, rates, state, total, targets, after, sums, maps):
    others = stream.shape[0]
    chips = others + 1
    rows, width = stream.shape[1] // CORES, stream.shape[2]
    map_row = CORES * rows // MAPS
    blocks = others * CORES
    carry = (targets, (width // LANES + 1) * NS, LANES)

    def slot(b, s):
        chip = b // CORES
        return lax.rem(s[0] - jnp.where(chip < s[0], chip, chip + 1) + chips, chips) - 1

    def core(b):
        return lax.rem(b, CORES)

    def in_row(b, s):
        return jnp.where(b // CORES < s[0], b, b + CORES)

    def fixed(*shape):
        return pl.BlockSpec(shape, lambda b, s: (0,) * len(shape))

    return pl.pallas_call(
        step_kernel,
        grid_spec=pltpu.PrefetchScalarGridSpec(
            num_scalar_prefetch=1,
            grid=(blocks,),
            in_specs=[
                pl.BlockSpec((1, rows, width), lambda b, s: (slot(b, s), core(b), 0)),
                pl.BlockSpec((1, rows, RANK), lambda b, s: (slot(b, s), core(b), 0)),
                pl.BlockSpec((1, MAPS, rows), lambda b, s: (slot(b, s), map_row, core(b))),
                fixed(*cols.shape),
                fixed(*bias.shape),
                fixed(*rates.shape),
                fixed(*state.shape),
                fixed(*total.shape),
            ]
            + [pl.BlockSpec(memory_space=pl.ANY)] * 3,
            out_specs=[
                pl.BlockSpec((rows, width), lambda b, s: (b, 0)),
                pl.BlockSpec((rows, width), lambda b, s: (in_row(b, s), 0)),
                pl.BlockSpec((1, 2 * NS, rows), lambda b, s: (in_row(b, s), 0, 0)),
                fixed(*carry),
            ],
            scratch_shapes=[
                pltpu.VMEM((NS, width), jnp.float32),
                pltpu.VMEM((1, width), jnp.float32),
                pltpu.VMEM((NS * NS, width), jnp.bfloat16),
                pltpu.VMEM((SUBLANES, LANES), jnp.float32),
            ],
        ),
        out_shape=[
            jax.ShapeDtypeStruct((blocks * rows, width), jnp.bfloat16),
            jax.ShapeDtypeStruct(sums.shape, sums.dtype),
            jax.ShapeDtypeStruct(maps.shape, maps.dtype),
            jax.ShapeDtypeStruct(carry, jnp.bfloat16),
        ],
        input_output_aliases={10: 1, 11: 2},
        compiler_params=params,
        name="step_sizes",
    )(place, stream, lows, lows, cols, bias, rates, state, total, after, sums, maps)


def write_carry(out_ref, state, total, turn_ref):
    tile = state.shape[1] // LANES
    turn_ref[...] = jnp.zeros_like(turn_ref)
    for item in range(tile):
        lanes = slice(item * LANES, (item + 1) * LANES)
        turn_ref[item : item + 1, :] = total[:, lanes]
        out_ref[item * NS : (item + 1) * NS, :] = state[:, lanes].astype(jnp.bfloat16)
    out_ref[tile * NS :, :] = jnp.concatenate(split(turn_ref[...]), axis=0)


def follow(carry_ref, rates_ref, state_ref):
    tile = state_ref.shape[1] // LANES
    sums = carry_ref[tile * NS :, :].astype(jnp.float32)
    sums = sums[:SUBLANES, :] + sums[SUBLANES:, :]
    for item in range(tile):
        lanes = slice(item * LANES, (item + 1) * LANES)
        decay = jnp.exp2(rates_ref[:, lanes] * sums[item : item + 1, :])
        added = carry_ref[item * NS : (item + 1) * NS, :].astype(jnp.float32)
        state_ref[:, lanes] = decay * state_ref[:, lanes] + added
    return sums


def scan_blocks(stream_ref, steps_ref, maps, rates_ref, gain_ref, out_ref, state_ref, work_refs):
    out_of_ref, *hist_refs = work_refs
    rows, width = steps_ref.shape
    source = lax.broadcasted_iota(jnp.int32, (LANES, NS * NS), 0)
    column = lax.rem(lax.broadcasted_iota(jnp.int32, (LANES, NS * NS), 1), NS)
    token = lax.rem(lax.broadcasted_iota(jnp.int32, (rows, NS * NS), 0), NS)
    slot = lax.broadcasted_iota(jnp.int32, (rows, NS * NS), 1) // NS
    turned = jnp.concatenate(
        [maps, jnp.zeros((LANES - 2 * NS, rows), jnp.float32)], axis=0
    ).T.astype(jnp.bfloat16)
    pick = jnp.where(source == NS + column, 1.0, 0.0).astype(jnp.bfloat16)
    spread = jnp.dot(turned, pick, preferred_element_type=jnp.float32)
    out_of_ref[...] = jnp.where(token == slot, spread, 0.0).astype(jnp.bfloat16)
    map_in = maps[:NS, :]
    half = width // 2

    def finish(first, hist_ref):
        here = pl.ds(first, NS)
        mixed = jnp.dot(out_of_ref[here, :], hist_ref[...], preferred_element_type=jnp.float32)
        direct = gain_ref[...] * stream_ref[0, here, :].astype(jnp.float32)
        out_ref[here, :] = (mixed + direct).astype(jnp.bfloat16)

    def advance(first, hist_ref):
        here = pl.ds(first, NS)
        into = pltpu.roll(map_in, lax.rem(rows - first, rows), 1)
        for lanes in (slice(0, half), slice(half, width)):
            state = state_ref[:, lanes]
            rates = rates_ref[:, lanes]
            steps = steps_ref[here, lanes].astype(jnp.float32)
            push = steps * stream_ref[0, here, lanes].astype(jnp.float32)
            for near in range(NS):
                this = slice(near, near + 1)
                state = jnp.exp2(rates * steps[this, :]) * state + into[:, this] * push[this, :]
                hist_ref[near * NS : (near + 1) * NS, lanes] = state.astype(jnp.bfloat16)
            state_ref[:, lanes] = state

    def at(group):
        return pl.multiple_of(group * NS, NS)

    def pair(index, nothing):
        finish(at(2 * index), hist_refs[1])
        advance(at(2 * index + 1), hist_refs[0])
        finish(at(2 * index + 1), hist_refs[0])
        advance(at(2 * index + 2), hist_refs[1])
        return nothing

    groups = rows // NS
    advance(0, hist_refs[1])
    lax.fori_loop(0, groups // 2 - 1, pair, 0)
    finish(rows - 2 * NS, hist_refs[1])
    advance(rows - NS, hist_refs[0])
    finish(rows - NS, hist_refs[0])


def work_shapes(rows, width):
    return [
        pltpu.VMEM((rows, NS * NS), jnp.bfloat16),
        pltpu.VMEM((NS * NS, width), jnp.bfloat16),
        pltpu.VMEM((NS * NS, width), jnp.bfloat16),
    ]


def own_kernel(
    place_ref, stream_ref, low_ref, map_ref, cols_ref, bias_ref, rates_ref, gain_ref,
    out_ref, sums_ref, maps_ref, state_ref, total_ref, steps_ref, *work_refs
):
    rows = steps_ref.shape[0]

    @pl.when(pl.program_id(0) == 0)
    def _():
        state_ref[...] = jnp.zeros_like(state_ref)
        total_ref[...] = jnp.zeros_like(total_ref)

    maps = map_ref[...].astype(jnp.float32)
    maps_ref[0] = maps
    logits = jnp.dot(low_ref[...], cols_ref[...], preferred_element_type=jnp.float32)
    steps = softplus(logits + bias_ref[...]).astype(jnp.bfloat16)
    steps_ref[...] = steps
    within = sums_within(steps)
    sums_ref[...] = within.astype(jnp.bfloat16)
    total_ref[...] = total_ref[...] + within[rows - 1 :, :]
    scan_blocks(stream_ref, steps_ref, maps, rates_ref, gain_ref, out_ref, state_ref, work_refs)


def scan_own(place, stream, lows, cols, bias, rates, gain):
    rows, width = stream.shape[1] // CORES, stream.shape[2]
    map_row = CORES * rows // MAPS

    blocks = lax.axis_size("seq")

    def in_row(b, s):
        return s[0] * CORES + b

    def fixed(*shape):
        return pl.BlockSpec(shape, lambda b, s: (0,) * len(shape))

    block = pl.BlockSpec((rows, width), lambda b, s: (in_row(b, s), 0))
    return pl.pallas_call(
        own_kernel,
        grid_spec=pltpu.PrefetchScalarGridSpec(
            num_scalar_prefetch=1,
            grid=(CORES,),
            in_specs=[
                pl.BlockSpec((1, rows, width), lambda b, s: (0, b, 0)),
                pl.BlockSpec((rows, RANK), lambda b, s: (b, 0)),
                pl.BlockSpec((MAPS, rows), lambda b, s: (map_row, b)),
                fixed(*cols.shape),
                fixed(*bias.shape),
                fixed(*rates.shape),
                fixed(*gain.shape),
            ],
            out_specs=[
                block,
                block,
                pl.BlockSpec((1, 2 * NS, rows), lambda b, s: (in_row(b, s), 0, 0)),
                fixed(NS, width),
                fixed(1, width),
            ],
            scratch_shapes=[pltpu.VMEM((rows, width), jnp.bfloat16)] + work_shapes(rows, width),
        ),
        out_shape=[
            jax.ShapeDtypeStruct((blocks * rows, width), jnp.bfloat16),
            jax.ShapeDtypeStruct((blocks * rows, width), jnp.bfloat16),
            jax.ShapeDtypeStruct((blocks, 2 * NS, rows), jnp.float32),
            jax.ShapeDtypeStruct((NS, width), jnp.float32),
            jax.ShapeDtypeStruct((1, width), jnp.float32),
        ],
        compiler_params=params,
        cost_estimate=pl.CostEstimate(flops=4 * 10**9, bytes_accessed=1 << 21, transcendentals=0),
        name="scan_own",
    )(place, stream, lows, lows, cols, bias, rates, gain)


def others_kernel(
    place_ref, stream_ref, steps_ref, maps_ref, rates_ref, gain_ref, part_ref, out_ref, last_ref,
    *work_refs
):
    del part_ref

    @pl.when(lax.rem(pl.program_id(0), CORES) == 0)
    def _():
        last_ref[...] = jnp.zeros_like(last_ref)

    scan_blocks(
        stream_ref, steps_ref, maps_ref[0], rates_ref, gain_ref, out_ref, last_ref.at[0], work_refs
    )


def scan_others(place, stream, steps, maps, rates, gain, part):
    others = stream.shape[0]
    chips = others + 1
    rows, width = stream.shape[1] // CORES, stream.shape[2]

    def slot(b, s):
        chip = b // CORES
        return lax.rem(s[0] - jnp.where(chip < s[0], chip, chip + 1) + chips, chips) - 1

    def in_row(b, s):
        return jnp.where(b // CORES < s[0], b, b + CORES)

    def fixed(*shape):
        return pl.BlockSpec(shape, lambda b, s: (0,) * len(shape))

    return pl.pallas_call(
        others_kernel,
        grid_spec=pltpu.PrefetchScalarGridSpec(
            num_scalar_prefetch=1,
            grid=(others * CORES,),
            in_specs=[
                pl.BlockSpec((1, rows, width), lambda b, s: (slot(b, s), lax.rem(b, CORES), 0)),
                pl.BlockSpec((rows, width), lambda b, s: (b, 0)),
                pl.BlockSpec((1, 2 * NS, rows), lambda b, s: (in_row(b, s), 0, 0)),
                fixed(*rates.shape),
                fixed(*gain.shape),
                pl.BlockSpec(memory_space=pl.ANY),
            ],
            out_specs=[
                pl.BlockSpec((rows, width), lambda b, s: (in_row(b, s), 0)),
                pl.BlockSpec((1, NS, width), lambda b, s: (b // CORES, 0, 0)),
            ],
            scratch_shapes=work_shapes(rows, width),
        ),
        out_shape=[
            jax.ShapeDtypeStruct(part.shape, part.dtype),
            jax.ShapeDtypeStruct((others, NS, width), jnp.float32),
        ],
        input_output_aliases={6: 0},
        compiler_params=params,
        cost_estimate=pl.CostEstimate(flops=4 * 10**9, bytes_accessed=1 << 21, transcendentals=0),
        name="scan_others",
    )(place, stream, steps, maps, rates, gain, part)


def carried_kernel(
    place_ref, part_ref, sums_ref, maps_ref, last_own_ref, last_come_ref, rates_ref, carries_ref,
    out_ref, state_ref, wide_ref, begin_ref, spread_ref,
):
    block = pl.program_id(0)
    rows, width = out_ref.shape
    chip = block // CORES

    @pl.when(block == 0)
    def _():
        state_ref[...] = jnp.zeros_like(state_ref)

        def compose(row, nothing):
            follow(carries_ref.at[row], rates_ref, state_ref)
            return nothing

        lax.fori_loop(0, lax.axis_index("chan"), compose, 0)
        for n in range(NS):
            wide_ref[n * NS : (n + 1) * NS, :] = jnp.broadcast_to(
                rates_ref[n : n + 1, :], (NS, width)
            ).astype(jnp.bfloat16)

    @pl.when((block > 0) & (lax.rem(block, CORES) == 0))
    def _():
        before = jnp.where(chip - 1 == place_ref[0], last_own_ref[...], last_come_ref[0])
        state_ref[...] = state_ref[...] + before

    state = state_ref[...]
    for n in range(NS):
        begin_ref[n * NS : (n + 1) * NS, :] = jnp.broadcast_to(
            state[n : n + 1, :], (NS, width)
        ).astype(jnp.bfloat16)
    maps = jnp.concatenate([maps_ref[0], jnp.zeros((LANES - 2 * NS, rows), jnp.float32)], axis=0).T
    for n in range(NS):
        spread_ref[:, n * LANES : (n + 1) * LANES] = jnp.broadcast_to(
            maps[:, NS + n : NS + n + 1], (rows, LANES)
        ).astype(jnp.bfloat16)
    last = sums_ref[rows - NS :, :].astype(jnp.float32)[NS - 1 :, :]
    state_ref[...] = jnp.exp2(rates_ref[...] * last) * state
    chunk, several = CORES * LANES, 4

    def some(index, nothing):
        near = pl.ds(pl.multiple_of(index * NS, NS), NS)
        for item in range(width // chunk):
            lanes = slice(item * chunk, (item + 1) * chunk)
            total = part_ref[near, lanes].astype(jnp.float32)
            sums = sums_ref[near, lanes]
            for first in range(0, NS, several):
                terms = []
                for n in range(first, first + several):
                    decay = jnp.exp2(sums * wide_ref[n * NS : (n + 1) * NS, lanes])
                    out_of = spread_ref[near, n * LANES : (n + 1) * LANES]
                    out_of = jnp.concatenate([out_of] * (chunk // LANES), axis=1)
                    terms.append(decay * begin_ref[n * NS : (n + 1) * NS, lanes] * out_of)
                four = (terms[0] + terms[1]) + (terms[2] + terms[3])
                total = total + four.astype(jnp.float32)
            out_ref[near, lanes] = total.astype(jnp.bfloat16)
        return nothing

    lax.fori_loop(0, rows // NS, some, 0)


def add_carried(place, part, sums, maps, lasts, rates, carries):
    blocks, _, rows = maps.shape
    others = lasts[1].shape[0]
    width = rates.shape[1]

    def before(b, s):
        chip = jnp.maximum(b // CORES - 1, 0)
        return jnp.minimum(jnp.where(chip < s[0], chip, jnp.maximum(chip - 1, 0)), others - 1)

    def fixed(*shape):
        return pl.BlockSpec(shape, lambda b, s: (0,) * len(shape))

    block = pl.BlockSpec((rows, width), lambda b, s: (b, 0))
    return pl.pallas_call(
        carried_kernel,
        grid_spec=pltpu.PrefetchScalarGridSpec(
            num_scalar_prefetch=1,
            grid=(blocks,),
            in_specs=[
                block,
                block,
                pl.BlockSpec((1, 2 * NS, rows), lambda b, s: (b, 0, 0)),
                fixed(NS, width),
                pl.BlockSpec((1, NS, width), lambda b, s: (before(b, s), 0, 0)),
                fixed(*rates.shape),
                fixed(*carries.shape),
            ],
            out_specs=block,
            scratch_shapes=[
                pltpu.VMEM((NS, width), jnp.float32),
                pltpu.VMEM((NS * NS, width), jnp.bfloat16),
                pltpu.VMEM((NS * NS, width), jnp.bfloat16),
                pltpu.VMEM((rows, NS * LANES), jnp.bfloat16),
            ],
        ),
        out_shape=jax.ShapeDtypeStruct(part.shape, jnp.bfloat16),
        compiler_params=params,
        name="add_carried",
    )(place, part, sums, maps, *lasts, rates, carries)


def local(
    queries, keys, values, doc_lengths, rank_in, bc_weight, rank_out, dt_bias, a_log, skip_gain
):
    devices = lax.axis_size("seq")
    chips = devices // CORES
    targets = lax.axis_size("chan")
    seq_place = lax.axis_index("seq").astype(jnp.int32)
    chip, core = seq_place // CORES, lax.rem(seq_place, CORES)
    place = jnp.stack([chip, core])
    width = queries.shape[2] // devices
    wide = max(HEAD_SIZE, keys.shape[2] // devices)

    def other(device):
        return device + 1 - 2 * (device % CORES)

    swap = [(device, other(device)) for device in range(devices)]
    near = [(device, device + CORES) for device in range(devices - CORES)]
    far = [(device, other(device + CORES)) for device in range(devices - CORES)]

    def onward(chips_on):
        return [(device, (device + chips_on * CORES) % devices) for device in range(devices)]

    own, theirs = select_heads(keys[0], values[0], chips, wide)
    from_near = lax.ppermute(own, "seq", near)
    from_far = lax.ppermute(theirs, "seq", far)
    swapped = lax.ppermute(theirs, "seq", swap)
    queries_after, _ = lax.optimization_barrier((queries[0], own))
    their_queries = lax.ppermute(queries_after, "seq", swap)
    blocks = (own, swapped, from_near, from_far)

    first = seq_place * width
    logs = lax.dynamic_slice_in_dim(a_log, first, width, 0)
    rates = (-LOG2E * jnp.exp(logs)).T
    cols = lax.dynamic_slice_in_dim(rank_out, first, width, 1)
    bias = lax.dynamic_slice_in_dim(dt_bias, first, width, 0)[None]
    gain = lax.dynamic_slice_in_dim(skip_gain, first, width, 0)[None]

    sent, stayed, part = attend(
        place, doc_lengths, (queries[0], their_queries), blocks, rank_in, bc_weight.T,
        (rates, cols, bias, gain),
    )
    come = [lax.ppermute(sent[step], "seq", onward(step + 1)) for step in range(chips - 1)]
    low_own = low_and_maps(part, lax.ppermute(part, "seq", swap))
    low_come = [lax.ppermute(low_own, "seq", onward(step + 1)) for step in range(chips - 1)]
    got_sent = lax.ppermute(sent, "seq", swap)
    got_stayed = lax.ppermute(stayed, "seq", swap)
    *come, got_stayed = lax.optimization_barrier((*come, got_stayed))
    attn_rows = join_heads(sent, stayed, got_sent, got_stayed)

    part, sums, maps, state, total = scan_own(place, stayed, low_own, cols, bias, rates, gain)
    come, low_come = jnp.stack(come), jnp.stack(low_come)
    steps, sums, maps, carry = step_sizes(
        place, come, low_come, cols, bias, rates, state, total, targets, attn_rows, sums, maps
    )
    carries = lax.all_to_all(carry, "chan", split_axis=0, concat_axis=0, tiled=True)
    part, last_come = scan_others(place, come, steps, maps, rates, gain, part)
    ssm_rows = add_carried(place, part, sums, maps, (state, last_come), rates, carries)
    return (attn_rows[None], ssm_rows[None])


def solution(mesh):
    return jax.shard_map(
        local,
        mesh=mesh,
        in_specs=(
            P("chan", "seq", None),
            P("chan", "seq", None),
            P("chan", "seq", None),
            P("chan", None),
            P(),
            P(),
            P(),
            P(),
            P(),
            P(),
        ),
        out_specs=(P("chan", "seq", None), P("chan", None, "seq")),
        check_vma=False,
    )
```

```python
import functools
import math

import jax
import jax.numpy as jnp
from jax import lax
from jax.experimental import pallas as pl
from jax.experimental.pallas import tpu as pltpu
from jax.sharding import PartitionSpec as P

QUERY_HEADS = 32
KEY_VALUE_HEADS = 8
HEAD_SIZE = 128
GROUP = QUERY_HEADS // KEY_VALUE_HEADS
NS = 16
RANK = 256
CORES = 2
LANES = 128
SUBLANES = 8
MAPS = 2 * NS
LOG2E = 1.4426950408889634

masked_fill = -1e30
params = pltpu.CompilerParams(vmem_limit_bytes=60 << 20)
less = pltpu.CompilerParams(vmem_limit_bytes=16 << 20)


def split(value):
    coarse = value.astype(jnp.bfloat16)
    return coarse, (value - coarse.astype(jnp.float32)).astype(jnp.bfloat16)


def run_copies(pairs, sems):
    copies = [
        pltpu.make_async_copy(source, target, sems.at[i]) for i, (source, target) in enumerate(pairs)
    ]
    for copy in copies:
        copy.start()
    for copy in copies:
        copy.wait()


def columns_of(ref, index, size):
    return ref.at[:, pl.ds(pl.multiple_of(index * size, LANES), size)]


def heads_kernel(key_ref, value_ref, own_ref, their_ref, sems):
    core = lax.rem(lax.axis_index("seq"), CORES)
    wide = own_ref.shape[3]
    halves = key_ref.shape[1] // wide // own_ref.shape[0]
    pairs = []
    for target, which in ((own_ref, core), (their_ref, 1 - core)):
        for chip in range(own_ref.shape[0]):
            index = chip * halves + (which if halves == CORES else 0)
            for kind, source in enumerate((key_ref, value_ref)):
                pairs.append((columns_of(source, index, wide), target.at[chip, kind]))
    run_copies(pairs, sems)


def select_heads(keys, values, chips, wide):
    shape = jax.ShapeDtypeStruct((chips, 2, keys.shape[0], wide), keys.dtype)
    return pl.pallas_call(
        heads_kernel,
        in_specs=[pl.BlockSpec(memory_space=pl.ANY)] * 2,
        out_shape=[shape, shape],
        scratch_shapes=[pltpu.SemaphoreType.DMA((4 * chips,))],
        compiler_params=params,
        name="select_heads",
    )(keys, values)


def join_kernel(sent_ref, stayed_ref, got_sent_ref, got_stayed_ref, out_ref, sems):
    place = lax.axis_index("seq")
    core, chip = lax.rem(place, CORES), place // CORES
    rows = out_ref.shape[0]
    others, _, width = sent_ref.shape
    here = pl.ds(pl.multiple_of(core * rows, rows), rows)
    pairs = []
    for first, rest, which in (
        (stayed_ref, sent_ref, core), (got_stayed_ref, got_sent_ref, 1 - core)
    ):
        for step in range(others + 1):
            source = first.at[0, here, :] if step == 0 else rest.at[step - 1, here, :]
            owner = lax.rem(chip + step, others + 1)
            pairs.append((source, columns_of(out_ref, owner * CORES + which, width)))
    run_copies(pairs, sems)


def join_heads(sent, stayed, got_sent, got_stayed):
    others, rows, width = sent.shape
    return pl.pallas_call(
        join_kernel,
        in_specs=[pl.BlockSpec(memory_space=pl.ANY)] * 4,
        out_shape=jax.ShapeDtypeStruct(
            (rows // CORES, (others + 1) * CORES * width), sent.dtype
        ),
        scratch_shapes=[pltpu.SemaphoreType.DMA((CORES * (others + 1),))],
        compiler_params=less,
        name="join_heads",
    )(sent, stayed, got_sent, got_stayed)


def attend_kernel(
    place_ref, doc_ref, mine_ref, theirs_ref, own_ref, swap_ref, near_ref, far_ref,
    rank_ref, map_ref, *rest, chips,
):
    send_ref, stay_ref, part_ref, mask_ref = rest[-4:]
    step = pl.program_id(0)
    rows = mine_ref.shape[0]
    group = mine_ref.shape[1] // HEAD_SIZE
    chip, core = place_ref[0], place_ref[1]
    first_core = core == 0

    def below(shape):
        column = lax.rem(lax.broadcasted_iota(jnp.int32, shape, 1), rows)
        return lax.broadcasted_iota(jnp.int32, shape, 0) > column

    @pl.when(step == 0)
    def _():
        part_ref[...] = jnp.zeros_like(part_ref)
        own = chip * CORES + core
        swapped = chip * CORES + 1 - core
        near, far = own - CORES, swapped - CORES
        query = lax.broadcasted_iota(jnp.int32, (rows, rows), 1)
        key = lax.broadcasted_iota(jnp.int32, (rows, rows), 0)
        for item, (place, before, middle) in enumerate(
            (
                (own, near, jnp.where(first_core, far, swapped)),
                (swapped, far, jnp.where(first_core, own, near)),
            )
        ):
            query_pos = place * rows + query
            start = jnp.zeros((rows, rows), jnp.int32)
            bound = jnp.int32(0)
            for doc in range(doc_ref.shape[1]):
                bound = bound + doc_ref[0, doc]
                start = jnp.where(query_pos >= bound, bound, start)
            ends = jnp.where(key > query, before, place) * rows + key
            mask_ref[item, :rows, :] = jnp.where(
                (ends >= start) & (ends <= query_pos), 0.0, masked_fill
            )
            mask_ref[item, rows:, :] = jnp.where(
                middle * rows + key >= start, 0.0, masked_fill
            )

    scale = LOG2E / math.sqrt(HEAD_SIZE)

    def windows(kind):
        own, swapped = own_ref[0, kind], swap_ref[0, kind]
        near, far = near_ref[0, kind], far_ref[0, kind]
        return (
            jnp.concatenate([near, own, jnp.where(first_core, far, swapped)], axis=0),
            jnp.concatenate([far, swapped, jnp.where(first_core, own, near)], axis=0),
        )

    scores = []
    for keys, query in zip(windows(0), (mine_ref[...], theirs_ref[...])):
        stacked = jnp.concatenate(
            [query[:, i * HEAD_SIZE : (i + 1) * HEAD_SIZE] for i in range(group)], axis=0
        )
        scores.append(
            lax.dot_general(
                keys, stacked, (((1,), (1,)), ((), ())), preferred_element_type=jnp.float32
            )
        )
    outputs = []
    before = below((rows, group * rows))
    none = jnp.zeros((rows, group * rows), jnp.bfloat16)
    for item, (values, score) in enumerate(zip(windows(1), scores)):
        fill = mask_ref[item]
        ends = jnp.where(before, score[:rows, :], score[rows : 2 * rows, :])
        kept = jnp.concatenate([ends, score[2 * rows :, :]], axis=0)
        kept = kept + jnp.concatenate([fill] * group, axis=1)
        peak = jnp.max(kept, axis=0, keepdims=True)
        raw = jnp.exp2((kept - peak) * scale)
        share = pl.reciprocal(jnp.sum(raw, axis=0, keepdims=True))
        raw = raw.astype(jnp.bfloat16)
        ends = raw[:rows, :]
        spread = jnp.concatenate(
            [jnp.where(before, ends, none), jnp.where(before, none, ends), raw[rows:, :]], axis=0
        )
        mixed = lax.dot_general(
            values, spread, (((0,), (0,)), ((), ())), preferred_element_type=jnp.float32
        )
        mixed = mixed * share
        outputs.append(
            jnp.concatenate(
                [mixed[:, i * rows : (i + 1) * rows].T.astype(jnp.bfloat16) for i in range(group)],
                axis=1,
            )
        )
    stream = jnp.concatenate(
        [
            jnp.where(first_core, outputs[0], outputs[1]),
            jnp.where(first_core, outputs[1], outputs[0]),
        ],
        axis=0,
    )
    last = step >= pl.num_programs(0) - pl.num_programs(0) // chips

    @pl.when(last)
    def _():
        stay_ref[0] = stream

    @pl.when(jnp.logical_not(last))
    def _():
        send_ref[0] = stream

    both = CORES * rows
    part_ref[:both, :] += jnp.dot(stream, rank_ref[...], preferred_element_type=jnp.float32)
    part_ref[both:, :] += lax.dot_general(
        map_ref[...], stream, (((1,), (1,)), ((), ())), preferred_element_type=jnp.float32
    )


def attend(place, doc_lengths, queries, blocks, rank_in, map_rows, after):
    mine, theirs = queries
    chips, _, rows, columns = blocks[0].shape
    heads = columns // HEAD_SIZE
    width = mine.shape[1] // (chips * CORES)
    wide = width // heads

    def owner(j, s):
        return lax.rem(s[0] + 1 + j // heads, chips)

    def column(j, s):
        return (owner(j, s) * CORES + s[1]) * heads + lax.rem(j, heads)

    def sent(j, s):
        at = jnp.minimum(j, (chips - 1) * heads - 1)
        return (at // heads, 0, lax.rem(at, heads))

    query = pl.BlockSpec((rows, wide), lambda j, s: (0, column(j, s)))
    block = pl.BlockSpec(
        (1, 2, rows, HEAD_SIZE), lambda j, s: (owner(j, s), 0, 0, lax.rem(j, heads))
    )
    return pl.pallas_call(
        functools.partial(attend_kernel, chips=chips),
        grid_spec=pltpu.PrefetchScalarGridSpec(
            num_scalar_prefetch=1,
            grid=(chips * heads,),
            in_specs=[pl.BlockSpec(memory_space=pltpu.SMEM), query, query]
            + [block] * 4
            + [
                pl.BlockSpec((wide, RANK), lambda j, s: (column(j, s), 0)),
                pl.BlockSpec((2 * NS, wide), lambda j, s: (0, column(j, s))),
            ]
            + [pl.BlockSpec(memory_space=pl.ANY)] * len(after),
            out_specs=[
                pl.BlockSpec((1, CORES * rows, wide), sent),
                pl.BlockSpec(
                    (1, CORES * rows, wide),
                    lambda j, s: (0, 0, jnp.maximum(j - (chips - 1) * heads, 0)),
                ),
                pl.BlockSpec((CORES * rows + 2 * NS, RANK), lambda j, s: (0, 0)),
            ],
            scratch_shapes=[pltpu.VMEM((2, 2 * rows, rows), jnp.float32)],
        ),
        out_shape=[
            jax.ShapeDtypeStruct((chips - 1, CORES * rows, width), jnp.bfloat16),
            jax.ShapeDtypeStruct((1, CORES * rows, width), jnp.bfloat16),
            jax.ShapeDtypeStruct((CORES * rows + 2 * NS, RANK), jnp.float32),
        ],
        compiler_params=params,
        cost_estimate=pl.CostEstimate(flops=5 * 10**9, bytes_accessed=1 << 22, transcendentals=0),
        name="attend",
    )(place, doc_lengths, mine, theirs, *blocks, rank_in, map_rows, *after)


def low_kernel(mine_ref, theirs_ref, out_ref):
    out_ref[...] = (mine_ref[...] + theirs_ref[...]).astype(jnp.bfloat16)


def low_and_maps(mine, theirs):
    return pl.pallas_call(
        low_kernel,
        out_shape=jax.ShapeDtypeStruct(mine.shape, jnp.bfloat16),
        compiler_params=less,
        cost_estimate=pl.CostEstimate(flops=1, bytes_accessed=1, transcendentals=0),
        name="low_and_maps",
    )(mine, theirs)


def softplus(value):
    small = jnp.exp(-jnp.abs(value))
    tail = jnp.where(small < 0.00390625, small * (1.0 - 0.5 * small), jnp.log(1.0 + small))
    return jnp.maximum(value, 0.0) + tail


def add_states(rates_ref, state_ref, total_ref, states, totals):
    state_ref[...] = jnp.exp2(rates_ref[...] * totals) * state_ref[...] + states
    total_ref[...] = total_ref[...] + totals


def sums_within(steps):
    rows = steps.shape[0]
    at = lax.broadcasted_iota(jnp.int32, (rows, rows), 0)
    of = lax.broadcasted_iota(jnp.int32, (rows, rows), 1)
    upto = jnp.where(of <= at, 1.0, 0.0).astype(jnp.bfloat16)
    return jnp.dot(upto, steps, preferred_element_type=jnp.float32)


def step_kernel(
    place_ref, stream_ref, low_ref, map_ref, cols_ref, bias_ref, rates_ref, *rest
):
    own_state_ref, own_total_ref = rest[:2]
    steps_ref, sums_ref, maps_ref, carry_ref, state_ref, total_ref, wide_ref, turn_ref = rest[5:]
    block = pl.program_id(0)
    rows, width = stream_ref.shape[1:]

    @pl.when(block == 0)
    def _():
        state_ref[...] = jnp.zeros_like(state_ref)
        total_ref[...] = jnp.zeros_like(total_ref)
        for n in range(NS):
            wide_ref[n * NS : (n + 1) * NS, :] = jnp.broadcast_to(
                rates_ref[n : n + 1, :], (NS, width)
            ).astype(jnp.bfloat16)

    @pl.when(block == place_ref[0] * CORES)
    def _():
        add_states(rates_ref, state_ref, total_ref, own_state_ref[...], own_total_ref[...])

    maps = map_ref[0].astype(jnp.float32)
    maps_ref[0] = maps
    logits = jnp.dot(low_ref[0], cols_ref[...], preferred_element_type=jnp.float32)
    steps = softplus(logits + bias_ref[...]).astype(jnp.bfloat16)
    steps_ref[...] = steps
    push = steps * stream_ref[0]
    within = sums_within(steps)
    sums_ref[...] = within.astype(jnp.bfloat16)
    whole = within[rows - 1 :, :]
    left = (whole - within).astype(jnp.bfloat16)
    some, chunk, several = rows // 2, CORES * LANES, 4
    state_row = lax.broadcasted_iota(jnp.int32, (NS, some), 0)
    for first in range(0, rows, some):
        span = slice(first, first + some)
        chosen = [
            jnp.concatenate(
                [
                    jnp.where(state_row == m, maps[:NS, span], 0.0).astype(jnp.bfloat16)
                    for m in range(n, n + several)
                ],
                axis=1,
            )
            for n in range(0, NS, several)
        ]
        for item in range(width // chunk):
            lanes = slice(item * chunk, (item + 1) * chunk)
            left_here = left[span, lanes].reshape(some // NS, NS, chunk)
            push_here = push[span, lanes].reshape(some // NS, NS, chunk)
            added = state_ref[:, lanes]
            if first == 0:
                added = jnp.exp2(rates_ref[:, lanes] * whole[:, lanes]) * added
            for n in range(0, NS, several):
                pushed = []
                for m in range(n, n + several):
                    decay = jnp.exp2(left_here * wide_ref[m * NS : (m + 1) * NS, lanes][None])
                    pushed.append((decay * push_here).reshape(some, chunk))
                added = added + jnp.dot(
                    chosen[n // several],
                    jnp.concatenate(pushed, axis=0),
                    preferred_element_type=jnp.float32,
                )
            state_ref[:, lanes] = added
    total_ref[...] = total_ref[...] + whole

    count = pl.num_programs(0)

    @pl.when(block == count - 1)
    def _():
        @pl.when(place_ref[0] * CORES == count)
        def _():
            add_states(rates_ref, state_ref, total_ref, own_state_ref[...], own_total_ref[...])

        write_carry(carry_ref.at[0], state_ref[...], total_ref[...], turn_ref)
        for target in range(1, carry_ref.shape[0]):
            carry_ref[target] = carry_ref[0]


def step_sizes(place, stream, lows, cols, bias, rates, state, total, targets, after, sums, maps):
    others = stream.shape[0]
    chips = others + 1
    rows, width = stream.shape[1] // CORES, stream.shape[2]
    map_row = CORES * rows // MAPS
    blocks = others * CORES
    carry = (targets, (width // LANES + 1) * NS, LANES)

    def slot(b, s):
        chip = b // CORES
        return lax.rem(s[0] - jnp.where(chip < s[0], chip, chip + 1) + chips, chips) - 1

    def core(b):
        return lax.rem(b, CORES)

    def in_row(b, s):
        return jnp.where(b // CORES < s[0], b, b + CORES)

    def fixed(*shape):
        return pl.BlockSpec(shape, lambda b, s: (0,) * len(shape))

    return pl.pallas_call(
        step_kernel,
        grid_spec=pltpu.PrefetchScalarGridSpec(
            num_scalar_prefetch=1,
            grid=(blocks,),
            in_specs=[
                pl.BlockSpec((1, rows, width), lambda b, s: (slot(b, s), core(b), 0)),
                pl.BlockSpec((1, rows, RANK), lambda b, s: (slot(b, s), core(b), 0)),
                pl.BlockSpec((1, MAPS, rows), lambda b, s: (slot(b, s), map_row, core(b))),
                fixed(*cols.shape),
                fixed(*bias.shape),
                fixed(*rates.shape),
                fixed(*state.shape),
                fixed(*total.shape),
            ]
            + [pl.BlockSpec(memory_space=pl.ANY)] * 3,
            out_specs=[
                pl.BlockSpec((rows, width), lambda b, s: (b, 0)),
                pl.BlockSpec((rows, width), lambda b, s: (in_row(b, s), 0)),
                pl.BlockSpec((1, 2 * NS, rows), lambda b, s: (in_row(b, s), 0, 0)),
                fixed(*carry),
            ],
            scratch_shapes=[
                pltpu.VMEM((NS, width), jnp.float32),
                pltpu.VMEM((1, width), jnp.float32),
                pltpu.VMEM((NS * NS, width), jnp.bfloat16),
                pltpu.VMEM((SUBLANES, LANES), jnp.float32),
            ],
        ),
        out_shape=[
            jax.ShapeDtypeStruct((blocks * rows, width), jnp.bfloat16),
            jax.ShapeDtypeStruct(sums.shape, sums.dtype),
            jax.ShapeDtypeStruct(maps.shape, maps.dtype),
            jax.ShapeDtypeStruct(carry, jnp.bfloat16),
        ],
        input_output_aliases={10: 1, 11: 2},
        compiler_params=params,
        name="step_sizes",
    )(place, stream, lows, lows, cols, bias, rates, state, total, after, sums, maps)


def write_carry(out_ref, state, total, turn_ref):
    tile = state.shape[1] // LANES
    turn_ref[...] = jnp.zeros_like(turn_ref)
    for item in range(tile):
        lanes = slice(item * LANES, (item + 1) * LANES)
        turn_ref[item : item + 1, :] = total[:, lanes]
        out_ref[item * NS : (item + 1) * NS, :] = state[:, lanes].astype(jnp.bfloat16)
    out_ref[tile * NS :, :] = jnp.concatenate(split(turn_ref[...]), axis=0)


def follow(carry_ref, rates_ref, state_ref):
    tile = state_ref.shape[1] // LANES
    sums = carry_ref[tile * NS :, :].astype(jnp.float32)
    sums = sums[:SUBLANES, :] + sums[SUBLANES:, :]
    for item in range(tile):
        lanes = slice(item * LANES, (item + 1) * LANES)
        decay = jnp.exp2(rates_ref[:, lanes] * sums[item : item + 1, :])
        added = carry_ref[item * NS : (item + 1) * NS, :].astype(jnp.float32)
        state_ref[:, lanes] = decay * state_ref[:, lanes] + added
    return sums


def scan_blocks(stream_ref, steps_ref, maps, rates_ref, gain_ref, out_ref, state_ref, work_refs):
    out_of_ref, *hist_refs = work_refs
    rows, width = steps_ref.shape
    source = lax.broadcasted_iota(jnp.int32, (LANES, NS * NS), 0)
    column = lax.rem(lax.broadcasted_iota(jnp.int32, (LANES, NS * NS), 1), NS)
    token = lax.rem(lax.broadcasted_iota(jnp.int32, (rows, NS * NS), 0), NS)
    slot = lax.broadcasted_iota(jnp.int32, (rows, NS * NS), 1) // NS
    turned = jnp.concatenate(
        [maps, jnp.zeros((LANES - 2 * NS, rows), jnp.float32)], axis=0
    ).T.astype(jnp.bfloat16)
    pick = jnp.where(source == NS + column, 1.0, 0.0).astype(jnp.bfloat16)
    spread = jnp.dot(turned, pick, preferred_element_type=jnp.float32)
    out_of_ref[...] = jnp.where(token == slot, spread, 0.0).astype(jnp.bfloat16)
    map_in = maps[:NS, :]
    half = width // 2

    def finish(first, hist_ref):
        here = pl.ds(first, NS)
        mixed = jnp.dot(out_of_ref[here, :], hist_ref[...], preferred_element_type=jnp.float32)
        direct = gain_ref[...] * stream_ref[0, here, :].astype(jnp.float32)
        out_ref[here, :] = (mixed + direct).astype(jnp.bfloat16)

    def advance(first, hist_ref):
        here = pl.ds(first, NS)
        into = pltpu.roll(map_in, lax.rem(rows - first, rows), 1)
        for lanes in (slice(0, half), slice(half, width)):
            state = state_ref[:, lanes]
            rates = rates_ref[:, lanes]
            steps = steps_ref[here, lanes].astype(jnp.float32)
            push = steps * stream_ref[0, here, lanes].astype(jnp.float32)
            for near in range(NS):
                this = slice(near, near + 1)
                state = jnp.exp2(rates * steps[this, :]) * state + into[:, this] * push[this, :]
                hist_ref[near * NS : (near + 1) * NS, lanes] = state.astype(jnp.bfloat16)
            state_ref[:, lanes] = state

    def at(group):
        return pl.multiple_of(group * NS, NS)

    def pair(index, nothing):
        finish(at(2 * index), hist_refs[1])
        advance(at(2 * index + 1), hist_refs[0])
        finish(at(2 * index + 1), hist_refs[0])
        advance(at(2 * index + 2), hist_refs[1])
        return nothing

    groups = rows // NS
    advance(0, hist_refs[1])
    lax.fori_loop(0, groups // 2 - 1, pair, 0)
    finish(rows - 2 * NS, hist_refs[1])
    advance(rows - NS, hist_refs[0])
    finish(rows - NS, hist_refs[0])


def work_shapes(rows, width):
    return [
        pltpu.VMEM((rows, NS * NS), jnp.bfloat16),
        pltpu.VMEM((NS * NS, width), jnp.bfloat16),
        pltpu.VMEM((NS * NS, width), jnp.bfloat16),
    ]


def own_kernel(
    place_ref, stream_ref, low_ref, map_ref, cols_ref, bias_ref, rates_ref, gain_ref,
    out_ref, sums_ref, maps_ref, state_ref, total_ref, steps_ref, *work_refs
):
    rows = steps_ref.shape[0]

    @pl.when(pl.program_id(0) == 0)
    def _():
        state_ref[...] = jnp.zeros_like(state_ref)
        total_ref[...] = jnp.zeros_like(total_ref)

    maps = map_ref[...].astype(jnp.float32)
    maps_ref[0] = maps
    logits = jnp.dot(low_ref[...], cols_ref[...], preferred_element_type=jnp.float32)
    steps = softplus(logits + bias_ref[...]).astype(jnp.bfloat16)
    steps_ref[...] = steps
    within = sums_within(steps)
    sums_ref[...] = within.astype(jnp.bfloat16)
    total_ref[...] = total_ref[...] + within[rows - 1 :, :]
    scan_blocks(stream_ref, steps_ref, maps, rates_ref, gain_ref, out_ref, state_ref, work_refs)


def scan_own(place, stream, lows, cols, bias, rates, gain):
    rows, width = stream.shape[1] // CORES, stream.shape[2]
    map_row = CORES * rows // MAPS

    blocks = lax.axis_size("seq")

    def in_row(b, s):
        return s[0] * CORES + b

    def fixed(*shape):
        return pl.BlockSpec(shape, lambda b, s: (0,) * len(shape))

    block = pl.BlockSpec((rows, width), lambda b, s: (in_row(b, s), 0))
    return pl.pallas_call(
        own_kernel,
        grid_spec=pltpu.PrefetchScalarGridSpec(
            num_scalar_prefetch=1,
            grid=(CORES,),
            in_specs=[
                pl.BlockSpec((1, rows, width), lambda b, s: (0, b, 0)),
                pl.BlockSpec((rows, RANK), lambda b, s: (b, 0)),
                pl.BlockSpec((MAPS, rows), lambda b, s: (map_row, b)),
                fixed(*cols.shape),
                fixed(*bias.shape),
                fixed(*rates.shape),
                fixed(*gain.shape),
            ],
            out_specs=[
                block,
                block,
                pl.BlockSpec((1, 2 * NS, rows), lambda b, s: (in_row(b, s), 0, 0)),
                fixed(NS, width),
                fixed(1, width),
            ],
            scratch_shapes=[pltpu.VMEM((rows, width), jnp.bfloat16)] + work_shapes(rows, width),
        ),
        out_shape=[
            jax.ShapeDtypeStruct((blocks * rows, width), jnp.bfloat16),
            jax.ShapeDtypeStruct((blocks * rows, width), jnp.bfloat16),
            jax.ShapeDtypeStruct((blocks, 2 * NS, rows), jnp.float32),
            jax.ShapeDtypeStruct((NS, width), jnp.float32),
            jax.ShapeDtypeStruct((1, width), jnp.float32),
        ],
        compiler_params=params,
        cost_estimate=pl.CostEstimate(flops=4 * 10**9, bytes_accessed=1 << 21, transcendentals=0),
        name="scan_own",
    )(place, stream, lows, lows, cols, bias, rates, gain)


def others_kernel(
    place_ref, stream_ref, steps_ref, maps_ref, rates_ref, gain_ref, part_ref, out_ref, last_ref,
    *work_refs
):
    del part_ref

    @pl.when(lax.rem(pl.program_id(0), CORES) == 0)
    def _():
        last_ref[...] = jnp.zeros_like(last_ref)

    scan_blocks(
        stream_ref, steps_ref, maps_ref[0], rates_ref, gain_ref, out_ref, last_ref.at[0], work_refs
    )


def scan_others(place, stream, steps, maps, rates, gain, part):
    others = stream.shape[0]
    chips = others + 1
    rows, width = stream.shape[1] // CORES, stream.shape[2]

    def slot(b, s):
        chip = b // CORES
        return lax.rem(s[0] - jnp.where(chip < s[0], chip, chip + 1) + chips, chips) - 1

    def in_row(b, s):
        return jnp.where(b // CORES < s[0], b, b + CORES)

    def fixed(*shape):
        return pl.BlockSpec(shape, lambda b, s: (0,) * len(shape))

    return pl.pallas_call(
        others_kernel,
        grid_spec=pltpu.PrefetchScalarGridSpec(
            num_scalar_prefetch=1,
            grid=(others * CORES,),
            in_specs=[
                pl.BlockSpec((1, rows, width), lambda b, s: (slot(b, s), lax.rem(b, CORES), 0)),
                pl.BlockSpec((rows, width), lambda b, s: (b, 0)),
                pl.BlockSpec((1, 2 * NS, rows), lambda b, s: (in_row(b, s), 0, 0)),
                fixed(*rates.shape),
                fixed(*gain.shape),
                pl.BlockSpec(memory_space=pl.ANY),
            ],
            out_specs=[
                pl.BlockSpec((rows, width), lambda b, s: (in_row(b, s), 0)),
                pl.BlockSpec((1, NS, width), lambda b, s: (b // CORES, 0, 0)),
            ],
            scratch_shapes=work_shapes(rows, width),
        ),
        out_shape=[
            jax.ShapeDtypeStruct(part.shape, part.dtype),
            jax.ShapeDtypeStruct((others, NS, width), jnp.float32),
        ],
        input_output_aliases={6: 0},
        compiler_params=params,
        cost_estimate=pl.CostEstimate(flops=4 * 10**9, bytes_accessed=1 << 21, transcendentals=0),
        name="scan_others",
    )(place, stream, steps, maps, rates, gain, part)


def carried_kernel(
    place_ref, part_ref, sums_ref, maps_ref, last_own_ref, last_come_ref, rates_ref, carries_ref,
    out_ref, state_ref, wide_ref, begin_ref, spread_ref,
):
    block = pl.program_id(0)
    rows, width = out_ref.shape
    chip = block // CORES

    @pl.when(block == 0)
    def _():
        state_ref[...] = jnp.zeros_like(state_ref)

        def compose(row, nothing):
            follow(carries_ref.at[row], rates_ref, state_ref)
            return nothing

        lax.fori_loop(0, lax.axis_index("chan"), compose, 0)
        for n in range(NS):
            wide_ref[n * NS : (n + 1) * NS, :] = jnp.broadcast_to(
                rates_ref[n : n + 1, :], (NS, width)
            ).astype(jnp.bfloat16)

    @pl.when((block > 0) & (lax.rem(block, CORES) == 0))
    def _():
        before = jnp.where(chip - 1 == place_ref[0], last_own_ref[...], last_come_ref[0])
        state_ref[...] = state_ref[...] + before

    state = state_ref[...]
    for n in range(NS):
        begin_ref[n * NS : (n + 1) * NS, :] = jnp.broadcast_to(
            state[n : n + 1, :], (NS, width)
        ).astype(jnp.bfloat16)
    maps = jnp.concatenate([maps_ref[0], jnp.zeros((LANES - 2 * NS, rows), jnp.float32)], axis=0).T
    for n in range(NS):
        spread_ref[:, n * LANES : (n + 1) * LANES] = jnp.broadcast_to(
            maps[:, NS + n : NS + n + 1], (rows, LANES)
        ).astype(jnp.bfloat16)
    last = sums_ref[rows - NS :, :].astype(jnp.float32)[NS - 1 :, :]
    state_ref[...] = jnp.exp2(rates_ref[...] * last) * state
    chunk, several = CORES * LANES, 4

    def some(index, nothing):
        near = pl.ds(pl.multiple_of(index * NS, NS), NS)
        for item in range(width // chunk):
            lanes = slice(item * chunk, (item + 1) * chunk)
            total = part_ref[near, lanes].astype(jnp.float32)
            sums = sums_ref[near, lanes]
            for first in range(0, NS, several):
                terms = []
                for n in range(first, first + several):
                    decay = jnp.exp2(sums * wide_ref[n * NS : (n + 1) * NS, lanes])
                    out_of = spread_ref[near, n * LANES : (n + 1) * LANES]
                    out_of = jnp.concatenate([out_of] * (chunk // LANES), axis=1)
                    terms.append(decay * begin_ref[n * NS : (n + 1) * NS, lanes] * out_of)
                four = (terms[0] + terms[1]) + (terms[2] + terms[3])
                total = total + four.astype(jnp.float32)
            out_ref[near, lanes] = total.astype(jnp.bfloat16)
        return nothing

    lax.fori_loop(0, rows // NS, some, 0)


def add_carried(place, part, sums, maps, lasts, rates, carries):
    blocks, _, rows = maps.shape
    others = lasts[1].shape[0]
    width = rates.shape[1]

    def before(b, s):
        chip = jnp.maximum(b // CORES - 1, 0)
        return jnp.minimum(jnp.where(chip < s[0], chip, jnp.maximum(chip - 1, 0)), others - 1)

    def fixed(*shape):
        return pl.BlockSpec(shape, lambda b, s: (0,) * len(shape))

    block = pl.BlockSpec((rows, width), lambda b, s: (b, 0))
    return pl.pallas_call(
        carried_kernel,
        grid_spec=pltpu.PrefetchScalarGridSpec(
            num_scalar_prefetch=1,
            grid=(blocks,),
            in_specs=[
                block,
                block,
                pl.BlockSpec((1, 2 * NS, rows), lambda b, s: (b, 0, 0)),
                fixed(NS, width),
                pl.BlockSpec((1, NS, width), lambda b, s: (before(b, s), 0, 0)),
                fixed(*rates.shape),
                fixed(*carries.shape),
            ],
            out_specs=block,
            scratch_shapes=[
                pltpu.VMEM((NS, width), jnp.float32),
                pltpu.VMEM((NS * NS, width), jnp.bfloat16),
                pltpu.VMEM((NS * NS, width), jnp.bfloat16),
                pltpu.VMEM((rows, NS * LANES), jnp.bfloat16),
            ],
        ),
        out_shape=jax.ShapeDtypeStruct(part.shape, jnp.bfloat16),
        compiler_params=params,
        name="add_carried",
    )(place, part, sums, maps, *lasts, rates, carries)


def local(
    queries, keys, values, doc_lengths, rank_in, bc_weight, rank_out, dt_bias, a_log, skip_gain
):
    devices = lax.axis_size("seq")
    chips = devices // CORES
    targets = lax.axis_size("chan")
    seq_place = lax.axis_index("seq").astype(jnp.int32)
    chip, core = seq_place // CORES, lax.rem(seq_place, CORES)
    place = jnp.stack([chip, core])
    width = queries.shape[2] // devices
    wide = max(HEAD_SIZE, keys.shape[2] // devices)

    def other(device):
        return device + 1 - 2 * (device % CORES)

    swap = [(device, other(device)) for device in range(devices)]
    near = [(device, device + CORES) for device in range(devices - CORES)]
    far = [(device, other(device + CORES)) for device in range(devices - CORES)]

    def onward(chips_on):
        return [(device, (device + chips_on * CORES) % devices) for device in range(devices)]

    own, theirs = select_heads(keys[0], values[0], chips, wide)
    from_near = lax.ppermute(own, "seq", near)
    from_far = lax.ppermute(theirs, "seq", far)
    swapped = lax.ppermute(theirs, "seq", swap)
    queries_after, _ = lax.optimization_barrier((queries[0], own))
    their_queries = lax.ppermute(queries_after, "seq", swap)
    blocks = (own, swapped, from_near, from_far)

    first = seq_place * width
    logs = lax.dynamic_slice_in_dim(a_log, first, width, 0)
    rates = (-LOG2E * jnp.exp(logs)).T
    cols = lax.dynamic_slice_in_dim(rank_out, first, width, 1)
    bias = lax.dynamic_slice_in_dim(dt_bias, first, width, 0)[None]
    gain = lax.dynamic_slice_in_dim(skip_gain, first, width, 0)[None]

    sent, stayed, part = attend(
        place, doc_lengths, (queries[0], their_queries), blocks, rank_in, bc_weight.T,
        (rates, cols, bias, gain),
    )
    come = [lax.ppermute(sent[step], "seq", onward(step + 1)) for step in range(chips - 1)]
    low_own = low_and_maps(part, lax.ppermute(part, "seq", swap))
    low_come = [lax.ppermute(low_own, "seq", onward(step + 1)) for step in range(chips - 1)]
    got_sent = lax.ppermute(sent, "seq", swap)
    got_stayed = lax.ppermute(stayed, "seq", swap)
    *come, got_stayed = lax.optimization_barrier((*come, got_stayed))
    attn_rows = join_heads(sent, stayed, got_sent, got_stayed)

    part, sums, maps, state, total = scan_own(place, stayed, low_own, cols, bias, rates, gain)
    come, low_come = jnp.stack(come), jnp.stack(low_come)
    steps, sums, maps, carry = step_sizes(
        place, come, low_come, cols, bias, rates, state, total, targets, attn_rows, sums, maps
    )
    carries = lax.all_to_all(carry, "chan", split_axis=0, concat_axis=0, tiled=True)
    part, last_come = scan_others(place, come, steps, maps, rates, gain, part)
    ssm_rows = add_carried(place, part, sums, maps, (state, last_come), rates, carries)
    return (attn_rows[None], ssm_rows[None])


def solution(mesh):
    return jax.shard_map(
        local,
        mesh=mesh,
        in_specs=(
            P("chan", "seq", None),
            P("chan", "seq", None),
            P("chan", "seq", None),
            P("chan", None),
            P(),
            P(),
            P(),
            P(),
            P(),
            P(),
        ),
        out_specs=(P("chan", "seq", None), P("chan", None, "seq")),
        check_vma=False,
    )
```

```python
import functools
import math

import jax
import jax.numpy as jnp
from jax import lax
from jax.experimental import pallas as pl
from jax.experimental.pallas import tpu as pltpu
from jax.sharding import PartitionSpec as P

QUERY_HEADS = 32
KEY_VALUE_HEADS = 8
HEAD_SIZE = 128
GROUP = QUERY_HEADS // KEY_VALUE_HEADS
NS = 16
RANK = 256
CORES = 2
LANES = 128
SUBLANES = 8
MAPS = 2 * NS
LOG2E = 1.4426950408889634

masked_fill = -1e30
params = pltpu.CompilerParams(vmem_limit_bytes=60 << 20)
less = pltpu.CompilerParams(vmem_limit_bytes=16 << 20)


def split(value):
    coarse = value.astype(jnp.bfloat16)
    return coarse, (value - coarse.astype(jnp.float32)).astype(jnp.bfloat16)


def run_copies(pairs, sems):
    copies = [
        pltpu.make_async_copy(source, target, sems.at[i]) for i, (source, target) in enumerate(pairs)
    ]
    for copy in copies:
        copy.start()
    for copy in copies:
        copy.wait()


def columns_of(ref, index, size):
    return ref.at[:, pl.ds(pl.multiple_of(index * size, LANES), size)]


def heads_kernel(key_ref, value_ref, own_ref, their_ref, sems):
    core = lax.rem(lax.axis_index("seq"), CORES)
    wide = own_ref.shape[3]
    halves = key_ref.shape[1] // wide // own_ref.shape[0]
    pairs = []
    for target, which in ((own_ref, core), (their_ref, 1 - core)):
        for chip in range(own_ref.shape[0]):
            index = chip * halves + (which if halves == CORES else 0)
            for kind, source in enumerate((key_ref, value_ref)):
                pairs.append((columns_of(source, index, wide), target.at[chip, kind]))
    run_copies(pairs, sems)


def select_heads(keys, values, chips, wide):
    shape = jax.ShapeDtypeStruct((chips, 2, keys.shape[0], wide), keys.dtype)
    return pl.pallas_call(
        heads_kernel,
        in_specs=[pl.BlockSpec(memory_space=pl.ANY)] * 2,
        out_shape=[shape, shape],
        scratch_shapes=[pltpu.SemaphoreType.DMA((4 * chips,))],
        compiler_params=params,
        name="select_heads",
    )(keys, values)


def join_kernel(sent_ref, stayed_ref, got_sent_ref, got_stayed_ref, out_ref, sems):
    place = lax.axis_index("seq")
    core, chip = lax.rem(place, CORES), place // CORES
    rows = out_ref.shape[0]
    others, _, width = sent_ref.shape
    here = pl.ds(pl.multiple_of(core * rows, rows), rows)
    pairs = []
    for first, rest, which in (
        (stayed_ref, sent_ref, core), (got_stayed_ref, got_sent_ref, 1 - core)
    ):
        for step in range(others + 1):
            source = first.at[0, here, :] if step == 0 else rest.at[step - 1, here, :]
            owner = lax.rem(chip + step, others + 1)
            pairs.append((source, columns_of(out_ref, owner * CORES + which, width)))
    run_copies(pairs, sems)


def join_heads(sent, stayed, got_sent, got_stayed):
    others, rows, width = sent.shape
    return pl.pallas_call(
        join_kernel,
        in_specs=[pl.BlockSpec(memory_space=pl.ANY)] * 4,
        out_shape=jax.ShapeDtypeStruct(
            (rows // CORES, (others + 1) * CORES * width), sent.dtype
        ),
        scratch_shapes=[pltpu.SemaphoreType.DMA((CORES * (others + 1),))],
        compiler_params=less,
        name="join_heads",
    )(sent, stayed, got_sent, got_stayed)


def attend_kernel(
    place_ref, doc_ref, mine_ref, theirs_ref, own_ref, swap_ref, near_ref, far_ref,
    rank_ref, map_ref, *rest, chips,
):
    send_ref, stay_ref, part_ref, mask_ref = rest[-4:]
    step = pl.program_id(0)
    rows = mine_ref.shape[0]
    group = mine_ref.shape[1] // HEAD_SIZE
    chip, core = place_ref[0], place_ref[1]
    first_core = core == 0

    def below(shape):
        column = lax.rem(lax.broadcasted_iota(jnp.int32, shape, 1), rows)
        return lax.broadcasted_iota(jnp.int32, shape, 0) > column

    @pl.when(step == 0)
    def _():
        part_ref[...] = jnp.zeros_like(part_ref)
        own = chip * CORES + core
        swapped = chip * CORES + 1 - core
        near, far = own - CORES, swapped - CORES
        query = lax.broadcasted_iota(jnp.int32, (rows, rows), 1)
        key = lax.broadcasted_iota(jnp.int32, (rows, rows), 0)
        for item, (place, before, middle) in enumerate(
            (
                (own, near, jnp.where(first_core, far, swapped)),
                (swapped, far, jnp.where(first_core, own, near)),
            )
        ):
            query_pos = place * rows + query
            start = jnp.zeros((rows, rows), jnp.int32)
            bound = jnp.int32(0)
            for doc in range(doc_ref.shape[1]):
                bound = bound + doc_ref[0, doc]
                start = jnp.where(query_pos >= bound, bound, start)
            ends = jnp.where(key > query, before, place) * rows + key
            mask_ref[item, :rows, :] = jnp.where(
                (ends >= start) & (ends <= query_pos), 0.0, masked_fill
            )
            mask_ref[item, rows:, :] = jnp.where(
                middle * rows + key >= start, 0.0, masked_fill
            )

    scale = LOG2E / math.sqrt(HEAD_SIZE)

    def windows(kind):
        own, swapped = own_ref[0, kind], swap_ref[0, kind]
        near, far = near_ref[0, kind], far_ref[0, kind]
        return (
            jnp.concatenate([near, own, jnp.where(first_core, far, swapped)], axis=0),
            jnp.concatenate([far, swapped, jnp.where(first_core, own, near)], axis=0),
        )

    scores = []
    for keys, query in zip(windows(0), (mine_ref[...], theirs_ref[...])):
        stacked = jnp.concatenate(
            [query[:, i * HEAD_SIZE : (i + 1) * HEAD_SIZE] for i in range(group)], axis=0
        )
        scores.append(
            lax.dot_general(
                keys, stacked, (((1,), (1,)), ((), ())), preferred_element_type=jnp.float32
            )
        )
    outputs = []
    before = below((rows, group * rows))
    none = jnp.zeros((rows, group * rows), jnp.bfloat16)
    for item, (values, score) in enumerate(zip(windows(1), scores)):
        fill = mask_ref[item]
        ends = jnp.where(before, score[:rows, :], score[rows : 2 * rows, :])
        kept = jnp.concatenate([ends, score[2 * rows :, :]], axis=0)
        kept = kept + jnp.concatenate([fill] * group, axis=1)
        peak = jnp.max(kept, axis=0, keepdims=True)
        raw = jnp.exp2((kept - peak) * scale)
        share = pl.reciprocal(jnp.sum(raw, axis=0, keepdims=True))
        raw = raw.astype(jnp.bfloat16)
        ends = raw[:rows, :]
        spread = jnp.concatenate(
            [jnp.where(before, ends, none), jnp.where(before, none, ends), raw[rows:, :]], axis=0
        )
        mixed = lax.dot_general(
            values, spread, (((0,), (0,)), ((), ())), preferred_element_type=jnp.float32
        )
        mixed = mixed * share
        outputs.append(
            jnp.concatenate(
                [mixed[:, i * rows : (i + 1) * rows].T.astype(jnp.bfloat16) for i in range(group)],
                axis=1,
            )
        )
    stream = jnp.concatenate(
        [
            jnp.where(first_core, outputs[0], outputs[1]),
            jnp.where(first_core, outputs[1], outputs[0]),
        ],
        axis=0,
    )
    last = step >= pl.num_programs(0) - pl.num_programs(0) // chips

    @pl.when(last)
    def _():
        stay_ref[0] = stream

    @pl.when(jnp.logical_not(last))
    def _():
        send_ref[0] = stream

    both = CORES * rows
    part_ref[:both, :] += jnp.dot(stream, rank_ref[...], preferred_element_type=jnp.float32)
    part_ref[both:, :] += lax.dot_general(
        map_ref[...], stream, (((1,), (1,)), ((), ())), preferred_element_type=jnp.float32
    )


def attend(place, doc_lengths, queries, blocks, rank_in, map_rows, after):
    mine, theirs = queries
    chips, _, rows, columns = blocks[0].shape
    heads = columns // HEAD_SIZE
    width = mine.shape[1] // (chips * CORES)
    wide = width // heads

    def owner(j, s):
        return lax.rem(s[0] + 1 + j // heads, chips)

    def column(j, s):
        return (owner(j, s) * CORES + s[1]) * heads + lax.rem(j, heads)

    def sent(j, s):
        at = jnp.minimum(j, (chips - 1) * heads - 1)
        return (at // heads, 0, lax.rem(at, heads))

    query = pl.BlockSpec((rows, wide), lambda j, s: (0, column(j, s)))
    block = pl.BlockSpec(
        (1, 2, rows, HEAD_SIZE), lambda j, s: (owner(j, s), 0, 0, lax.rem(j, heads))
    )
    return pl.pallas_call(
        functools.partial(attend_kernel, chips=chips),
        grid_spec=pltpu.PrefetchScalarGridSpec(
            num_scalar_prefetch=1,
            grid=(chips * heads,),
            in_specs=[pl.BlockSpec(memory_space=pltpu.SMEM), query, query]
            + [block] * 4
            + [
                pl.BlockSpec((wide, RANK), lambda j, s: (column(j, s), 0)),
                pl.BlockSpec((2 * NS, wide), lambda j, s: (0, column(j, s))),
            ]
            + [pl.BlockSpec(memory_space=pl.ANY)] * len(after),
            out_specs=[
                pl.BlockSpec((1, CORES * rows, wide), sent),
                pl.BlockSpec(
                    (1, CORES * rows, wide),
                    lambda j, s: (0, 0, jnp.maximum(j - (chips - 1) * heads, 0)),
                ),
                pl.BlockSpec((CORES * rows + 2 * NS, RANK), lambda j, s: (0, 0)),
            ],
            scratch_shapes=[pltpu.VMEM((2, 2 * rows, rows), jnp.float32)],
        ),
        out_shape=[
            jax.ShapeDtypeStruct((chips - 1, CORES * rows, width), jnp.bfloat16),
            jax.ShapeDtypeStruct((1, CORES * rows, width), jnp.bfloat16),
            jax.ShapeDtypeStruct((CORES * rows + 2 * NS, RANK), jnp.float32),
        ],
        compiler_params=params,
        cost_estimate=pl.CostEstimate(flops=5 * 10**9, bytes_accessed=1 << 22, transcendentals=0),
        name="attend",
    )(place, doc_lengths, mine, theirs, *blocks, rank_in, map_rows, *after)


def low_kernel(mine_ref, theirs_ref, out_ref):
    total = mine_ref[...] + theirs_ref[...].astype(jnp.float32)
    out_ref[...] = total.astype(jnp.bfloat16)


def low_and_maps(mine, theirs):
    return pl.pallas_call(
        low_kernel,
        out_shape=jax.ShapeDtypeStruct(mine.shape, jnp.bfloat16),
        compiler_params=less,
        cost_estimate=pl.CostEstimate(flops=1, bytes_accessed=1, transcendentals=0),
        name="low_and_maps",
    )(mine, theirs)


def softplus(value):
    small = jnp.exp(-jnp.abs(value))
    tail = jnp.where(small < 0.00390625, small * (1.0 - 0.5 * small), jnp.log(1.0 + small))
    return jnp.maximum(value, 0.0) + tail


def add_states(rates_ref, state_ref, total_ref, states, totals):
    state_ref[...] = jnp.exp2(rates_ref[...] * totals) * state_ref[...] + states
    total_ref[...] = total_ref[...] + totals


def sums_within(steps):
    rows = steps.shape[0]
    at = lax.broadcasted_iota(jnp.int32, (rows, rows), 0)
    of = lax.broadcasted_iota(jnp.int32, (rows, rows), 1)
    upto = jnp.where(of <= at, 1.0, 0.0).astype(jnp.bfloat16)
    return jnp.dot(upto, steps, preferred_element_type=jnp.float32)


def step_kernel(
    place_ref, stream_ref, low_ref, map_ref, cols_ref, bias_ref, rates_ref, *rest
):
    own_state_ref, own_total_ref = rest[:2]
    steps_ref, sums_ref, maps_ref, carry_ref, state_ref, total_ref, wide_ref, turn_ref = rest[5:]
    block = pl.program_id(0)
    rows, width = stream_ref.shape[1:]

    @pl.when(block == 0)
    def _():
        state_ref[...] = jnp.zeros_like(state_ref)
        total_ref[...] = jnp.zeros_like(total_ref)
        for n in range(NS):
            wide_ref[n * NS : (n + 1) * NS, :] = jnp.broadcast_to(
                rates_ref[n : n + 1, :], (NS, width)
            ).astype(jnp.bfloat16)

    @pl.when(block == place_ref[0] * CORES)
    def _():
        add_states(rates_ref, state_ref, total_ref, own_state_ref[...], own_total_ref[...])

    maps = map_ref[0].astype(jnp.float32)
    maps_ref[0] = maps
    logits = jnp.dot(low_ref[0], cols_ref[...], preferred_element_type=jnp.float32)
    steps = softplus(logits + bias_ref[...]).astype(jnp.bfloat16)
    steps_ref[...] = steps
    push = steps * stream_ref[0]
    within = sums_within(steps)
    sums_ref[...] = within.astype(jnp.bfloat16)
    whole = within[rows - 1 :, :]
    left = (whole - within).astype(jnp.bfloat16)
    some, chunk, several = rows // 2, CORES * LANES, 4
    state_row = lax.broadcasted_iota(jnp.int32, (NS, some), 0)
    for first in range(0, rows, some):
        span = slice(first, first + some)
        chosen = [
            jnp.concatenate(
                [
                    jnp.where(state_row == m, maps[:NS, span], 0.0).astype(jnp.bfloat16)
                    for m in range(n, n + several)
                ],
                axis=1,
            )
            for n in range(0, NS, several)
        ]
        for item in range(width // chunk):
            lanes = slice(item * chunk, (item + 1) * chunk)
            left_here = left[span, lanes].reshape(some // NS, NS, chunk)
            push_here = push[span, lanes].reshape(some // NS, NS, chunk)
            added = state_ref[:, lanes]
            if first == 0:
                added = jnp.exp2(rates_ref[:, lanes] * whole[:, lanes]) * added
            for n in range(0, NS, several):
                pushed = []
                for m in range(n, n + several):
                    decay = jnp.exp2(left_here * wide_ref[m * NS : (m + 1) * NS, lanes][None])
                    pushed.append((decay * push_here).reshape(some, chunk))
                added = added + jnp.dot(
                    chosen[n // several],
                    jnp.concatenate(pushed, axis=0),
                    preferred_element_type=jnp.float32,
                )
            state_ref[:, lanes] = added
    total_ref[...] = total_ref[...] + whole

    count = pl.num_programs(0)

    @pl.when(block == count - 1)
    def _():
        @pl.when(place_ref[0] * CORES == count)
        def _():
            add_states(rates_ref, state_ref, total_ref, own_state_ref[...], own_total_ref[...])

        write_carry(carry_ref.at[0], state_ref[...], total_ref[...], turn_ref)
        for target in range(1, carry_ref.shape[0]):
            carry_ref[target] = carry_ref[0]


def step_sizes(place, stream, lows, cols, bias, rates, state, total, targets, after, sums, maps):
    others = stream.shape[0]
    chips = others + 1
    rows, width = stream.shape[1] // CORES, stream.shape[2]
    map_row = CORES * rows // MAPS
    blocks = others * CORES
    carry = (targets, (width // LANES + 1) * NS, LANES)

    def slot(b, s):
        chip = b // CORES
        return lax.rem(s[0] - jnp.where(chip < s[0], chip, chip + 1) + chips, chips) - 1

    def core(b):
        return lax.rem(b, CORES)

    def in_row(b, s):
        return jnp.where(b // CORES < s[0], b, b + CORES)

    def fixed(*shape):
        return pl.BlockSpec(shape, lambda b, s: (0,) * len(shape))

    return pl.pallas_call(
        step_kernel,
        grid_spec=pltpu.PrefetchScalarGridSpec(
            num_scalar_prefetch=1,
            grid=(blocks,),
            in_specs=[
                pl.BlockSpec((1, rows, width), lambda b, s: (slot(b, s), core(b), 0)),
                pl.BlockSpec((1, rows, RANK), lambda b, s: (slot(b, s), core(b), 0)),
                pl.BlockSpec((1, MAPS, rows), lambda b, s: (slot(b, s), map_row, core(b))),
                fixed(*cols.shape),
                fixed(*bias.shape),
                fixed(*rates.shape),
                fixed(*state.shape),
                fixed(*total.shape),
            ]
            + [pl.BlockSpec(memory_space=pl.ANY)] * 3,
            out_specs=[
                pl.BlockSpec((rows, width), lambda b, s: (b, 0)),
                pl.BlockSpec((rows, width), lambda b, s: (in_row(b, s), 0)),
                pl.BlockSpec((1, 2 * NS, rows), lambda b, s: (in_row(b, s), 0, 0)),
                fixed(*carry),
            ],
            scratch_shapes=[
                pltpu.VMEM((NS, width), jnp.float32),
                pltpu.VMEM((1, width), jnp.float32),
                pltpu.VMEM((NS * NS, width), jnp.bfloat16),
                pltpu.VMEM((SUBLANES, LANES), jnp.float32),
            ],
        ),
        out_shape=[
            jax.ShapeDtypeStruct((blocks * rows, width), jnp.bfloat16),
            jax.ShapeDtypeStruct(sums.shape, sums.dtype),
            jax.ShapeDtypeStruct(maps.shape, maps.dtype),
            jax.ShapeDtypeStruct(carry, jnp.bfloat16),
        ],
        input_output_aliases={10: 1, 11: 2},
        compiler_params=params,
        name="step_sizes",
    )(place, stream, lows, lows, cols, bias, rates, state, total, after, sums, maps)


def write_carry(out_ref, state, total, turn_ref):
    tile = state.shape[1] // LANES
    turn_ref[...] = jnp.zeros_like(turn_ref)
    for item in range(tile):
        lanes = slice(item * LANES, (item + 1) * LANES)
        turn_ref[item : item + 1, :] = total[:, lanes]
        out_ref[item * NS : (item + 1) * NS, :] = state[:, lanes].astype(jnp.bfloat16)
    out_ref[tile * NS :, :] = jnp.concatenate(split(turn_ref[...]), axis=0)


def follow(carry_ref, rates_ref, state_ref):
    tile = state_ref.shape[1] // LANES
    sums = carry_ref[tile * NS :, :].astype(jnp.float32)
    sums = sums[:SUBLANES, :] + sums[SUBLANES:, :]
    for item in range(tile):
        lanes = slice(item * LANES, (item + 1) * LANES)
        decay = jnp.exp2(rates_ref[:, lanes] * sums[item : item + 1, :])
        added = carry_ref[item * NS : (item + 1) * NS, :].astype(jnp.float32)
        state_ref[:, lanes] = decay * state_ref[:, lanes] + added
    return sums


def scan_blocks(stream_ref, steps_ref, maps, rates_ref, gain_ref, out_ref, state_ref, work_refs):
    out_of_ref, *hist_refs = work_refs
    rows, width = steps_ref.shape
    source = lax.broadcasted_iota(jnp.int32, (LANES, NS * NS), 0)
    column = lax.rem(lax.broadcasted_iota(jnp.int32, (LANES, NS * NS), 1), NS)
    token = lax.rem(lax.broadcasted_iota(jnp.int32, (rows, NS * NS), 0), NS)
    slot = lax.broadcasted_iota(jnp.int32, (rows, NS * NS), 1) // NS
    turned = jnp.concatenate(
        [maps, jnp.zeros((LANES - 2 * NS, rows), jnp.float32)], axis=0
    ).T.astype(jnp.bfloat16)
    pick = jnp.where(source == NS + column, 1.0, 0.0).astype(jnp.bfloat16)
    spread = jnp.dot(turned, pick, preferred_element_type=jnp.float32)
    out_of_ref[...] = jnp.where(token == slot, spread, 0.0).astype(jnp.bfloat16)
    map_in = maps[:NS, :]
    half = width // 2

    def finish(first, hist_ref):
        here = pl.ds(first, NS)
        mixed = jnp.dot(out_of_ref[here, :], hist_ref[...], preferred_element_type=jnp.float32)
        direct = gain_ref[...] * stream_ref[0, here, :].astype(jnp.float32)
        out_ref[here, :] = (mixed + direct).astype(jnp.bfloat16)

    def advance(first, hist_ref):
        here = pl.ds(first, NS)
        into = pltpu.roll(map_in, lax.rem(rows - first, rows), 1)
        for lanes in (slice(0, half), slice(half, width)):
            state = state_ref[:, lanes]
            rates = rates_ref[:, lanes]
            steps = steps_ref[here, lanes].astype(jnp.float32)
            push = steps * stream_ref[0, here, lanes].astype(jnp.float32)
            for near in range(NS):
                this = slice(near, near + 1)
                state = jnp.exp2(rates * steps[this, :]) * state + into[:, this] * push[this, :]
                hist_ref[near * NS : (near + 1) * NS, lanes] = state.astype(jnp.bfloat16)
            state_ref[:, lanes] = state

    def at(group):
        return pl.multiple_of(group * NS, NS)

    def pair(index, nothing):
        finish(at(2 * index), hist_refs[1])
        advance(at(2 * index + 1), hist_refs[0])
        finish(at(2 * index + 1), hist_refs[0])
        advance(at(2 * index + 2), hist_refs[1])
        return nothing

    groups = rows // NS
    advance(0, hist_refs[1])
    lax.fori_loop(0, groups // 2 - 1, pair, 0)
    finish(rows - 2 * NS, hist_refs[1])
    advance(rows - NS, hist_refs[0])
    finish(rows - NS, hist_refs[0])


def work_shapes(rows, width):
    return [
        pltpu.VMEM((rows, NS * NS), jnp.bfloat16),
        pltpu.VMEM((NS * NS, width), jnp.bfloat16),
        pltpu.VMEM((NS * NS, width), jnp.bfloat16),
    ]


def own_kernel(
    place_ref, stream_ref, low_ref, map_ref, cols_ref, bias_ref, rates_ref, gain_ref,
    out_ref, sums_ref, maps_ref, state_ref, total_ref, steps_ref, *work_refs
):
    rows = steps_ref.shape[0]

    @pl.when(pl.program_id(0) == 0)
    def _():
        state_ref[...] = jnp.zeros_like(state_ref)
        total_ref[...] = jnp.zeros_like(total_ref)

    maps = map_ref[...].astype(jnp.float32)
    maps_ref[0] = maps
    logits = jnp.dot(low_ref[...], cols_ref[...], preferred_element_type=jnp.float32)
    steps = softplus(logits + bias_ref[...]).astype(jnp.bfloat16)
    steps_ref[...] = steps
    within = sums_within(steps)
    sums_ref[...] = within.astype(jnp.bfloat16)
    total_ref[...] = total_ref[...] + within[rows - 1 :, :]
    scan_blocks(stream_ref, steps_ref, maps, rates_ref, gain_ref, out_ref, state_ref, work_refs)


def scan_own(place, stream, lows, cols, bias, rates, gain):
    rows, width = stream.shape[1] // CORES, stream.shape[2]
    map_row = CORES * rows // MAPS

    blocks = lax.axis_size("seq")

    def in_row(b, s):
        return s[0] * CORES + b

    def fixed(*shape):
        return pl.BlockSpec(shape, lambda b, s: (0,) * len(shape))

    block = pl.BlockSpec((rows, width), lambda b, s: (in_row(b, s), 0))
    return pl.pallas_call(
        own_kernel,
        grid_spec=pltpu.PrefetchScalarGridSpec(
            num_scalar_prefetch=1,
            grid=(CORES,),
            in_specs=[
                pl.BlockSpec((1, rows, width), lambda b, s: (0, b, 0)),
                pl.BlockSpec((rows, RANK), lambda b, s: (b, 0)),
                pl.BlockSpec((MAPS, rows), lambda b, s: (map_row, b)),
                fixed(*cols.shape),
                fixed(*bias.shape),
                fixed(*rates.shape),
                fixed(*gain.shape),
            ],
            out_specs=[
                block,
                block,
                pl.BlockSpec((1, 2 * NS, rows), lambda b, s: (in_row(b, s), 0, 0)),
                fixed(NS, width),
                fixed(1, width),
            ],
            scratch_shapes=[pltpu.VMEM((rows, width), jnp.bfloat16)] + work_shapes(rows, width),
        ),
        out_shape=[
            jax.ShapeDtypeStruct((blocks * rows, width), jnp.bfloat16),
            jax.ShapeDtypeStruct((blocks * rows, width), jnp.bfloat16),
            jax.ShapeDtypeStruct((blocks, 2 * NS, rows), jnp.float32),
            jax.ShapeDtypeStruct((NS, width), jnp.float32),
            jax.ShapeDtypeStruct((1, width), jnp.float32),
        ],
        compiler_params=params,
        cost_estimate=pl.CostEstimate(flops=4 * 10**9, bytes_accessed=1 << 21, transcendentals=0),
        name="scan_own",
    )(place, stream, lows, lows, cols, bias, rates, gain)


def others_kernel(
    place_ref, stream_ref, steps_ref, maps_ref, rates_ref, gain_ref, part_ref, out_ref, last_ref,
    *work_refs
):
    del part_ref

    @pl.when(lax.rem(pl.program_id(0), CORES) == 0)
    def _():
        last_ref[...] = jnp.zeros_like(last_ref)

    scan_blocks(
        stream_ref, steps_ref, maps_ref[0], rates_ref, gain_ref, out_ref, last_ref.at[0], work_refs
    )


def scan_others(place, stream, steps, maps, rates, gain, part):
    others = stream.shape[0]
    chips = others + 1
    rows, width = stream.shape[1] // CORES, stream.shape[2]

    def slot(b, s):
        chip = b // CORES
        return lax.rem(s[0] - jnp.where(chip < s[0], chip, chip + 1) + chips, chips) - 1

    def in_row(b, s):
        return jnp.where(b // CORES < s[0], b, b + CORES)

    def fixed(*shape):
        return pl.BlockSpec(shape, lambda b, s: (0,) * len(shape))

    return pl.pallas_call(
        others_kernel,
        grid_spec=pltpu.PrefetchScalarGridSpec(
            num_scalar_prefetch=1,
            grid=(others * CORES,),
            in_specs=[
                pl.BlockSpec((1, rows, width), lambda b, s: (slot(b, s), lax.rem(b, CORES), 0)),
                pl.BlockSpec((rows, width), lambda b, s: (b, 0)),
                pl.BlockSpec((1, 2 * NS, rows), lambda b, s: (in_row(b, s), 0, 0)),
                fixed(*rates.shape),
                fixed(*gain.shape),
                pl.BlockSpec(memory_space=pl.ANY),
            ],
            out_specs=[
                pl.BlockSpec((rows, width), lambda b, s: (in_row(b, s), 0)),
                pl.BlockSpec((1, NS, width), lambda b, s: (b // CORES, 0, 0)),
            ],
            scratch_shapes=work_shapes(rows, width),
        ),
        out_shape=[
            jax.ShapeDtypeStruct(part.shape, part.dtype),
            jax.ShapeDtypeStruct((others, NS, width), jnp.float32),
        ],
        input_output_aliases={6: 0},
        compiler_params=params,
        cost_estimate=pl.CostEstimate(flops=4 * 10**9, bytes_accessed=1 << 21, transcendentals=0),
        name="scan_others",
    )(place, stream, steps, maps, rates, gain, part)


def carried_kernel(
    place_ref, part_ref, sums_ref, maps_ref, last_own_ref, last_come_ref, rates_ref, carries_ref,
    out_ref, state_ref, wide_ref, begin_ref, spread_ref,
):
    block = pl.program_id(0)
    rows, width = out_ref.shape
    chip = block // CORES

    @pl.when(block == 0)
    def _():
        state_ref[...] = jnp.zeros_like(state_ref)

        def compose(row, nothing):
            follow(carries_ref.at[row], rates_ref, state_ref)
            return nothing

        lax.fori_loop(0, lax.axis_index("chan"), compose, 0)
        for n in range(NS):
            wide_ref[n * NS : (n + 1) * NS, :] = jnp.broadcast_to(
                rates_ref[n : n + 1, :], (NS, width)
            ).astype(jnp.bfloat16)

    @pl.when((block > 0) & (lax.rem(block, CORES) == 0))
    def _():
        before = jnp.where(chip - 1 == place_ref[0], last_own_ref[...], last_come_ref[0])
        state_ref[...] = state_ref[...] + before

    state = state_ref[...]
    for n in range(NS):
        begin_ref[n * NS : (n + 1) * NS, :] = jnp.broadcast_to(
            state[n : n + 1, :], (NS, width)
        ).astype(jnp.bfloat16)
    maps = jnp.concatenate([maps_ref[0], jnp.zeros((LANES - 2 * NS, rows), jnp.float32)], axis=0).T
    for n in range(NS):
        spread_ref[:, n * LANES : (n + 1) * LANES] = jnp.broadcast_to(
            maps[:, NS + n : NS + n + 1], (rows, LANES)
        ).astype(jnp.bfloat16)
    last = sums_ref[rows - NS :, :].astype(jnp.float32)[NS - 1 :, :]
    state_ref[...] = jnp.exp2(rates_ref[...] * last) * state
    chunk, several = CORES * LANES, 4

    def some(index, nothing):
        near = pl.ds(pl.multiple_of(index * NS, NS), NS)
        for item in range(width // chunk):
            lanes = slice(item * chunk, (item + 1) * chunk)
            total = part_ref[near, lanes].astype(jnp.float32)
            sums = sums_ref[near, lanes]
            for first in range(0, NS, several):
                terms = []
                for n in range(first, first + several):
                    decay = jnp.exp2(sums * wide_ref[n * NS : (n + 1) * NS, lanes])
                    out_of = spread_ref[near, n * LANES : (n + 1) * LANES]
                    out_of = jnp.concatenate([out_of] * (chunk // LANES), axis=1)
                    terms.append(decay * begin_ref[n * NS : (n + 1) * NS, lanes] * out_of)
                four = (terms[0] + terms[1]) + (terms[2] + terms[3])
                total = total + four.astype(jnp.float32)
            out_ref[near, lanes] = total.astype(jnp.bfloat16)
        return nothing

    lax.fori_loop(0, rows // NS, some, 0)


def add_carried(place, part, sums, maps, lasts, rates, carries):
    blocks, _, rows = maps.shape
    others = lasts[1].shape[0]
    width = rates.shape[1]

    def before(b, s):
        chip = jnp.maximum(b // CORES - 1, 0)
        return jnp.minimum(jnp.where(chip < s[0], chip, jnp.maximum(chip - 1, 0)), others - 1)

    def fixed(*shape):
        return pl.BlockSpec(shape, lambda b, s: (0,) * len(shape))

    block = pl.BlockSpec((rows, width), lambda b, s: (b, 0))
    return pl.pallas_call(
        carried_kernel,
        grid_spec=pltpu.PrefetchScalarGridSpec(
            num_scalar_prefetch=1,
            grid=(blocks,),
            in_specs=[
                block,
                block,
                pl.BlockSpec((1, 2 * NS, rows), lambda b, s: (b, 0, 0)),
                fixed(NS, width),
                pl.BlockSpec((1, NS, width), lambda b, s: (before(b, s), 0, 0)),
                fixed(*rates.shape),
                fixed(*carries.shape),
            ],
            out_specs=block,
            scratch_shapes=[
                pltpu.VMEM((NS, width), jnp.float32),
                pltpu.VMEM((NS * NS, width), jnp.bfloat16),
                pltpu.VMEM((NS * NS, width), jnp.bfloat16),
                pltpu.VMEM((rows, NS * LANES), jnp.bfloat16),
            ],
        ),
        out_shape=jax.ShapeDtypeStruct(part.shape, jnp.bfloat16),
        compiler_params=params,
        name="add_carried",
    )(place, part, sums, maps, *lasts, rates, carries)


def local(
    queries, keys, values, doc_lengths, rank_in, bc_weight, rank_out, dt_bias, a_log, skip_gain
):
    devices = lax.axis_size("seq")
    chips = devices // CORES
    targets = lax.axis_size("chan")
    seq_place = lax.axis_index("seq").astype(jnp.int32)
    chip, core = seq_place // CORES, lax.rem(seq_place, CORES)
    place = jnp.stack([chip, core])
    width = queries.shape[2] // devices
    wide = max(HEAD_SIZE, keys.shape[2] // devices)

    def other(device):
        return device + 1 - 2 * (device % CORES)

    swap = [(device, other(device)) for device in range(devices)]
    near = [(device, device + CORES) for device in range(devices - CORES)]
    far = [(device, other(device + CORES)) for device in range(devices - CORES)]

    def onward(chips_on):
        return [(device, (device + chips_on * CORES) % devices) for device in range(devices)]

    own, theirs = select_heads(keys[0], values[0], chips, wide)
    from_near = lax.ppermute(own, "seq", near)
    from_far = lax.ppermute(theirs, "seq", far)
    swapped = lax.ppermute(theirs, "seq", swap)
    queries_after, _ = lax.optimization_barrier((queries[0], own))
    their_queries = lax.ppermute(queries_after, "seq", swap)
    blocks = (own, swapped, from_near, from_far)

    first = seq_place * width
    logs = lax.dynamic_slice_in_dim(a_log, first, width, 0)
    rates = (-LOG2E * jnp.exp(logs)).T
    cols = lax.dynamic_slice_in_dim(rank_out, first, width, 1)
    bias = lax.dynamic_slice_in_dim(dt_bias, first, width, 0)[None]
    gain = lax.dynamic_slice_in_dim(skip_gain, first, width, 0)[None]

    sent, stayed, part = attend(
        place, doc_lengths, (queries[0], their_queries), blocks, rank_in, bc_weight.T,
        (rates, cols, bias, gain),
    )
    come = [lax.ppermute(sent[step], "seq", onward(step + 1)) for step in range(chips - 1)]
    low_own = low_and_maps(part, lax.ppermute(part.astype(jnp.bfloat16), "seq", swap))
    low_come = [lax.ppermute(low_own, "seq", onward(step + 1)) for step in range(chips - 1)]
    got_sent = lax.ppermute(sent, "seq", swap)
    got_stayed = lax.ppermute(stayed, "seq", swap)
    *come, got_stayed = lax.optimization_barrier((*come, got_stayed))
    attn_rows = join_heads(sent, stayed, got_sent, got_stayed)

    part, sums, maps, state, total = scan_own(place, stayed, low_own, cols, bias, rates, gain)
    come, low_come = jnp.stack(come), jnp.stack(low_come)
    steps, sums, maps, carry = step_sizes(
        place, come, low_come, cols, bias, rates, state, total, targets, attn_rows, sums, maps
    )
    carries = lax.all_to_all(carry, "chan", split_axis=0, concat_axis=0, tiled=True)
    part, last_come = scan_others(place, come, steps, maps, rates, gain, part)
    ssm_rows = add_carried(place, part, sums, maps, (state, last_come), rates, carries)
    return (attn_rows[None], ssm_rows[None])


def solution(mesh):
    return jax.shard_map(
        local,
        mesh=mesh,
        in_specs=(
            P("chan", "seq", None),
            P("chan", "seq", None),
            P("chan", "seq", None),
            P("chan", None),
            P(),
            P(),
            P(),
            P(),
            P(),
            P(),
        ),
        out_specs=(P("chan", "seq", None), P("chan", None, "seq")),
        check_vma=False,
    )
```

```python
import functools
import math

import jax
import jax.numpy as jnp
from jax import lax
from jax.experimental import pallas as pl
from jax.experimental.pallas import tpu as pltpu
from jax.sharding import PartitionSpec as P

QUERY_HEADS = 32
KEY_VALUE_HEADS = 8
HEAD_SIZE = 128
GROUP = QUERY_HEADS // KEY_VALUE_HEADS
NS = 16
RANK = 256
CORES = 2
LANES = 128
SUBLANES = 8
MAPS = 2 * NS
LOG2E = 1.4426950408889634

masked_fill = -1e30
params = pltpu.CompilerParams(vmem_limit_bytes=60 << 20)
less = pltpu.CompilerParams(vmem_limit_bytes=16 << 20)


def split(value):
    coarse = value.astype(jnp.bfloat16)
    return coarse, (value - coarse.astype(jnp.float32)).astype(jnp.bfloat16)


def run_copies(pairs, sems):
    copies = [
        pltpu.make_async_copy(source, target, sems.at[i]) for i, (source, target) in enumerate(pairs)
    ]
    for copy in copies:
        copy.start()
    for copy in copies:
        copy.wait()


def columns_of(ref, index, size):
    return ref.at[:, pl.ds(pl.multiple_of(index * size, LANES), size)]


def heads_kernel(key_ref, value_ref, own_ref, their_ref, sems):
    core = lax.rem(lax.axis_index("seq"), CORES)
    wide = own_ref.shape[3]
    halves = key_ref.shape[1] // wide // own_ref.shape[0]
    pairs = []
    for target, which in ((own_ref, core), (their_ref, 1 - core)):
        for chip in range(own_ref.shape[0]):
            index = chip * halves + (which if halves == CORES else 0)
            for kind, source in enumerate((key_ref, value_ref)):
                pairs.append((columns_of(source, index, wide), target.at[chip, kind]))
    run_copies(pairs, sems)


def select_heads(keys, values, chips, wide):
    shape = jax.ShapeDtypeStruct((chips, 2, keys.shape[0], wide), keys.dtype)
    return pl.pallas_call(
        heads_kernel,
        in_specs=[pl.BlockSpec(memory_space=pl.ANY)] * 2,
        out_shape=[shape, shape],
        scratch_shapes=[pltpu.SemaphoreType.DMA((4 * chips,))],
        compiler_params=params,
        name="select_heads",
    )(keys, values)


def join_kernel(sent_ref, stayed_ref, got_sent_ref, got_stayed_ref, out_ref, sems):
    place = lax.axis_index("seq")
    core, chip = lax.rem(place, CORES), place // CORES
    rows = out_ref.shape[0]
    others, _, width = sent_ref.shape
    here = pl.ds(pl.multiple_of(core * rows, rows), rows)
    pairs = []
    for first, rest, which in (
        (stayed_ref, sent_ref, core), (got_stayed_ref, got_sent_ref, 1 - core)
    ):
        for step in range(others + 1):
            source = first.at[0, here, :] if step == 0 else rest.at[step - 1, here, :]
            owner = lax.rem(chip + step, others + 1)
            pairs.append((source, columns_of(out_ref, owner * CORES + which, width)))
    run_copies(pairs, sems)


def join_heads(sent, stayed, got_sent, got_stayed):
    others, rows, width = sent.shape
    return pl.pallas_call(
        join_kernel,
        in_specs=[pl.BlockSpec(memory_space=pl.ANY)] * 4,
        out_shape=jax.ShapeDtypeStruct(
            (rows // CORES, (others + 1) * CORES * width), sent.dtype
        ),
        scratch_shapes=[pltpu.SemaphoreType.DMA((CORES * (others + 1),))],
        compiler_params=less,
        name="join_heads",
    )(sent, stayed, got_sent, got_stayed)


def attend_kernel(
    place_ref, doc_ref, mine_ref, theirs_ref, own_ref, swap_ref, near_ref, far_ref,
    rank_ref, map_ref, *rest, chips,
):
    send_ref, stay_ref, part_ref, mask_ref = rest[-4:]
    step = pl.program_id(0)
    rows = mine_ref.shape[0]
    group = mine_ref.shape[1] // HEAD_SIZE
    chip, core = place_ref[0], place_ref[1]
    first_core = core == 0

    def below(shape):
        column = lax.rem(lax.broadcasted_iota(jnp.int32, shape, 1), rows)
        return lax.broadcasted_iota(jnp.int32, shape, 0) > column

    @pl.when(step == 0)
    def _():
        part_ref[...] = jnp.zeros_like(part_ref)
        own = chip * CORES + core
        swapped = chip * CORES + 1 - core
        near, far = own - CORES, swapped - CORES
        query = lax.broadcasted_iota(jnp.int32, (rows, rows), 1)
        key = lax.broadcasted_iota(jnp.int32, (rows, rows), 0)
        for item, (place, before, middle) in enumerate(
            (
                (own, near, jnp.where(first_core, far, swapped)),
                (swapped, far, jnp.where(first_core, own, near)),
            )
        ):
            query_pos = place * rows + query
            start = jnp.zeros((rows, rows), jnp.int32)
            bound = jnp.int32(0)
            for doc in range(doc_ref.shape[1]):
                bound = bound + doc_ref[0, doc]
                start = jnp.where(query_pos >= bound, bound, start)
            ends = jnp.where(key > query, before, place) * rows + key
            mask_ref[item, :rows, :] = jnp.where(
                (ends >= start) & (ends <= query_pos), 0.0, masked_fill
            )
            mask_ref[item, rows:, :] = jnp.where(
                middle * rows + key >= start, 0.0, masked_fill
            )

    scale = LOG2E / math.sqrt(HEAD_SIZE)

    def windows(kind):
        own, swapped = own_ref[0, kind], swap_ref[0, kind]
        near, far = near_ref[0, kind], far_ref[0, kind]
        return (
            jnp.concatenate([near, own, jnp.where(first_core, far, swapped)], axis=0),
            jnp.concatenate([far, swapped, jnp.where(first_core, own, near)], axis=0),
        )

    scores = []
    for keys, query in zip(windows(0), (mine_ref[...], theirs_ref[...])):
        stacked = jnp.concatenate(
            [query[:, i * HEAD_SIZE : (i + 1) * HEAD_SIZE] for i in range(group)], axis=0
        )
        scores.append(
            lax.dot_general(
                keys, stacked, (((1,), (1,)), ((), ())), preferred_element_type=jnp.float32
            )
        )
    outputs = []
    before = below((rows, group * rows))
    none = jnp.zeros((rows, group * rows), jnp.bfloat16)
    for item, (values, score) in enumerate(zip(windows(1), scores)):
        fill = mask_ref[item]
        ends = jnp.where(before, score[:rows, :], score[rows : 2 * rows, :])
        kept = jnp.concatenate([ends, score[2 * rows :, :]], axis=0)
        kept = kept + jnp.concatenate([fill] * group, axis=1)
        peak = jnp.max(kept, axis=0, keepdims=True)
        raw = jnp.exp2((kept - peak) * scale)
        share = pl.reciprocal(jnp.sum(raw, axis=0, keepdims=True))
        raw = raw.astype(jnp.bfloat16)
        ends = raw[:rows, :]
        spread = jnp.concatenate(
            [jnp.where(before, ends, none), jnp.where(before, none, ends), raw[rows:, :]], axis=0
        )
        mixed = lax.dot_general(
            values, spread, (((0,), (0,)), ((), ())), preferred_element_type=jnp.float32
        )
        mixed = mixed * share
        outputs.append(
            jnp.concatenate(
                [mixed[:, i * rows : (i + 1) * rows].T.astype(jnp.bfloat16) for i in range(group)],
                axis=1,
            )
        )
    stream = jnp.concatenate(
        [
            jnp.where(first_core, outputs[0], outputs[1]),
            jnp.where(first_core, outputs[1], outputs[0]),
        ],
        axis=0,
    )
    last = step >= pl.num_programs(0) - pl.num_programs(0) // chips

    @pl.when(last)
    def _():
        stay_ref[0] = stream

    @pl.when(jnp.logical_not(last))
    def _():
        send_ref[0] = stream

    both = CORES * rows
    part_ref[:both, :] += jnp.dot(stream, rank_ref[...], preferred_element_type=jnp.float32)
    part_ref[both:, :] += lax.dot_general(
        map_ref[...], stream, (((1,), (1,)), ((), ())), preferred_element_type=jnp.float32
    )


def attend(place, doc_lengths, queries, blocks, rank_in, map_rows, after):
    mine, theirs = queries
    chips, _, rows, columns = blocks[0].shape
    heads = columns // HEAD_SIZE
    width = mine.shape[1] // (chips * CORES)
    wide = width // heads

    def owner(j, s):
        return lax.rem(s[0] + 1 + j // heads, chips)

    def column(j, s):
        return (owner(j, s) * CORES + s[1]) * heads + lax.rem(j, heads)

    def sent(j, s):
        at = jnp.minimum(j, (chips - 1) * heads - 1)
        return (at // heads, 0, lax.rem(at, heads))

    query = pl.BlockSpec((rows, wide), lambda j, s: (0, column(j, s)))
    block = pl.BlockSpec(
        (1, 2, rows, HEAD_SIZE), lambda j, s: (owner(j, s), 0, 0, lax.rem(j, heads))
    )
    return pl.pallas_call(
        functools.partial(attend_kernel, chips=chips),
        grid_spec=pltpu.PrefetchScalarGridSpec(
            num_scalar_prefetch=1,
            grid=(chips * heads,),
            in_specs=[pl.BlockSpec(memory_space=pltpu.SMEM), query, query]
            + [block] * 4
            + [
                pl.BlockSpec((wide, RANK), lambda j, s: (column(j, s), 0)),
                pl.BlockSpec((2 * NS, wide), lambda j, s: (0, column(j, s))),
            ]
            + [pl.BlockSpec(memory_space=pl.ANY)] * len(after),
            out_specs=[
                pl.BlockSpec((1, CORES * rows, wide), sent),
                pl.BlockSpec(
                    (1, CORES * rows, wide),
                    lambda j, s: (0, 0, jnp.maximum(j - (chips - 1) * heads, 0)),
                ),
                pl.BlockSpec((CORES * rows + 2 * NS, RANK), lambda j, s: (0, 0)),
            ],
            scratch_shapes=[pltpu.VMEM((2, 2 * rows, rows), jnp.float32)],
        ),
        out_shape=[
            jax.ShapeDtypeStruct((chips - 1, CORES * rows, width), jnp.bfloat16),
            jax.ShapeDtypeStruct((1, CORES * rows, width), jnp.bfloat16),
            jax.ShapeDtypeStruct((CORES * rows + 2 * NS, RANK), jnp.float32),
        ],
        compiler_params=params,
        cost_estimate=pl.CostEstimate(flops=5 * 10**9, bytes_accessed=1 << 22, transcendentals=0),
        name="attend",
    )(place, doc_lengths, mine, theirs, *blocks, rank_in, map_rows, *after)


def low_kernel(mine_ref, theirs_ref, out_ref):
    out_ref[...] = (mine_ref[...] + theirs_ref[...]).astype(jnp.bfloat16)


def low_and_maps(mine, theirs):
    return pl.pallas_call(
        low_kernel,
        out_shape=jax.ShapeDtypeStruct(mine.shape, jnp.bfloat16),
        compiler_params=params,
        cost_estimate=pl.CostEstimate(flops=1, bytes_accessed=1, transcendentals=0),
        name="low_and_maps",
    )(mine, theirs)


def softplus(value):
    small = jnp.exp(-jnp.abs(value))
    tail = jnp.where(small < 0.00390625, small * (1.0 - 0.5 * small), jnp.log(1.0 + small))
    return jnp.maximum(value, 0.0) + tail


def add_states(rates_ref, state_ref, total_ref, states, totals):
    state_ref[...] = jnp.exp2(rates_ref[...] * totals) * state_ref[...] + states
    total_ref[...] = total_ref[...] + totals


def sums_within(steps):
    rows = steps.shape[0]
    at = lax.broadcasted_iota(jnp.int32, (rows, rows), 0)
    of = lax.broadcasted_iota(jnp.int32, (rows, rows), 1)
    upto = jnp.where(of <= at, 1.0, 0.0).astype(jnp.bfloat16)
    return jnp.dot(upto, steps, preferred_element_type=jnp.float32)


def step_kernel(
    place_ref, stream_ref, low_ref, map_ref, cols_ref, bias_ref, rates_ref, *rest
):
    own_state_ref, own_total_ref = rest[:2]
    steps_ref, sums_ref, maps_ref, carry_ref, state_ref, total_ref, wide_ref, turn_ref = rest[5:]
    block = pl.program_id(0)
    rows, width = stream_ref.shape[1:]

    @pl.when(block == 0)
    def _():
        state_ref[...] = jnp.zeros_like(state_ref)
        total_ref[...] = jnp.zeros_like(total_ref)
        for n in range(NS):
            wide_ref[n * NS : (n + 1) * NS, :] = jnp.broadcast_to(
                rates_ref[n : n + 1, :], (NS, width)
            ).astype(jnp.bfloat16)

    @pl.when(block == place_ref[0] * CORES)
    def _():
        add_states(rates_ref, state_ref, total_ref, own_state_ref[...], own_total_ref[...])

    maps = map_ref[0].astype(jnp.float32)
    maps_ref[0] = maps
    logits = jnp.dot(low_ref[0], cols_ref[...], preferred_element_type=jnp.float32)
    steps = softplus(logits + bias_ref[...]).astype(jnp.bfloat16)
    steps_ref[...] = steps
    push = steps * stream_ref[0]
    within = sums_within(steps)
    sums_ref[...] = within.astype(jnp.bfloat16)
    whole = within[rows - 1 :, :]
    left = (whole - within).astype(jnp.bfloat16)
    some, chunk, several = rows // 2, CORES * LANES, 4
    state_row = lax.broadcasted_iota(jnp.int32, (NS, some), 0)
    for first in range(0, rows, some):
        span = slice(first, first + some)
        chosen = [
            jnp.concatenate(
                [
                    jnp.where(state_row == m, maps[:NS, span], 0.0).astype(jnp.bfloat16)
                    for m in range(n, n + several)
                ],
                axis=1,
            )
            for n in range(0, NS, several)
        ]
        for item in range(width // chunk):
            lanes = slice(item * chunk, (item + 1) * chunk)
            left_here = left[span, lanes].reshape(some // NS, NS, chunk)
            push_here = push[span, lanes].reshape(some // NS, NS, chunk)
            added = state_ref[:, lanes]
            if first == 0:
                added = jnp.exp2(rates_ref[:, lanes] * whole[:, lanes]) * added
            for n in range(0, NS, several):
                pushed = []
                for m in range(n, n + several):
                    decay = jnp.exp2(left_here * wide_ref[m * NS : (m + 1) * NS, lanes][None])
                    pushed.append((decay * push_here).reshape(some, chunk))
                added = added + jnp.dot(
                    chosen[n // several],
                    jnp.concatenate(pushed, axis=0),
                    preferred_element_type=jnp.float32,
                )
            state_ref[:, lanes] = added
    total_ref[...] = total_ref[...] + whole

    count = pl.num_programs(0)

    @pl.when(block == count - 1)
    def _():
        @pl.when(place_ref[0] * CORES == count)
        def _():
            add_states(rates_ref, state_ref, total_ref, own_state_ref[...], own_total_ref[...])

        write_carry(carry_ref.at[0], state_ref[...], total_ref[...], turn_ref)
        for target in range(1, carry_ref.shape[0]):
            carry_ref[target] = carry_ref[0]


def step_sizes(place, stream, lows, cols, bias, rates, state, total, targets, after, sums, maps):
    others = stream.shape[0]
    chips = others + 1
    rows, width = stream.shape[1] // CORES, stream.shape[2]
    map_row = CORES * rows // MAPS
    blocks = others * CORES
    carry = (targets, (width // LANES + 1) * NS, LANES)

    def slot(b, s):
        chip = b // CORES
        return lax.rem(s[0] - jnp.where(chip < s[0], chip, chip + 1) + chips, chips) - 1

    def core(b):
        return lax.rem(b, CORES)

    def in_row(b, s):
        return jnp.where(b // CORES < s[0], b, b + CORES)

    def fixed(*shape):
        return pl.BlockSpec(shape, lambda b, s: (0,) * len(shape))

    return pl.pallas_call(
        step_kernel,
        grid_spec=pltpu.PrefetchScalarGridSpec(
            num_scalar_prefetch=1,
            grid=(blocks,),
            in_specs=[
                pl.BlockSpec((1, rows, width), lambda b, s: (slot(b, s), core(b), 0)),
                pl.BlockSpec((1, rows, RANK), lambda b, s: (slot(b, s), core(b), 0)),
                pl.BlockSpec((1, MAPS, rows), lambda b, s: (slot(b, s), map_row, core(b))),
                fixed(*cols.shape),
                fixed(*bias.shape),
                fixed(*rates.shape),
                fixed(*state.shape),
                fixed(*total.shape),
            ]
            + [pl.BlockSpec(memory_space=pl.ANY)] * 3,
            out_specs=[
                pl.BlockSpec((rows, width), lambda b, s: (b, 0)),
                pl.BlockSpec((rows, width), lambda b, s: (in_row(b, s), 0)),
                pl.BlockSpec((1, 2 * NS, rows), lambda b, s: (in_row(b, s), 0, 0)),
                fixed(*carry),
            ],
            scratch_shapes=[
                pltpu.VMEM((NS, width), jnp.float32),
                pltpu.VMEM((1, width), jnp.float32),
                pltpu.VMEM((NS * NS, width), jnp.bfloat16),
                pltpu.VMEM((SUBLANES, LANES), jnp.float32),
            ],
        ),
        out_shape=[
            jax.ShapeDtypeStruct((blocks * rows, width), jnp.bfloat16),
            jax.ShapeDtypeStruct(sums.shape, sums.dtype),
            jax.ShapeDtypeStruct(maps.shape, maps.dtype),
            jax.ShapeDtypeStruct(carry, jnp.bfloat16),
        ],
        input_output_aliases={10: 1, 11: 2},
        compiler_params=params,
        name="step_sizes",
    )(place, stream, lows, lows, cols, bias, rates, state, total, after, sums, maps)


def write_carry(out_ref, state, total, turn_ref):
    tile = state.shape[1] // LANES
    turn_ref[...] = jnp.zeros_like(turn_ref)
    for item in range(tile):
        lanes = slice(item * LANES, (item + 1) * LANES)
        turn_ref[item : item + 1, :] = total[:, lanes]
        out_ref[item * NS : (item + 1) * NS, :] = state[:, lanes].astype(jnp.bfloat16)
    out_ref[tile * NS :, :] = jnp.concatenate(split(turn_ref[...]), axis=0)


def follow(carry_ref, rates_ref, state_ref):
    tile = state_ref.shape[1] // LANES
    sums = carry_ref[tile * NS :, :].astype(jnp.float32)
    sums = sums[:SUBLANES, :] + sums[SUBLANES:, :]
    for item in range(tile):
        lanes = slice(item * LANES, (item + 1) * LANES)
        decay = jnp.exp2(rates_ref[:, lanes] * sums[item : item + 1, :])
        added = carry_ref[item * NS : (item + 1) * NS, :].astype(jnp.float32)
        state_ref[:, lanes] = decay * state_ref[:, lanes] + added
    return sums


def scan_blocks(stream_ref, steps_ref, maps, rates_ref, gain_ref, out_ref, state_ref, work_refs):
    out_of_ref, *hist_refs = work_refs
    rows, width = steps_ref.shape
    source = lax.broadcasted_iota(jnp.int32, (LANES, NS * NS), 0)
    column = lax.rem(lax.broadcasted_iota(jnp.int32, (LANES, NS * NS), 1), NS)
    token = lax.rem(lax.broadcasted_iota(jnp.int32, (rows, NS * NS), 0), NS)
    slot = lax.broadcasted_iota(jnp.int32, (rows, NS * NS), 1) // NS
    turned = jnp.concatenate(
        [maps, jnp.zeros((LANES - 2 * NS, rows), jnp.float32)], axis=0
    ).T.astype(jnp.bfloat16)
    pick = jnp.where(source == NS + column, 1.0, 0.0).astype(jnp.bfloat16)
    spread = jnp.dot(turned, pick, preferred_element_type=jnp.float32)
    out_of_ref[...] = jnp.where(token == slot, spread, 0.0).astype(jnp.bfloat16)
    map_in = maps[:NS, :]
    half = width // 2

    def finish(first, hist_ref):
        here = pl.ds(first, NS)
        mixed = jnp.dot(out_of_ref[here, :], hist_ref[...], preferred_element_type=jnp.float32)
        direct = gain_ref[...] * stream_ref[0, here, :].astype(jnp.float32)
        out_ref[here, :] = (mixed + direct).astype(jnp.bfloat16)

    def advance(first, hist_ref):
        here = pl.ds(first, NS)
        into = pltpu.roll(map_in, lax.rem(rows - first, rows), 1)
        for lanes in (slice(0, half), slice(half, width)):
            state = state_ref[:, lanes]
            rates = rates_ref[:, lanes]
            steps = steps_ref[here, lanes].astype(jnp.float32)
            push = steps * stream_ref[0, here, lanes].astype(jnp.float32)
            for near in range(NS):
                this = slice(near, near + 1)
                state = jnp.exp2(rates * steps[this, :]) * state + into[:, this] * push[this, :]
                hist_ref[near * NS : (near + 1) * NS, lanes] = state.astype(jnp.bfloat16)
            state_ref[:, lanes] = state

    def at(group):
        return pl.multiple_of(group * NS, NS)

    def pair(index, nothing):
        finish(at(2 * index), hist_refs[1])
        advance(at(2 * index + 1), hist_refs[0])
        finish(at(2 * index + 1), hist_refs[0])
        advance(at(2 * index + 2), hist_refs[1])
        return nothing

    groups = rows // NS
    advance(0, hist_refs[1])
    lax.fori_loop(0, groups // 2 - 1, pair, 0)
    finish(rows - 2 * NS, hist_refs[1])
    advance(rows - NS, hist_refs[0])
    finish(rows - NS, hist_refs[0])


def work_shapes(rows, width):
    return [
        pltpu.VMEM((rows, NS * NS), jnp.bfloat16),
        pltpu.VMEM((NS * NS, width), jnp.bfloat16),
        pltpu.VMEM((NS * NS, width), jnp.bfloat16),
    ]


def own_kernel(
    place_ref, stream_ref, low_ref, map_ref, cols_ref, bias_ref, rates_ref, gain_ref,
    out_ref, sums_ref, maps_ref, state_ref, total_ref, steps_ref, *work_refs
):
    rows = steps_ref.shape[0]

    @pl.when(pl.program_id(0) == 0)
    def _():
        state_ref[...] = jnp.zeros_like(state_ref)
        total_ref[...] = jnp.zeros_like(total_ref)

    maps = map_ref[...].astype(jnp.float32)
    maps_ref[0] = maps
    logits = jnp.dot(low_ref[...], cols_ref[...], preferred_element_type=jnp.float32)
    steps = softplus(logits + bias_ref[...]).astype(jnp.bfloat16)
    steps_ref[...] = steps
    within = sums_within(steps)
    sums_ref[...] = within.astype(jnp.bfloat16)
    total_ref[...] = total_ref[...] + within[rows - 1 :, :]
    scan_blocks(stream_ref, steps_ref, maps, rates_ref, gain_ref, out_ref, state_ref, work_refs)


def scan_own(place, stream, lows, cols, bias, rates, gain):
    rows, width = stream.shape[1] // CORES, stream.shape[2]
    map_row = CORES * rows // MAPS

    blocks = lax.axis_size("seq")

    def in_row(b, s):
        return s[0] * CORES + b

    def fixed(*shape):
        return pl.BlockSpec(shape, lambda b, s: (0,) * len(shape))

    block = pl.BlockSpec((rows, width), lambda b, s: (in_row(b, s), 0))
    return pl.pallas_call(
        own_kernel,
        grid_spec=pltpu.PrefetchScalarGridSpec(
            num_scalar_prefetch=1,
            grid=(CORES,),
            in_specs=[
                pl.BlockSpec((1, rows, width), lambda b, s: (0, b, 0)),
                pl.BlockSpec((rows, RANK), lambda b, s: (b, 0)),
                pl.BlockSpec((MAPS, rows), lambda b, s: (map_row, b)),
                fixed(*cols.shape),
                fixed(*bias.shape),
                fixed(*rates.shape),
                fixed(*gain.shape),
            ],
            out_specs=[
                block,
                block,
                pl.BlockSpec((1, 2 * NS, rows), lambda b, s: (in_row(b, s), 0, 0)),
                fixed(NS, width),
                fixed(1, width),
            ],
            scratch_shapes=[pltpu.VMEM((rows, width), jnp.bfloat16)] + work_shapes(rows, width),
        ),
        out_shape=[
            jax.ShapeDtypeStruct((blocks * rows, width), jnp.bfloat16),
            jax.ShapeDtypeStruct((blocks * rows, width), jnp.bfloat16),
            jax.ShapeDtypeStruct((blocks, 2 * NS, rows), jnp.float32),
            jax.ShapeDtypeStruct((NS, width), jnp.float32),
            jax.ShapeDtypeStruct((1, width), jnp.float32),
        ],
        compiler_params=params,
        cost_estimate=pl.CostEstimate(flops=4 * 10**9, bytes_accessed=1 << 21, transcendentals=0),
        name="scan_own",
    )(place, stream, lows, lows, cols, bias, rates, gain)


def others_kernel(
    place_ref, stream_ref, steps_ref, maps_ref, rates_ref, gain_ref, part_ref, out_ref, last_ref,
    *work_refs
):
    del part_ref

    @pl.when(lax.rem(pl.program_id(0), CORES) == 0)
    def _():
        last_ref[...] = jnp.zeros_like(last_ref)

    scan_blocks(
        stream_ref, steps_ref, maps_ref[0], rates_ref, gain_ref, out_ref, last_ref.at[0], work_refs
    )


def scan_others(place, stream, steps, maps, rates, gain, part):
    others = stream.shape[0]
    chips = others + 1
    rows, width = stream.shape[1] // CORES, stream.shape[2]

    def slot(b, s):
        chip = b // CORES
        return lax.rem(s[0] - jnp.where(chip < s[0], chip, chip + 1) + chips, chips) - 1

    def in_row(b, s):
        return jnp.where(b // CORES < s[0], b, b + CORES)

    def fixed(*shape):
        return pl.BlockSpec(shape, lambda b, s: (0,) * len(shape))

    return pl.pallas_call(
        others_kernel,
        grid_spec=pltpu.PrefetchScalarGridSpec(
            num_scalar_prefetch=1,
            grid=(others * CORES,),
            in_specs=[
                pl.BlockSpec((1, rows, width), lambda b, s: (slot(b, s), lax.rem(b, CORES), 0)),
                pl.BlockSpec((rows, width), lambda b, s: (b, 0)),
                pl.BlockSpec((1, 2 * NS, rows), lambda b, s: (in_row(b, s), 0, 0)),
                fixed(*rates.shape),
                fixed(*gain.shape),
                pl.BlockSpec(memory_space=pl.ANY),
            ],
            out_specs=[
                pl.BlockSpec((rows, width), lambda b, s: (in_row(b, s), 0)),
                pl.BlockSpec((1, NS, width), lambda b, s: (b // CORES, 0, 0)),
            ],
            scratch_shapes=work_shapes(rows, width),
        ),
        out_shape=[
            jax.ShapeDtypeStruct(part.shape, part.dtype),
            jax.ShapeDtypeStruct((others, NS, width), jnp.float32),
        ],
        input_output_aliases={6: 0},
        compiler_params=params,
        cost_estimate=pl.CostEstimate(flops=4 * 10**9, bytes_accessed=1 << 21, transcendentals=0),
        name="scan_others",
    )(place, stream, steps, maps, rates, gain, part)


def carried_kernel(
    place_ref, part_ref, sums_ref, maps_ref, last_own_ref, last_come_ref, rates_ref, carries_ref,
    out_ref, state_ref, wide_ref, begin_ref, spread_ref,
):
    block = pl.program_id(0)
    rows, width = out_ref.shape
    chip = block // CORES

    @pl.when(block == 0)
    def _():
        state_ref[...] = jnp.zeros_like(state_ref)

        def compose(row, nothing):
            follow(carries_ref.at[row], rates_ref, state_ref)
            return nothing

        lax.fori_loop(0, lax.axis_index("chan"), compose, 0)
        for n in range(NS):
            wide_ref[n * NS : (n + 1) * NS, :] = jnp.broadcast_to(
                rates_ref[n : n + 1, :], (NS, width)
            ).astype(jnp.bfloat16)

    @pl.when((block > 0) & (lax.rem(block, CORES) == 0))
    def _():
        before = jnp.where(chip - 1 == place_ref[0], last_own_ref[...], last_come_ref[0])
        state_ref[...] = state_ref[...] + before

    state = state_ref[...]
    for n in range(NS):
        begin_ref[n * NS : (n + 1) * NS, :] = jnp.broadcast_to(
            state[n : n + 1, :], (NS, width)
        ).astype(jnp.bfloat16)
    maps = jnp.concatenate([maps_ref[0], jnp.zeros((LANES - 2 * NS, rows), jnp.float32)], axis=0).T
    for n in range(NS):
        spread_ref[:, n * LANES : (n + 1) * LANES] = jnp.broadcast_to(
            maps[:, NS + n : NS + n + 1], (rows, LANES)
        ).astype(jnp.bfloat16)
    last = sums_ref[rows - NS :, :].astype(jnp.float32)[NS - 1 :, :]
    state_ref[...] = jnp.exp2(rates_ref[...] * last) * state
    chunk, several = CORES * LANES, 8

    def some(index, nothing):
        near = pl.ds(pl.multiple_of(index * NS, NS), NS)
        for item in range(width // chunk):
            lanes = slice(item * chunk, (item + 1) * chunk)
            total = part_ref[near, lanes].astype(jnp.float32)
            sums = sums_ref[near, lanes]
            for first in range(0, NS, several):
                terms = []
                for n in range(first, first + several):
                    decay = jnp.exp2(sums * wide_ref[n * NS : (n + 1) * NS, lanes])
                    out_of = spread_ref[near, n * LANES : (n + 1) * LANES]
                    out_of = jnp.concatenate([out_of] * (chunk // LANES), axis=1)
                    terms.append(decay * begin_ref[n * NS : (n + 1) * NS, lanes] * out_of)
                while len(terms) > 1:
                    terms = [one + two for one, two in zip(terms[::2], terms[1::2])]
                total = total + terms[0].astype(jnp.float32)
            out_ref[near, lanes] = total.astype(jnp.bfloat16)
        return nothing

    lax.fori_loop(0, rows // NS, some, 0)


def add_carried(place, part, sums, maps, lasts, rates, carries):
    blocks, _, rows = maps.shape
    others = lasts[1].shape[0]
    width = rates.shape[1]

    def before(b, s):
        chip = jnp.maximum(b // CORES - 1, 0)
        return jnp.minimum(jnp.where(chip < s[0], chip, jnp.maximum(chip - 1, 0)), others - 1)

    def fixed(*shape):
        return pl.BlockSpec(shape, lambda b, s: (0,) * len(shape))

    block = pl.BlockSpec((rows, width), lambda b, s: (b, 0))
    return pl.pallas_call(
        carried_kernel,
        grid_spec=pltpu.PrefetchScalarGridSpec(
            num_scalar_prefetch=1,
            grid=(blocks,),
            in_specs=[
                block,
                block,
                pl.BlockSpec((1, 2 * NS, rows), lambda b, s: (b, 0, 0)),
                fixed(NS, width),
                pl.BlockSpec((1, NS, width), lambda b, s: (before(b, s), 0, 0)),
                fixed(*rates.shape),
                fixed(*carries.shape),
            ],
            out_specs=block,
            scratch_shapes=[
                pltpu.VMEM((NS, width), jnp.float32),
                pltpu.VMEM((NS * NS, width), jnp.bfloat16),
                pltpu.VMEM((NS * NS, width), jnp.bfloat16),
                pltpu.VMEM((rows, NS * LANES), jnp.bfloat16),
            ],
        ),
        out_shape=jax.ShapeDtypeStruct(part.shape, jnp.bfloat16),
        compiler_params=params,
        name="add_carried",
    )(place, part, sums, maps, *lasts, rates, carries)


def local(
    queries, keys, values, doc_lengths, rank_in, bc_weight, rank_out, dt_bias, a_log, skip_gain
):
    devices = lax.axis_size("seq")
    chips = devices // CORES
    targets = lax.axis_size("chan")
    seq_place = lax.axis_index("seq").astype(jnp.int32)
    chip, core = seq_place // CORES, lax.rem(seq_place, CORES)
    place = jnp.stack([chip, core])
    width = queries.shape[2] // devices
    wide = max(HEAD_SIZE, keys.shape[2] // devices)

    def other(device):
        return device + 1 - 2 * (device % CORES)

    swap = [(device, other(device)) for device in range(devices)]
    near = [(device, device + CORES) for device in range(devices - CORES)]
    far = [(device, other(device + CORES)) for device in range(devices - CORES)]

    def onward(chips_on):
        return [(device, (device + chips_on * CORES) % devices) for device in range(devices)]

    own, theirs = select_heads(keys[0], values[0], chips, wide)
    from_near = lax.ppermute(own, "seq", near)
    from_far = lax.ppermute(theirs, "seq", far)
    swapped = lax.ppermute(theirs, "seq", swap)
    queries_after, _ = lax.optimization_barrier((queries[0], own))
    their_queries = lax.ppermute(queries_after, "seq", swap)
    blocks = (own, swapped, from_near, from_far)

    first = seq_place * width
    logs = lax.dynamic_slice_in_dim(a_log, first, width, 0)
    rates = (-LOG2E * jnp.exp(logs)).T
    cols = lax.dynamic_slice_in_dim(rank_out, first, width, 1)
    bias = lax.dynamic_slice_in_dim(dt_bias, first, width, 0)[None]
    gain = lax.dynamic_slice_in_dim(skip_gain, first, width, 0)[None]

    sent, stayed, part = attend(
        place, doc_lengths, (queries[0], their_queries), blocks, rank_in, bc_weight.T,
        (rates, cols, bias, gain),
    )
    come = [lax.ppermute(sent[step], "seq", onward(step + 1)) for step in range(chips - 1)]
    low_own = low_and_maps(part, lax.ppermute(part, "seq", swap))
    low_come = [lax.ppermute(low_own, "seq", onward(step + 1)) for step in range(chips - 1)]
    got_sent = lax.ppermute(sent, "seq", swap)
    got_stayed = lax.ppermute(stayed, "seq", swap)
    *come, got_stayed = lax.optimization_barrier((*come, got_stayed))
    attn_rows = join_heads(sent, stayed, got_sent, got_stayed)

    part, sums, maps, state, total = scan_own(place, stayed, low_own, cols, bias, rates, gain)
    come, low_come = jnp.stack(come), jnp.stack(low_come)
    steps, sums, maps, carry = step_sizes(
        place, come, low_come, cols, bias, rates, state, total, targets, attn_rows, sums, maps
    )
    carries = lax.all_to_all(carry, "chan", split_axis=0, concat_axis=0, tiled=True)
    part, last_come = scan_others(place, come, steps, maps, rates, gain, part)
    ssm_rows = add_carried(place, part, sums, maps, (state, last_come), rates, carries)
    return (attn_rows[None], ssm_rows[None])


def solution(mesh):
    return jax.shard_map(
        local,
        mesh=mesh,
        in_specs=(
            P("chan", "seq", None),
            P("chan", "seq", None),
            P("chan", "seq", None),
            P("chan", None),
            P(),
            P(),
            P(),
            P(),
            P(),
            P(),
        ),
        out_specs=(P("chan", "seq", None), P("chan", None, "seq")),
        check_vma=False,
    )
```
